32 devices in a mesh: pipe: 2 (over y), dp: 4 (over z), tensor: 4 (over x, core).
Axes of the slice: x: 2, y: 2, z: 4, core: 2. Of those that a mesh axis runs over, the one named last changes fastest.
Arguments:
- acts_in: bfloat16 [8, 1024, 1024], P('dp', 'tensor'), may hold values from -6 to 6
- out_grad: bfloat16 [8, 1024, 1024], P('dp', 'tensor'), may hold values from -6 to 6
- mix_gain: bfloat16 [2, 1024], P('pipe', 'dp'), may hold values from 0.5 to 1.5
- w_mixer_in: bfloat16 [2, 1024, 2, 1536], P('pipe', 'dp', None, 'tensor'), may hold values from -0.1875 to 0.1875
- w_query: bfloat16 [2, 1024, 512], P('pipe', 'dp', 'tensor'), may hold values from -0.1875 to 0.1875
- w_shared: bfloat16 [2, 1024, 512], P('pipe', 'dp'), may hold values from -0.1875 to 0.1875
- w_step: bfloat16 [2, 1024, 24], P('pipe', 'dp'), may hold values from -0.1875 to 0.1875
- a_log: float32 [2, 24], P('pipe', 'tensor'), may hold values from 0 to 2.77
- dt_bias: float32 [2, 24], P('pipe', 'tensor'), may hold values from -7 to -2.3
- d_skip: float32 [2, 24], P('pipe', 'tensor'), may hold values from 0.5 to 1.5
- w_mamba_out: bfloat16 [2, 1536, 1024], P('pipe', 'tensor', 'dp'), may hold values from -0.3125 to 0.3125
- w_attn_out: bfloat16 [2, 512, 1024], P('pipe', 'tensor', 'dp'), may hold values from -1.5 to 1.5
- ffn_gain: bfloat16 [2, 1024], P('pipe', 'dp'), may hold values from 0.5 to 1.5
- w_gate_up: bfloat16 [2, 1024, 2, 2048], P('pipe', 'dp', None, 'tensor'), may hold values from -0.1875 to 0.1875
- w_down: bfloat16 [2, 2048, 1024], P('pipe', 'tensor', 'dp'), may hold values from -0.25 to 0.25
Outputs:
- acts_out: bfloat16 [2, 8, 1024, 1024], P('pipe', 'dp', 'tensor')
- in_grads: bfloat16 [2, 8, 1024, 1024], P('pipe', 'dp', 'tensor')
- grad_gains: float32 [2, 2, 1024], P('pipe', None, ('dp', 'tensor'))
- grad_mixer_in: float32 [2, 1024, 2, 1536], P('pipe', 'dp', None, 'tensor')
- grad_query: float32 [2, 1024, 512], P('pipe', 'dp', 'tensor')
- grad_shared: float32 [2, 1024, 512], P('pipe', ('dp', 'tensor'))
- grad_step: float32 [2, 1024, 24], P('pipe', ('dp', 'tensor'))
- grad_heads: float32 [2, 3, 24], P('pipe', None, 'tensor')
- grad_mamba_out: float32 [2, 1536, 1024], P('pipe', 'tensor', 'dp')
- grad_attn_out: float32 [2, 512, 1024], P('pipe', 'tensor', 'dp')
- grad_gate_up: float32 [2, 1024, 2, 2048], P('pipe', 'dp', None, 'tensor')
- grad_down: float32 [2, 2048, 1024], P('pipe', 'tensor', 'dp')
The draws below stay inside these ranges and needn't reach their ends.
All inputs are finite; a program needn't handle non-finite values.
Results may differ from the reference program's by a relative error of at most 0.04.
Values may be sent and summed in bfloat16 or wider, within the bound.
A program may use at most 256 MiB of HBM per device.

```python
import jax
import jax.numpy as jnp
from jax import lax

D = 1024
HM = 24
P_SIZE = 64
NS = 128
HA = 8
KVH = 2
HD = 64
FF = 2048
SEQ = 1024
BLOCK = 128
QBLOCK = 512
SEQS = 8
SHW = 512


def steps_of(stream_key, dims, cuts, smallest, top_value):
    gain, own = 1.0, jax.random.fold_in(stream_key, 6)
    for position, blocks in cuts:
        steps = jnp.exp(jax.random.uniform(jax.random.fold_in(own, position), (blocks,), jnp.float32, smallest / len(cuts), top_value / len(cuts)))
        gain = gain * jnp.repeat(steps, dims[position] // blocks).reshape([-1 if axis == position else 1 for axis in range(len(dims))])
    return gain


def gaussian(own_key, shape, width, bound, shards=(), held_as=jnp.bfloat16):
    factor_of = steps_of(own_key, shape, shards, -0.22, 0.18) if shards else 1.0
    entries = jax.random.normal(own_key, shape, jnp.float32) * width * factor_of
    return jnp.minimum(jnp.maximum(entries, -bound), bound).astype(held_as)


def setup_inputs(seed: int = 0) -> dict:
    key_list = jax.random.split(jax.random.key(seed), 16)
    acts_in = gaussian(key_list[0], (SEQS, SEQ, D), 1.0, 6.0, ((0, 4), (1, 4)))
    out_grad = gaussian(key_list[1], (SEQS, SEQ, D), 1.0, 6.0, ((0, 4), (1, 4)))
    mix_gain = jnp.clip(1.0 + 0.1 * jax.random.normal(key_list[2], (2, D), jnp.float32), 0.5, 1.5).astype(jnp.bfloat16)
    w_mixer_in = gaussian(key_list[3], (2, D, 2, HM * P_SIZE), D ** -0.5, 0.1875, ((0, 2), (1, 4), (3, 4)))
    w_query = gaussian(key_list[4], (2, D, HA * HD), D ** -0.5, 0.1875, ((0, 2), (1, 4), (2, 4)))
    w_shared = gaussian(key_list[5], (2, D, SHW), D ** -0.5, 0.1875, ((0, 2), (1, 4)))
    w_step = gaussian(key_list[6], (2, D, HM), D ** -0.5, 0.1875, ((0, 2), (1, 4)))
    a_log = jnp.clip(2.77 * jax.random.uniform(key_list[7], (2, HM), jnp.float32) ** steps_of(key_list[7], (2, HM), ((0, 2), (1, 4)), -0.2, 0.2), 0.0, 2.77)
    dt_bias = jnp.clip(-7.0 + 4.7 * jax.random.uniform(key_list[8], (2, HM), jnp.float32) ** steps_of(key_list[8], (2, HM), ((0, 2), (1, 4)), -0.2, 0.2), -7.0, -2.3)
    d_skip = jnp.clip(0.5 + 1.0 * jax.random.uniform(key_list[9], (2, HM), jnp.float32) ** steps_of(key_list[9], (2, HM), ((0, 2), (1, 4)), -0.2, 0.2), 0.5, 1.5)
    w_mamba_out = gaussian(key_list[10], (2, HM * P_SIZE, D), (HM * P_SIZE // 4) ** -0.5, 0.3125, ((0, 2), (1, 4), (2, 4)))
    w_attn_out = gaussian(key_list[11], (2, HA * HD, D), (HA * HD // 32) ** -0.5, 1.5, ((0, 2), (1, 4), (2, 4)))
    ffn_gain = jnp.clip(1.0 + 0.1 * jax.random.normal(key_list[12], (2, D), jnp.float32), 0.5, 1.5).astype(jnp.bfloat16)
    w_gate_up = gaussian(key_list[13], (2, D, 2, FF), D ** -0.5, 0.1875, ((0, 2), (1, 4), (3, 4)))
    w_down = gaussian(key_list[14], (2, FF, D), (FF // 4) ** -0.5, 0.25, ((0, 2), (1, 4), (2, 4)))
    return dict(acts_in=acts_in, out_grad=out_grad, mix_gain=mix_gain, w_mixer_in=w_mixer_in, w_query=w_query, w_shared=w_shared, w_step=w_step, a_log=a_log, dt_bias=dt_bias, d_skip=d_skip, w_mamba_out=w_mamba_out, w_attn_out=w_attn_out, ffn_gain=ffn_gain, w_gate_up=w_gate_up, w_down=w_down)


epsilon = 1e-05
highest = lax.Precision.HIGHEST

@jax.custom_vjp
def low(v):
    return lax.optimization_barrier(v.astype(jnp.bfloat16)).astype(jnp.float32)

@jax.custom_vjp
def low_back(v):
    return v

def low_keep(v):
    return (low(v), None)

def low_pass(kept, grad):
    return (grad,)

def back_keep(v):
    return (v, None)

def back_low(kept, grad):
    return (low(grad),)
low.defvjp(low_keep, low_pass)
low_back.defvjp(back_keep, back_low)

def normed(operand, gain_row):
    inverse_rms = lax.rsqrt(lax.optimization_barrier(jnp.mean(operand * operand, axis=-1, keepdims=True)) + epsilon)
    return operand * inverse_rms * gain_row

def swiglu(gate_up):
    return jax.nn.silu(gate_up[:, 0]) * gate_up[:, 1]

def mamba_core(projected, step_raw, b_and_c, a_log, dt_bias, d_skip):
    length = projected.shape[0]
    head_count = step_raw.shape[1]
    head_width = projected.shape[2] // head_count
    gate_values = projected[:, 0].reshape(length, head_count, head_width)
    signal = projected[:, 1].reshape(length, head_count, head_width)
    in_state = b_and_c[:, :NS]
    out_state = b_and_c[:, NS:]
    step_size = jax.nn.softplus(step_raw + dt_bias)
    log_keep = -step_size * jnp.exp(a_log)
    blocks = length // BLOCK
    causal = (lax.iota(jnp.int32, BLOCK)[:, None] >= lax.iota(jnp.int32, BLOCK)[None, :])[:, :, None]

    def one_block(states, pieces):
        signal_block, in_block, out_block, keep_block, size_block = pieces
        running = jnp.cumsum(keep_block, axis=0)
        log_gaps = running[:, None, :] - running[None, :, :]
        fading = jnp.exp(jnp.where(causal, log_gaps, -1e+30))
        inner_cb = jnp.einsum('in,jn->ij', out_block, in_block, precision=highest)
        mixing = fading * inner_cb[:, :, None] * size_block[None, :, :]
        inside = jnp.einsum('ijh,jhp->ihp', mixing, signal_block, precision=highest)
        carried = jnp.einsum('in,hpn->ihp', out_block, states, precision=highest) * jnp.exp(running)[:, :, None]
        tail_weights = jnp.exp(running[-1][None, :] - running) * size_block
        fresh_state = jnp.einsum('jh,jhp,jn->hpn', tail_weights, signal_block, in_block, precision=highest)
        states = states * jnp.exp(running[-1])[:, None, None] + fresh_state
        return (states, inside + carried)
    initial = jnp.zeros((head_count, head_width, NS), jnp.float32)
    _, outputs = lax.scan(jax.checkpoint(one_block), initial, (signal.reshape(blocks, BLOCK, head_count, head_width), in_state.reshape(blocks, BLOCK, NS), out_state.reshape(blocks, BLOCK, NS), log_keep.reshape(blocks, BLOCK, head_count), step_size.reshape(blocks, BLOCK, head_count)))
    mixed_rows = outputs.reshape(length, head_count, head_width) + d_skip[None, :, None] * signal
    return (mixed_rows * jax.nn.silu(gate_values)).reshape(length, head_count * head_width)

def attention_core(queries, key_rows, value_rows):
    length = queries.shape[0]
    head_count = queries.shape[1] // HD
    repeat = head_count // key_rows.shape[1]
    heads_query = queries.reshape(length, head_count, HD)
    keys_all = jnp.repeat(key_rows, repeat, axis=1)
    values_all = jnp.repeat(value_rows, repeat, axis=1)
    positions = lax.iota(jnp.int32, length)

    def one_block(block_index):
        first_row = block_index * QBLOCK
        block_query = lax.dynamic_slice_in_dim(heads_query, first_row, QBLOCK, 0)
        scores = jnp.einsum('qhd,khd->hqk', block_query, keys_all, precision=highest) * HD ** (-0.5)
        allowed = positions[None, :] <= (first_row + lax.iota(jnp.int32, QBLOCK))[:, None]
        scores = jnp.where(allowed[None], scores, -1e+30)
        largest = lax.optimization_barrier(jnp.max(scores, axis=-1, keepdims=True))
        weights = jnp.exp(scores - largest)
        sums_row = lax.optimization_barrier(jnp.sum(weights, axis=-1, keepdims=True))
        return jnp.einsum('hqk,khd->qhd', weights / sums_row, values_all, precision=highest)
    outputs = lax.map(jax.checkpoint(one_block), jnp.arange(length // QBLOCK, dtype=jnp.int32))
    return outputs.reshape(length, head_count * HD)

def hybrid_layer(inputs, params, layer_index):
    mix_gain, w_mixer_in, w_query, w_shared, w_step, a_log, dt_bias, d_skip, w_mamba_out, w_attn_out, ffn_gain, w_gate_up, w_down = [stacked[layer_index] for stacked in params]
    length = inputs.shape[0]
    normed_mix = low(normed(inputs, mix_gain))
    mixer_in = low_back(jnp.dot(normed_mix, w_mixer_in.reshape(D, 2 * HM * P_SIZE), precision=highest, preferred_element_type=jnp.float32)).reshape(length, 2, HM * P_SIZE)
    queries = low_back(jnp.dot(normed_mix, w_query, precision=highest, preferred_element_type=jnp.float32))
    shared = low_back(jnp.dot(normed_mix, w_shared, precision=highest, preferred_element_type=jnp.float32))
    step_raw = low_back(jnp.dot(normed_mix, w_step, precision=highest, preferred_element_type=jnp.float32))
    mamba_out = low(low_back(mamba_core(mixer_in, step_raw, shared[:, :2 * NS], a_log, dt_bias, d_skip)))
    kv_all = shared[:, 2 * NS:].reshape(length, 2, KVH, HD)
    attn_out = low(low_back(attention_core(queries, kv_all[:, 0], kv_all[:, 1])))
    mixed_rows = low_back(jnp.dot(mamba_out, w_mamba_out, precision=highest, preferred_element_type=jnp.float32) + jnp.dot(attn_out, w_attn_out, precision=highest, preferred_element_type=jnp.float32))
    residual = inputs + mixed_rows
    normed_ffn = low(normed(residual, ffn_gain))
    gate_up = low_back(jnp.dot(normed_ffn, w_gate_up.reshape(D, 2 * FF), precision=highest, preferred_element_type=jnp.float32)).reshape(length, 2, FF)
    hidden = low(swiglu(gate_up))
    ffn_out = low_back(jnp.dot(hidden, w_down, precision=highest, preferred_element_type=jnp.float32))
    return residual + ffn_out

def reference(acts_in, out_grad, mix_gain, w_mixer_in, w_query, w_shared, w_step, a_log, dt_bias, d_skip, w_mamba_out, w_attn_out, ffn_gain, w_gate_up, w_down):
    params = tuple((stacked.astype(jnp.float32) for stacked in (mix_gain, w_mixer_in, w_query, w_shared, w_step, a_log, dt_bias, d_skip, w_mamba_out, w_attn_out, ffn_gain, w_gate_up, w_down)))

    def both_sections(weights, inputs, extra_term):
        first_out = low(hybrid_layer(inputs, weights, 0))
        second_in = low_back(first_out + extra_term)
        return (first_out, hybrid_layer(second_in, weights, 1))

    def per_sequence(totals, pieces):
        inputs, cotangent = pieces
        extra_term = jnp.zeros_like(inputs)
        section_outs, backward_fn = jax.vjp(both_sections, params, inputs, extra_term)
        grad_params, grad_inputs, grad_extra = backward_fn((jnp.zeros_like(section_outs[0]), cotangent))
        totals = jax.tree.map(jnp.add, totals, grad_params)
        return (totals, (section_outs[0], section_outs[1], grad_inputs, grad_extra))
    zero_grads = jax.tree.map(jnp.zeros_like, params)
    totals, (first_outs, second_outs, first_grads, second_grads) = lax.scan(per_sequence, zero_grads, (acts_in.astype(jnp.float32), out_grad.astype(jnp.float32)))
    acts_out = jnp.stack([first_outs, second_outs]).astype(jnp.bfloat16)
    in_grads = jnp.stack([first_grads, second_grads]).astype(jnp.bfloat16)
    grad_gains = jnp.stack([totals[0], totals[10]], axis=1)
    grad_heads = jnp.stack([totals[5], totals[6], totals[7]], axis=1)
    return (acts_out, in_grads, grad_gains, totals[1], totals[2], totals[3], totals[4], grad_heads, totals[8], totals[9], totals[11], totals[12])
```

```python
import functools

import jax
import jax.numpy as jnp
from jax import lax
from jax.experimental import pallas as pl
from jax.experimental.pallas import tpu as pltpu
from jax.sharding import PartitionSpec as P

HM = 24
HA = 8
KVH = 2
NS = 128
HD = 64
LANES = 128
STEP = 128
TILE = 256
EPS = 1e-05
F32 = jnp.float32
B16 = jnp.bfloat16
VMEM_LIMIT = 60 << 20


def nn(a, b):
    return lax.dot_general(a, b, (((1,), (0,)), ((), ())), preferred_element_type=F32)


def nt(a, b):
    return lax.dot_general(a, b, (((1,), (1,)), ((), ())), preferred_element_type=F32)


def tn(a, b):
    return lax.dot_general(a, b, (((0,), (0,)), ((), ())), preferred_element_type=F32)


def exact(a, b):
    return lax.dot_general(
        a, b, (((1,), (0,)), ((), ())), precision=lax.Precision.HIGHEST, preferred_element_type=F32
    )


def softplus(v):
    small = jnp.exp(-jnp.abs(v))
    series = small * (1.0 - small * (0.5 - small * (1.0 / 3.0 - small * 0.25)))
    return jnp.maximum(v, 0.0) + jnp.where(small < 0.02, series, jnp.log(1.0 + small))


def sigmoid(v):
    return 1.0 / (1.0 + jnp.exp(-v))


def iotas(rows, columns):
    return (
        lax.broadcasted_iota(jnp.int32, (rows, columns), 0),
        lax.broadcasted_iota(jnp.int32, (rows, columns), 1),
    )


def spread(column_block, head, rows):
    return jnp.broadcast_to(column_block[:, head : head + 1], (rows, LANES))


class Cols:
    def __init__(self, width):
        self.width = width
        self.z = 0
        self.u = width
        self.q = 2 * width
        self.b = self.q + LANES
        self.c = self.b + LANES
        self.k = self.c + LANES
        self.v = self.k + LANES
        self.step = self.v + LANES
        self.total = self.step + LANES
        self.pairs = width // LANES


def split_heads(block, low_lanes):
    zero = jnp.zeros_like(block)
    return jnp.concatenate(
        [jnp.where(low_lanes, block, zero), jnp.where(low_lanes, zero, block)], axis=0
    )


def core_fwd_kernel(
    cols, rows_ref, wcat_ref, wout_ref, hp_ref, dsk_ref,
    proj_ref, step_ref, y_ref, lows_ref, states_ref, lse_ref, part_ref, state,
):
    length = rows_ref.shape[0]
    width = cols.width

    def project(i, _):
        rows = pl.ds(pl.multiple_of(i * TILE, TILE), TILE)
        block = rows_ref[rows, :]
        for first in range(0, cols.total, 512):
            last = min(first + 512, cols.total)
            value = nn(block, wcat_ref[:, first:last])
            if last == cols.total:
                step_ref[rows, :] = value[:, cols.step - first :]
                value = value[:, : cols.step - first]
                last = cols.step
            if first <= cols.q < last:
                at = cols.q - first
                value = jnp.concatenate(
                    [value[:, :at], value[:, at : at + LANES] * HD**-0.5, value[:, at + LANES :]],
                    axis=1,
                ) if at else jnp.concatenate(
                    [value[:, :LANES] * HD**-0.5, value[:, LANES:]], axis=1
                )
            proj_ref[rows, first:last] = value.astype(B16)
        return 0

    lax.fori_loop(0, length // TILE, project, 0)

    ri, ci = iotas(STEP, STEP)
    lower = ri >= ci
    tril = lower.astype(F32)
    low_lanes = ci < HD
    decay = jnp.exp(hp_ref[0:1, :])
    bias = hp_ref[1:2, :]
    state[...] = jnp.zeros_like(state)

    def scan_block(b, _):
        rows = pl.ds(pl.multiple_of(b * STEP, STEP), STEP)
        dt = softplus(step_ref[rows, :] + bias)
        run = exact(tril, -dt * decay)
        run_t = run.T
        bm = proj_ref[rows, cols.b : cols.b + LANES]
        cm = proj_ref[rows, cols.c : cols.c + LANES]
        cb = jnp.where(lower, nt(cm, bm), 0.0)
        states_in = state[...]
        low_state = states_in.astype(B16)
        states_ref[b] = low_state
        carried = nn(cm, low_state)
        tails, fades = [], []
        for p in range(cols.pairs):
            lanes = slice(LANES * p, LANES * (p + 1))
            u = proj_ref[rows, cols.u + LANES * p : cols.u + LANES * (p + 1)].astype(F32)
            z = proj_ref[rows, cols.z + LANES * p : cols.z + LANES * (p + 1)].astype(F32)
            run_b = [spread(run, 2 * p + k, STEP) for k in range(2)]
            run_w = jnp.where(low_lanes, run_b[0], run_b[1])
            ud = u * jnp.where(low_lanes, spread(dt, 2 * p, STEP), spread(dt, 2 * p + 1, STEP))
            mix = jnp.concatenate(
                [
                    (
                        jnp.exp(jnp.minimum(run_b[k] - run_t[2 * p + k : 2 * p + k + 1, :], 0.0))
                        * cb
                    ).astype(B16)
                    for k in range(2)
                ],
                axis=1,
            )
            inside = nn(mix, split_heads(ud, low_lanes).astype(B16))
            y = inside + carried[:, lanes] * jnp.exp(run_w) + dsk_ref[0:1, lanes] * u
            y_ref[rows, lanes] = y.astype(B16)
            lows_ref[rows, lanes] = (y * z * sigmoid(z)).astype(B16)
            end = run_w[STEP - 1 : STEP, :]
            tails.append((ud * jnp.exp(end - run_w)).astype(B16))
            fades.append(jnp.exp(end))
        fresh = tn(bm, jnp.concatenate(tails, axis=1))
        state[...] = states_in * jnp.concatenate(fades, axis=1) + fresh
        return 0

    lax.fori_loop(0, length // STEP, scan_block, 0)

    rk, ck = iotas(TILE, 2 * TILE)
    diagonal = rk <= jnp.where(ck < TILE, ck, ck - TILE)
    q_low = iotas(TILE, LANES)[1] < HD

    def attend(i, _):
        rows = pl.ds(pl.multiple_of(i * TILE, TILE), TILE)
        q2 = split_heads(proj_ref[rows, cols.q : cols.q + LANES], q_low)

        def piece(j, carry, masked):
            top, total, out = carry
            keys = pl.ds(pl.multiple_of(j * TILE, TILE), TILE)
            s = nt(proj_ref[keys, cols.k : cols.k + LANES], q2)
            if masked:
                s = jnp.where(diagonal, s, -1e30)
            new_top = jnp.maximum(top, jnp.max(s, axis=0, keepdims=True))
            p = jnp.exp(s - new_top)
            scale = jnp.exp(top - new_top)
            total = total * scale + jnp.sum(p, axis=0, keepdims=True)
            out = out * scale + tn(proj_ref[keys, cols.v : cols.v + LANES], p.astype(B16))
            return new_top, total, out

        carry = (
            jnp.full((1, 2 * TILE), -1e30, F32),
            jnp.zeros((1, 2 * TILE), F32),
            jnp.zeros((LANES, 2 * TILE), F32),
        )
        carry = lax.fori_loop(0, i, lambda j, c: piece(j, c, False), carry)
        top, total, out = piece(i, carry, True)
        out = out / total
        joined = jnp.concatenate([out[:HD, :TILE], out[HD:, TILE:]], axis=0)
        lows_ref[rows, width : width + LANES] = joined.T.astype(B16)
        lse_ref[i] = jnp.broadcast_to(top + jnp.log(total), (8, 2 * TILE))
        return 0

    lax.fori_loop(0, length // TILE, attend, 0)
    multiply_out(lows_ref, wout_ref, part_ref)


def multiply_out(lows_ref, wout_ref, part_ref):
    ways, _, piece = wout_ref.shape

    def out_rows(i, _):
        rows = pl.ds(pl.multiple_of(i * TILE, TILE), TILE)
        block = lows_ref[rows, :]
        for k in range(ways):
            part_ref[rows, k * piece : (k + 1) * piece] = nn(block, wout_ref[k]).astype(B16)
        return 0

    lax.fori_loop(0, lows_ref.shape[0] // TILE, out_rows, 0)


def core_bwd_kernel(
    cols, back_ref, wcat_ref, wout_ref, hp_ref, dsk_ref, group_ref, proj_ref, step_ref, y_ref, lows_ref,
    states_ref, lse_ref,
    dproj_ref, heads_ref, part_ref, dcore, grad_state, skip_sum, dk_sum, dv_sum,
):
    length = back_ref.shape[0]
    width = cols.width
    ways, _, piece = wout_ref.shape
    blocks = length // STEP

    def into_core(i, _):
        rows = pl.ds(pl.multiple_of(i * TILE, TILE), TILE)
        total = nt(back_ref[rows, 0:piece], wout_ref[0])
        for k in range(1, ways):
            total += nt(back_ref[rows, k * piece : (k + 1) * piece], wout_ref[k])
        dcore[rows, :] = total.astype(B16)
        return 0

    lax.fori_loop(0, length // TILE, into_core, 0)

    rk, ck = iotas(TILE, 2 * TILE)
    diagonal = rk <= jnp.where(ck < TILE, ck, ck - TILE)
    q_low = iotas(TILE, LANES)[1] < HD
    dk_sum[...] = jnp.zeros_like(dk_sum)
    dv_sum[...] = jnp.zeros_like(dv_sum)
    half = iotas(8, LANES)
    pick_low = (half[1] < HD).astype(F32)
    pick_high = (half[1] >= HD).astype(F32)

    def attend(i, _):
        rows = pl.ds(pl.multiple_of(i * TILE, TILE), TILE)
        q2 = split_heads(proj_ref[rows, cols.q : cols.q + LANES], q_low)
        d_out = dcore[rows, width : width + LANES]
        do2 = split_heads(d_out, q_low)
        both = d_out.astype(F32) * lows_ref[rows, width : width + LANES].astype(F32)
        high = lax.Precision.HIGHEST
        deltas = [
            lax.dot_general(
                pick, both, (((1,), (1,)), ((), ())), precision=high, preferred_element_type=F32
            )[0:1, :]
            for pick in (pick_low, pick_high)
        ]
        delta = jnp.concatenate(deltas, axis=1)
        lse = lse_ref[i][0:1, :]

        def piece_of(j, dq, masked):
            keys = pl.ds(pl.multiple_of(j * TILE, TILE), TILE)
            kk = proj_ref[keys, cols.k : cols.k + LANES]
            p = jnp.exp(nt(kk, q2) - lse)
            if masked:
                p = jnp.where(diagonal, p, 0.0)
            ds = (p * (nt(proj_ref[keys, cols.v : cols.v + LANES], do2) - delta)).astype(B16)
            dv_sum[keys, :] += nn(p.astype(B16), do2)
            dk_sum[keys, :] += nn(ds, q2)
            return dq + tn(kk, ds)

        dq = jnp.zeros((LANES, 2 * TILE), F32)
        dq = lax.fori_loop(0, i, lambda j, c: piece_of(j, c, False), dq)
        dq = piece_of(i, dq, True)
        joined = jnp.concatenate([dq[:HD, :TILE], dq[HD:, TILE:]], axis=0) * HD**-0.5
        dproj_ref[rows, cols.q : cols.q + LANES] = joined.T.astype(B16)
        return 0

    lax.fori_loop(0, length // TILE, attend, 0)
    dproj_ref[:, cols.k : cols.k + LANES] = dk_sum[...].astype(B16)
    dproj_ref[:, cols.v : cols.v + LANES] = dv_sum[...].astype(B16)

    ri, ci = iotas(STEP, STEP)
    upper = ri <= ci
    tril = (ri >= ci).astype(F32)
    triu = upper.astype(F32)
    low_lanes = ci < HD
    decay = jnp.exp(hp_ref[0:1, :])
    bias = hp_ref[1:2, :]
    grad_state[...] = jnp.zeros_like(grad_state)
    skip_sum[...] = jnp.zeros_like(skip_sum)
    heads_ref[...] = jnp.zeros_like(heads_ref)
    zero_rows = jnp.zeros((STEP - 2 * cols.pairs, LANES), F32)

    def scan_block(back, _):
        b = blocks - 1 - back
        rows = pl.ds(pl.multiple_of(b * STEP, STEP), STEP)
        raw = step_ref[rows, :] + bias
        dt = softplus(raw)
        a = -dt * decay
        run = exact(tril, a)
        run_t = run.T
        bm = proj_ref[rows, cols.b : cols.b + LANES]
        cm = proj_ref[rows, cols.c : cols.c + LANES]
        cbt = jnp.where(upper, nt(bm, cm), 0.0)
        low_state = states_ref[b]
        grads_out = grad_state[...]
        low_grad = grads_out.astype(B16)
        carried = nn(cm, low_state)
        pulled = nn(bm, low_grad)
        dcb = jnp.zeros((STEP, STEP), F32)
        dy_fades, u_tails, fades = [], [], []
        carry_terms, direct_terms, tail_terms = [], [], []
        row_sums = []
        col_sums = jnp.zeros((STEP, LANES), F32)
        for p in range(cols.pairs):
            lanes = slice(LANES * p, LANES * (p + 1))
            u16 = proj_ref[rows, cols.u + LANES * p : cols.u + LANES * (p + 1)]
            u = u16.astype(F32)
            z = proj_ref[rows, cols.z + LANES * p : cols.z + LANES * (p + 1)].astype(F32)
            y = y_ref[rows, lanes].astype(F32)
            dm = dcore[rows, lanes].astype(F32)
            sg = sigmoid(z)
            dy = dm * z * sg
            dproj_ref[rows, cols.z + LANES * p : cols.z + LANES * (p + 1)] = (
                dm * y * sg * (1.0 + z * (1.0 - sg))
            ).astype(B16)
            dy16 = dy.astype(B16)
            skip_sum[:, lanes] += u * dy
            run_b = [spread(run, 2 * p + k, STEP) for k in range(2)]
            dt_b = [spread(dt, 2 * p + k, STEP) for k in range(2)]
            run_w = jnp.where(low_lanes, run_b[0], run_b[1])
            dt_w = jnp.where(low_lanes, dt_b[0], dt_b[1])
            end = run_w[STEP - 1 : STEP, :]
            fade = jnp.exp(run_w)
            tail = jnp.exp(end - run_w)
            dmix = nt(split_heads(u16, low_lanes), dy16)
            mixes = []
            for k in range(2):
                gap = jnp.exp(jnp.minimum(run_t[2 * p + k : 2 * p + k + 1, :] - run_b[k], 0.0))
                mixes.append((gap * cbt).astype(B16))
                weighted = gap * dt_b[k] * dmix[STEP * k : STEP * (k + 1), :]
                dcb += weighted
                moved = weighted * cbt
                row_sums.append(jnp.sum(moved, axis=0, keepdims=True))
                col_sums = jnp.where(
                    ci == 2 * p + k, jnp.sum(moved, axis=1, keepdims=True), col_sums
                )
            inside = nn(jnp.concatenate(mixes, axis=1), split_heads(dy16, low_lanes))
            pull_tail = tail * pulled[:, lanes]
            g = inside + pull_tail
            dproj_ref[rows, cols.u + LANES * p : cols.u + LANES * (p + 1)] = (
                dt_w * g + dsk_ref[0:1, lanes] * dy
            ).astype(B16)
            dy_fade = dy * fade
            dy_fades.append(dy_fade.astype(B16))
            u_tails.append((u * dt_w * tail).astype(B16))
            fades.append(jnp.exp(end))
            carry_terms.append((dy_fade * carried[:, lanes]).astype(B16))
            direct_terms.append((u * g).astype(B16))
            tail_terms.append((u * pull_tail).astype(B16))
        dy_fade = jnp.concatenate(dy_fades, axis=1)
        dcb = jnp.where(upper, dcb, 0.0).astype(B16)
        dproj_ref[rows, cols.c : cols.c + LANES] = (tn(dcb, bm) + nt(dy_fade, low_state)).astype(B16)
        dproj_ref[rows, cols.b : cols.b + LANES] = (
            nn(dcb, cm) + nt(jnp.concatenate(u_tails, axis=1), low_grad)
        ).astype(B16)
        group = group_ref[...]
        carry_term = nn(jnp.concatenate(carry_terms, axis=1), group)
        direct_term = nn(jnp.concatenate(direct_terms, axis=1), group)
        tail_term = dt * nn(jnp.concatenate(tail_terms, axis=1), group)
        overlap = jnp.sum(low_state.astype(F32) * grads_out, axis=0, keepdims=True)
        overlap = exact(jnp.broadcast_to(overlap, (8, width)), group.astype(F32))[0:1, :]
        overlap = overlap * jnp.exp(run[STEP - 1 : STEP, :])
        row_sum = jnp.concatenate(row_sums + [zero_rows], axis=0).T
        d_run = row_sum - col_sums + carry_term - tail_term
        d_a = exact(triu, d_run) + (jnp.sum(tail_term, axis=0, keepdims=True) + overlap)
        d_step = (direct_term - decay * d_a) * sigmoid(raw)
        dproj_ref[rows, cols.step : cols.step + LANES] = d_step.astype(B16)
        heads_ref[0:1, :] += jnp.sum(d_a * a, axis=0, keepdims=True)
        heads_ref[1:2, :] += jnp.sum(d_step, axis=0, keepdims=True)
        grad_state[...] = grads_out * jnp.concatenate(fades, axis=1) + tn(cm, dy_fade)
        return 0

    lax.fori_loop(0, blocks, scan_block, 0)
    skip = jnp.sum(skip_sum[...], axis=0, keepdims=True)
    heads_ref[2:3, :] = exact(jnp.broadcast_to(skip, (8, width)), group_ref[...].astype(F32))[0:1, :]
    multiply_back(dproj_ref, wcat_ref, part_ref)


def multiply_back(grad_ref, weight_ref, part_ref):
    def out_rows(i, _):
        rows = pl.ds(pl.multiple_of(i * TILE, TILE), TILE)
        block = grad_ref[rows, :]
        for first in range(0, weight_ref.shape[0], 256):
            part_ref[rows, first : first + 256] = nt(
                block, weight_ref[first : first + 256, :]
            ).astype(B16)
        return 0

    lax.fori_loop(0, grad_ref.shape[0] // TILE, out_rows, 0)


def ffn_fwd_kernel(rows_ref, wgu_ref, wdown_ref, gu_ref, hidden_ref, part_ref):
    units = hidden_ref.shape[1]

    def up(i, _):
        rows = pl.ds(pl.multiple_of(i * TILE, TILE), TILE)
        block = rows_ref[rows, :]
        g = nn(block, wgu_ref[:, :units])
        v = nn(block, wgu_ref[:, units:])
        gu_ref[rows, :units] = g.astype(B16)
        gu_ref[rows, units:] = v.astype(B16)
        hidden_ref[rows, :] = (g * sigmoid(g) * v).astype(B16)
        return 0

    lax.fori_loop(0, rows_ref.shape[0] // TILE, up, 0)
    multiply_out(hidden_ref, wdown_ref, part_ref)


def ffn_bwd_kernel(out_ref, wgu_ref, wdown_ref, gu_ref, dgu_ref, part_ref):
    ways, units, piece = wdown_ref.shape

    def down(i, _):
        rows = pl.ds(pl.multiple_of(i * TILE, TILE), TILE)
        dh = nt(out_ref[rows, 0:piece], wdown_ref[0])
        for k in range(1, ways):
            dh += nt(out_ref[rows, k * piece : (k + 1) * piece], wdown_ref[k])
        g = gu_ref[rows, :units].astype(F32)
        v = gu_ref[rows, units:].astype(F32)
        sg = sigmoid(g)
        dgu_ref[rows, :units] = (dh * v * sg * (1.0 + g * (1.0 - sg))).astype(B16)
        dgu_ref[rows, units:] = (dh * g * sg).astype(B16)
        return 0

    lax.fori_loop(0, out_ref.shape[0] // TILE, down, 0)
    multiply_back(dgu_ref, wgu_ref, part_ref)


def whole_call(kernel, outs, scratch, flops, name):
    vmem = pl.BlockSpec(memory_space=pltpu.VMEM)

    def call(*operands):
        moved = sum(o.size * o.dtype.itemsize for o in operands)
        return pl.pallas_call(
            kernel,
            out_shape=[jax.ShapeDtypeStruct(s, t) for s, t in outs],
            in_specs=[vmem] * len(operands),
            out_specs=[vmem] * len(outs),
            scratch_shapes=scratch,
            compiler_params=pltpu.CompilerParams(vmem_limit_bytes=VMEM_LIMIT),
            cost_estimate=pl.CostEstimate(flops=flops, bytes_accessed=2 * moved, transcendentals=0),
            name=name,
        )(*operands)

    return call


def core_fwd(cols, rows, wcat, wout, hp, dsk):
    length, depth = rows.shape
    width = cols.width
    return whole_call(
        functools.partial(core_fwd_kernel, cols),
        [
            ((length, cols.step), B16),
            ((length, LANES), F32),
            ((length, width), B16),
            ((length, width + LANES), B16),
            ((length // STEP, NS, width), B16),
            ((length // TILE, 8, 2 * TILE), F32),
            ((length, depth), B16),
        ],
        [pltpu.VMEM((NS, width), F32)],
        20 * length * depth * cols.total,
        "core_fwd",
    )(rows, wcat, wout, hp, dsk)


def core_bwd(cols, back, wcat, wout, hp, dsk, group, kept):
    length, depth = back.shape
    width = cols.width
    return whole_call(
        functools.partial(core_bwd_kernel, cols),
        [((length, cols.total), B16), ((8, LANES), F32), ((length, depth), B16)],
        [
            pltpu.VMEM((length, width + LANES), B16),
            pltpu.VMEM((NS, width), F32),
            pltpu.VMEM((STEP, width), F32),
            pltpu.VMEM((length, LANES), F32),
            pltpu.VMEM((length, LANES), F32),
        ],
        40 * length * depth * cols.total,
        "core_bwd",
    )(back, wcat, wout, hp, dsk, group, *kept)


def ffn_fwd(rows, wgu, wdown):
    length, depth = rows.shape
    units = wdown.shape[1]
    return whole_call(
        ffn_fwd_kernel,
        [((length, 2 * units), B16), ((length, units), B16), ((length, depth), B16)],
        [],
        6 * length * depth * units,
        "ffn_fwd",
    )(rows, wgu, wdown)


def ffn_bwd(out, wgu, wdown, gu):
    length, depth = out.shape
    units = wdown.shape[1]
    return whole_call(
        ffn_bwd_kernel,
        [((length, 2 * units), B16), ((length, depth), B16)],
        [],
        6 * length * depth * units,
        "ffn_bwd",
    )(out, wgu, wdown, gu)


def widen(block, axis, size):
    missing = size - block.shape[axis]
    if missing == 0:
        return block
    pads = [(0, 0)] * block.ndim
    pads[axis] = (0, missing)
    return jnp.pad(block, pads)


def rms(rows, gain):
    scale = lax.rsqrt(jnp.mean(rows * rows, axis=-1, keepdims=True) + EPS)
    return rows * scale * gain


def rms_back(rows, gain, grad):
    scale = lax.rsqrt(jnp.mean(rows * rows, axis=-1, keepdims=True) + EPS)
    scaled = gain * grad
    mean = jnp.mean(scaled * rows, axis=-1, keepdims=True)
    return scale * scaled - rows * (scale * scale * scale * mean), jnp.sum(
        grad * rows * scale, axis=0
    )


def gather_rows(block):
    return lax.all_gather(block, "tensor", axis=0, tiled=True)


def scatter_rows(block):
    return lax.psum_scatter(block, "tensor", scatter_dimension=0, tiled=True).astype(F32)


def on_device(
    acts_in, out_grad, mix_gain, w_mixer_in, w_query, w_shared, w_step, a_log, dt_bias, d_skip,
    w_mamba_out, w_attn_out, ffn_gain, w_gate_up, w_down,
):
    section = lax.axis_index("pipe")
    member = lax.axis_index("tensor")
    dp = lax.axis_size("dp")
    heads = a_log.shape[1]
    even = heads + heads % 2
    real = heads * HD
    width = even * HD
    q_real = w_query.shape[2]
    group = member * (q_real // HD) // (HA // KVH)
    cols = Cols(width)
    units = w_gate_up.shape[3]
    depth = acts_in.shape[2]
    piece = depth // dp

    shared = w_shared[0]
    keys = lax.dynamic_slice_in_dim(shared, 2 * NS + group * HD, HD, 1)
    values = lax.dynamic_slice_in_dim(shared, 2 * NS + KVH * HD + group * HD, HD, 1)
    steps = lax.dynamic_slice_in_dim(w_step[0], member * heads, heads, 1)
    wcat = jnp.concatenate(
        [
            widen(w_mixer_in[0, :, 0], 1, width),
            widen(w_mixer_in[0, :, 1], 1, width),
            widen(w_query[0], 1, LANES),
            shared[:, : 2 * NS],
            keys, keys, values, values,
            widen(steps, 1, LANES),
        ],
        axis=1,
    )
    gates = w_gate_up[0].reshape(piece, 2 * units)
    wout = jnp.concatenate(
        [
            widen(w_mamba_out[0], 0, width),
            widen(w_attn_out[0], 0, LANES),
            w_down[0],
            widen(jnp.concatenate([mix_gain, ffn_gain]), 0, 16),
        ],
        axis=0,
    )
    both = ("pipe", "dp")
    wcat_all = lax.all_gather(wcat, both, axis=0, tiled=True).reshape(2, depth, cols.total)
    wout_all = lax.all_gather(wout, both, axis=0)
    gates_all = lax.all_gather(gates, both, axis=0, tiled=True).reshape(2, depth, 2 * units)
    wout_all = wout_all.reshape((2, dp) + wout.shape)
    heads_all = lax.all_gather(jnp.concatenate([a_log, dt_bias, d_skip]), "pipe", axis=0)

    core_rows = width + LANES
    sub = jnp.arange(width)[:, None] // HD == jnp.arange(LANES)[None, :]
    layers = []
    for layer in range(2):
        gains = wout_all[layer, :, core_rows + units : core_rows + units + 2]
        gains = gains.transpose(1, 0, 2).reshape(2, depth).astype(F32)
        hp = widen(widen(heads_all[layer], 1, LANES), 0, 8)
        layers.append(
            dict(
                wcat=wcat_all[layer],
                wout=wout_all[layer, :, :core_rows],
                wdown=wout_all[layer, :, core_rows : core_rows + units],
                wgu=gates_all[layer],
                gains=gains,
                hp=hp,
                dsk=jnp.broadcast_to(jnp.repeat(hp[2, :even], HD)[None], (8, width)),
                group=sub.astype(B16),
            )
        )

    x = lax.dynamic_index_in_dim(acts_in, section, 0, False).astype(F32)
    y_grad = lax.dynamic_index_in_dim(out_grad, section, 0, False)
    kept = []
    for w in layers:
        rows_mix = gather_rows(rms(x, w["gains"][0]).astype(B16))
        *saved, part = core_fwd(cols, rows_mix, w["wcat"], w["wout"], w["hp"], w["dsk"])
        residual = x + scatter_rows(part)
        rows_ffn = gather_rows(rms(residual, w["gains"][1]).astype(B16))
        gu, hidden, part = ffn_fwd(rows_ffn, w["wgu"], w["wdown"])
        out = (residual + scatter_rows(part)).astype(B16)
        kept.append((x, rows_mix, saved, residual, rows_ffn, gu, hidden, out))
        x = out.astype(F32)

    x_grads, grads = [None, None], [None, None]
    for layer in (1, 0):
        w = layers[layer]
        x, rows_mix, saved, residual, rows_ffn, gu, hidden, _ = kept[layer]
        rows_out = gather_rows(y_grad)
        dgu, part = ffn_bwd(rows_out, w["wgu"], w["wdown"], gu)
        step_back, gain_ffn = rms_back(residual, w["gains"][1], scatter_rows(part))
        d_residual = y_grad.astype(F32) + step_back
        rows_back = gather_rows(d_residual.astype(B16))
        dproj, head_grads, part = core_bwd(
            cols, rows_back, w["wcat"], w["wout"], w["hp"], w["dsk"], w["group"], saved
        )
        step_back, gain_mix = rms_back(x, w["gains"][0], scatter_rows(part))
        y_grad = (d_residual + step_back).astype(B16)
        x_grads[layer] = y_grad
        g_gu = tn(rows_ffn, dgu).astype(B16)
        g_cat = tn(rows_mix, dproj).astype(B16)
        lows = saved[3]
        by_piece = lambda rows: rows.reshape(rows.shape[0], dp, piece)
        g_down = jnp.einsum("lf,lkd->kfd", hidden, by_piece(rows_out), preferred_element_type=F32)
        g_out = jnp.einsum("lf,lkd->kfd", lows, by_piece(rows_back), preferred_element_type=F32)
        g_rows = jnp.concatenate([g_out, g_down], axis=1).astype(B16)
        g_cols = jnp.concatenate([g_cat[:, : cols.b], g_gu], axis=1)
        g_kv = g_cat[:, cols.k : cols.k + 2 * LANES].astype(F32).reshape(depth, 2, 2, HD).sum(2)
        g_kv = lax.dynamic_update_slice(
            jnp.zeros((depth, 2, KVH, HD), F32), g_kv[:, :, None, :], (0, 0, group, 0)
        )
        g_step = lax.dynamic_update_slice_in_dim(
            jnp.zeros((depth, LANES), F32),
            g_cat[:, cols.step : cols.step + heads].astype(F32), member * heads, 1,
        )
        g_shared = jnp.concatenate(
            [g_cat[:, cols.b : cols.k].astype(F32), g_kv.reshape(depth, -1), g_step], axis=1
        ).astype(B16)
        small = jnp.concatenate([gain_mix, gain_ffn])
        grads[layer] = (
            lax.psum_scatter(g_cols, "dp", scatter_dimension=0, tiled=True),
            lax.psum_scatter(g_rows, "dp", scatter_dimension=0, tiled=False),
            lax.psum_scatter(g_shared, ("dp", "tensor"), scatter_dimension=0, tiled=True),
            small,
            head_grads[:3, :heads],
        )

    def swap(own, other):
        return lax.ppermute(jnp.where(section == 0, other, own), "pipe", [(0, 1), (1, 0)])

    def pick(pair):
        return jnp.where(section == 0, pair[0], pair[1])

    def placed(pair):
        mine, received = pick(pair), swap(*pair)
        return jnp.where(
            section == 0, jnp.stack([mine, received]), jnp.stack([received, mine])
        )

    acts = placed([k[-1] for k in kept])
    in_grads = placed(x_grads)
    totals = [
        pick(pair).astype(F32) + swap(*pair).astype(F32)
        for pair in zip(grads[0][:3], grads[1][:3])
    ]
    small = jnp.stack([g[3] for g in grads]).reshape(2, 2, depth)
    small = lax.psum(lax.psum_scatter(small, ("dp", "tensor"), scatter_dimension=2, tiled=True), "pipe")
    head_sum = lax.psum(jnp.stack([g[4] for g in grads]), both)
    g_cols, g_rows, g_shared = totals
    g_mixer = jnp.stack([g_cols[:, :real], g_cols[:, width : width + real]], axis=1)
    g_gates = g_cols[:, cols.b :].reshape(piece, 2, units)
    return (
        acts[None],
        in_grads[None],
        pick(small)[None],
        g_mixer[None],
        g_cols[None, :, cols.q : cols.q + q_real],
        g_shared[None, :, : 2 * NS + 2 * KVH * HD],
        g_shared[None, :, 2 * NS + 2 * KVH * HD :][:, :, :HM],
        pick(head_sum)[None],
        g_rows[None, :real],
        g_rows[None, width : width + q_real],
        g_gates[None],
        g_rows[None, core_rows:],
    )


def solution(mesh):
    placed = (
        P("dp", "tensor", None),
        P("dp", "tensor", None),
        P("pipe", "dp"),
        P("pipe", "dp", None, "tensor"),
        P("pipe", "dp", "tensor"),
        P("pipe", "dp", None),
        P("pipe", "dp", None),
        P("pipe", "tensor"),
        P("pipe", "tensor"),
        P("pipe", "tensor"),
        P("pipe", "tensor", "dp"),
        P("pipe", "tensor", "dp"),
        P("pipe", "dp"),
        P("pipe", "dp", None, "tensor"),
        P("pipe", "tensor", "dp"),
    )
    return jax.shard_map(
        on_device,
        mesh=mesh,
        in_specs=placed,
        out_specs=(
            P("pipe", "dp", "tensor", None),
            P("pipe", "dp", "tensor", None),
            P("pipe", None, ("dp", "tensor")),
            P("pipe", "dp", None, "tensor"),
            P("pipe", "dp", "tensor"),
            P("pipe", ("dp", "tensor"), None),
            P("pipe", ("dp", "tensor"), None),
            P("pipe", None, "tensor"),
            P("pipe", "tensor", "dp"),
            P("pipe", "tensor", "dp"),
            P("pipe", "dp", None, "tensor"),
            P("pipe", "tensor", "dp"),
        ),
        check_vma=False,
    )
```

```python
import functools

import jax
import jax.numpy as jnp
from jax import lax
from jax.experimental import pallas as pl
from jax.experimental.pallas import tpu as pltpu
from jax.sharding import PartitionSpec as P

HM = 24
HA = 8
KVH = 2
NS = 128
HD = 64
LANES = 128
STEP = 128
TILE = 256
EPS = 1e-05
F32 = jnp.float32
B16 = jnp.bfloat16
VMEM_LIMIT = 60 << 20


def nn(a, b):
    return lax.dot_general(a, b, (((1,), (0,)), ((), ())), preferred_element_type=F32)


def nt(a, b):
    return lax.dot_general(a, b, (((1,), (1,)), ((), ())), preferred_element_type=F32)


def tn(a, b):
    return lax.dot_general(a, b, (((0,), (0,)), ((), ())), preferred_element_type=F32)


def exact(a, b):
    return lax.dot_general(
        a, b, (((1,), (0,)), ((), ())), precision=lax.Precision.HIGHEST, preferred_element_type=F32
    )


def softplus(v):
    small = jnp.exp(-jnp.abs(v))
    series = small * (1.0 - small * (0.5 - small * (1.0 / 3.0 - small * 0.25)))
    return jnp.maximum(v, 0.0) + jnp.where(small < 0.02, series, jnp.log(1.0 + small))


def sigmoid(v):
    return 1.0 / (1.0 + jnp.exp(-v))


def iotas(rows, columns):
    return (
        lax.broadcasted_iota(jnp.int32, (rows, columns), 0),
        lax.broadcasted_iota(jnp.int32, (rows, columns), 1),
    )


def spread(column_block, head, rows):
    return jnp.broadcast_to(column_block[:, head : head + 1], (rows, LANES))


class Cols:
    def __init__(self, width):
        self.width = width
        self.z = 0
        self.u = width
        self.q = 2 * width
        self.b = self.q + LANES
        self.c = self.b + LANES
        self.k = self.c + LANES
        self.v = self.k + LANES
        self.step = self.v + LANES
        self.total = self.step + LANES
        self.pairs = width // LANES


def split_heads(block, low_lanes):
    zero = jnp.zeros_like(block)
    return jnp.concatenate(
        [jnp.where(low_lanes, block, zero), jnp.where(low_lanes, zero, block)], axis=0
    )


def core_fwd_kernel(
    cols, rows_ref, wcat_ref, wout_ref, hp_ref, dsk_ref,
    proj_ref, step_ref, y_ref, lows_ref, states_ref, lse_ref, part_ref, state,
):
    length = rows_ref.shape[0]
    width = cols.width

    def project(i, _):
        rows = pl.ds(pl.multiple_of(i * TILE, TILE), TILE)
        block = rows_ref[rows, :]
        for first in range(0, cols.total, 512):
            last = min(first + 512, cols.total)
            value = nn(block, wcat_ref[:, first:last])
            if last == cols.total:
                step_ref[rows, :] = value[:, cols.step - first :]
                value = value[:, : cols.step - first]
                last = cols.step
            if first <= cols.q < last:
                at = cols.q - first
                value = jnp.concatenate(
                    [value[:, :at], value[:, at : at + LANES] * HD**-0.5, value[:, at + LANES :]],
                    axis=1,
                ) if at else jnp.concatenate(
                    [value[:, :LANES] * HD**-0.5, value[:, LANES:]], axis=1
                )
            proj_ref[rows, first:last] = value.astype(B16)
        return 0

    lax.fori_loop(0, length // TILE, project, 0)

    ri, ci = iotas(STEP, STEP)
    lower = ri >= ci
    tril = lower.astype(F32)
    low_lanes = ci < HD
    decay = jnp.exp(hp_ref[0:1, :])
    bias = hp_ref[1:2, :]
    state[...] = jnp.zeros_like(state)

    def scan_block(b, _):
        rows = pl.ds(pl.multiple_of(b * STEP, STEP), STEP)
        dt = softplus(step_ref[rows, :] + bias)
        run = exact(tril, -dt * decay)
        run_t = run.T
        bm = proj_ref[rows, cols.b : cols.b + LANES]
        cm = proj_ref[rows, cols.c : cols.c + LANES]
        cb = jnp.where(lower, nt(cm, bm), 0.0)
        states_in = state[...]
        low_state = states_in.astype(B16)
        states_ref[b] = low_state
        carried = nn(cm, low_state)
        tails, fades = [], []
        for p in range(cols.pairs):
            lanes = slice(LANES * p, LANES * (p + 1))
            u = proj_ref[rows, cols.u + LANES * p : cols.u + LANES * (p + 1)].astype(F32)
            z = proj_ref[rows, cols.z + LANES * p : cols.z + LANES * (p + 1)].astype(F32)
            run_b = [spread(run, 2 * p + k, STEP) for k in range(2)]
            run_w = jnp.where(low_lanes, run_b[0], run_b[1])
            ud = u * jnp.where(low_lanes, spread(dt, 2 * p, STEP), spread(dt, 2 * p + 1, STEP))
            mix = jnp.concatenate(
                [
                    (
                        jnp.exp(jnp.minimum(run_b[k] - run_t[2 * p + k : 2 * p + k + 1, :], 0.0))
                        * cb
                    ).astype(B16)
                    for k in range(2)
                ],
                axis=1,
            )
            inside = nn(mix, split_heads(ud, low_lanes).astype(B16))
            y = inside + carried[:, lanes] * jnp.exp(run_w) + dsk_ref[0:1, lanes] * u
            y_ref[rows, lanes] = y.astype(B16)
            lows_ref[rows, lanes] = (y * z * sigmoid(z)).astype(B16)
            end = run_w[STEP - 1 : STEP, :]
            tails.append((ud * jnp.exp(end - run_w)).astype(B16))
            fades.append(jnp.exp(end))
        fresh = tn(bm, jnp.concatenate(tails, axis=1))
        state[...] = states_in * jnp.concatenate(fades, axis=1) + fresh
        return 0

    lax.fori_loop(0, length // STEP, scan_block, 0)

    rk, ck = iotas(TILE, 2 * TILE)
    diagonal = rk <= jnp.where(ck < TILE, ck, ck - TILE)
    q_low = iotas(TILE, LANES)[1] < HD

    def attend(i, _):
        rows = pl.ds(pl.multiple_of(i * TILE, TILE), TILE)
        q2 = split_heads(proj_ref[rows, cols.q : cols.q + LANES], q_low)

        def piece(j, carry, masked):
            top, total, out = carry
            keys = pl.ds(pl.multiple_of(j * TILE, TILE), TILE)
            s = nt(proj_ref[keys, cols.k : cols.k + LANES], q2)
            if masked:
                s = jnp.where(diagonal, s, -1e30)
            new_top = jnp.maximum(top, jnp.max(s, axis=0, keepdims=True))
            p = jnp.exp(s - new_top)
            scale = jnp.exp(top - new_top)
            total = total * scale + jnp.sum(p, axis=0, keepdims=True)
            out = out * scale + tn(proj_ref[keys, cols.v : cols.v + LANES], p.astype(B16))
            return new_top, total, out

        carry = (
            jnp.full((1, 2 * TILE), -1e30, F32),
            jnp.zeros((1, 2 * TILE), F32),
            jnp.zeros((LANES, 2 * TILE), F32),
        )
        carry = lax.fori_loop(0, i, lambda j, c: piece(j, c, False), carry)
        top, total, out = piece(i, carry, True)
        out = out / total
        joined = jnp.concatenate([out[:HD, :TILE], out[HD:, TILE:]], axis=0)
        lows_ref[rows, width : width + LANES] = joined.T.astype(B16)
        lse_ref[i] = jnp.broadcast_to(top + jnp.log(total), (8, 2 * TILE))
        return 0

    lax.fori_loop(0, length // TILE, attend, 0)
    multiply_out(lows_ref, wout_ref, part_ref)


def multiply_out(lows_ref, wout_ref, part_ref):
    ways, _, piece = wout_ref.shape

    def out_rows(i, _):
        rows = pl.ds(pl.multiple_of(i * TILE, TILE), TILE)
        block = lows_ref[rows, :]
        for k in range(ways):
            part_ref[rows, k * piece : (k + 1) * piece] = nn(block, wout_ref[k]).astype(B16)
        return 0

    lax.fori_loop(0, lows_ref.shape[0] // TILE, out_rows, 0)


def core_bwd_kernel(
    cols, members, back_ref, wcat_ref, wout_ref, hp_ref, dsk_ref, group_ref, rows_ref, fold_ref,
    proj_ref, step_ref, y_ref, lows_ref, states_ref, lse_ref,
    dproj_ref, heads_ref, part_ref, dcore, grad_state, skip_sum, dk_sum, dv_sum, folded,
):
    length = back_ref.shape[0]
    width = cols.width
    ways, _, piece = wout_ref.shape
    blocks = length // STEP

    def into_core(i, _):
        rows = pl.ds(pl.multiple_of(i * TILE, TILE), TILE)
        total = nt(back_ref[rows, 0:piece], wout_ref[0])
        for k in range(1, ways):
            total += nt(back_ref[rows, k * piece : (k + 1) * piece], wout_ref[k])
        dcore[rows, :] = total.astype(B16)
        return 0

    lax.fori_loop(0, length // TILE, into_core, 0)

    rk, ck = iotas(TILE, 2 * TILE)
    diagonal = rk <= jnp.where(ck < TILE, ck, ck - TILE)
    q_low = iotas(TILE, LANES)[1] < HD
    dk_sum[...] = jnp.zeros_like(dk_sum)
    dv_sum[...] = jnp.zeros_like(dv_sum)
    half = iotas(8, LANES)
    pick_low = (half[1] < HD).astype(F32)
    pick_high = (half[1] >= HD).astype(F32)

    def attend(i, _):
        rows = pl.ds(pl.multiple_of(i * TILE, TILE), TILE)
        q2 = split_heads(proj_ref[rows, cols.q : cols.q + LANES], q_low)
        d_out = dcore[rows, width : width + LANES]
        do2 = split_heads(d_out, q_low)
        both = d_out.astype(F32) * lows_ref[rows, width : width + LANES].astype(F32)
        high = lax.Precision.HIGHEST
        deltas = [
            lax.dot_general(
                pick, both, (((1,), (1,)), ((), ())), precision=high, preferred_element_type=F32
            )[0:1, :]
            for pick in (pick_low, pick_high)
        ]
        delta = jnp.concatenate(deltas, axis=1)
        lse = lse_ref[i][0:1, :]

        def piece_of(j, dq, masked):
            keys = pl.ds(pl.multiple_of(j * TILE, TILE), TILE)
            kk = proj_ref[keys, cols.k : cols.k + LANES]
            p = jnp.exp(nt(kk, q2) - lse)
            if masked:
                p = jnp.where(diagonal, p, 0.0)
            ds = (p * (nt(proj_ref[keys, cols.v : cols.v + LANES], do2) - delta)).astype(B16)
            dv_sum[keys, :] += nn(p.astype(B16), do2)
            dk_sum[keys, :] += nn(ds, q2)
            return dq + tn(kk, ds)

        dq = jnp.zeros((LANES, 2 * TILE), F32)
        dq = lax.fori_loop(0, i, lambda j, c: piece_of(j, c, False), dq)
        dq = piece_of(i, dq, True)
        joined = jnp.concatenate([dq[:HD, :TILE], dq[HD:, TILE:]], axis=0) * HD**-0.5
        dproj_ref[rows, cols.q : cols.q + LANES] = joined.T.astype(B16)
        return 0

    lax.fori_loop(0, length // TILE, attend, 0)
    dproj_ref[:, cols.k : cols.k + LANES] = dk_sum[...].astype(B16)
    dproj_ref[:, cols.v : cols.v + LANES] = dv_sum[...].astype(B16)

    ri, ci = iotas(STEP, STEP)
    upper = ri <= ci
    tril = (ri >= ci).astype(F32)
    triu = upper.astype(F32)
    low_lanes = ci < HD
    decay = jnp.exp(hp_ref[0:1, :])
    bias = hp_ref[1:2, :]
    grad_state[...] = jnp.zeros_like(grad_state)
    skip_sum[...] = jnp.zeros_like(skip_sum)
    heads_ref[...] = jnp.zeros_like(heads_ref)
    zero_rows = jnp.zeros((STEP - 2 * cols.pairs, LANES), F32)

    def scan_block(back, _):
        b = blocks - 1 - back
        rows = pl.ds(pl.multiple_of(b * STEP, STEP), STEP)
        raw = step_ref[rows, :] + bias
        dt = softplus(raw)
        a = -dt * decay
        run = exact(tril, a)
        run_t = run.T
        bm = proj_ref[rows, cols.b : cols.b + LANES]
        cm = proj_ref[rows, cols.c : cols.c + LANES]
        cbt = jnp.where(upper, nt(bm, cm), 0.0)
        low_state = states_ref[b]
        grads_out = grad_state[...]
        low_grad = grads_out.astype(B16)
        carried = nn(cm, low_state)
        pulled = nn(bm, low_grad)
        dcb = jnp.zeros((STEP, STEP), F32)
        dy_fades, u_tails, fades = [], [], []
        carry_terms, direct_terms, tail_terms = [], [], []
        row_sums = []
        col_sums = jnp.zeros((STEP, LANES), F32)
        for p in range(cols.pairs):
            lanes = slice(LANES * p, LANES * (p + 1))
            u16 = proj_ref[rows, cols.u + LANES * p : cols.u + LANES * (p + 1)]
            u = u16.astype(F32)
            z = proj_ref[rows, cols.z + LANES * p : cols.z + LANES * (p + 1)].astype(F32)
            y = y_ref[rows, lanes].astype(F32)
            dm = dcore[rows, lanes].astype(F32)
            sg = sigmoid(z)
            dy = dm * z * sg
            dproj_ref[rows, cols.z + LANES * p : cols.z + LANES * (p + 1)] = (
                dm * y * sg * (1.0 + z * (1.0 - sg))
            ).astype(B16)
            dy16 = dy.astype(B16)
            skip_sum[:, lanes] += u * dy
            run_b = [spread(run, 2 * p + k, STEP) for k in range(2)]
            dt_b = [spread(dt, 2 * p + k, STEP) for k in range(2)]
            run_w = jnp.where(low_lanes, run_b[0], run_b[1])
            dt_w = jnp.where(low_lanes, dt_b[0], dt_b[1])
            end = run_w[STEP - 1 : STEP, :]
            fade = jnp.exp(run_w)
            tail = jnp.exp(end - run_w)
            dmix = nt(split_heads(u16, low_lanes), dy16)
            mixes = []
            for k in range(2):
                gap = jnp.exp(jnp.minimum(run_t[2 * p + k : 2 * p + k + 1, :] - run_b[k], 0.0))
                mixes.append((gap * cbt).astype(B16))
                weighted = gap * dt_b[k] * dmix[STEP * k : STEP * (k + 1), :]
                dcb += weighted
                moved = weighted * cbt
                row_sums.append(jnp.sum(moved, axis=0, keepdims=True))
                col_sums = jnp.where(
                    ci == 2 * p + k, jnp.sum(moved, axis=1, keepdims=True), col_sums
                )
            inside = nn(jnp.concatenate(mixes, axis=1), split_heads(dy16, low_lanes))
            pull_tail = tail * pulled[:, lanes]
            g = inside + pull_tail
            dproj_ref[rows, cols.u + LANES * p : cols.u + LANES * (p + 1)] = (
                dt_w * g + dsk_ref[0:1, lanes] * dy
            ).astype(B16)
            dy_fade = dy * fade
            dy_fades.append(dy_fade.astype(B16))
            u_tails.append((u * dt_w * tail).astype(B16))
            fades.append(jnp.exp(end))
            carry_terms.append((dy_fade * carried[:, lanes]).astype(B16))
            direct_terms.append((u * g).astype(B16))
            tail_terms.append((u * pull_tail).astype(B16))
        dy_fade = jnp.concatenate(dy_fades, axis=1)
        dcb = jnp.where(upper, dcb, 0.0).astype(B16)
        dproj_ref[rows, cols.c : cols.c + LANES] = (tn(dcb, bm) + nt(dy_fade, low_state)).astype(B16)
        dproj_ref[rows, cols.b : cols.b + LANES] = (
            nn(dcb, cm) + nt(jnp.concatenate(u_tails, axis=1), low_grad)
        ).astype(B16)
        group = group_ref[...]
        carry_term = nn(jnp.concatenate(carry_terms, axis=1), group)
        direct_term = nn(jnp.concatenate(direct_terms, axis=1), group)
        tail_term = dt * nn(jnp.concatenate(tail_terms, axis=1), group)
        overlap = jnp.sum(low_state.astype(F32) * grads_out, axis=0, keepdims=True)
        overlap = exact(jnp.broadcast_to(overlap, (8, width)), group.astype(F32))[0:1, :]
        overlap = overlap * jnp.exp(run[STEP - 1 : STEP, :])
        row_sum = jnp.concatenate(row_sums + [zero_rows], axis=0).T
        d_run = row_sum - col_sums + carry_term - tail_term
        d_a = exact(triu, d_run) + (jnp.sum(tail_term, axis=0, keepdims=True) + overlap)
        d_step = (direct_term - decay * d_a) * sigmoid(raw)
        dproj_ref[rows, cols.step : cols.step + LANES] = d_step.astype(B16)
        heads_ref[0:1, :] += jnp.sum(d_a * a, axis=0, keepdims=True)
        heads_ref[1:2, :] += jnp.sum(d_step, axis=0, keepdims=True)
        grad_state[...] = grads_out * jnp.concatenate(fades, axis=1) + tn(cm, dy_fade)
        return 0

    lax.fori_loop(0, blocks, scan_block, 0)
    skip = jnp.sum(skip_sum[...], axis=0, keepdims=True)
    heads_ref[2:3, :] = exact(jnp.broadcast_to(skip, (8, width)), group_ref[...].astype(F32))[0:1, :]
    multiply_back(dproj_ref, wcat_ref, part_ref)

    def fold(i, _):
        rows = pl.ds(pl.multiple_of(i * TILE, TILE), TILE)
        folded[rows, :] = nn(dproj_ref[rows, cols.b :], fold_ref[...]).astype(B16)
        return 0

    lax.fori_loop(0, length // TILE, fold, 0)
    depth = wcat_ref.shape[0]
    share = depth // members
    sub = piece // members
    for k in range(ways):
        grad = tn(rows_ref[:, k * piece : (k + 1) * piece], folded[...]).astype(B16)
        for t in range(members):
            part_ref[t * share + k * sub : t * share + (k + 1) * sub, depth:] = grad[
                t * sub : (t + 1) * sub, :
            ]


def multiply_back(grad_ref, weight_ref, part_ref):
    def out_rows(i, _):
        rows = pl.ds(pl.multiple_of(i * TILE, TILE), TILE)
        block = grad_ref[rows, :]
        for first in range(0, weight_ref.shape[0], 256):
            part_ref[rows, first : first + 256] = nt(
                block, weight_ref[first : first + 256, :]
            ).astype(B16)
        return 0

    lax.fori_loop(0, grad_ref.shape[0] // TILE, out_rows, 0)


def ffn_fwd_kernel(rows_ref, wgu_ref, wdown_ref, gu_ref, hidden_ref, part_ref):
    units = hidden_ref.shape[1]

    def up(i, _):
        rows = pl.ds(pl.multiple_of(i * TILE, TILE), TILE)
        block = rows_ref[rows, :]
        g = nn(block, wgu_ref[:, :units])
        v = nn(block, wgu_ref[:, units:])
        gu_ref[rows, :units] = g.astype(B16)
        gu_ref[rows, units:] = v.astype(B16)
        hidden_ref[rows, :] = (g * sigmoid(g) * v).astype(B16)
        return 0

    lax.fori_loop(0, rows_ref.shape[0] // TILE, up, 0)
    multiply_out(hidden_ref, wdown_ref, part_ref)


def ffn_bwd_kernel(out_ref, wgu_ref, wdown_ref, gu_ref, dgu_ref, part_ref):
    ways, units, piece = wdown_ref.shape

    def down(i, _):
        rows = pl.ds(pl.multiple_of(i * TILE, TILE), TILE)
        dh = nt(out_ref[rows, 0:piece], wdown_ref[0])
        for k in range(1, ways):
            dh += nt(out_ref[rows, k * piece : (k + 1) * piece], wdown_ref[k])
        g = gu_ref[rows, :units].astype(F32)
        v = gu_ref[rows, units:].astype(F32)
        sg = sigmoid(g)
        dgu_ref[rows, :units] = (dh * v * sg * (1.0 + g * (1.0 - sg))).astype(B16)
        dgu_ref[rows, units:] = (dh * g * sg).astype(B16)
        return 0

    lax.fori_loop(0, out_ref.shape[0] // TILE, down, 0)
    multiply_back(dgu_ref, wgu_ref, part_ref)


def whole_call(kernel, outs, scratch, flops, name):
    vmem = pl.BlockSpec(memory_space=pltpu.VMEM)

    def call(*operands):
        moved = sum(o.size * o.dtype.itemsize for o in operands)
        return pl.pallas_call(
            kernel,
            out_shape=[jax.ShapeDtypeStruct(s, t) for s, t in outs],
            in_specs=[vmem] * len(operands),
            out_specs=[vmem] * len(outs),
            scratch_shapes=scratch,
            compiler_params=pltpu.CompilerParams(vmem_limit_bytes=VMEM_LIMIT),
            cost_estimate=pl.CostEstimate(flops=flops, bytes_accessed=2 * moved, transcendentals=0),
            name=name,
        )(*operands)

    return call


def core_fwd(cols, rows, wcat, wout, hp, dsk):
    length, depth = rows.shape
    width = cols.width
    return whole_call(
        functools.partial(core_fwd_kernel, cols),
        [
            ((length, cols.step), B16),
            ((length, LANES), F32),
            ((length, width), B16),
            ((length, width + LANES), B16),
            ((length // STEP, NS, width), B16),
            ((length // TILE, 8, 2 * TILE), F32),
            ((length, depth), B16),
        ],
        [pltpu.VMEM((NS, width), F32)],
        20 * length * depth * cols.total,
        "core_fwd",
    )(rows, wcat, wout, hp, dsk)


def core_bwd(cols, members, back, wcat, wout, hp, dsk, group, rows, fold, kept):
    length, depth = back.shape
    width = cols.width
    wide = cols.total - cols.b
    return whole_call(
        functools.partial(core_bwd_kernel, cols, members),
        [((length, cols.total), B16), ((8, LANES), F32), ((length, depth + wide), B16)],
        [
            pltpu.VMEM((length, width + LANES), B16),
            pltpu.VMEM((NS, width), F32),
            pltpu.VMEM((STEP, width), F32),
            pltpu.VMEM((length, LANES), F32),
            pltpu.VMEM((length, LANES), F32),
            pltpu.VMEM((length, wide), B16),
        ],
        40 * length * depth * cols.total,
        "core_bwd",
    )(back, wcat, wout, hp, dsk, group, rows, fold, *kept)


def ffn_fwd(rows, wgu, wdown):
    length, depth = rows.shape
    units = wdown.shape[1]
    return whole_call(
        ffn_fwd_kernel,
        [((length, 2 * units), B16), ((length, units), B16), ((length, depth), B16)],
        [],
        6 * length * depth * units,
        "ffn_fwd",
    )(rows, wgu, wdown)


def ffn_bwd(out, wgu, wdown, gu):
    length, depth = out.shape
    units = wdown.shape[1]
    return whole_call(
        ffn_bwd_kernel,
        [((length, 2 * units), B16), ((length, depth), B16)],
        [],
        6 * length * depth * units,
        "ffn_bwd",
    )(out, wgu, wdown, gu)


def grad_columns(rows_ref, grad_ref, out_ref):
    _, ways, half, width = out_ref.shape
    for k in range(ways):
        block = rows_ref[:, 2 * half * k : 2 * half * (k + 1)]
        for first in range(0, width, 512):
            last = min(first + 512, width)
            value = tn(block, grad_ref[:, first:last]).astype(B16)
            out_ref[0, k, :, first:last] = value[:half, :]
            out_ref[1, k, :, first:last] = value[half:, :]


def grad_rows(lows_ref, back_ref, out_ref):
    _, ways, half, piece = out_ref.shape
    for h in range(2):
        block = lows_ref[:, h * half : (h + 1) * half]
        for k in range(ways):
            out_ref[h, k] = tn(block, back_ref[:, k * piece : (k + 1) * piece]).astype(B16)


def ffn_grads_kernel(rows_ref, dgu_ref, hidden_ref, out_ref, gu_ref, down_ref):
    grad_columns(rows_ref, dgu_ref, gu_ref)
    grad_rows(hidden_ref, out_ref, down_ref)


def ffn_grads(ways, rows, dgu, hidden, out):
    length, depth = rows.shape
    half = depth // ways // 2
    units = hidden.shape[1]
    return whole_call(
        ffn_grads_kernel,
        [((2, ways, half, 2 * units), B16), ((2, ways, units // 2, depth // ways), B16)],
        [],
        6 * length * depth * units,
        "ffn_grads",
    )(rows, dgu, hidden, out)


def cat_grads(ways, width, rows, dproj):
    length, depth = rows.shape
    return whole_call(
        grad_columns,
        [((2, ways, depth // ways // 2, width), B16)],
        [],
        2 * length * depth * width,
        "cat_grads",
    )(rows, dproj)[0]


def out_grads(ways, lows, back):
    length, depth = back.shape
    units = lows.shape[1]
    return whole_call(
        grad_rows,
        [((2, ways, units // 2, depth // ways), B16)],
        [],
        2 * length * depth * units,
        "out_grads",
    )(lows, back)[0]


def exchange_kernel(plan, *refs):
    refs = list(refs)
    take = lambda count: [refs.pop(0) for _ in range(count)]
    part_ref = take(1)[0] if plan.scatter else None
    local_refs = take(plan.locals)
    out_refs = take(plan.outs)
    rows_ref = take(1)[0] if plan.gather else None
    if plan.scatter:
        pair_in, far_out, far_in, pair_send, pair_recv, far_send, far_recv = take(7)
    if plan.gather:
        give_send, give_recv, spread_send, spread_recv = take(4)

    members, pieces = plan.members, plan.pieces
    pairs = members // 2
    me = lax.axis_index("tensor")
    mine, side = me // 2, me % 2
    sibling = 2 * mine + 1 - side
    size = plan.rows // pieces

    def far(k):
        return 2 * ((mine + k) % pairs) + side

    def across(k):
        return 2 * ((mine + k) % pairs) + 1 - side

    def rows_of(member, c):
        return pl.ds(pl.multiple_of(member * plan.rows + c * size, size), size)

    def chunk(c):
        return pl.ds(c * size, size)

    def copy(source, target, send, receive, member):
        return pltpu.make_async_remote_copy(
            src_ref=source, dst_ref=target, send_sem=send, recv_sem=receive,
            device_id={"tensor": member}, device_id_type=pl.DeviceIdType.MESH,
        )

    barrier = pltpu.get_barrier_semaphore()
    for member in [sibling] + [far(k) for k in range(1, pairs)]:
        pl.semaphore_signal(
            barrier, inc=1, device_id={"tensor": member}, device_id_type=pl.DeviceIdType.MESH
        )
    pl.semaphore_wait(barrier, pairs)

    if plan.scatter:
        to_pair = {}
        for c in range(pieces):
            for k in range(1, pairs):
                to_pair[k, c] = copy(
                    part_ref.at[rows_of(across(k), c), :], pair_in.at[k, chunk(c), :],
                    pair_send.at[k, c], pair_recv.at[k, c], sibling,
                )
                to_pair[k, c].start()
        for c in range(pieces):
            to_pair[0, c] = copy(
                part_ref.at[rows_of(sibling, c), :], pair_in.at[0, chunk(c), :],
                pair_send.at[0, c], pair_recv.at[0, c], sibling,
            )
            to_pair[0, c].start()
        to_far = {}
        for c in range(pieces):
            for k in range(1, pairs):
                to_pair[k, c].wait_recv()
                far_out[k - 1, chunk(c), :] = (
                    part_ref[rows_of(far(k), c), :].astype(F32)
                    + pair_in[k, chunk(c), :].astype(F32)
                ).astype(B16)
                to_far[k, c] = copy(
                    far_out.at[k - 1, chunk(c), :], far_in.at[pairs - k - 1, chunk(c), :],
                    far_send.at[k - 1, c], far_recv.at[pairs - k - 1, c], far(k),
                )
                to_far[k, c].start()

    given, spreads = {}, {}
    for c in range(pieces):
        total = None
        if plan.scatter:
            to_pair[0, c].wait_recv()
            total = part_ref[rows_of(me, c), :].astype(F32) + pair_in[0, chunk(c), :].astype(F32)
            for k in range(1, pairs):
                copy(
                    far_out.at[k - 1, chunk(c), :], far_in.at[k - 1, chunk(c), :],
                    far_send.at[k - 1, c], far_recv.at[k - 1, c], far(k),
                ).wait_recv()
                total += far_in[k - 1, chunk(c), :].astype(F32)
        result = plan.work(c, chunk(c), total, local_refs, out_refs)
        if plan.gather:
            own = rows_ref.at[rows_of(me, c), :]
            rows_ref[rows_of(me, c), :] = result
            for k in range(1, pairs):
                spreads[k, c] = copy(
                    own, own, spread_send.at[k - 1, c], spread_recv.at[pairs - k - 1, c], far(k)
                )
                spreads[k, c].start()
            given[0, c] = copy(own, own, give_send.at[0, c], give_recv.at[0, c], sibling)
            given[0, c].start()
    if plan.gather:
        for c in range(pieces):
            for k in range(1, pairs):
                block = rows_ref.at[rows_of(far(k), c), :]
                copy(
                    block, block, spread_send.at[k - 1, c], spread_recv.at[k - 1, c], far(k)
                ).wait_recv()
                given[k, c] = copy(block, block, give_send.at[k, c], give_recv.at[k, c], sibling)
                given[k, c].start()
        for c in range(pieces):
            for k in range(pairs):
                block = rows_ref.at[rows_of(sibling if k == 0 else across(k), c), :]
                copy(block, block, give_send.at[k, c], give_recv.at[k, c], sibling).wait_recv()
        for c in range(pieces):
            for k in range(pairs):
                given[k, c].wait_send()
            for k in range(1, pairs):
                spreads[k, c].wait_send()
    if plan.scatter:
        for c in range(pieces):
            for k in range(pairs):
                to_pair[k, c].wait_send()
            for k in range(1, pairs):
                to_far[k, c].wait_send()


class Plan:
    def __init__(self, members, rows, pieces, scatter, gather, count, outs, work):
        self.members = members
        self.rows = rows
        self.pieces = pieces
        self.scatter = scatter
        self.gather = gather
        self.locals = count
        self.outs = outs
        self.work = work


def exchange(name, number, members, part, local, outs, work, gather, pieces=4):
    rows, depth = local[0].shape
    scatter = part is not None
    pairs = members // 2
    plan = Plan(members, rows, pieces, scatter, gather, len(local), len(outs), work)
    vmem = pl.BlockSpec(memory_space=pltpu.VMEM)
    shapes = [jax.ShapeDtypeStruct(s, t) for s, t in outs]
    scratch = []
    dma = pltpu.SemaphoreType.DMA
    if scatter:
        wide = part.shape[1]
        others = max(pairs - 1, 1)
        scratch += [
            pltpu.VMEM((pairs, rows, wide), B16),
            pltpu.VMEM((others, rows, wide), B16),
            pltpu.VMEM((others, rows, wide), B16),
            dma((pairs, pieces)), dma((pairs, pieces)), dma((others, pieces)), dma((others, pieces)),
        ]
    if gather:
        shapes.append(jax.ShapeDtypeStruct((members * rows, depth), B16))
        others = max(pairs - 1, 1)
        scratch += [
            dma((pairs, pieces)), dma((pairs, pieces)), dma((others, pieces)), dma((others, pieces)),
        ]
    operands = ([part] if scatter else []) + list(local)
    return pl.pallas_call(
        functools.partial(exchange_kernel, plan),
        out_shape=shapes,
        in_specs=[vmem] * len(operands),
        out_specs=[vmem] * len(shapes),
        scratch_shapes=scratch,
        compiler_params=pltpu.CompilerParams(
            collective_id=number, has_side_effects=True, vmem_limit_bytes=VMEM_LIMIT
        ),
        cost_estimate=pl.CostEstimate(
            flops=20_000_000_000, bytes_accessed=50_000_000, transcendentals=0
        ),
        name=name,
    )(*operands)


def rms(rows, gain):
    scale = lax.rsqrt(jnp.mean(rows * rows, axis=-1, keepdims=True) + EPS)
    return rows * scale * gain


def rms_back(rows, gain, grad):
    scale = lax.rsqrt(jnp.mean(rows * rows, axis=-1, keepdims=True) + EPS)
    scaled = gain * grad
    mean = jnp.mean(scaled * rows, axis=-1, keepdims=True)
    into_gain = jnp.sum(grad * rows * scale, axis=0, keepdims=True)
    return scale * scaled - rows * (scale * scale * scale * mean), into_gain


def work_first(c, at, total, local, outs):
    x, gain = local
    return rms(x[at, :].astype(F32), gain[0:1, :]).astype(B16)


def work_hand(c, at, total, local, outs):
    return local[0][at, :]


def work_mid(c, at, total, local, outs):
    x, gain = local
    residual = x[at, :].astype(F32) + total
    outs[0][at, :] = residual
    return rms(residual, gain[0:1, :]).astype(B16)


def work_turn(c, at, total, local, outs):
    residual, gain = local
    out = (residual[at, :] + total).astype(B16)
    outs[0][at, :] = out
    return rms(out.astype(F32), gain[0:1, :]).astype(B16)


def work_last(c, at, total, local, outs):
    outs[0][at, :] = (local[0][at, :] + total).astype(B16)


def add_gain(c, ref, row):
    if c == 0:
        ref[...] = jnp.zeros_like(ref)
    ref[0:1, :] += row


def work_back_ffn(c, at, total, local, outs):
    residual, cotangent, gain = local
    step, into_gain = rms_back(residual[at, :], gain[0:1, :], total)
    grad = cotangent[at, :].astype(F32) + step
    outs[0][at, :] = grad
    add_gain(c, outs[1], into_gain)
    return grad.astype(B16)


def work_back_mix(c, at, total, local, outs):
    x, d_residual, gain = local
    depth = x.shape[1]
    step, into_gain = rms_back(x[at, :].astype(F32), gain[0:1, :], total[:, :depth])
    grad = (d_residual[at, :] + step).astype(B16)
    outs[0][at, :] = grad
    outs[2][at, :] = total[:, depth:].astype(B16)
    add_gain(c, outs[1], into_gain)
    return grad


def widen(block, axis, size):
    missing = size - block.shape[axis]
    if missing == 0:
        return block
    pads = [(0, 0)] * block.ndim
    pads[axis] = (0, missing)
    return jnp.pad(block, pads)


def on_device(
    acts_in, out_grad, mix_gain, w_mixer_in, w_query, w_shared, w_step, a_log, dt_bias, d_skip,
    w_mamba_out, w_attn_out, ffn_gain, w_gate_up, w_down,
):
    section = lax.axis_index("pipe")
    member = lax.axis_index("tensor")
    dp = lax.axis_size("dp")
    heads = a_log.shape[1]
    even = heads + heads % 2
    real = heads * HD
    width = even * HD
    q_real = w_query.shape[2]
    group = member * (q_real // HD) // (HA // KVH)
    cols = Cols(width)
    units = w_gate_up.shape[3]
    depth = acts_in.shape[2]
    piece = depth // dp

    shared = w_shared[0]
    keys = lax.dynamic_slice_in_dim(shared, 2 * NS + group * HD, HD, 1)
    values = lax.dynamic_slice_in_dim(shared, 2 * NS + KVH * HD + group * HD, HD, 1)
    steps = lax.dynamic_slice_in_dim(w_step[0], member * heads, heads, 1)
    wcat = jnp.concatenate(
        [
            widen(w_mixer_in[0, :, 0], 1, width),
            widen(w_mixer_in[0, :, 1], 1, width),
            widen(w_query[0], 1, LANES),
            shared[:, : 2 * NS],
            keys, keys, values, values,
            widen(steps, 1, LANES),
        ],
        axis=1,
    )
    gates = w_gate_up[0].reshape(piece, 2 * units)
    wout = jnp.concatenate(
        [
            widen(w_mamba_out[0], 0, width),
            widen(w_attn_out[0], 0, LANES),
            w_down[0],
            widen(jnp.concatenate([mix_gain, ffn_gain]), 0, 16),
        ],
        axis=0,
    )
    both = ("pipe", "dp")
    wcat_all = lax.all_gather(wcat, both, axis=0, tiled=True).reshape(2, depth, cols.total)
    wout_all = lax.all_gather(wout, both, axis=0)
    gates_all = lax.all_gather(gates, both, axis=0, tiled=True).reshape(2, depth, 2 * units)
    wout_all = wout_all.reshape((2, dp) + wout.shape)
    heads_all = lax.all_gather(jnp.concatenate([a_log, dt_bias, d_skip]), "pipe", axis=0)

    core_rows = width + LANES
    wide = cols.total - cols.b
    source, target = iotas(wide, wide)
    kind = source // LANES
    wanted = jnp.where(
        kind < 2,
        source,
        jnp.where(
            kind < 4,
            2 * NS + (kind - 2) * KVH * HD + group * HD + source % HD,
            source + member * heads,
        ),
    )
    fold = ((target == wanted) & (source < 4 * LANES + heads)).astype(B16)
    sub = jnp.arange(width)[:, None] // HD == jnp.arange(LANES)[None, :]
    layers = []
    for layer in range(2):
        gains = wout_all[layer, :, core_rows + units : core_rows + units + 2]
        gains = gains.transpose(1, 0, 2).reshape(2, depth).astype(F32)
        hp = widen(widen(heads_all[layer], 1, LANES), 0, 8)
        layers.append(
            dict(
                wcat=wcat_all[layer],
                wout=wout_all[layer, :, :core_rows],
                wdown=wout_all[layer, :, core_rows : core_rows + units],
                wgu=gates_all[layer],
                mix=jnp.broadcast_to(gains[:1], (8, depth)),
                ffn=jnp.broadcast_to(gains[1:], (8, depth)),
                hp=hp,
                dsk=jnp.broadcast_to(jnp.repeat(hp[2, :even], HD)[None], (8, width)),
                group=sub.astype(B16),
            )
        )

    members = lax.axis_size("tensor")
    rows = acts_in.shape[1]
    x = lax.dynamic_index_in_dim(acts_in, section, 0, False)
    y_grad = lax.dynamic_index_in_dim(out_grad, section, 0, False)
    wide = cols.total - cols.b
    block, block32, gain_row = ((rows, depth), B16), ((rows, depth), F32), ((8, depth), F32)

    def run(name, number, part, local, outs, work, gather):
        return exchange(name, number, members, part, local, outs, work, gather)

    acts, kept = [], []
    first, second = layers
    rows_mix = run("first", 0, None, [x, first["mix"]], [], work_first, True)[0]
    rows_out = run("hand", 1, None, [y_grad], [], work_hand, True)[0]
    for layer, w in enumerate(layers):
        *saved, part = core_fwd(cols, rows_mix, w["wcat"], w["wout"], w["hp"], w["dsk"])
        residual, rows_ffn = run(
            f"mid_{layer}", 2 + layer, part, [x, w["ffn"]], [block32], work_mid, True
        )
        gu, hidden, part = ffn_fwd(rows_ffn, w["wgu"], w["wdown"])
        kept.append((x, rows_mix, saved, residual, rows_ffn, gu, hidden))
        if layer == 0:
            x, rows_mix = run(
                "turn", 4, part, [residual, second["mix"]], [block], work_turn, True
            )
            acts.append(x)
        else:
            acts += run("last", 5, part, [residual], [block], work_last, False)

    def swap(block):
        return lax.ppermute(block, "pipe", [(0, 1), (1, 0)])

    def pick(pair):
        return jnp.where(section == 0, pair[0], pair[1])

    def other(pair):
        return jnp.where(section == 0, pair[1], pair[0])

    def by_section(mine, received):
        return jnp.where(section == 0, jnp.stack([mine, received]), jnp.stack([received, mine]))

    def half_sum(halves):
        received = swap(lax.dynamic_index_in_dim(halves, 1 - section, 0, False))
        mine = lax.dynamic_index_in_dim(halves, section, 0, False)
        total = (mine.astype(F32) + received.astype(F32)).astype(B16)
        return lax.psum_scatter(total, "dp", scatter_dimension=0, tiled=False)

    x_grads, gains, head_grads, sums = [None] * 2, [None] * 2, [None] * 2, [None] * 2
    for layer in (1, 0):
        w = layers[layer]
        x, rows_mix, saved, residual, rows_ffn, gu, hidden = kept[layer]
        dgu, part = ffn_bwd(rows_out, w["wgu"], w["wdown"], gu)
        d_residual, gain_ffn, rows_back = run(
            f"back_ffn_{layer}", 6 + layer, part, [residual, y_grad, w["ffn"]],
            [block32, gain_row], work_back_ffn, True,
        )
        g_gu, g_down = ffn_grads(dp, rows_ffn, dgu, hidden, rows_out)
        g_out = out_grads(dp, saved[3], rows_back)
        dproj, head_grads[layer], part = core_bwd(
            cols, members, rows_back, w["wcat"], w["wout"], w["hp"], w["dsk"], w["group"],
            rows_mix, fold, saved,
        )
        y_grad, gain_mix, shared_part, *more = run(
            f"back_mix_{layer}", 8 + layer, part, [x, d_residual, w["mix"]],
            [block, gain_row, ((rows, wide), B16)], work_back_mix, layer == 1,
        )
        rows_out = more[0] if more else None
        x_grads[layer] = y_grad
        g_cat = cat_grads(dp, cols.b, rows_mix, dproj)
        gains[layer] = jnp.stack([gain_mix[0], gain_ffn[0]])
        shared_sum = lax.psum_scatter(
            shared_part.reshape(dp, rows // dp, wide), "dp", scatter_dimension=0, tiled=False
        )
        sums[layer] = [half_sum(g) for g in (g_gu, g_down, g_out, g_cat)] + [shared_sum]

    acts = by_section(pick(acts), swap(other(acts)))
    in_grads = by_section(pick(x_grads), swap(other(x_grads)))
    pairs = list(zip(*sums))
    g_gates, g_down, g_out, g_cat = [
        by_section(pick(pair), swap(other(pair))).reshape((-1,) + pair[0].shape[1:]).astype(F32)
        for pair in pairs[:4]
    ]
    g_shared = pick(pairs[4]).astype(F32) + swap(other(pairs[4])).astype(F32)
    slots = [
        lax.dynamic_update_index_in_dim(
            jnp.zeros((members, 3, heads), F32), h[:3, :heads], member, 0
        ).reshape(-1)
        for h in head_grads
    ]
    small = jnp.stack([jnp.concatenate([g.reshape(-1), s]) for g, s in zip(gains, slots)])
    small = lax.psum(small, ("pipe", "dp", "tensor"))
    small = lax.dynamic_index_in_dim(small, section, 0, False)
    place = lax.axis_index("dp") * members + member
    share = depth // (dp * members)
    g_gains = lax.dynamic_slice_in_dim(small[: 2 * depth].reshape(2, depth), place * share, share, 1)
    g_heads = small[2 * depth :].reshape(members, 3, heads)
    g_heads = lax.dynamic_index_in_dim(g_heads, member, 0, False)
    g_mixer = jnp.stack([g_cat[:, :real], g_cat[:, width : width + real]], axis=1)
    table = 2 * NS + 2 * KVH * HD
    return (
        acts[None],
        in_grads[None],
        g_gains[None],
        g_mixer[None],
        g_cat[None, :, cols.q : cols.q + q_real],
        g_shared[None, :, :table],
        g_shared[None, :, table : table + HM],
        g_heads[None],
        g_out[None, :real],
        g_out[None, width : width + q_real],
        g_gates.reshape(1, piece, 2, units),
        g_down[None],
    )


def solution(mesh):
    placed = (
        P("dp", "tensor", None),
        P("dp", "tensor", None),
        P("pipe", "dp"),
        P("pipe", "dp", None, "tensor"),
        P("pipe", "dp", "tensor"),
        P("pipe", "dp", None),
        P("pipe", "dp", None),
        P("pipe", "tensor"),
        P("pipe", "tensor"),
        P("pipe", "tensor"),
        P("pipe", "tensor", "dp"),
        P("pipe", "tensor", "dp"),
        P("pipe", "dp"),
        P("pipe", "dp", None, "tensor"),
        P("pipe", "tensor", "dp"),
    )
    return jax.shard_map(
        on_device,
        mesh=mesh,
        in_specs=placed,
        out_specs=(
            P("pipe", "dp", "tensor", None),
            P("pipe", "dp", "tensor", None),
            P("pipe", None, ("dp", "tensor")),
            P("pipe", "dp", None, "tensor"),
            P("pipe", "dp", "tensor"),
            P("pipe", ("dp", "tensor"), None),
            P("pipe", ("dp", "tensor"), None),
            P("pipe", None, "tensor"),
            P("pipe", "tensor", "dp"),
            P("pipe", "tensor", "dp"),
            P("pipe", "dp", None, "tensor"),
            P("pipe", "tensor", "dp"),
        ),
        check_vma=False,
    )
```

```python
import functools

import jax
import jax.numpy as jnp
from jax import lax
from jax.experimental import pallas as pl
from jax.experimental.pallas import tpu as pltpu
from jax.sharding import PartitionSpec as P

HM = 24
HA = 8
KVH = 2
NS = 128
HD = 64
LANES = 128
STEP = 128
TILE = 256
EPS = 1e-05
F32 = jnp.float32
B16 = jnp.bfloat16
VMEM_LIMIT = 60 << 20
HEADS_AT = 32
GAINS_AT = 64


def nn(a, b):
    return lax.dot_general(a, b, (((1,), (0,)), ((), ())), preferred_element_type=F32)


def nt(a, b):
    return lax.dot_general(a, b, (((1,), (1,)), ((), ())), preferred_element_type=F32)


def tn(a, b):
    return lax.dot_general(a, b, (((0,), (0,)), ((), ())), preferred_element_type=F32)


def exact(a, b):
    return lax.dot_general(
        a, b, (((1,), (0,)), ((), ())), precision=lax.Precision.HIGHEST, preferred_element_type=F32
    )


def softplus(v):
    small = jnp.exp(-jnp.abs(v))
    series = small * (1.0 - small * (0.5 - small * (1.0 / 3.0 - small * 0.25)))
    return jnp.maximum(v, 0.0) + jnp.where(small < 0.02, series, jnp.log(1.0 + small))


def sigmoid(v):
    return 1.0 / (1.0 + jnp.exp(-v))


def iotas(rows, columns):
    return (
        lax.broadcasted_iota(jnp.int32, (rows, columns), 0),
        lax.broadcasted_iota(jnp.int32, (rows, columns), 1),
    )


def spread(column_block, head, rows):
    return jnp.broadcast_to(column_block[:, head : head + 1], (rows, LANES))


class Cols:
    def __init__(self, width):
        self.width = width
        self.z = 0
        self.u = width
        self.q = 2 * width
        self.b = self.q + LANES
        self.c = self.b + LANES
        self.k = self.c + LANES
        self.v = self.k + LANES
        self.step = self.v + LANES
        self.total = self.step + LANES
        self.pairs = width // LANES


class MixerRows:
    def __init__(self, cols, members):
        self.shared = 4 * LANES // members
        self.query = self.shared
        self.inner = self.query + LANES
        self.low = self.inner + 2 * cols.width
        self.total = self.low + cols.width + LANES


def fold_lanes(block):
    def folded(piece):
        count = piece // LANES
        size = block.shape[0] // count
        return jnp.concatenate([block[i * size : (i + 1) * size] for i in range(count)], axis=1)

    return folded


def unfold_lanes(block):
    return jnp.concatenate(
        [block[:, at : at + LANES] for at in range(0, block.shape[1], LANES)], axis=0
    )


def join_shared(cols, members, layer, q_heads, r):
    mixer, shared, few, rest = r.mixer, r.shared_w, r.few, r.rest
    ways, _, piece = mixer.shape
    at = MixerRows(cols, members)
    group = lax.axis_index(TENSOR) * q_heads // (HA // KVH)
    source, target = iotas(LANES, LANES)
    choose = (source == group * HD + (target & (HD - 1))).astype(B16)
    size = piece // members
    for d in range(ways):
        rows = slice(d * piece, (d + 1) * piece)
        rest[rows, :LANES] = unfold_lanes(mixer[d, at.query : at.query + LANES, :])
        for m in range(members):
            block = unfold_lanes(shared[m, d])
            to = slice(d * piece + m * size, d * piece + (m + 1) * size)
            for j in range(4):
                lanes = block[j * size : (j + 1) * size, :]
                if j >= 2:
                    lanes = nn(lanes, choose).astype(B16)
                rest[to, LANES * (j + 1) : LANES * (j + 2)] = lanes
        steps = few[layer, d, 8:16, :]
        steps = jnp.concatenate([steps, jnp.zeros((LANES - 8, piece), F32)], axis=0).T
        rest[rows, 5 * LANES :] = steps.astype(B16)


def split_heads(block, low_lanes):
    zero = jnp.zeros_like(block)
    return jnp.concatenate(
        [jnp.where(low_lanes, block, zero), jnp.where(low_lanes, zero, block)], axis=0
    )


def blocks_nn(rows_ref, rows, weights_ref, c, first=0):
    ways, _, piece = weights_ref.shape
    at = slice(first + c * piece, first + (c + 1) * piece)
    total = nn(rows_ref[rows, 0:piece], weights_ref[0, at, :])
    for d in range(1, ways):
        total += nn(rows_ref[rows, d * piece : (d + 1) * piece], weights_ref[d, at, :])
    return total


def multiply_out(lows_ref, weights_ref, first, part_ref, at=0):
    ways, _, piece = weights_ref.shape
    last = first + lows_ref.shape[1]

    def out_rows(i, _):
        rows = pl.ds(pl.multiple_of(i * TILE, TILE), TILE)
        block = lows_ref[rows, :]
        for k in range(ways):
            part_ref[rows, at + k * piece : at + (k + 1) * piece] = nn(
                block, weights_ref[k, first:last, :]
            ).astype(B16)
        return 0

    lax.fori_loop(0, lows_ref.shape[0] // TILE, out_rows, 0)


def multiply_back(grad_ref, weights_ref, first, count, part_ref, rows_ref, gain_sum, rest=None):
    ways, _, piece = weights_ref.shape
    gain_sum[...] = jnp.zeros_like(gain_sum)

    def out_rows(i, _):
        rows = pl.ds(pl.multiple_of(i * TILE, TILE), TILE)
        for d in range(ways):
            to = slice(d * piece, (d + 1) * piece)
            total = nt(grad_ref[rows, 0:piece], weights_ref[d, first : first + piece, :])
            for c in range(1, count):
                at = slice(first + c * piece, first + (c + 1) * piece)
                total += nt(grad_ref[rows, c * piece : (c + 1) * piece], weights_ref[d, at, :])
            if rest is not None:
                total += nt(grad_ref[rows, count * piece :], rest[to, :])
            part_ref[rows, to] = total.astype(B16)
            gain_sum[0:1, to] += jnp.sum(
                total * rows_ref[rows, to].astype(F32), axis=0, keepdims=True
            )
        return 0

    lax.fori_loop(0, grad_ref.shape[0] // TILE, out_rows, 0)


def skip_lanes(few_ref, layer, width):
    row, lane = iotas(width, LANES)
    own = ((row >> 6) == lane).astype(F32)
    skip = jnp.broadcast_to(few_ref[layer, 0, 4:5, :LANES], (8, LANES))
    return lax.dot_general(
        skip, own, (((1,), (1,)), ((), ())),
        precision=lax.Precision.HIGHEST, preferred_element_type=F32,
    )[0:1, :]


def core_fwd_phases(cols, members, layer, q_heads, r):
    rows_ref, weights_ref, few_ref = r.rows_mix, r.mixer, r.few
    proj_ref, step_ref, y_ref, lows_ref = r.proj, r.step, r.y, r.lows
    states_ref, lse_ref, part_ref, state = r.states, r.lse, r.part, r.state
    length = rows_ref.shape[0]
    width = cols.width
    piece = weights_ref.shape[2]

    at_row = MixerRows(cols, members)

    def join_all():
        join_shared(cols, members, layer, q_heads, r)

    def project_all():
        def project(i, _):
            rows = pl.ds(pl.multiple_of(i * TILE, TILE), TILE)
            for c in range(cols.q // piece):
                value = blocks_nn(rows_ref, rows, weights_ref, c, at_row.inner)
                proj_ref[rows, c * piece : (c + 1) * piece] = value.astype(B16)
            rest = nn(rows_ref[rows, :], r.rest[...])
            proj_ref[rows, cols.q : cols.b] = (rest[:, :LANES] * HD**-0.5).astype(B16)
            proj_ref[rows, cols.b : cols.step] = rest[:, LANES : 5 * LANES].astype(B16)
            step_ref[rows, :] = rest[:, 5 * LANES :]
            return 0

        lax.fori_loop(0, length // TILE, project, 0)

    def scan_all():
        ri, ci = iotas(STEP, STEP)
        lower = ri >= ci
        tril = lower.astype(F32)
        low_lanes = ci < HD
        decay = jnp.exp(few_ref[layer, 0, 2:3, :LANES])
        bias = few_ref[layer, 0, 3:4, :LANES]
        skips = skip_lanes(few_ref, layer, width)
        state[...] = jnp.zeros_like(state)

        def scan_block(b, _):
            rows = pl.ds(pl.multiple_of(b * STEP, STEP), STEP)
            dt = softplus(step_ref[rows, :] + bias)
            run = exact(tril, -dt * decay)
            run_t = run.T
            bm = proj_ref[rows, cols.b : cols.b + LANES]
            cm = proj_ref[rows, cols.c : cols.c + LANES]
            cb = jnp.where(lower, nt(cm, bm), 0.0)
            states_in = state[...]
            low_state = states_in.astype(B16)
            states_ref[b] = low_state
            carried = nn(cm, low_state)
            tails, fades = [], []
            for p in range(cols.pairs):
                lanes = slice(LANES * p, LANES * (p + 1))
                u = proj_ref[rows, cols.u + LANES * p : cols.u + LANES * (p + 1)].astype(F32)
                z = proj_ref[rows, cols.z + LANES * p : cols.z + LANES * (p + 1)].astype(F32)
                run_b = [spread(run, 2 * p + k, STEP) for k in range(2)]
                run_w = jnp.where(low_lanes, run_b[0], run_b[1])
                ud = u * jnp.where(low_lanes, spread(dt, 2 * p, STEP), spread(dt, 2 * p + 1, STEP))
                mix = jnp.concatenate(
                    [
                        (
                            jnp.exp(jnp.minimum(run_b[k] - run_t[2 * p + k : 2 * p + k + 1, :], 0.0))
                            * cb
                        ).astype(B16)
                        for k in range(2)
                    ],
                    axis=1,
                )
                inside = nn(mix, split_heads(ud, low_lanes).astype(B16))
                y = inside + carried[:, lanes] * jnp.exp(run_w) + skips[:, lanes] * u
                y_ref[rows, lanes] = y.astype(B16)
                lows_ref[rows, lanes] = (y * z * sigmoid(z)).astype(B16)
                end = run_w[STEP - 1 : STEP, :]
                tails.append((ud * jnp.exp(end - run_w)).astype(B16))
                fades.append(jnp.exp(end))
            fresh = tn(bm, jnp.concatenate(tails, axis=1))
            state[...] = states_in * jnp.concatenate(fades, axis=1) + fresh
            return 0

        lax.fori_loop(0, length // STEP, scan_block, 0)

    def attend_all():
        rk, ck = iotas(TILE, 2 * TILE)
        diagonal = rk <= jnp.where(ck < TILE, ck, ck - TILE)
        q_low = iotas(TILE, LANES)[1] < HD

        def attend(i, _):
            rows = pl.ds(pl.multiple_of(i * TILE, TILE), TILE)
            q2 = split_heads(proj_ref[rows, cols.q : cols.q + LANES], q_low)

            def piece(j, carry, masked):
                top, total, out = carry
                keys = pl.ds(pl.multiple_of(j * TILE, TILE), TILE)
                s = nt(proj_ref[keys, cols.k : cols.k + LANES], q2)
                if masked:
                    s = jnp.where(diagonal, s, -1e30)
                new_top = jnp.maximum(top, jnp.max(s, axis=0, keepdims=True))
                p = jnp.exp(s - new_top)
                scale = jnp.exp(top - new_top)
                total = total * scale + jnp.sum(p, axis=0, keepdims=True)
                out = out * scale + tn(proj_ref[keys, cols.v : cols.v + LANES], p.astype(B16))
                return new_top, total, out

            carry = (
                jnp.full((1, 2 * TILE), -1e30, F32),
                jnp.zeros((1, 2 * TILE), F32),
                jnp.zeros((LANES, 2 * TILE), F32),
            )
            carry = lax.fori_loop(0, i, lambda j, c: piece(j, c, False), carry)
            top, total, out = piece(i, carry, True)
            out = out / total
            joined = jnp.concatenate([out[:HD, :TILE], out[HD:, TILE:]], axis=0)
            lows_ref[rows, width : width + LANES] = joined.T.astype(B16)
            lse_ref[i] = jnp.broadcast_to(top + jnp.log(total), (8, 2 * TILE))
            return 0

        lax.fori_loop(0, length // TILE, attend, 0)

    def finish():
        multiply_out(lows_ref, weights_ref, at_row.low, part_ref)

    return [join_all, project_all, scan_all, attend_all, finish]


def core_bwd_phases(cols, layer, members, q_heads, r):
    back_ref, weights_ref, few_ref, rows_ref = r.rows_back, r.mixer, r.few, r.rows_mix
    proj_ref, step_ref, y_ref, lows_ref = r.proj, r.step, r.y, r.lows
    states_ref, lse_ref, part_ref = r.states, r.lse, r.part
    dproj_ref, heads_ref, dcore, grad_state, skip_sum = r.dproj, r.heads, r.dcore, r.grad_state, r.skip_sum
    dk_sum, dv_sum, folded, gain_sum, staged = r.dk_sum, r.dv_sum, r.folded, r.gain_sum, r.staged
    length = back_ref.shape[0]
    width = cols.width
    ways, _, piece = weights_ref.shape
    blocks = length // STEP
    depth = ways * piece
    at_row = MixerRows(cols, members)
    low_rows = slice(at_row.low, at_row.low + width + LANES)

    def into_all():
        def into_core(i, _):
            rows = pl.ds(pl.multiple_of(i * TILE, TILE), TILE)
            total = nt(back_ref[rows, 0:piece], weights_ref[0, low_rows, :])
            for k in range(1, ways):
                total += nt(
                    back_ref[rows, k * piece : (k + 1) * piece], weights_ref[k, low_rows, :]
                )
            dcore[rows, :] = total.astype(B16)
            return 0

        lax.fori_loop(0, length // TILE, into_core, 0)

    def attend_all():
        rk, ck = iotas(TILE, 2 * TILE)
        diagonal = rk <= jnp.where(ck < TILE, ck, ck - TILE)
        q_low = iotas(TILE, LANES)[1] < HD
        dk_sum[...] = jnp.zeros_like(dk_sum)
        dv_sum[...] = jnp.zeros_like(dv_sum)
        half = iotas(8, LANES)
        pick_low = (half[1] < HD).astype(F32)
        pick_high = (half[1] >= HD).astype(F32)

        def attend(i, _):
            rows = pl.ds(pl.multiple_of(i * TILE, TILE), TILE)
            q2 = split_heads(proj_ref[rows, cols.q : cols.q + LANES], q_low)
            d_out = dcore[rows, width : width + LANES]
            do2 = split_heads(d_out, q_low)
            both = d_out.astype(F32) * lows_ref[rows, width : width + LANES].astype(F32)
            high = lax.Precision.HIGHEST
            deltas = [
                lax.dot_general(
                    pick, both, (((1,), (1,)), ((), ())), precision=high, preferred_element_type=F32
                )[0:1, :]
                for pick in (pick_low, pick_high)
            ]
            delta = jnp.concatenate(deltas, axis=1)
            lse = lse_ref[i][0:1, :]

            def piece_of(j, dq, masked):
                keys = pl.ds(pl.multiple_of(j * TILE, TILE), TILE)
                kk = proj_ref[keys, cols.k : cols.k + LANES]
                p = jnp.exp(nt(kk, q2) - lse)
                if masked:
                    p = jnp.where(diagonal, p, 0.0)
                ds = (p * (nt(proj_ref[keys, cols.v : cols.v + LANES], do2) - delta)).astype(B16)
                dv_sum[keys, :] += nn(p.astype(B16), do2)
                dk_sum[keys, :] += nn(ds, q2)
                return dq + tn(kk, ds)

            dq = jnp.zeros((LANES, 2 * TILE), F32)
            dq = lax.fori_loop(0, i, lambda j, c: piece_of(j, c, False), dq)
            dq = piece_of(i, dq, True)
            joined = jnp.concatenate([dq[:HD, :TILE], dq[HD:, TILE:]], axis=0) * HD**-0.5
            dproj_ref[rows, cols.q : cols.q + LANES] = joined.T.astype(B16)
            return 0

        lax.fori_loop(0, length // TILE, attend, 0)
        dproj_ref[:, cols.k : cols.k + LANES] = dk_sum[...].astype(B16)
        dproj_ref[:, cols.v : cols.v + LANES] = dv_sum[...].astype(B16)

    def scan_all():
        ri, ci = iotas(STEP, STEP)
        upper = ri <= ci
        tril = (ri >= ci).astype(F32)
        triu = upper.astype(F32)
        low_lanes = ci < HD
        decay = jnp.exp(few_ref[layer, 0, 2:3, :LANES])
        bias = few_ref[layer, 0, 3:4, :LANES]
        skips = skip_lanes(few_ref, layer, width)
        row, lane = iotas(width, LANES)
        group = ((row >> 6) == lane).astype(B16)
        grad_state[...] = jnp.zeros_like(grad_state)
        skip_sum[...] = jnp.zeros_like(skip_sum)
        heads_ref[...] = jnp.zeros_like(heads_ref)
        zero_rows = jnp.zeros((STEP - 2 * cols.pairs, LANES), F32)

        def scan_block(back, _):
            b = blocks - 1 - back
            rows = pl.ds(pl.multiple_of(b * STEP, STEP), STEP)
            raw = step_ref[rows, :] + bias
            dt = softplus(raw)
            a = -dt * decay
            run = exact(tril, a)
            run_t = run.T
            bm = proj_ref[rows, cols.b : cols.b + LANES]
            cm = proj_ref[rows, cols.c : cols.c + LANES]
            cbt = jnp.where(upper, nt(bm, cm), 0.0)
            low_state = states_ref[b]
            grads_out = grad_state[...]
            low_grad = grads_out.astype(B16)
            carried = nn(cm, low_state)
            pulled = nn(bm, low_grad)
            dcb = jnp.zeros((STEP, STEP), F32)
            dy_fades, u_tails, fades = [], [], []
            carry_terms, direct_terms, tail_terms = [], [], []
            row_sums = []
            col_sums = jnp.zeros((STEP, LANES), F32)
            for p in range(cols.pairs):
                lanes = slice(LANES * p, LANES * (p + 1))
                u16 = proj_ref[rows, cols.u + LANES * p : cols.u + LANES * (p + 1)]
                u = u16.astype(F32)
                z = proj_ref[rows, cols.z + LANES * p : cols.z + LANES * (p + 1)].astype(F32)
                y = y_ref[rows, lanes].astype(F32)
                dm = dcore[rows, lanes].astype(F32)
                sg = sigmoid(z)
                dy = dm * z * sg
                dproj_ref[rows, cols.z + LANES * p : cols.z + LANES * (p + 1)] = (
                    dm * y * sg * (1.0 + z * (1.0 - sg))
                ).astype(B16)
                dy16 = dy.astype(B16)
                skip_sum[:, lanes] += u * dy
                run_b = [spread(run, 2 * p + k, STEP) for k in range(2)]
                dt_b = [spread(dt, 2 * p + k, STEP) for k in range(2)]
                run_w = jnp.where(low_lanes, run_b[0], run_b[1])
                dt_w = jnp.where(low_lanes, dt_b[0], dt_b[1])
                end = run_w[STEP - 1 : STEP, :]
                fade = jnp.exp(run_w)
                tail = jnp.exp(end - run_w)
                dmix = nt(split_heads(u16, low_lanes), dy16)
                mixes = []
                for k in range(2):
                    gap = jnp.exp(jnp.minimum(run_t[2 * p + k : 2 * p + k + 1, :] - run_b[k], 0.0))
                    mixes.append((gap * cbt).astype(B16))
                    weighted = gap * dt_b[k] * dmix[STEP * k : STEP * (k + 1), :]
                    dcb += weighted
                    moved = weighted * cbt
                    row_sums.append(jnp.sum(moved, axis=0, keepdims=True))
                    col_sums = jnp.where(
                        ci == 2 * p + k, jnp.sum(moved, axis=1, keepdims=True), col_sums
                    )
                inside = nn(jnp.concatenate(mixes, axis=1), split_heads(dy16, low_lanes))
                pull_tail = tail * pulled[:, lanes]
                g = inside + pull_tail
                dproj_ref[rows, cols.u + LANES * p : cols.u + LANES * (p + 1)] = (
                    dt_w * g + skips[:, lanes] * dy
                ).astype(B16)
                dy_fade = dy * fade
                dy_fades.append(dy_fade.astype(B16))
                u_tails.append((u * dt_w * tail).astype(B16))
                fades.append(jnp.exp(end))
                carry_terms.append((dy_fade * carried[:, lanes]).astype(B16))
                direct_terms.append((u * g).astype(B16))
                tail_terms.append((u * pull_tail).astype(B16))
            dy_fade = jnp.concatenate(dy_fades, axis=1)
            dcb = jnp.where(upper, dcb, 0.0).astype(B16)
            dproj_ref[rows, cols.c : cols.c + LANES] = (tn(dcb, bm) + nt(dy_fade, low_state)).astype(B16)
            dproj_ref[rows, cols.b : cols.b + LANES] = (
                nn(dcb, cm) + nt(jnp.concatenate(u_tails, axis=1), low_grad)
            ).astype(B16)
            carry_term = nn(jnp.concatenate(carry_terms, axis=1), group)
            direct_term = nn(jnp.concatenate(direct_terms, axis=1), group)
            tail_term = dt * nn(jnp.concatenate(tail_terms, axis=1), group)
            overlap = jnp.sum(low_state.astype(F32) * grads_out, axis=0, keepdims=True)
            overlap = exact(jnp.broadcast_to(overlap, (8, width)), group.astype(F32))[0:1, :]
            overlap = overlap * jnp.exp(run[STEP - 1 : STEP, :])
            row_sum = jnp.concatenate(row_sums + [zero_rows], axis=0).T
            d_run = row_sum - col_sums + carry_term - tail_term
            d_a = exact(triu, d_run) + (jnp.sum(tail_term, axis=0, keepdims=True) + overlap)
            d_step = (direct_term - decay * d_a) * sigmoid(raw)
            dproj_ref[rows, cols.step : cols.step + LANES] = d_step.astype(B16)
            heads_ref[0:1, :] += jnp.sum(d_a * a, axis=0, keepdims=True)
            heads_ref[1:2, :] += jnp.sum(d_step, axis=0, keepdims=True)
            grad_state[...] = grads_out * jnp.concatenate(fades, axis=1) + tn(cm, dy_fade)
            return 0

        lax.fori_loop(0, blocks, scan_block, 0)
        skip = jnp.sum(skip_sum[...], axis=0, keepdims=True)
        heads_ref[2:3, :] = exact(jnp.broadcast_to(skip, (8, width)), group.astype(F32))[0:1, :]

    def back_all():
        multiply_back(
            dproj_ref, weights_ref, at_row.inner, cols.q // piece, part_ref, rows_ref, gain_sum, r.rest
        )

    def shared_all():
        wide = cols.total - cols.b
        member = lax.axis_index(TENSOR)
        heads = q_heads[1]
        group = member * q_heads[0] // (HA // KVH)
        source, target = iotas(wide, wide)
        kind = source >> 7
        wanted = jnp.where(
            kind < 2,
            source,
            jnp.where(
                kind < 4,
                2 * NS + (kind - 2) * KVH * HD + group * HD + (source & (HD - 1)),
                source + member * heads,
            ),
        )
        fold = ((target == wanted) & (source < 4 * LANES + heads)).astype(B16)

        def fold_rows(i, _):
            rows = pl.ds(pl.multiple_of(i * TILE, TILE), TILE)
            folded[rows, :] = nn(dproj_ref[rows, cols.b :], fold).astype(B16)
            return 0

        lax.fori_loop(0, length // TILE, fold_rows, 0)
        sub = piece // members
        half = sub // 2
        lane = iotas(piece, LANES)[1]
        head_lane = iotas(8, LANES)[1]
        shifted = jnp.where(
            (head_lane >= HEADS_AT) & (head_lane < HEADS_AT + heads),
            pltpu.roll(heads_ref[...], HEADS_AT, 1),
            0.0,
        )
        for k in range(ways):
            at = slice(k * piece, (k + 1) * piece)
            grad = tn(rows_ref[:, at], folded[...])
            columns = []
            for row, sums in ((0, gain_sum), (1, r.gain_ffn)):
                gain = few_ref[layer, k, row : row + 1, :]
                columns.append(jnp.broadcast_to(sums[0:1, at] / gain, (LANES, piece)).T)
            last = grad[:, wide - LANES :]
            last = jnp.where(lane == GAINS_AT, columns[0], last)
            last = jnp.where(lane == GAINS_AT + 1, columns[1], last)
            for t in range(members):
                for h in range(2):
                    to = t * (depth // members) + (h * ways + k) * half
                    rows = slice(t * sub + h * half, t * sub + (h + 1) * half)
                    staged[to : to + half, : wide - LANES] = grad[rows, : wide - LANES]
                    staged[to : to + half, wide - LANES :] = last[rows, :]
            to = pl.multiple_of(member * (depth // members) + k * half, 8)
            staged[pl.ds(to, 8), wide - LANES :] += shifted
        part_ref[:, depth:] = staged[...].astype(B16)

    return [into_all, attend_all, scan_all, back_all, shared_all]


def ffn_fwd_phases(r, at=0):
    rows_ref, weights_ref, gu_ref, hidden_ref = r.rows_ffn, r.gates, r.gu, r.hidden
    units = hidden_ref.shape[1]
    piece = weights_ref.shape[2]
    count = units // piece

    def up(i, _):
        rows = pl.ds(pl.multiple_of(i * TILE, TILE), TILE)
        for c in range(count):
            at = slice(c * piece, (c + 1) * piece)
            g = blocks_nn(rows_ref, rows, weights_ref, c)
            v = blocks_nn(rows_ref, rows, weights_ref, c + count)
            gu_ref[rows, at] = g.astype(B16)
            gu_ref[rows, units + c * piece : units + (c + 1) * piece] = v.astype(B16)
            hidden_ref[rows, at] = (g * sigmoid(g) * v).astype(B16)
        return 0

    def up_all():
        lax.fori_loop(0, rows_ref.shape[0] // TILE, up, 0)

    def down_all():
        multiply_out(hidden_ref, weights_ref, 2 * units, r.part, at)

    return [up_all, down_all]


def ffn_bwd_phases(r):
    out_ref, weights_ref, gu_ref, dgu_ref = r.rows_out, r.gates, r.gu, r.dgu
    ways, _, piece = weights_ref.shape
    units = gu_ref.shape[1] // 2
    down_rows = slice(2 * units, 3 * units)

    def down(i, _):
        rows = pl.ds(pl.multiple_of(i * TILE, TILE), TILE)
        dh = nt(out_ref[rows, 0:piece], weights_ref[0, down_rows, :])
        for k in range(1, ways):
            dh += nt(out_ref[rows, k * piece : (k + 1) * piece], weights_ref[k, down_rows, :])
        g = gu_ref[rows, :units].astype(F32)
        v = gu_ref[rows, units:].astype(F32)
        sg = sigmoid(g)
        dgu_ref[rows, :units] = (dh * v * sg * (1.0 + g * (1.0 - sg))).astype(B16)
        dgu_ref[rows, units:] = (dh * g * sg).astype(B16)
        return 0

    def down_all():
        lax.fori_loop(0, out_ref.shape[0] // TILE, down, 0)

    def back_all():
        multiply_back(
            dgu_ref, weights_ref, 0, 2 * units // piece, r.part, r.rows_ffn, r.gain_ffn
        )

    return [down_all, back_all]


def grad_columns(rows_ref, grad_ref, out_ref):
    _, ways, half, width = out_ref.shape
    for k in range(ways):
        block = rows_ref[:, 2 * half * k : 2 * half * (k + 1)]
        for first in range(0, width, 512):
            last = min(first + 512, width)
            value = tn(block, grad_ref[:, first:last]).astype(B16)
            out_ref[0, k, :, first:last] = value[:half, :]
            out_ref[1, k, :, first:last] = value[half:, :]


def grad_rows(lows_ref, back_ref, out_ref):
    _, ways, half, piece = out_ref.shape
    for h in range(2):
        block = lows_ref[:, h * half : (h + 1) * half]
        for k in range(ways):
            out_ref[h, k] = tn(block, back_ref[:, k * piece : (k + 1) * piece]).astype(B16)


DMA = pltpu.SemaphoreType.DMA
MESH = pl.DeviceIdType.MESH
PIPE, DP, TENSOR = "pipe", "dp", "tensor"

BEGIN, SENT, CHUNK, SPREAD, GIVEN, END = -1, 20, 30, 40, 50, 60


class Bag:
    def __init__(self, **entries):
        self.__dict__.update(entries)

    def add(self, other):
        self.__dict__.update(other.__dict__)


def remote(source, target, send, receive, device):
    return pltpu.make_async_remote_copy(
        src_ref=source, dst_ref=target, send_sem=send, recv_sem=receive,
        device_id=device, device_id_type=MESH,
    )


class Helper:
    def __init__(self, when):
        self.when = when
        self.inputs, self.outs, self.scratch = [], [], []
        self.results = None

    @property
    def result(self):
        return self.results[0]


def cross_devices(ways):
    section, place = lax.axis_index(PIPE), lax.axis_index(DP)
    return [{PIPE: 1 - section}] + [{DP: (place + k) % ways} for k in range(1, ways)]


class Few(Helper):
    def __init__(self, ways, shard, when):
        super().__init__(when)
        self.ways = ways
        self.inputs = [shard]
        self.outs = [((2, ways) + shard.shape, F32, pltpu.VMEM)]
        self.scratch = [DMA((1,)), DMA((1,)), DMA((2, ways)), DMA((2, ways)), DMA((1,))]

    def bind(self, r, inputs, outs, scratch):
        (shard,), (few,) = inputs, outs
        r.few = few
        section, place, ways = lax.axis_index(PIPE), lax.axis_index(DP), self.ways
        pair_send, pair_recv, line_send, line_recv, local = scratch
        mine = few.at[section, place]

        def over():
            return remote(shard, mine, pair_send.at[0], pair_recv.at[0], {PIPE: 1 - section})

        def line(layer, k, there):
            block = few.at[layer, there]
            return remote(
                block, block, line_send.at[layer, k], line_recv.at[layer, k], {DP: (place + k) % ways}
            )

        def start():
            over().start()
            own = pltpu.make_async_copy(shard, mine, local.at[0])
            own.start()
            own.wait()

        def spread():
            over().wait_recv()
            for layer in range(2):
                for k in range(1, ways):
                    line(layer, k, place).start()

        def finish():
            for layer in range(2):
                for k in range(1, ways):
                    line(layer, k, (place + ways - k) % ways).wait_recv()
            over().wait_send()
            for layer in range(2):
                for k in range(1, ways):
                    line(layer, k, place).wait_send()

        return [start, spread, finish]


class Cargo(Helper):
    CHUNKS = 4

    def __init__(self, layer, ways, shard, when, members=0, shared=0):
        super().__init__(when)
        self.layer, self.ways, self.rows = layer, ways, shard.shape[0]
        self.members, self.shared = members, shared
        n = self.CHUNKS
        self.first = (self.rows * 2 // 5 + 8 * n) // (16 * n) * (16 * n)
        self.inputs = [shard]
        self.outs = [((ways,) + shard.shape, shard.dtype, pl.ANY)]
        self.scratch = [DMA((n,)), DMA((n,))] + [DMA((ways, n))] * 6 + [DMA((1,))]
        if shared:
            self.outs.append(((members, ways, shared, shard.shape[1]), shard.dtype, pl.ANY))
            self.scratch += [DMA((members,))] * 4 + [DMA((1,))]

    def bind(self, r, inputs, outs, scratch):
        (shard_ref,), out_ref = inputs, outs[0]
        early_send, early_recv, up_send, up_recv, down_send, down_recv, over_send, over_recv, local = scratch[:9]
        section, place = lax.axis_index(PIPE), lax.axis_index(DP)
        partner = {PIPE: 1 - section}
        ways, chunks = self.ways, self.CHUNKS
        sizes = {True: self.first // chunks, False: (self.rows - self.first) // chunks}

        def by_role(step):
            def both():
                pl.when(section == self.layer)(lambda: step(True))
                pl.when(section != self.layer)(lambda: step(False))

            return both

        def part(owner, c):
            return pl.ds((0 if owner else self.first) + c * sizes[owner], sizes[owner])

        def early(c):
            at = part(False, c)
            return remote(
                shard_ref.at[at, :], out_ref.at[place, at, :], early_send.at[c], early_recv.at[c], partner
            )

        def line(owner, up, hop, c):
            at = part(owner, c)
            send, receive = (up_send, up_recv) if up else (down_send, down_recv)
            shard = place - hop if up else place + hop
            source = shard_ref if owner and hop == 0 else out_ref.at[shard]
            return remote(
                source.at[at, :], out_ref.at[shard, at, :], send.at[hop, c], receive.at[hop, c],
                {DP: (place + (1 if up else ways - 1)) % ways},
            )

        def sends(up, hop):
            if up:
                return (place >= hop) & (place < ways - 1)
            return (place < ways - hop) & (place > 0)

        def over(owner, shard, c, own=False):
            at = part(owner, c)
            source = shard_ref if own else out_ref.at[shard]
            return remote(
                source.at[at, :], out_ref.at[shard, at, :], over_send.at[shard, c], over_recv.at[shard, c],
                partner,
            )

        def own_copy():
            return pltpu.make_async_copy(shard_ref, out_ref.at[place], local.at[0])

        def launch(owner, c):
            for up in (True, False):
                pl.when(sends(up, 0))(lambda up=up: line(owner, up, 0, c).start())

        def start(owner):
            if owner:
                for c in range(chunks):
                    early(c).start()
                    launch(True, c)
                for c in range(chunks):
                    over(True, place, c, True).start()
                own_copy().start()

        def spread(c, owner):
            if not owner:
                early(c).wait_recv()
                launch(False, c)

        def hop(count, c, owner):
            for up in (True, False):
                shard = place - count if up else place + count

                @pl.when(shard >= 0 if up else shard < ways)
                def _(up=up, shard=shard):
                    line(owner, up, count - 1, c).wait_recv()
                    if count < ways - 1:
                        pl.when(sends(up, count))(lambda: line(owner, up, count, c).start())
                    over(owner, shard, c).start()

        def wait_over(owner, c):
            for shard in range(ways):

                def wait(shard=shard):
                    block = out_ref.at[shard, part(not owner, c), :]
                    remote(
                        block, block, over_send.at[shard, c], over_recv.at[shard, c], partner
                    ).wait_recv()

                if owner:
                    pl.when(place != shard)(wait)
                else:
                    wait()

        first_waited = 1 if self.shared else 0

        def finish(owner):
            for c in range(chunks):
                if owner or c >= first_waited:
                    wait_over(owner, c)
            for c in range(chunks):
                if owner:
                    early(c).wait_send()
                for count in range(ways - 1):
                    for up in (True, False):
                        pl.when(sends(up, count))(
                            lambda up=up, count=count: line(owner, up, count, c).wait_send()
                        )
                for shard in range(ways):

                    def wait(shard=shard):
                        over(owner, shard, c).wait_send()

                    if owner:
                        wait()
                    else:
                        pl.when(place != shard)(wait)
            if owner and not self.shared:
                own_copy().wait()

        steps = [start]
        steps += [functools.partial(spread, c) for c in range(chunks)]
        steps += [functools.partial(hop, count, c) for count in range(1, ways) for c in range(chunks)]
        steps = [by_role(step) for step in steps]
        if not self.shared:
            return steps + [by_role(finish)]

        assert self.shared <= sizes[True]
        all_ref = outs[1]
        give_send, give_recv, far_send, far_recv, keep = scratch[9:]
        me = lax.axis_index(TENSOR)
        pairs = self.members // 2
        mine, side = me // 2, me % 2
        sibling = 2 * mine + 1 - side
        share = out_ref.at[:, pl.ds(0, self.shared), :]

        def far(count):
            return 2 * ((mine + count) % pairs) + side

        def across(count):
            return 2 * ((mine + count) % pairs) + 1 - side

        def give(count):
            block = all_ref.at[far(count)]
            return remote(
                share if count == 0 else block, block, give_send.at[count], give_recv.at[count],
                {TENSOR: sibling},
            )

        def send_far(count, slot):
            return remote(
                share, all_ref.at[me], far_send.at[count], far_recv.at[slot], {TENSOR: far(count)}
            )

        def own_share():
            return pltpu.make_async_copy(share, all_ref.at[me], keep.at[0])

        def share_out():
            pl.when(section != self.layer)(lambda: wait_over(False, 0))
            pl.when(section == self.layer)(lambda: own_copy().wait())
            for count in range(1, pairs):
                send_far(count, pairs - count).start()
            give(0).start()
            own_share().start()

        def pass_on():
            for count in range(1, pairs):
                send_far(count, count).wait_recv()
                give(count).start()

        def finish_all():
            by_role(finish)()
            for count in range(pairs):
                block = all_ref.at[sibling if count == 0 else across(count)]
                remote(
                    block, block, give_send.at[count], give_recv.at[count], {TENSOR: sibling}
                ).wait_recv()
            for count in range(pairs):
                give(count).wait_send()
                if count:
                    send_far(count, pairs - count).wait_send()
            own_share().wait()

        at = len(steps) - (chunks - 1)
        return steps[:at] + [share_out] + steps[at:] + [pass_on, finish_all]


class Haul(Helper):
    def __init__(self, layer, ways, sources, specs, when, swap=True, line=True):
        super().__init__(when)
        self.layer, self.ways, self.sources, self.swap, self.line = layer, ways, sources, swap, line
        self.count = len(specs)
        self.order = sorted(range(1, ways), key=lambda k: abs(2 * k - ways)) + [0]
        for (_, blocks, rows, columns), dtype in specs:
            block = pltpu.VMEM((blocks, rows, columns), dtype)
            if swap and not line:
                self.outs.append(((blocks, rows, columns), dtype, pltpu.VMEM))
            if line:
                self.outs.append(((2, rows, columns), dtype, pltpu.VMEM))
            if swap:
                self.scratch += [block, DMA((ways,)), DMA((ways,))]
            if swap and line:
                self.scratch.append(block)
            if line:
                self.scratch += [block, pltpu.VMEM((rows, columns), dtype), DMA((ways,)), DMA((ways,))]
                self.scratch += [DMA((1,)), DMA((1,))]

    def bind(self, r, inputs, outs, scratch):
        section, place, ways = lax.axis_index(PIPE), lax.axis_index(DP), self.ways
        partner = {PIPE: 1 - section}
        scratch = list(scratch)
        arrays = []
        for source, out in zip(self.sources, outs):
            a = Bag(out=out)
            a.sent, a.read = source(r)
            a.sums = a.read
            if self.swap:
                a.swapped, a.swap_send, a.swap_recv = [scratch.pop(0) for _ in range(3)]
                a.sums = scratch.pop(0) if self.line else out
                a.sums_sent = a.sums
            else:
                a.sums_sent = a.sent
            if self.line:
                a.arrived, a.result, a.line_send, a.line_recv, a.last_send, a.last_recv = [
                    scratch.pop(0) for _ in range(6)
                ]
            arrays.append(a)

        def to(k):
            return (place + k) % ways

        def swap(a, k):
            return remote(
                a.sent.at[1 - section, to(k)], a.swapped.at[to(k)], a.swap_send.at[k], a.swap_recv.at[k],
                partner,
            )

        def line(a, k):
            return remote(
                a.sums_sent.at[to(k)], a.arrived.at[k], a.line_send.at[k], a.line_recv.at[k], {DP: to(k)}
            )

        def last(a):
            return remote(
                a.result, a.out.at[1 - self.layer], a.last_send.at[0], a.last_recv.at[0], partner
            )

        def start():
            for k in self.order:
                for a in arrays:
                    if self.swap:
                        swap(a, k).start()
                    elif k:
                        line(a, k).start()

        def fold(k):
            def step():
                for a in arrays:
                    swap(a, k).wait_recv()
                    total = a.read[section, to(k)].astype(F32) + a.swapped[to(k)].astype(F32)
                    a.sums[to(k)] = total.astype(a.sums.dtype)
                    if k and self.line:
                        line(a, k).start()

            return step

        def reduce():
            for a in arrays:
                total = a.sums[place].astype(F32)
                for k in range(1, ways):
                    line(a, k).wait_recv()
                    total += a.arrived[k].astype(F32)
                a.result[...] = total.astype(a.out.dtype)

            @pl.when(section == self.layer)
            def _():
                for a in arrays:
                    a.out[self.layer] = a.result[...]

            @pl.when(section != self.layer)
            def _():
                for a in arrays:
                    last(a).start()

        def finish():
            if self.line:

                @pl.when(section == self.layer)
                def _():
                    for a in arrays:
                        last(a).wait_recv()

                @pl.when(section != self.layer)
                def _():
                    for a in arrays:
                        last(a).wait_send()
                        a.out[...] = jnp.zeros_like(a.out)

            for k in self.order:
                for a in arrays:
                    if self.swap:
                        swap(a, k).wait_send()
                    if k and self.line:
                        line(a, k).wait_send()

        steps = [start]
        if self.swap:
            steps += [fold(k) for k in self.order]
        if self.line:
            steps.append(reduce)
        return steps + [finish]


class Straight(Helper):
    def __init__(self, layer, ways, source, spec, when):
        super().__init__(when)
        self.layer, self.ways, self.source = layer, ways, source
        (_, blocks, rows, columns), dtype = spec
        result = (2, rows, columns)
        self.outs = [(result, dtype, pltpu.VMEM)]
        self.scratch = [pltpu.VMEM((blocks,) + result, dtype), pltpu.VMEM(result, dtype)]
        self.scratch += [pltpu.VMEM(result, dtype), DMA((2, ways)), DMA((2, ways)), DMA((1,)), DMA((1,))]

    def bind(self, r, inputs, outs, scratch):
        sent, read = self.source(r)
        (out,) = outs
        arrived, result, handed, line_send, line_recv, last_send, last_recv = scratch
        section, place, ways = lax.axis_index(PIPE), lax.axis_index(DP), self.ways
        order = sorted(range(1, ways), key=lambda k: abs(2 * k - ways))

        def line(half, k):
            to = (place + k) % ways
            return remote(
                sent.at[half, to], arrived.at[k, half], line_send.at[half, k], line_recv.at[half, k], {DP: to}
            )

        def last():
            return remote(result, handed, last_send.at[0], last_recv.at[0], {PIPE: 1 - section})

        def start():
            for k in order:
                for half in range(2):
                    line(half, k).start()

        def reduce():
            for half in range(2):
                total = read[half, place].astype(F32)
                for k in range(1, ways):
                    line(half, k).wait_recv()
                    total += arrived[k, half].astype(F32)
                result[half] = total.astype(result.dtype)

            @pl.when(section != self.layer)
            def _():
                last().start()

        def finish():
            @pl.when(section == self.layer)
            def _():
                last().wait_recv()
                out[...] = (result[...].astype(F32) + handed[...].astype(F32)).astype(out.dtype)

            @pl.when(section != self.layer)
            def _():
                last().wait_send()
                out[...] = jnp.zeros_like(out)

            for k in order:
                for half in range(2):
                    line(half, k).wait_send()

        return [start, reduce, finish]


class Place(Helper):
    PIECES = 4

    def __init__(self, source, shape, late, when):
        super().__init__(when)
        self.source, self.late, self.size = source, late, shape[0] // self.PIECES
        self.outs = [((2,) + shape, B16, pl.ANY)]
        self.scratch = [DMA((self.PIECES,)), DMA((self.PIECES,)), DMA((self.PIECES,))]

    def bind(self, r, inputs, outs, scratch):
        (out,) = outs
        send, receive, local = scratch
        section = lax.axis_index(PIPE)
        rows = self.source(r)

        def over(layer, c):
            at = pl.ds(c * self.size, self.size)
            return remote(
                rows[layer].at[at, :], out.at[1 - layer, at, :], send.at[c], receive.at[c], {PIPE: 1 - section}
            )

        def own(layer, c):
            at = pl.ds(c * self.size, self.size)
            return pltpu.make_async_copy(rows[layer].at[at, :], out.at[layer, at, :], local.at[c])

        def hand(layer, c):
            pl.when(section != layer)(lambda: over(layer, c).start())
            pl.when(section == layer)(lambda: own(layer, c).start())

        def early():
            for c in range(self.PIECES):
                hand(1 - self.late, c)

        def finish():
            for c in range(self.PIECES):
                for layer in range(2):

                    @pl.when(section == layer)
                    def _(layer=layer):
                        over(1 - layer, c).wait()
                        own(layer, c).wait()

        return [early] + [functools.partial(hand, self.late, c) for c in range(self.PIECES)] + [finish]


def exchange_kernel(plan, *refs):
    refs = list(refs)

    def take(count):
        return [refs.pop(0) for _ in range(count)]

    r = Bag(raw=Bag())
    held = {}
    for name in plan.inputs:
        held[name] = take(1)[0]
    r.raw = Bag(**held)
    helper_inputs = [take(len(h.inputs)) for h in plan.helpers]
    targets = {name: take(1)[0] for name in plan.outs}
    gathered = take(len(plan.gathers))
    helper_outs = [take(len(h.outs)) for h in plan.helpers]
    loaded = [name for name in plan.inputs if plan.need(name) is not None]
    for name in loaded:
        setattr(r, name, take(1)[0])
    for name in plan.outs:
        setattr(r, name, take(1)[0])
    for name in plan.scratch:
        setattr(r, name, take(1)[0])
    load_sem, store_sem = take(2)
    if plan.scatter:
        part_ref, pair_in, far_out, far_in, pair_send, pair_recv, far_send, far_recv = take(8)
        r.part = part_ref
    if plan.gathers:
        mine_refs = take(len(plan.gathers))
        give_send, give_recv, spread_send, spread_recv, keep_sem = take(5)
    helpers = []
    for h, inputs, outs in zip(plan.helpers, helper_inputs, helper_outs):
        helpers.append((h.bind(r, inputs, outs, take(len(h.scratch))), h.when))

    members, pieces = plan.members, plan.pieces
    pairs = members // 2
    me = lax.axis_index(TENSOR)
    mine, side = me // 2, me % 2
    sibling = 2 * mine + 1 - side
    size = plan.rows // pieces

    def far(k):
        return 2 * ((mine + k) % pairs) + side

    def across(k):
        return 2 * ((mine + k) % pairs) + 1 - side

    def rows_of(member, c):
        return pl.ds(pl.multiple_of(member * plan.rows + c * size, size), size)

    def chunk(c):
        return pl.ds(c * size, size)

    def copy(source, target, send, receive, member):
        return remote(source, target, send, receive, {TENSOR: member})

    loads = {}
    for i, name in enumerate(sorted(loaded, key=plan.need)):
        loads[name] = pltpu.make_async_copy(held[name], getattr(r, name), load_sem.at[i])
        loads[name].start()

    def arrive(stage):
        for name in list(loads):
            if plan.need(name) <= stage:
                loads.pop(name).wait()

    stores = []

    def flush(stage):
        for i, name in enumerate(plan.outs):
            if plan.done(name) == stage:
                store = pltpu.make_async_copy(getattr(r, name), targets[name], store_sem.at[i])
                store.start()
                stores.append(store)

    def point(stage):
        for steps, when in helpers:
            count = len(steps) if stage == END else when.get(stage, 0)
            for _ in range(min(count, len(steps))):
                steps.pop(0)()
        flush(stage)

    def run_fill(i):
        if i < len(plan.fills):
            plan.fills[i](r)

    barrier = pltpu.get_barrier_semaphore()
    greeted = [{TENSOR: sibling}] + [{TENSOR: far(k)} for k in range(1, pairs)]
    if helpers:
        greeted += cross_devices(plan.ways)
    for device in greeted:
        pl.semaphore_signal(barrier, inc=1, device_id=device, device_id_type=MESH)
    pl.semaphore_wait(barrier, len(greeted))

    arrive(BEGIN)
    point(BEGIN)
    for i, phase in enumerate(plan.phases(r) if plan.phases else []):
        arrive(i)
        phase()
        point(i)

    if plan.scatter:
        to_pair = {}
        for c in range(pieces):
            for k in range(1, pairs):
                to_pair[k, c] = copy(
                    part_ref.at[rows_of(across(k), c), :], pair_in.at[k, chunk(c), :],
                    pair_send.at[k, c], pair_recv.at[k, c], sibling,
                )
                to_pair[k, c].start()
        for c in range(pieces):
            to_pair[0, c] = copy(
                part_ref.at[rows_of(sibling, c), :], pair_in.at[0, chunk(c), :],
                pair_send.at[0, c], pair_recv.at[0, c], sibling,
            )
            to_pair[0, c].start()
        to_far = {}
        for c in range(pieces):
            for k in range(1, pairs):
                to_pair[k, c].wait_recv()
                far_out[k - 1, chunk(c), :] = (
                    part_ref[rows_of(far(k), c), :].astype(F32)
                    + pair_in[k, chunk(c), :].astype(F32)
                ).astype(B16)
                to_far[k, c] = copy(
                    far_out.at[k - 1, chunk(c), :], far_in.at[pairs - k - 1, chunk(c), :],
                    far_send.at[k - 1, c], far_recv.at[pairs - k - 1, c], far(k),
                )
                to_far[k, c].start()
    arrive(SENT)
    if plan.scatter:
        run_fill(0)
    point(SENT)

    given, spreads, keeps = {}, {}, []
    for c in range(pieces):
        total = None
        if plan.scatter:
            to_pair[0, c].wait_recv()
            total = part_ref[rows_of(me, c), :].astype(F32) + pair_in[0, chunk(c), :].astype(F32)
            for k in range(1, pairs):
                copy(
                    far_out.at[k - 1, chunk(c), :], far_in.at[k - 1, chunk(c), :],
                    far_send.at[k - 1, c], far_recv.at[k - 1, c], far(k),
                ).wait_recv()
                total += far_in[k - 1, chunk(c), :].astype(F32)
        results = plan.work(r, c, chunk(c), total)
        for g, rows_ref in enumerate(gathered):
            own = mine_refs[g].at[chunk(c), :]
            there = rows_ref.at[rows_of(me, c), :]
            mine_refs[g][chunk(c), :] = results[g]
            for k in range(1, pairs):
                spreads[g, k, c] = copy(
                    own, there, spread_send.at[g, k - 1, c], spread_recv.at[g, pairs - k - 1, c], far(k)
                )
                spreads[g, k, c].start()
            given[g, 0, c] = copy(own, there, give_send.at[g, 0, c], give_recv.at[g, 0, c], sibling)
            given[g, 0, c].start()
            keeps.append(pltpu.make_async_copy(own, there, keep_sem.at[g, c]))
            keeps[-1].start()
        point(CHUNK + c)
    run_fill(1)
    point(SPREAD)
    for g, rows_ref in enumerate(gathered):
        for c in range(pieces):
            for k in range(1, pairs):
                block = rows_ref.at[rows_of(far(k), c), :]
                copy(
                    block, block, spread_send.at[g, k - 1, c], spread_recv.at[g, k - 1, c], far(k)
                ).wait_recv()
                given[g, k, c] = copy(
                    block, block, give_send.at[g, k, c], give_recv.at[g, k, c], sibling
                )
                given[g, k, c].start()
    point(GIVEN)
    for g, rows_ref in enumerate(gathered):
        for c in range(pieces):
            for k in range(pairs):
                block = rows_ref.at[rows_of(sibling if k == 0 else across(k), c), :]
                copy(block, block, give_send.at[g, k, c], give_recv.at[g, k, c], sibling).wait_recv()
        for c in range(pieces):
            for k in range(pairs):
                given[g, k, c].wait_send()
            for k in range(1, pairs):
                spreads[g, k, c].wait_send()
    if plan.scatter:
        for c in range(pieces):
            for k in range(pairs):
                to_pair[k, c].wait_send()
            for k in range(1, pairs):
                to_far[k, c].wait_send()
    arrive(END)
    point(END)
    for store in stores + keeps:
        store.wait()


def exchange(
    name, number, members, ways, rows, depth, work, inputs, outs=None, need=None, done=None, scratch=None,
    phases=None, fills=(), part_width=0, gathers=None, helpers=(), pieces=4,
):
    pairs = members // 2
    others = max(pairs - 1, 1)
    outs, scratch, need, done = outs or {}, scratch or {}, need or {}, done or {}
    gathers = gathers or []
    hbm, vmem = pl.BlockSpec(memory_space=pl.ANY), pl.BlockSpec(memory_space=pltpu.VMEM)
    plan = Bag(
        inputs=list(inputs), outs=list(outs), scratch=list(scratch), gathers=gathers, helpers=list(helpers),
        members=members, ways=ways, rows=rows, pieces=pieces, scatter=bool(part_width),
        phases=phases, fills=list(fills), work=work,
        need=lambda n: need.get(n, 0 if phases else BEGIN), done=lambda n: done.get(n, END),
    )
    staging = [pltpu.VMEM(a.shape, a.dtype) for n, a in inputs.items() if plan.need(n) is not None]
    staging += [pltpu.VMEM(*spec) for spec in outs.values()]
    staging += list(scratch.values())
    staging += [DMA((max(len(inputs), 1),)), DMA((max(len(outs), 1),))]
    if part_width:
        staging += [
            pltpu.VMEM((members * rows, part_width), B16),
            pltpu.VMEM((pairs, rows, part_width), B16),
            pltpu.VMEM((others, rows, part_width), B16),
            pltpu.VMEM((others, rows, part_width), B16),
            DMA((pairs, pieces)), DMA((pairs, pieces)), DMA((others, pieces)), DMA((others, pieces)),
        ]
    count = len(gathers)
    if count:
        staging += [pltpu.VMEM((rows, depth), B16)] * count
        staging += [
            DMA((count, pairs, pieces)), DMA((count, pairs, pieces)),
            DMA((count, others, pieces)), DMA((count, others, pieces)), DMA((count, pieces)),
        ]
    operands = list(inputs.values())
    shapes = [jax.ShapeDtypeStruct(*spec) for spec in outs.values()]
    shapes += [jax.ShapeDtypeStruct((members * rows, depth), B16)] * count
    spaces = [hbm] * len(shapes)
    for h in helpers:
        operands += h.inputs
        shapes += [jax.ShapeDtypeStruct(shape, dtype) for shape, dtype, _ in h.outs]
        spaces += [pl.BlockSpec(memory_space=space) for _, _, space in h.outs]
        staging += h.scratch
    results = pl.pallas_call(
        functools.partial(exchange_kernel, plan),
        out_shape=shapes,
        in_specs=[hbm] * len(operands),
        out_specs=spaces,
        scratch_shapes=staging,
        compiler_params=pltpu.CompilerParams(
            collective_id=number, has_side_effects=True, vmem_limit_bytes=VMEM_LIMIT
        ),
        cost_estimate=pl.CostEstimate(
            flops=20_000_000_000, bytes_accessed=50_000_000, transcendentals=0
        ),
        name=name,
    )(*operands)
    results = list(results)
    got = {n: results.pop(0) for n in list(outs) + list(gathers)}
    for h in helpers:
        h.results = [results.pop(0) for _ in h.outs]
    return Bag(**got)


def rms(rows, gain):
    scale = lax.rsqrt(jnp.mean(rows * rows, axis=-1, keepdims=True) + EPS)
    return rows * scale * gain


def rms_back(rows, gain, grad):
    scale = lax.rsqrt(jnp.mean(rows * rows, axis=-1, keepdims=True) + EPS)
    scaled = gain * grad
    mean = jnp.mean(scaled * rows, axis=-1, keepdims=True)
    return scale * scaled - rows * (scale * scale * scale * mean)


def gain_of(r, layer, row):
    ways = r.few.shape[1]
    return jnp.concatenate([r.few[layer, k, row : row + 1, :] for k in range(ways)], axis=1)


def layer_input(r, layer, at):
    if layer == 0:
        return r.acts_in[lax.axis_index(PIPE), at, :].astype(F32)
    return r.x[at, :].astype(F32)


def layer_cotangent(r, layer, at):
    if layer == 1:
        return r.out_grad[lax.axis_index(PIPE), at, :]
    return r.cotangent[at, :]


def work_first(r, c, at, total):
    return rms(layer_input(r, 0, at), gain_of(r, 0, 0)).astype(B16), layer_cotangent(r, 1, at)


def work_mid(layer, r, c, at, total):
    residual = layer_input(r, layer, at) + total
    r.residual[at, :] = residual
    return (rms(residual, gain_of(r, layer, 1)).astype(B16),)


def work_turn(r, c, at, total):
    out = (r.residual[at, :] + total).astype(B16)
    r.x[at, :] = out
    return (rms(out.astype(F32), gain_of(r, 1, 0)).astype(B16),)


def work_back_ffn(layer, r, c, at, total):
    depth = r.residual.shape[1]
    residual = r.residual[at, :]
    if layer == 1:
        r.last[at, :] = (residual + total[:, depth:]).astype(B16)
    grad = layer_cotangent(r, layer, at).astype(F32) + rms_back(
        residual, gain_of(r, layer, 1), total[:, :depth]
    )
    r.d_residual[at, :] = grad
    return (grad.astype(B16),)


def work_back_mix(layer, r, c, at, total):
    depth = r.d_residual.shape[1]
    step = rms_back(layer_input(r, layer, at), gain_of(r, layer, 0), total[:, :depth])
    grad = (r.d_residual[at, :] + step).astype(B16)
    r.x_grad[at, :] = grad
    _, ways, block, _ = r.shared.shape
    blocks = total.shape[0] // block
    for i in range(blocks):
        j = c * blocks + i
        r.shared[j // ways, j % ways] = total[i * block : (i + 1) * block, depth:]
    return (grad,)


def widen(block, axis, size):
    missing = size - block.shape[axis]
    if missing == 0:
        return block
    pads = [(0, 0)] * block.ndim
    pads[axis] = (0, missing)
    return jnp.pad(block, pads)


def on_device(
    acts_in, out_grad, mix_gain, w_mixer_in, w_query, w_shared, w_step, a_log, dt_bias, d_skip,
    w_mamba_out, w_attn_out, ffn_gain, w_gate_up, w_down,
):
    section = lax.axis_index(PIPE)
    member = lax.axis_index(TENSOR)
    members = lax.axis_size(TENSOR)
    dp = lax.axis_size(DP)
    heads = a_log.shape[1]
    real = heads * HD
    width = (heads + heads % 2) * HD
    q_real = w_query.shape[2]
    cols = Cols(width)
    units = w_gate_up.shape[3]
    rows, depth = acts_in.shape[1:]
    length = rows * members
    piece = depth // dp
    wide = cols.total - cols.b

    at_row = MixerRows(cols, members)
    q_heads = q_real // HD
    inner = jnp.concatenate(
        [widen(w_mixer_in[0, :, 0], 1, width), widen(w_mixer_in[0, :, 1], 1, width)], axis=1
    )
    share = lax.dynamic_slice_in_dim(w_shared[0], member * (piece // members), piece // members, 0)
    share = jnp.concatenate([share[:, at : at + LANES] for at in range(0, 4 * LANES, LANES)], axis=0)
    mixer_shard = jnp.concatenate(
        [fold_lanes(share)(piece), fold_lanes(widen(w_query[0], 1, LANES))(piece)]
        + [inner[:, at : at + piece] for at in range(0, 2 * width, piece)]
        + [widen(w_mamba_out[0], 0, width), widen(w_attn_out[0], 0, LANES)],
        axis=0,
    )
    steps = lax.dynamic_slice_in_dim(w_step[0], member * heads, heads, 1).T.astype(F32)
    ffn_shard = jnp.concatenate(
        [w_gate_up[0, :, j, at : at + piece] for j in range(2) for at in range(0, units, piece)]
        + [w_down[0]],
        axis=0,
    )
    few_shard = jnp.concatenate(
        [mix_gain.astype(F32), ffn_gain.astype(F32)]
        + [widen(row, 1, piece) for row in (a_log, dt_bias, d_skip)]
        + [jnp.zeros((3, piece), F32), widen(steps, 0, 8)],
        axis=0,
    )

    def run(name, number, work, inputs, outs, **more):
        return exchange(name, number, members, dp, rows, depth, work, inputs, outs, **more)

    half = piece // 2
    low_units = width + LANES
    block32, block16 = ((rows, depth), F32), ((rows, depth), B16)
    core_keeps = dict(
        proj=((length, cols.step), B16),
        step=((length, LANES), F32),
        y=((length, width), B16),
        lows=((length, low_units), B16),
        states=((length // STEP, NS, width), B16),
        lse=((length // TILE, 8, 2 * TILE), F32),
    )
    ffn_keeps = dict(gu=((length, 2 * units), B16), hidden=((length, units), B16))
    gu_spec, down_spec = ((2, dp, half, 2 * units), B16), ((2, dp, units // 2, piece), B16)
    cat_spec, out_spec = ((2, dp, half, cols.b), B16), ((2, dp, low_units // 2, piece), B16)
    shared_spec = ((2, dp, half // members, wide), F32)
    gain_row = ((8, depth), F32)
    fills_ffn = [
        lambda r: grad_columns(r.rows_ffn, r.dgu, r.g_gu),
        lambda r: grad_rows(r.hidden, r.rows_out, r.g_down),
    ]
    fill_cat = lambda r: grad_columns(r.rows_mix, r.dproj, r.g_cat)
    fill_out = lambda r: grad_rows(r.lows, r.rows_back, r.g_out)

    load = Cargo(
        0, dp, mixer_shard,
        {BEGIN: 1, SENT: 2, CHUNK: 1, CHUNK + 1: 1, CHUNK + 2: 2, CHUNK + 3: 2, SPREAD: 2, GIVEN: 4},
        members, at_row.shared,
    )
    few = Few(dp, few_shard, {BEGIN: 3})
    got = run(
        "first", 0, work_first, dict(acts_in=acts_in, out_grad=out_grad), {},
        gathers=dict(rows_mix=0, rows_out=0), helpers=[few, load],
    )
    few = few.result
    first = Bag(rows_mix=got.rows_mix, mixer=load.results[0], shared_w=load.results[1], acts_in=acts_in)
    second = Bag(rows_out=got.rows_out, out_grad=out_grad)
    for layer, k in enumerate((first, second)):
        x = dict(acts_in=acts_in) if layer == 0 else dict(x=second.x)
        load = Cargo(
            layer, dp, ffn_shard,
            {
                BEGIN: 1, 1: 1, 2: 3, 3: 3, SENT: 2, CHUNK: 1, CHUNK + 1: 1, CHUNK + 2: 1, CHUNK + 3: 1,
                SPREAD: 1, GIVEN: 2,
            },
        )
        k.add(
            run(
                f"mixer{layer}", 1 + layer, functools.partial(work_mid, layer),
                dict(x, few=few, rows_mix=k.rows_mix, mixer=k.mixer, shared_w=k.shared_w),
                dict(core_keeps, residual=block32, rest=((depth, 6 * LANES), B16)),
                need=dict({n: SENT for n in x}, rows_mix=1),
                done=dict(rest=0, proj=1, step=1, y=2, states=2, lows=3, lse=3, residual=CHUNK + 3),
                scratch=dict(state=pltpu.VMEM((NS, width), F32)),
                phases=functools.partial(core_fwd_phases, cols, members, layer, q_heads),
                part_width=depth, gathers=dict(rows_ffn=0), helpers=[load],
            )
        )
        k.gates = load.result
        if layer == 0:
            load = Cargo(
                1, dp, mixer_shard,
                {
                    BEGIN: 1, 0: 1, 1: 1, SENT: 3, CHUNK: 1, CHUNK + 1: 1, CHUNK + 2: 1, CHUNK + 3: 2, SPREAD: 1,
                    GIVEN: 3,
                },
                members, at_row.shared,
            )
            got = run(
                "turn", 3, work_turn,
                dict(residual=k.residual, few=few, rows_ffn=k.rows_ffn, gates=k.gates),
                dict(ffn_keeps, x=block16),
                need=dict(residual=SENT, few=SENT), done=dict(gu=0, hidden=0, x=CHUNK + 3),
                phases=ffn_fwd_phases, part_width=depth, gathers=dict(rows_mix=0), helpers=[load],
            )
            k.gu, k.hidden = got.gu, got.hidden
            second.rows_mix, second.x = got.rows_mix, got.x
            second.mixer, second.shared_w = load.results

    acts = Place(
        lambda r: (r.raw.x, r.last), (rows, depth), 1,
        {BEGIN: 1, CHUNK: 1, CHUNK + 1: 1, CHUNK + 2: 1, CHUNK + 3: 1},
    )
    second.add(
        run(
            "ffn1", 4, functools.partial(work_back_ffn, 1),
            dict(
                out_grad=out_grad, residual=second.residual, few=few, rows_ffn=second.rows_ffn,
                rows_out=second.rows_out, gates=second.gates, x=second.x,
            ),
            dict(gain_ffn=gain_row, g_gu=gu_spec, g_down=down_spec, d_residual=block32),
            need=dict(out_grad=SENT, residual=SENT, few=SENT, x=None, rows_out=2),
            done=dict(gain_ffn=3, g_gu=SENT, d_residual=CHUNK + 3, g_down=SPREAD),
            scratch=dict(
                last=pltpu.VMEM(*block16),
                **{n: pltpu.VMEM(*spec) for n, spec in ffn_keeps.items()},
                dgu=pltpu.VMEM((length, 2 * units), B16),
            ),
            phases=lambda r: ffn_fwd_phases(r, depth) + ffn_bwd_phases(r),
            fills=fills_ffn, part_width=2 * depth, gathers=dict(rows_back=0), helpers=[acts],
        )
    )

    core_scratch = dict(
        dproj=pltpu.VMEM((length, cols.total), B16),
        heads=pltpu.VMEM((8, LANES), F32),
        dcore=pltpu.VMEM((length, low_units), B16),
        grad_state=pltpu.VMEM((NS, width), F32),
        skip_sum=pltpu.VMEM((STEP, width), F32),
        dk_sum=pltpu.VMEM((length, LANES), F32),
        dv_sum=pltpu.VMEM((length, LANES), F32),
        folded=pltpu.VMEM((length, wide), B16),
        gain_sum=pltpu.VMEM((8, depth), F32),
        staged=pltpu.VMEM((depth, wide), F32),
    )

    def core_inputs(k):
        return dict(
            few=few, rows_mix=k.rows_mix, mixer=k.mixer, rows_back=k.rows_back, d_residual=k.d_residual,
            gain_ffn=k.gain_ffn, proj=k.proj, step=k.step, y=k.y, lows=k.lows, states=k.states,
            lse=k.lse, rest=k.rest,
        )

    core_need = dict(
        lows=1, proj=2, lse=2, few=3, step=3, y=3, states=3, rows_mix=4, gain_ffn=5, g_gu=2, g_down=1,
        d_residual=SENT, x=SENT, acts_in=SENT,
    )

    def core_phases(layer, r):
        return core_bwd_phases(cols, layer, members, (q_heads, heads), r)

    def from_input(pick):
        return lambda r: (pick(r.raw), pick(r))

    def from_kernel(pick):
        return lambda r: (pick(r), pick(r))

    take_gu, take_down = (lambda r: r.g_gu), (lambda r: r.g_down)
    take_cat, take_out, take_shared = (lambda r: r.g_cat), (lambda r: r.g_out), (lambda r: r.shared)

    def back_phases(layer, r):
        into, attend, scan, back, shared = core_phases(layer, r)
        steps = [into, lambda: fill_out(r), attend, scan]
        return steps + ([back, shared] if layer else [lambda: fill_cat(r), back, shared])

    hauls = [
        Haul(
            1, dp, [from_input(take_gu), from_input(take_down)], [gu_spec, down_spec],
            {BEGIN: 1, 2: 1, 3: 1, 4: 1, SENT: 1, CHUNK + 2: 1},
        ),
        Straight(1, dp, from_kernel(take_out), out_spec, {1: 1, CHUNK + 2: 1}),
        Haul(
            1, dp, [from_kernel(take_cat)], [cat_spec], {SENT: 1, SPREAD: 1, GIVEN: 1}, line=False
        ),
    ]
    inner = dict(g_cat=pltpu.VMEM(*cat_spec), g_out=pltpu.VMEM(*out_spec))
    got = run(
        "back1", 5, functools.partial(work_back_mix, 1),
        dict(core_inputs(second), x=second.x, g_gu=second.g_gu, g_down=second.g_down),
        dict(x_grad=block16, shared=shared_spec),
        need=dict(core_need, rest=4),
        done=dict(x_grad=CHUNK + 3, shared=CHUNK + 3),
        scratch=dict(core_scratch, **inner), phases=functools.partial(back_phases, 1), fills=[fill_cat],
        part_width=depth + wide, gathers=dict(rows_out=0), helpers=hauls,
    )
    second.add(got)
    cat_sums = hauls[2].result
    second.sums = hauls[0].results + hauls[1].results

    hauls = [
        Haul(
            1, dp, [from_input(lambda r: r.cat_sums)], [cat_spec], {BEGIN: 1, CHUNK + 3: 1}, swap=False
        ),
        Haul(
            1, dp, [from_input(take_shared)], [shared_spec], {BEGIN: 1, 1: 1, SENT: 2, CHUNK + 1: 1, GIVEN: 1}
        ),
        Haul(
            0, dp, [from_kernel(take_gu)], [gu_spec], {SENT: 1, CHUNK + 3: 1, SPREAD: 1, GIVEN: 1},
            line=False,
        ),
    ]
    got = run(
        "ffn0", 6, functools.partial(work_back_ffn, 0),
        dict(
            cotangent=second.x_grad, residual=first.residual, few=few, rows_ffn=first.rows_ffn,
            rows_out=second.rows_out, gates=first.gates, gu=first.gu, hidden=first.hidden,
            cat_sums=cat_sums, shared=second.shared,
        ),
        dict(gain_ffn=gain_row, g_down=down_spec, d_residual=block32),
        need=dict(
            cotangent=SENT, residual=SENT, few=SENT, rows_ffn=1, hidden=SENT, cat_sums=SENT, shared=1
        ),
        done=dict(gain_ffn=1, d_residual=CHUNK + 3, g_down=SPREAD),
        scratch=dict(dgu=pltpu.VMEM((length, 2 * units), B16), g_gu=pltpu.VMEM(*gu_spec)),
        phases=ffn_bwd_phases, fills=fills_ffn, part_width=depth, gathers=dict(rows_back=0),
        helpers=hauls,
    )
    gu_sums = hauls[2].result
    second.sums += hauls[0].results + hauls[1].results
    first.add(got)

    hauls = [
        Haul(0, dp, [from_input(lambda r: r.gu_sums)], [gu_spec], {BEGIN: 1, 3: 1}, swap=False),
        Haul(
            0, dp, [from_input(take_down)], [down_spec], {BEGIN: 1, 1: 1, 2: 2, 3: 1, 5: 1}
        ),
        Haul(0, dp, [from_kernel(take_out)], [out_spec], {1: 1, 3: 2, 4: 2, SENT: 1}),
        Haul(
            0, dp, [from_kernel(take_cat)], [cat_spec],
            {4: 1, 6: 1, SENT: 1, CHUNK: 1, CHUNK + 1: 1},
        ),
        Straight(0, dp, from_kernel(take_shared), shared_spec, {CHUNK + 3: 1}),
    ]
    x_grads = Place(
        lambda r: (r.x_grad, r.raw.x_grad1), (rows, depth), 0,
        {4: 1, CHUNK: 1, CHUNK + 1: 1, CHUNK + 2: 1, CHUNK + 3: 1},
    )
    run(
        "back0", 7, functools.partial(work_back_mix, 0),
        dict(core_inputs(first), acts_in=acts_in, x_grad1=second.x_grad, gu_sums=gu_sums, g_down=first.g_down),
        {},
        need=dict(core_need, x_grad1=None, gu_sums=3, rest=5, gain_ffn=6),
        scratch=dict(
            core_scratch, **inner, x_grad=pltpu.VMEM(*block16), shared=pltpu.VMEM(*shared_spec)
        ),
        phases=functools.partial(back_phases, 0), part_width=depth + wide, helpers=hauls + [x_grads],
    )
    first.sums = [h.result for h in hauls]
    order = [0, 1, 3, 2, 4]
    g_gates, g_down, g_cat, g_out, g_shared = [
        jnp.where(section == 0, first.sums[i], second.sums[j]).astype(F32).reshape(
            (-1,) + first.sums[i].shape[2:]
        )
        for i, j in zip(order, (0, 1, 3, 2, 4))
    ]
    g_mixer = jnp.stack([g_cat[:, :real], g_cat[:, width : width + real]], axis=1)
    table = 2 * NS + 2 * KVH * HD
    g_gains = g_shared[:, table + GAINS_AT : table + GAINS_AT + 2].T
    g_heads = g_shared[:3, table + HEADS_AT : table + HEADS_AT + heads]
    return (
        acts.result[None],
        x_grads.result[None],
        g_gains[None],
        g_mixer[None],
        g_cat[None, :, cols.q : cols.q + q_real],
        g_shared[None, :, :table],
        g_shared[None, :, table : table + HM],
        g_heads[None],
        g_out[None, :real],
        g_out[None, width : width + q_real],
        g_gates.reshape(1, piece, 2, units),
        g_down[None],
    )


def solution(mesh):
    rows = P(DP, TENSOR, None)
    by_dp, by_tensor, by_both = P(PIPE, DP), P(PIPE, TENSOR), P(PIPE, DP, TENSOR)
    wide, tall, whole = P(PIPE, DP, None, TENSOR), P(PIPE, TENSOR, DP), P(PIPE, DP, None)
    joint = P(PIPE, (DP, TENSOR), None)
    return jax.shard_map(
        on_device,
        mesh=mesh,
        in_specs=(
            rows, rows, by_dp, wide, by_both, whole, whole, by_tensor, by_tensor, by_tensor, tall, tall,
            by_dp, wide, tall,
        ),
        out_specs=(
            P(PIPE, DP, TENSOR, None), P(PIPE, DP, TENSOR, None), P(PIPE, None, (DP, TENSOR)),
            wide, by_both, joint, joint, P(PIPE, None, TENSOR), tall, tall, wide, tall,
        ),
        check_vma=False,
    )
```

```python
import functools

import jax
import jax.numpy as jnp
from jax import lax
from jax.experimental import pallas as pl
from jax.experimental.pallas import tpu as pltpu
from jax.sharding import PartitionSpec as P

HM = 24
HA = 8
KVH = 2
NS = 128
HD = 64
LANES = 128
STEP = 128
TILE = 256
EPS = 1e-05
F32 = jnp.float32
B16 = jnp.bfloat16
VMEM_LIMIT = 60 << 20
HEADS_AT = 32
GAINS_AT = 64


def nn(a, b):
    return lax.dot_general(a, b, (((1,), (0,)), ((), ())), preferred_element_type=F32)


def nt(a, b):
    return lax.dot_general(a, b, (((1,), (1,)), ((), ())), preferred_element_type=F32)


def tn(a, b):
    return lax.dot_general(a, b, (((0,), (0,)), ((), ())), preferred_element_type=F32)


def exact(a, b):
    return lax.dot_general(
        a, b, (((1,), (0,)), ((), ())), precision=lax.Precision.HIGHEST, preferred_element_type=F32
    )


def softplus(v):
    small = jnp.exp(-jnp.abs(v))
    series = small * (1.0 - small * (0.5 - small * (1.0 / 3.0 - small * 0.25)))
    return jnp.maximum(v, 0.0) + jnp.where(small < 0.02, series, jnp.log(1.0 + small))


def sigmoid(v):
    return 1.0 / (1.0 + jnp.exp(-v))


def iotas(rows, columns):
    return (
        lax.broadcasted_iota(jnp.int32, (rows, columns), 0),
        lax.broadcasted_iota(jnp.int32, (rows, columns), 1),
    )


def spread(column_block, head, rows):
    return jnp.broadcast_to(column_block[:, head : head + 1], (rows, LANES))


class Cols:
    def __init__(self, width):
        self.width = width
        self.z = 0
        self.u = width
        self.q = 2 * width
        self.b = self.q + LANES
        self.c = self.b + LANES
        self.k = self.c + LANES
        self.v = self.k + LANES
        self.step = self.v + LANES
        self.total = self.step + LANES
        self.pairs = width // LANES


class MixerRows:
    def __init__(self, cols, members):
        self.shared = 4 * LANES // members
        self.query = self.shared
        self.inner = self.query + LANES
        self.low = self.inner + 2 * cols.width
        self.total = self.low + cols.width + LANES


def fold_lanes(block):
    def folded(piece):
        count = piece // LANES
        size = block.shape[0] // count
        return jnp.concatenate([block[i * size : (i + 1) * size] for i in range(count)], axis=1)

    return folded


def unfold_lanes(block):
    return jnp.concatenate(
        [block[:, at : at + LANES] for at in range(0, block.shape[1], LANES)], axis=0
    )


def join_shared(cols, members, layer, q_heads, r):
    mixer, shared, few, rest = r.mixer, r.shared_w, r.few, r.rest
    ways, _, piece = mixer.shape
    at = MixerRows(cols, members)
    group = lax.axis_index(TENSOR) * q_heads // (HA // KVH)
    source, target = iotas(LANES, LANES)
    choose = (source == group * HD + (target & (HD - 1))).astype(B16)
    size = piece // members
    for d in range(ways):
        rows = slice(d * piece, (d + 1) * piece)
        rest[rows, :LANES] = unfold_lanes(mixer[d, at.query : at.query + LANES, :])
        for m in range(members):
            block = unfold_lanes(shared[m, d])
            to = slice(d * piece + m * size, d * piece + (m + 1) * size)
            for j in range(4):
                lanes = block[j * size : (j + 1) * size, :]
                if j >= 2:
                    lanes = nn(lanes, choose).astype(B16)
                rest[to, LANES * (j + 1) : LANES * (j + 2)] = lanes
        steps = few[layer, d, 8:16, :]
        steps = jnp.concatenate([steps, jnp.zeros((LANES - 8, piece), F32)], axis=0).T
        rest[rows, 5 * LANES :] = steps.astype(B16)


def split_heads(block, low_lanes):
    zero = jnp.zeros_like(block)
    return jnp.concatenate(
        [jnp.where(low_lanes, block, zero), jnp.where(low_lanes, zero, block)], axis=0
    )


def blocks_nn(rows_ref, rows, weights_ref, c, first=0):
    ways, _, piece = weights_ref.shape
    at = slice(first + c * piece, first + (c + 1) * piece)
    total = nn(rows_ref[rows, 0:piece], weights_ref[0, at, :])
    for d in range(1, ways):
        total += nn(rows_ref[rows, d * piece : (d + 1) * piece], weights_ref[d, at, :])
    return total


def multiply_out(lows_ref, weights_ref, first, part_ref, rows, at=0):
    ways, _, piece = weights_ref.shape
    last = first + lows_ref.shape[1]
    block = lows_ref[rows, :]
    for k in range(ways):
        part_ref[rows, at + k * piece : at + (k + 1) * piece] = nn(
            block, weights_ref[k, first:last, :]
        ).astype(B16)


def multiply_back(grad_ref, weights_ref, first, count, part_ref, rows, rows_ref, gain_sum, rest=None):
    ways, _, piece = weights_ref.shape
    for d in range(ways):
        to = slice(d * piece, (d + 1) * piece)
        total = nt(grad_ref[rows, 0:piece], weights_ref[d, first : first + piece, :])
        for c in range(1, count):
            at = slice(first + c * piece, first + (c + 1) * piece)
            total += nt(grad_ref[rows, c * piece : (c + 1) * piece], weights_ref[d, at, :])
        if rest is not None:
            total += nt(grad_ref[rows, count * piece :], rest[to, :])
        part_ref[rows, to] = total.astype(B16)
        if gain_sum is not None:
            gain_sum[0:1, to] += jnp.sum(total * rows_ref[rows, to].astype(F32), axis=0, keepdims=True)


def by_blocks(order, rows, step):
    def phase(group):
        def run():
            for member in group:
                step(pl.ds(pl.multiple_of(member * rows, rows), rows), member)

        return run

    return [phase(group) for group in order]


def skip_lanes(few_ref, layer, width):
    row, lane = iotas(width, LANES)
    own = ((row >> 6) == lane).astype(F32)
    skip = jnp.broadcast_to(few_ref[layer, 0, 4:5, :LANES], (8, LANES))
    return lax.dot_general(
        skip, own, (((1,), (1,)), ((), ())),
        precision=lax.Precision.HIGHEST, preferred_element_type=F32,
    )[0:1, :]


def core_fwd_phases(cols, members, layer, q_heads, r, order):
    rows_ref, weights_ref, few_ref = r.rows_mix, r.mixer, r.few
    proj_ref, step_ref, y_ref, lows_ref = r.proj, r.step, r.y, r.lows
    states_ref, lse_ref, part_ref, state = r.states, r.lse, r.part, r.state
    length = rows_ref.shape[0]
    width = cols.width
    piece = weights_ref.shape[2]

    at_row = MixerRows(cols, members)

    def join_all():
        join_shared(cols, members, layer, q_heads, r)

    def project_all():
        def project(i, _):
            rows = pl.ds(pl.multiple_of(i * TILE, TILE), TILE)
            for c in range(cols.q // piece):
                value = blocks_nn(rows_ref, rows, weights_ref, c, at_row.inner)
                proj_ref[rows, c * piece : (c + 1) * piece] = value.astype(B16)
            rest = nn(rows_ref[rows, :], r.rest[...])
            proj_ref[rows, cols.q : cols.b] = (rest[:, :LANES] * HD**-0.5).astype(B16)
            proj_ref[rows, cols.b : cols.step] = rest[:, LANES : 5 * LANES].astype(B16)
            step_ref[rows, :] = rest[:, 5 * LANES :]
            return 0

        lax.fori_loop(0, length // TILE, project, 0)

    def scan_part(low, high):
        ri, ci = iotas(STEP, STEP)
        lower = ri >= ci
        tril = lower.astype(F32)
        low_lanes = ci < HD
        decay = jnp.exp(few_ref[layer, 0, 2:3, :LANES])
        bias = few_ref[layer, 0, 3:4, :LANES]
        skips = skip_lanes(few_ref, layer, width)
        if low == 0:
            state[...] = jnp.zeros_like(state)

        def scan_block(b, _):
            rows = pl.ds(pl.multiple_of(b * STEP, STEP), STEP)
            dt = softplus(step_ref[rows, :] + bias)
            run = exact(tril, -dt * decay)
            run_t = run.T
            bm = proj_ref[rows, cols.b : cols.b + LANES]
            cm = proj_ref[rows, cols.c : cols.c + LANES]
            cb = jnp.where(lower, nt(cm, bm), 0.0)
            states_in = state[...]
            low_state = states_in.astype(B16)
            states_ref[b] = low_state
            carried = nn(cm, low_state)
            tails, fades = [], []
            for p in range(cols.pairs):
                lanes = slice(LANES * p, LANES * (p + 1))
                u = proj_ref[rows, cols.u + LANES * p : cols.u + LANES * (p + 1)].astype(F32)
                z = proj_ref[rows, cols.z + LANES * p : cols.z + LANES * (p + 1)].astype(F32)
                run_b = [spread(run, 2 * p + k, STEP) for k in range(2)]
                run_w = jnp.where(low_lanes, run_b[0], run_b[1])
                ud = u * jnp.where(low_lanes, spread(dt, 2 * p, STEP), spread(dt, 2 * p + 1, STEP))
                mix = jnp.concatenate(
                    [
                        (
                            jnp.exp(jnp.minimum(run_b[k] - run_t[2 * p + k : 2 * p + k + 1, :], 0.0))
                            * cb
                        ).astype(B16)
                        for k in range(2)
                    ],
                    axis=1,
                )
                inside = nn(mix, split_heads(ud, low_lanes).astype(B16))
                y = inside + carried[:, lanes] * jnp.exp(run_w) + skips[:, lanes] * u
                y_ref[rows, lanes] = y.astype(B16)
                lows_ref[rows, lanes] = (y * z * sigmoid(z)).astype(B16)
                end = run_w[STEP - 1 : STEP, :]
                tails.append((ud * jnp.exp(end - run_w)).astype(B16))
                fades.append(jnp.exp(end))
            fresh = tn(bm, jnp.concatenate(tails, axis=1))
            state[...] = states_in * jnp.concatenate(fades, axis=1) + fresh
            return 0

        lax.fori_loop(low, high, scan_block, 0)

    def attend(i):
        rk, ck = iotas(TILE, 2 * TILE)
        diagonal = rk <= jnp.where(ck < TILE, ck, ck - TILE)
        q_low = iotas(TILE, LANES)[1] < HD

        rows = pl.ds(pl.multiple_of(i * TILE, TILE), TILE)
        q2 = split_heads(proj_ref[rows, cols.q : cols.q + LANES], q_low)

        def piece(j, carry, masked):
            top, total, out = carry
            keys = pl.ds(pl.multiple_of(j * TILE, TILE), TILE)
            s = nt(proj_ref[keys, cols.k : cols.k + LANES], q2)
            if masked:
                s = jnp.where(diagonal, s, -1e30)
            new_top = jnp.maximum(top, jnp.max(s, axis=0, keepdims=True))
            p = jnp.exp(s - new_top)
            scale = jnp.exp(top - new_top)
            total = total * scale + jnp.sum(p, axis=0, keepdims=True)
            out = out * scale + tn(proj_ref[keys, cols.v : cols.v + LANES], p.astype(B16))
            return new_top, total, out

        carry = (
            jnp.full((1, 2 * TILE), -1e30, F32),
            jnp.zeros((1, 2 * TILE), F32),
            jnp.zeros((LANES, 2 * TILE), F32),
        )
        carry = lax.fori_loop(0, i, lambda j, c: piece(j, c, False), carry)
        top, total, out = piece(i, carry, True)
        out = out / total
        joined = jnp.concatenate([out[:HD, :TILE], out[HD:, TILE:]], axis=0)
        lows_ref[rows, width : width + LANES] = joined.T.astype(B16)
        lse_ref[i] = jnp.broadcast_to(top + jnp.log(total), (8, 2 * TILE))

    rows = length // members
    blocks, tiles = length // STEP, length // TILE
    together = rows == TILE

    def attend_all():
        for i in range(tiles):
            attend(i)

    def finish(at, member):
        if together:
            attend(member)
        multiply_out(lows_ref, weights_ref, at_row.low, part_ref, at)

    phases = [
        join_all,
        project_all,
        lambda: scan_part(0, blocks // 2),
        lambda: scan_part(blocks // 2, blocks),
    ]
    if not together:
        phases[3] = lambda: (scan_part(blocks // 2, blocks), attend_all())
    return phases + by_blocks(order, rows, finish)


def core_bwd_phases(cols, layer, members, q_heads, r, order):
    back_ref, weights_ref, few_ref, rows_ref = r.rows_back, r.mixer, r.few, r.rows_mix
    proj_ref, step_ref, y_ref, lows_ref = r.proj, r.step, r.y, r.lows
    states_ref, lse_ref, part_ref = r.states, r.lse, r.part
    dproj_ref, heads_ref, dcore, grad_state, skip_sum = r.dproj, r.heads, r.dcore, r.grad_state, r.skip_sum
    dk_sum, dv_sum, folded, staged = r.dk_sum, r.dv_sum, r.folded, r.staged
    length = back_ref.shape[0]
    width = cols.width
    ways, _, piece = weights_ref.shape
    blocks = length // STEP
    depth = ways * piece
    at_row = MixerRows(cols, members)
    low_rows = slice(at_row.low, at_row.low + width + LANES)

    def into_all():
        def into_core(i, _):
            rows = pl.ds(pl.multiple_of(i * TILE, TILE), TILE)
            total = nt(back_ref[rows, 0:piece], weights_ref[0, low_rows, :])
            for k in range(1, ways):
                total += nt(
                    back_ref[rows, k * piece : (k + 1) * piece], weights_ref[k, low_rows, :]
                )
            dcore[rows, :] = total.astype(B16)
            return 0

        lax.fori_loop(0, length // TILE, into_core, 0)

    def attend_all():
        rk, ck = iotas(TILE, 2 * TILE)
        diagonal = rk <= jnp.where(ck < TILE, ck, ck - TILE)
        q_low = iotas(TILE, LANES)[1] < HD
        dk_sum[...] = jnp.zeros_like(dk_sum)
        dv_sum[...] = jnp.zeros_like(dv_sum)
        half = iotas(8, LANES)
        pick_low = (half[1] < HD).astype(F32)
        pick_high = (half[1] >= HD).astype(F32)

        def attend(i, _):
            rows = pl.ds(pl.multiple_of(i * TILE, TILE), TILE)
            q2 = split_heads(proj_ref[rows, cols.q : cols.q + LANES], q_low)
            d_out = dcore[rows, width : width + LANES]
            do2 = split_heads(d_out, q_low)
            both = d_out.astype(F32) * lows_ref[rows, width : width + LANES].astype(F32)
            high = lax.Precision.HIGHEST
            deltas = [
                lax.dot_general(
                    pick, both, (((1,), (1,)), ((), ())), precision=high, preferred_element_type=F32
                )[0:1, :]
                for pick in (pick_low, pick_high)
            ]
            delta = jnp.concatenate(deltas, axis=1)
            lse = lse_ref[i][0:1, :]

            def piece_of(j, dq, masked):
                keys = pl.ds(pl.multiple_of(j * TILE, TILE), TILE)
                kk = proj_ref[keys, cols.k : cols.k + LANES]
                p = jnp.exp(nt(kk, q2) - lse)
                if masked:
                    p = jnp.where(diagonal, p, 0.0)
                ds = (p * (nt(proj_ref[keys, cols.v : cols.v + LANES], do2) - delta)).astype(B16)
                dv_sum[keys, :] += nn(p.astype(B16), do2)
                dk_sum[keys, :] += nn(ds, q2)
                return dq + tn(kk, ds)

            dq = jnp.zeros((LANES, 2 * TILE), F32)
            dq = lax.fori_loop(0, i, lambda j, c: piece_of(j, c, False), dq)
            dq = piece_of(i, dq, True)
            joined = jnp.concatenate([dq[:HD, :TILE], dq[HD:, TILE:]], axis=0) * HD**-0.5
            dproj_ref[rows, cols.q : cols.q + LANES] = joined.T.astype(B16)
            return 0

        lax.fori_loop(0, length // TILE, attend, 0)
        dproj_ref[:, cols.k : cols.k + LANES] = dk_sum[...].astype(B16)
        dproj_ref[:, cols.v : cols.v + LANES] = dv_sum[...].astype(B16)

    def scan_all():
        ri, ci = iotas(STEP, STEP)
        upper = ri <= ci
        tril = (ri >= ci).astype(F32)
        triu = upper.astype(F32)
        low_lanes = ci < HD
        decay = jnp.exp(few_ref[layer, 0, 2:3, :LANES])
        bias = few_ref[layer, 0, 3:4, :LANES]
        skips = skip_lanes(few_ref, layer, width)
        row, lane = iotas(width, LANES)
        group = ((row >> 6) == lane).astype(B16)
        grad_state[...] = jnp.zeros_like(grad_state)
        skip_sum[...] = jnp.zeros_like(skip_sum)
        heads_ref[...] = jnp.zeros_like(heads_ref)
        zero_rows = jnp.zeros((STEP - 2 * cols.pairs, LANES), F32)

        def scan_block(back, _):
            b = blocks - 1 - back
            rows = pl.ds(pl.multiple_of(b * STEP, STEP), STEP)
            raw = step_ref[rows, :] + bias
            dt = softplus(raw)
            a = -dt * decay
            run = exact(tril, a)
            run_t = run.T
            bm = proj_ref[rows, cols.b : cols.b + LANES]
            cm = proj_ref[rows, cols.c : cols.c + LANES]
            cbt = jnp.where(upper, nt(bm, cm), 0.0)
            low_state = states_ref[b]
            grads_out = grad_state[...]
            low_grad = grads_out.astype(B16)
            carried = nn(cm, low_state)
            pulled = nn(bm, low_grad)
            dcb = jnp.zeros((STEP, STEP), F32)
            dy_fades, u_tails, fades = [], [], []
            carry_terms, direct_terms, tail_terms = [], [], []
            row_sums = []
            col_sums = jnp.zeros((STEP, LANES), F32)
            for p in range(cols.pairs):
                lanes = slice(LANES * p, LANES * (p + 1))
                u16 = proj_ref[rows, cols.u + LANES * p : cols.u + LANES * (p + 1)]
                u = u16.astype(F32)
                z = proj_ref[rows, cols.z + LANES * p : cols.z + LANES * (p + 1)].astype(F32)
                y = y_ref[rows, lanes].astype(F32)
                dm = dcore[rows, lanes].astype(F32)
                sg = sigmoid(z)
                dy = dm * z * sg
                dproj_ref[rows, cols.z + LANES * p : cols.z + LANES * (p + 1)] = (
                    dm * y * sg * (1.0 + z * (1.0 - sg))
                ).astype(B16)
                dy16 = dy.astype(B16)
                skip_sum[:, lanes] += u * dy
                run_b = [spread(run, 2 * p + k, STEP) for k in range(2)]
                dt_b = [spread(dt, 2 * p + k, STEP) for k in range(2)]
                run_w = jnp.where(low_lanes, run_b[0], run_b[1])
                dt_w = jnp.where(low_lanes, dt_b[0], dt_b[1])
                end = run_w[STEP - 1 : STEP, :]
                fade = jnp.exp(run_w)
                tail = jnp.exp(end - run_w)
                dmix = nt(split_heads(u16, low_lanes), dy16)
                mixes = []
                for k in range(2):
                    gap = jnp.exp(jnp.minimum(run_t[2 * p + k : 2 * p + k + 1, :] - run_b[k], 0.0))
                    mixes.append((gap * cbt).astype(B16))
                    weighted = gap * dt_b[k] * dmix[STEP * k : STEP * (k + 1), :]
                    dcb += weighted
                    moved = weighted * cbt
                    row_sums.append(jnp.sum(moved, axis=0, keepdims=True))
                    col_sums = jnp.where(
                        ci == 2 * p + k, jnp.sum(moved, axis=1, keepdims=True), col_sums
                    )
                inside = nn(jnp.concatenate(mixes, axis=1), split_heads(dy16, low_lanes))
                pull_tail = tail * pulled[:, lanes]
                g = inside + pull_tail
                dproj_ref[rows, cols.u + LANES * p : cols.u + LANES * (p + 1)] = (
                    dt_w * g + skips[:, lanes] * dy
                ).astype(B16)
                dy_fade = dy * fade
                dy_fades.append(dy_fade.astype(B16))
                u_tails.append((u * dt_w * tail).astype(B16))
                fades.append(jnp.exp(end))
                carry_terms.append((dy_fade * carried[:, lanes]).astype(B16))
                direct_terms.append((u * g).astype(B16))
                tail_terms.append((u * pull_tail).astype(B16))
            dy_fade = jnp.concatenate(dy_fades, axis=1)
            dcb = jnp.where(upper, dcb, 0.0).astype(B16)
            dproj_ref[rows, cols.c : cols.c + LANES] = (tn(dcb, bm) + nt(dy_fade, low_state)).astype(B16)
            dproj_ref[rows, cols.b : cols.b + LANES] = (
                nn(dcb, cm) + nt(jnp.concatenate(u_tails, axis=1), low_grad)
            ).astype(B16)
            carry_term = nn(jnp.concatenate(carry_terms, axis=1), group)
            direct_term = nn(jnp.concatenate(direct_terms, axis=1), group)
            tail_term = dt * nn(jnp.concatenate(tail_terms, axis=1), group)
            overlap = jnp.sum(low_state.astype(F32) * grads_out, axis=0, keepdims=True)
            overlap = exact(jnp.broadcast_to(overlap, (8, width)), group.astype(F32))[0:1, :]
            overlap = overlap * jnp.exp(run[STEP - 1 : STEP, :])
            row_sum = jnp.concatenate(row_sums + [zero_rows], axis=0).T
            d_run = row_sum - col_sums + carry_term - tail_term
            d_a = exact(triu, d_run) + (jnp.sum(tail_term, axis=0, keepdims=True) + overlap)
            d_step = (direct_term - decay * d_a) * sigmoid(raw)
            dproj_ref[rows, cols.step : cols.step + LANES] = d_step.astype(B16)
            heads_ref[0:1, :] += jnp.sum(d_a * a, axis=0, keepdims=True)
            heads_ref[1:2, :] += jnp.sum(d_step, axis=0, keepdims=True)
            grad_state[...] = grads_out * jnp.concatenate(fades, axis=1) + tn(cm, dy_fade)
            return 0

        lax.fori_loop(0, blocks, scan_block, 0)
        skip = jnp.sum(skip_sum[...], axis=0, keepdims=True)
        heads_ref[2:3, :] = exact(jnp.broadcast_to(skip, (8, width)), group.astype(F32))[0:1, :]

    def back(at, member):
        multiply_back(
            dproj_ref, weights_ref, at_row.inner, cols.q // piece, part_ref, at, rows_ref, None, r.rest
        )

    def shared_all():
        wide = cols.total - cols.b
        member = lax.axis_index(TENSOR)
        heads = q_heads[1]
        group = member * q_heads[0] // (HA // KVH)
        source, target = iotas(wide, wide)
        kind = source >> 7
        wanted = jnp.where(
            kind < 2,
            source,
            jnp.where(
                kind < 4,
                2 * NS + (kind - 2) * KVH * HD + group * HD + (source & (HD - 1)),
                source + member * heads,
            ),
        )
        fold = ((target == wanted) & (source < 4 * LANES + heads)).astype(B16)

        def fold_rows(i, _):
            rows = pl.ds(pl.multiple_of(i * TILE, TILE), TILE)
            folded[rows, :] = nn(dproj_ref[rows, cols.b :], fold).astype(B16)
            return 0

        lax.fori_loop(0, length // TILE, fold_rows, 0)
        sub = piece // members
        half = sub // 2
        lane = iotas(piece, LANES)[1]
        head_lane = iotas(8, LANES)[1]
        shifted = jnp.where(
            (head_lane >= HEADS_AT) & (head_lane < HEADS_AT + heads),
            pltpu.roll(heads_ref[...], HEADS_AT, 1),
            0.0,
        )
        for k in range(ways):
            at = slice(k * piece, (k + 1) * piece)
            grad = tn(rows_ref[:, at], folded[...])
            raw = nn(r.rest[at, LANES:], fold)
            twice = (iotas(piece, wide)[1] >= 2 * LANES) & (iotas(piece, wide)[1] < 4 * LANES)
            own = jnp.sum(grad * jnp.where(twice, 0.5 * raw, raw), axis=1, keepdims=True)
            gains = [jnp.broadcast_to(few_ref[layer, k, i : i + 1, :], (LANES, piece)).T for i in (0, 1)]
            from_ffn = jnp.broadcast_to(r.gain_ffn[0:1, at], (LANES, piece)).T
            columns = [(own + r.gain_column[at, 0:1]) / gains[0], from_ffn / gains[1]]
            last = grad[:, wide - LANES :]
            last = jnp.where(lane == GAINS_AT, columns[0], last)
            last = jnp.where(lane == GAINS_AT + 1, columns[1], last)
            for t in range(members):
                for h in range(2):
                    to = t * (depth // members) + (h * ways + k) * half
                    rows = slice(t * sub + h * half, t * sub + (h + 1) * half)
                    staged[to : to + half, : wide - LANES] = grad[rows, : wide - LANES]
                    staged[to : to + half, wide - LANES :] = last[rows, :]
            to = pl.multiple_of(member * (depth // members) + k * half, 8)
            staged[pl.ds(to, 8), wide - LANES :] += shifted
        r.extra[...] = staged[...].astype(B16)

    return [into_all, attend_all, scan_all, shared_all] + by_blocks(order, length // members, back)


def ffn_forward(r, rows, at=0):
    rows_ref, weights_ref, gu_ref, hidden_ref = r.rows_ffn, r.gates, r.gu, r.hidden
    units = hidden_ref.shape[1]
    piece = weights_ref.shape[2]
    count = units // piece
    for c in range(count):
        to = slice(c * piece, (c + 1) * piece)
        g = blocks_nn(rows_ref, rows, weights_ref, c)
        v = blocks_nn(rows_ref, rows, weights_ref, c + count)
        gu_ref[rows, to] = g.astype(B16)
        gu_ref[rows, units + c * piece : units + (c + 1) * piece] = v.astype(B16)
        hidden_ref[rows, to] = (g * sigmoid(g) * v).astype(B16)
    multiply_out(hidden_ref, weights_ref, 2 * units, r.part, rows, at)


def ffn_backward(r, rows):
    out_ref, weights_ref, gu_ref, dgu_ref = r.rows_out, r.gates, r.gu, r.dgu
    ways, _, piece = weights_ref.shape
    units = gu_ref.shape[1] // 2
    down_rows = slice(2 * units, 3 * units)
    dh = nt(out_ref[rows, 0:piece], weights_ref[0, down_rows, :])
    for k in range(1, ways):
        dh += nt(out_ref[rows, k * piece : (k + 1) * piece], weights_ref[k, down_rows, :])
    g = gu_ref[rows, :units].astype(F32)
    v = gu_ref[rows, units:].astype(F32)
    sg = sigmoid(g)
    dgu_ref[rows, :units] = (dh * v * sg * (1.0 + g * (1.0 - sg))).astype(B16)
    dgu_ref[rows, units:] = (dh * g * sg).astype(B16)
    multiply_back(
        dgu_ref, weights_ref, 0, 2 * units // piece, r.part, rows, r.rows_ffn, r.gain_ffn
    )


def grad_columns(rows_ref, grad_ref, out_ref, step=512, weigh=None):
    _, ways, half, width = out_ref.shape
    for k in range(ways):
        block = rows_ref[:, 2 * half * k : 2 * half * (k + 1)]
        for first in range(0, width, step):
            last = min(first + step, width)
            value = tn(block, grad_ref[:, first:last])
            if weigh:
                weigh(k, first, last, value)
            value = value.astype(B16)
            out_ref[0, k, :, first:last] = value[:half, :]
            out_ref[1, k, :, first:last] = value[half:, :]


def mixer_columns(cols, members, r):
    _, _, piece = r.mixer.shape
    inner = MixerRows(cols, members).inner
    r.gain_column[...] = jnp.zeros_like(r.gain_column)

    def weigh(k, first, last, value):
        rows = slice(k * piece, (k + 1) * piece)
        if first < cols.q:
            weight = r.mixer[k, inner + first : inner + last, :]
        else:
            weight = r.rest[rows, :LANES]
        r.gain_column[rows, 0:1] += jnp.sum(value * weight.astype(F32), axis=1, keepdims=True)

    grad_columns(r.rows_mix, r.dproj, r.g_cat, piece, weigh)


def grad_rows(lows_ref, back_ref, out_ref):
    _, ways, half, piece = out_ref.shape
    for h in range(2):
        block = lows_ref[:, h * half : (h + 1) * half]
        for k in range(ways):
            out_ref[h, k] = tn(block, back_ref[:, k * piece : (k + 1) * piece]).astype(B16)


DMA = pltpu.SemaphoreType.DMA
MESH = pl.DeviceIdType.MESH
PIPE, DP, TENSOR = "pipe", "dp", "tensor"
PART, SHARED = "part", "extra"

BEGIN, SENT, EXTRA, CHUNK, SPREAD, GIVEN, END = -1, 20, 25, 30, 40, 50, 60


class Bag:
    def __init__(self, **entries):
        self.__dict__.update(entries)

    def add(self, other):
        self.__dict__.update(other.__dict__)


def remote(source, target, send, receive, device):
    return pltpu.make_async_remote_copy(
        src_ref=source, dst_ref=target, send_sem=send, recv_sem=receive,
        device_id=device, device_id_type=MESH,
    )


class Helper:
    def __init__(self, when):
        self.when = when
        self.inputs, self.outs, self.scratch = [], [], []
        self.results = None

    @property
    def result(self):
        return self.results[0]


def cross_devices(ways):
    section, place = lax.axis_index(PIPE), lax.axis_index(DP)
    return [{PIPE: 1 - section}] + [{DP: (place + k) % ways} for k in range(1, ways)]


class Few(Helper):
    def __init__(self, ways, shard, when):
        super().__init__(when)
        self.ways = ways
        self.inputs = [shard]
        self.outs = [((2, ways) + shard.shape, F32, pltpu.VMEM)]
        self.scratch = [DMA((1,)), DMA((1,)), DMA((2, ways)), DMA((2, ways)), DMA((1,))]

    def bind(self, r, inputs, outs, scratch):
        (shard,), (few,) = inputs, outs
        r.few = few
        section, place, ways = lax.axis_index(PIPE), lax.axis_index(DP), self.ways
        pair_send, pair_recv, line_send, line_recv, local = scratch
        mine = few.at[section, place]

        def over():
            return remote(shard, mine, pair_send.at[0], pair_recv.at[0], {PIPE: 1 - section})

        def line(layer, k, there):
            block = few.at[layer, there]
            return remote(
                block, block, line_send.at[layer, k], line_recv.at[layer, k], {DP: (place + k) % ways}
            )

        def start():
            over().start()
            own = pltpu.make_async_copy(shard, mine, local.at[0])
            own.start()
            own.wait()

        def spread():
            over().wait_recv()
            for layer in range(2):
                for k in range(1, ways):
                    line(layer, k, place).start()

        def finish():
            for layer in range(2):
                for k in range(1, ways):
                    line(layer, k, (place + ways - k) % ways).wait_recv()
            over().wait_send()
            for layer in range(2):
                for k in range(1, ways):
                    line(layer, k, place).wait_send()

        return [start, spread, finish]


class Cargo(Helper):
    CHUNKS = 4

    def __init__(self, layer, ways, shard, when, members=0, shared=0):
        super().__init__(when)
        self.layer, self.ways, self.rows = layer, ways, shard.shape[0]
        self.members, self.shared = members, shared
        n = self.CHUNKS
        self.first = (self.rows * 2 // 5 + 8 * n) // (16 * n) * (16 * n)
        self.inputs = [shard]
        self.outs = [((ways,) + shard.shape, shard.dtype, pl.ANY)]
        self.scratch = [DMA((n,)), DMA((n,))] + [DMA((ways, n))] * 6 + [DMA((1,))]
        if shared:
            self.outs.append(((members, ways, shared, shard.shape[1]), shard.dtype, pl.ANY))
            self.scratch += [DMA((members,))] * 4 + [DMA((1,))]

    def bind(self, r, inputs, outs, scratch):
        (shard_ref,), out_ref = inputs, outs[0]
        early_send, early_recv, up_send, up_recv, down_send, down_recv, over_send, over_recv, local = scratch[:9]
        section, place = lax.axis_index(PIPE), lax.axis_index(DP)
        partner = {PIPE: 1 - section}
        ways, chunks = self.ways, self.CHUNKS
        sizes = {True: self.first // chunks, False: (self.rows - self.first) // chunks}

        def by_role(step):
            def both():
                pl.when(section == self.layer)(lambda: step(True))
                pl.when(section != self.layer)(lambda: step(False))

            return both

        def part(owner, c):
            return pl.ds((0 if owner else self.first) + c * sizes[owner], sizes[owner])

        def early(c):
            at = part(False, c)
            return remote(
                shard_ref.at[at, :], out_ref.at[place, at, :], early_send.at[c], early_recv.at[c], partner
            )

        def line(owner, up, hop, c):
            at = part(owner, c)
            send, receive = (up_send, up_recv) if up else (down_send, down_recv)
            shard = place - hop if up else place + hop
            source = shard_ref if owner and hop == 0 else out_ref.at[shard]
            return remote(
                source.at[at, :], out_ref.at[shard, at, :], send.at[hop, c], receive.at[hop, c],
                {DP: (place + (1 if up else ways - 1)) % ways},
            )

        def sends(up, hop):
            if up:
                return (place >= hop) & (place < ways - 1)
            return (place < ways - hop) & (place > 0)

        def over(owner, shard, c, own=False):
            at = part(owner, c)
            source = shard_ref if own else out_ref.at[shard]
            return remote(
                source.at[at, :], out_ref.at[shard, at, :], over_send.at[shard, c], over_recv.at[shard, c],
                partner,
            )

        def own_copy():
            return pltpu.make_async_copy(shard_ref, out_ref.at[place], local.at[0])

        def launch(owner, c):
            for up in (True, False):
                pl.when(sends(up, 0))(lambda up=up: line(owner, up, 0, c).start())

        def start(owner):
            if owner:
                for c in range(chunks):
                    early(c).start()
                    launch(True, c)
                for c in range(chunks):
                    over(True, place, c, True).start()
                own_copy().start()

        def spread(c, owner):
            if not owner:
                early(c).wait_recv()
                launch(False, c)

        def hop(count, c, owner):
            for up in (True, False):
                shard = place - count if up else place + count

                @pl.when(shard >= 0 if up else shard < ways)
                def _(up=up, shard=shard):
                    line(owner, up, count - 1, c).wait_recv()
                    if count < ways - 1:
                        pl.when(sends(up, count))(lambda: line(owner, up, count, c).start())
                    over(owner, shard, c).start()

        def wait_over(owner, c):
            for shard in range(ways):

                def wait(shard=shard):
                    block = out_ref.at[shard, part(not owner, c), :]
                    remote(
                        block, block, over_send.at[shard, c], over_recv.at[shard, c], partner
                    ).wait_recv()

                if owner:
                    pl.when(place != shard)(wait)
                else:
                    wait()

        first_waited = 1 if self.shared else 0

        def finish(owner):
            for c in range(chunks):
                if owner or c >= first_waited:
                    wait_over(owner, c)
            for c in range(chunks):
                if owner:
                    early(c).wait_send()
                for count in range(ways - 1):
                    for up in (True, False):
                        pl.when(sends(up, count))(
                            lambda up=up, count=count: line(owner, up, count, c).wait_send()
                        )
                for shard in range(ways):

                    def wait(shard=shard):
                        over(owner, shard, c).wait_send()

                    if owner:
                        wait()
                    else:
                        pl.when(place != shard)(wait)
            if owner and not self.shared:
                own_copy().wait()

        steps = [start]
        steps += [functools.partial(spread, c) for c in range(chunks)]
        steps += [functools.partial(hop, count, c) for count in range(1, ways) for c in range(chunks)]
        steps = [by_role(step) for step in steps]
        if not self.shared:
            return steps + [by_role(finish)]

        assert self.shared <= sizes[True]
        all_ref = outs[1]
        give_send, give_recv, far_send, far_recv, keep = scratch[9:]
        me = lax.axis_index(TENSOR)
        pairs = self.members // 2
        mine, side = me // 2, me % 2
        sibling = 2 * mine + 1 - side
        share = out_ref.at[:, pl.ds(0, self.shared), :]

        def far(count):
            return 2 * ((mine + count) % pairs) + side

        def across(count):
            return 2 * ((mine + count) % pairs) + 1 - side

        def give(count):
            block = all_ref.at[far(count)]
            return remote(
                share if count == 0 else block, block, give_send.at[count], give_recv.at[count],
                {TENSOR: sibling},
            )

        def send_far(count, slot):
            return remote(
                share, all_ref.at[me], far_send.at[count], far_recv.at[slot], {TENSOR: far(count)}
            )

        def own_share():
            return pltpu.make_async_copy(share, all_ref.at[me], keep.at[0])

        def share_out():
            pl.when(section != self.layer)(lambda: wait_over(False, 0))
            pl.when(section == self.layer)(lambda: own_copy().wait())
            for count in range(1, pairs):
                send_far(count, pairs - count).start()
            give(0).start()
            own_share().start()

        def pass_on():
            for count in range(1, pairs):
                send_far(count, count).wait_recv()
                give(count).start()

        def finish_all():
            by_role(finish)()
            for count in range(pairs):
                block = all_ref.at[sibling if count == 0 else across(count)]
                remote(
                    block, block, give_send.at[count], give_recv.at[count], {TENSOR: sibling}
                ).wait_recv()
            for count in range(pairs):
                give(count).wait_send()
                if count:
                    send_far(count, pairs - count).wait_send()
            own_share().wait()

        at = len(steps) - (chunks - 1)
        return steps[:at] + [share_out] + steps[at:] + [pass_on, finish_all]


class Haul(Helper):
    def __init__(self, layer, ways, sources, specs, when, swap=True, line=True):
        super().__init__(when)
        self.layer, self.ways, self.sources, self.swap, self.line = layer, ways, sources, swap, line
        self.count = len(specs)
        self.order = sorted(range(1, ways), key=lambda k: abs(2 * k - ways)) + [0]
        for (_, blocks, rows, columns), dtype in specs:
            block = pltpu.VMEM((blocks, rows, columns), dtype)
            if swap and not line:
                self.outs.append(((blocks, rows, columns), dtype, pltpu.VMEM))
            if line:
                self.outs.append(((2, rows, columns), dtype, pltpu.VMEM))
            if swap:
                self.scratch += [block, DMA((ways,)), DMA((ways,))]
            if swap and line:
                self.scratch.append(block)
            if line:
                self.scratch += [block, pltpu.VMEM((rows, columns), dtype), DMA((ways,)), DMA((ways,))]
                self.scratch += [DMA((1,)), DMA((1,))]

    def bind(self, r, inputs, outs, scratch):
        section, place, ways = lax.axis_index(PIPE), lax.axis_index(DP), self.ways
        partner = {PIPE: 1 - section}
        scratch = list(scratch)
        arrays = []
        for source, out in zip(self.sources, outs):
            a = Bag(out=out)
            a.sent, a.read = source(r)
            a.sums = a.read
            if self.swap:
                a.swapped, a.swap_send, a.swap_recv = [scratch.pop(0) for _ in range(3)]
                a.sums = scratch.pop(0) if self.line else out
                a.sums_sent = a.sums
            else:
                a.sums_sent = a.sent
            if self.line:
                a.arrived, a.result, a.line_send, a.line_recv, a.last_send, a.last_recv = [
                    scratch.pop(0) for _ in range(6)
                ]
            arrays.append(a)

        def to(k):
            return (place + k) % ways

        def swap(a, k):
            return remote(
                a.sent.at[1 - section, to(k)], a.swapped.at[to(k)], a.swap_send.at[k], a.swap_recv.at[k],
                partner,
            )

        def line(a, k):
            return remote(
                a.sums_sent.at[to(k)], a.arrived.at[k], a.line_send.at[k], a.line_recv.at[k], {DP: to(k)}
            )

        def last(a):
            return remote(
                a.result, a.out.at[1 - self.layer], a.last_send.at[0], a.last_recv.at[0], partner
            )

        def start():
            for k in self.order:
                for a in arrays:
                    if self.swap:
                        swap(a, k).start()
                    elif k:
                        line(a, k).start()

        def fold(k):
            def step():
                for a in arrays:
                    swap(a, k).wait_recv()
                    total = a.read[section, to(k)].astype(F32) + a.swapped[to(k)].astype(F32)
                    a.sums[to(k)] = total.astype(a.sums.dtype)
                    if k and self.line:
                        line(a, k).start()

            return step

        def reduce():
            for a in arrays:
                total = a.sums[place].astype(F32)
                for k in range(1, ways):
                    line(a, k).wait_recv()
                    total += a.arrived[k].astype(F32)
                a.result[...] = total.astype(a.out.dtype)

            @pl.when(section == self.layer)
            def _():
                for a in arrays:
                    a.out[self.layer] = a.result[...]

            @pl.when(section != self.layer)
            def _():
                for a in arrays:
                    last(a).start()

        def finish():
            if self.line:

                @pl.when(section == self.layer)
                def _():
                    for a in arrays:
                        last(a).wait_recv()

                @pl.when(section != self.layer)
                def _():
                    for a in arrays:
                        last(a).wait_send()
                        a.out[...] = jnp.zeros_like(a.out)

            for k in self.order:
                for a in arrays:
                    if self.swap:
                        swap(a, k).wait_send()
                    if k and self.line:
                        line(a, k).wait_send()

        steps = [start]
        if self.swap:
            steps += [fold(k) for k in self.order]
        if self.line:
            steps.append(reduce)
        return steps + [finish]


class Straight(Helper):
    def __init__(self, layer, ways, source, spec, when):
        super().__init__(when)
        self.layer, self.ways, self.source = layer, ways, source
        (_, blocks, rows, columns), dtype = spec
        result = (2, rows, columns)
        self.outs = [(result, dtype, pltpu.VMEM)]
        self.scratch = [pltpu.VMEM((blocks,) + result, dtype), pltpu.VMEM(result, dtype)]
        self.scratch += [pltpu.VMEM(result, dtype), DMA((2, ways)), DMA((2, ways)), DMA((1,)), DMA((1,))]

    def bind(self, r, inputs, outs, scratch):
        sent, read = self.source(r)
        (out,) = outs
        arrived, result, handed, line_send, line_recv, last_send, last_recv = scratch
        section, place, ways = lax.axis_index(PIPE), lax.axis_index(DP), self.ways
        order = sorted(range(1, ways), key=lambda k: abs(2 * k - ways))

        def line(half, k):
            to = (place + k) % ways
            return remote(
                sent.at[half, to], arrived.at[k, half], line_send.at[half, k], line_recv.at[half, k], {DP: to}
            )

        def last():
            return remote(result, handed, last_send.at[0], last_recv.at[0], {PIPE: 1 - section})

        def start():
            for k in order:
                for half in range(2):
                    line(half, k).start()

        def reduce():
            for half in range(2):
                total = read[half, place].astype(F32)
                for k in range(1, ways):
                    line(half, k).wait_recv()
                    total += arrived[k, half].astype(F32)
                result[half] = total.astype(result.dtype)

            @pl.when(section != self.layer)
            def _():
                last().start()

        def finish():
            @pl.when(section == self.layer)
            def _():
                last().wait_recv()
                out[...] = (result[...].astype(F32) + handed[...].astype(F32)).astype(out.dtype)

            @pl.when(section != self.layer)
            def _():
                last().wait_send()
                out[...] = jnp.zeros_like(out)

            for k in order:
                for half in range(2):
                    line(half, k).wait_send()

        return [start, reduce, finish]


class Place(Helper):
    PIECES = 4

    def __init__(self, source, shape, late, when):
        super().__init__(when)
        self.source, self.late, self.size = source, late, shape[0] // self.PIECES
        self.outs = [((2,) + shape, B16, pl.ANY)]
        self.scratch = [DMA((self.PIECES,)), DMA((self.PIECES,)), DMA((self.PIECES,))]

    def bind(self, r, inputs, outs, scratch):
        (out,) = outs
        send, receive, local = scratch
        section = lax.axis_index(PIPE)
        rows = self.source(r)

        def over(layer, c):
            at = pl.ds(c * self.size, self.size)
            return remote(
                rows[layer].at[at, :], out.at[1 - layer, at, :], send.at[c], receive.at[c], {PIPE: 1 - section}
            )

        def own(layer, c):
            at = pl.ds(c * self.size, self.size)
            return pltpu.make_async_copy(rows[layer].at[at, :], out.at[layer, at, :], local.at[c])

        def hand(layer, c):
            pl.when(section != layer)(lambda: over(layer, c).start())
            pl.when(section == layer)(lambda: own(layer, c).start())

        def early():
            for c in range(self.PIECES):
                hand(1 - self.late, c)

        def finish():
            for c in range(self.PIECES):
                for layer in range(2):

                    @pl.when(section == layer)
                    def _(layer=layer):
                        over(1 - layer, c).wait()
                        own(layer, c).wait()

        return [early] + [functools.partial(hand, self.late, c) for c in range(self.PIECES)] + [finish]


class Members:
    def __init__(self, count):
        self.pairs = count // 2
        self.me = lax.axis_index(TENSOR)
        self.mine, self.side = self.me // 2, self.me % 2
        self.sibling = 2 * self.mine + 1 - self.side

    def far(self, k):
        return 2 * ((self.mine + k) % self.pairs) + self.side

    def across(self, k):
        return 2 * ((self.mine + k) % self.pairs) + 1 - self.side

    def order(self):
        others = range(1, self.pairs)
        return [[self.across(k) for k in others], [self.far(k) for k in others], [self.sibling], [self.me]]


def member_copy(source, target, send, receive, member):
    return remote(source, target, send, receive, {TENSOR: member})


class Scatter:
    @staticmethod
    def scratch(members, rows, width, pieces):
        pairs = members // 2
        others = max(pairs - 1, 1)
        return [
            pltpu.VMEM((pairs, rows, width), B16),
            pltpu.VMEM((others, rows, width), B16),
            pltpu.VMEM((others, rows, width), B16),
            DMA((pairs, pieces)), DMA((pairs, pieces)), DMA((others, pieces)), DMA((others, pieces)),
        ]

    def __init__(self, part_ref, members, rows, pieces, scratch):
        self.part, self.at, self.rows, self.pieces = part_ref, members, rows, pieces
        self.size = rows // pieces
        self.pair_in, self.far_out, self.far_in = scratch[:3]
        self.pair_send, self.pair_recv, self.far_send, self.far_recv = scratch[3:]

    def rows_of(self, member, c):
        return pl.ds(pl.multiple_of(member * self.rows + c * self.size, self.size), self.size)

    def chunk(self, c):
        return pl.ds(c * self.size, self.size)

    def to_pair(self, k, c):
        member = self.at.across(k) if k else self.at.sibling
        return member_copy(
            self.part.at[self.rows_of(member, c), :], self.pair_in.at[k, self.chunk(c), :],
            self.pair_send.at[k, c], self.pair_recv.at[k, c], self.at.sibling,
        )

    def to_far(self, k, c, slot):
        return member_copy(
            self.far_out.at[k - 1, self.chunk(c), :], self.far_in.at[slot - 1, self.chunk(c), :],
            self.far_send.at[k - 1, c], self.far_recv.at[slot - 1, c], self.at.far(k),
        )

    def send_across(self):
        for c in range(self.pieces):
            for k in range(1, self.at.pairs):
                self.to_pair(k, c).start()

    def send_far(self):
        for c in range(self.pieces):
            for k in range(1, self.at.pairs):
                self.to_pair(k, c).wait_recv()
                total = self.part[self.rows_of(self.at.far(k), c), :].astype(F32)
                total += self.pair_in[k, self.chunk(c), :].astype(F32)
                self.far_out[k - 1, self.chunk(c), :] = total.astype(B16)
                self.to_far(k, c, self.at.pairs - k).start()

    def send_sibling(self):
        for c in range(self.pieces):
            self.to_pair(0, c).start()

    def receive(self, c):
        self.to_pair(0, c).wait_recv()
        total = self.part[self.rows_of(self.at.me, c), :].astype(F32)
        total += self.pair_in[0, self.chunk(c), :].astype(F32)
        for k in range(1, self.at.pairs):
            self.to_far(k, c, k).wait_recv()
            total += self.far_in[k - 1, self.chunk(c), :].astype(F32)
        return total

    def finish(self):
        for c in range(self.pieces):
            for k in range(self.at.pairs):
                self.to_pair(k, c).wait_send()
                if k:
                    self.to_far(k, c, self.at.pairs - k).wait_send()


def exchange_kernel(plan, *refs):
    refs = list(refs)

    def take(count):
        return [refs.pop(0) for _ in range(count)]

    r = Bag()
    held = {name: take(1)[0] for name in plan.inputs}
    r.raw = Bag(**held)
    helper_inputs = [take(len(h.inputs)) for h in plan.helpers]
    targets = {name: take(1)[0] for name in plan.outs}
    gathered = take(len(plan.gathers))
    helper_outs = [take(len(h.outs)) for h in plan.helpers]
    loaded = [name for name in plan.inputs if plan.need(name) is not None]
    for name in loaded + plan.outs + plan.scratch:
        setattr(r, name, take(1)[0])
    load_sem, store_sem = take(2)
    at = Members(plan.members)
    pairs, pieces = at.pairs, plan.pieces
    scatters = {}
    for name, (_, count, _) in plan.scatters.items():
        setattr(r, name, take(1)[0])
        scatters[name] = Scatter(getattr(r, name), at, plan.rows, count, take(7))
    if plan.gathers:
        mine_refs = take(len(plan.gathers))
        give_send, give_recv, spread_send, spread_recv, keep_sem = take(5)
    helpers = []
    for h, inputs, outs in zip(plan.helpers, helper_inputs, helper_outs):
        helpers.append((h.bind(r, inputs, outs, take(len(h.scratch))), h.when))
    size = plan.rows // pieces

    def rows_of(member, c):
        return pl.ds(pl.multiple_of(member * plan.rows + c * size, size), size)

    def chunk(c):
        return pl.ds(c * size, size)

    loads = {}
    for i, name in enumerate(sorted(loaded, key=plan.need)):
        loads[name] = pltpu.make_async_copy(held[name], getattr(r, name), load_sem.at[i])
        loads[name].start()

    def arrive(stage):
        for name in list(loads):
            if plan.need(name) <= stage:
                loads.pop(name).wait()

    stores = []

    def flush(stage):
        for i, name in enumerate(plan.outs):
            if plan.done(name) == stage:
                store = pltpu.make_async_copy(getattr(r, name), targets[name], store_sem.at[i])
                store.start()
                stores.append(store)

    def point(stage):
        for steps, when in helpers:
            count = len(steps) - 1 if stage == END else when.get(stage, 0)
            for _ in range(min(count, len(steps))):
                steps.pop(0)()
        if stage == END:
            for steps, _ in helpers:
                while steps:
                    steps.pop(0)()
        flush(stage)

    def run_fill(i):
        if i < len(plan.fills):
            plan.fills[i](r)

    barrier = pltpu.get_barrier_semaphore()
    greeted = [{TENSOR: at.sibling}] + [{TENSOR: at.far(k)} for k in range(1, pairs)]
    if helpers:
        greeted += cross_devices(plan.ways)
    for device in greeted:
        pl.semaphore_signal(barrier, inc=1, device_id=device, device_id_type=MESH)
    pl.semaphore_wait(barrier, len(greeted))

    arrive(BEGIN)
    point(BEGIN)
    for i, phase in enumerate(plan.phases(r, at.order()) if plan.phases else []):
        arrive(i)
        phase()
        for name, (_, _, ready) in plan.scatters.items():
            for last, send in zip(
                ready, (scatters[name].send_across, scatters[name].send_far, scatters[name].send_sibling)
            ):
                if last == i:
                    send()
        point(i)
    arrive(SENT)
    if plan.phases:
        run_fill(0)
    point(SENT)
    if plan.extra_work:
        plan.extra_work(r, scatters)
        point(EXTRA)

    given, spreads, keeps = {}, {}, []
    for c in range(pieces):
        total = None
        if plan.phases:
            for name in plan.scatters:
                total = scatters[name].receive(c)
                break
        results = plan.work(r, c, chunk(c), total)
        for g, rows_ref in enumerate(gathered):
            own = mine_refs[g].at[chunk(c), :]
            there = rows_ref.at[rows_of(at.me, c), :]
            mine_refs[g][chunk(c), :] = results[g]
            for k in range(1, pairs):
                spreads[g, k, c] = member_copy(
                    own, there, spread_send.at[g, k - 1, c], spread_recv.at[g, pairs - k - 1, c], at.far(k)
                )
                spreads[g, k, c].start()
            given[g, 0, c] = member_copy(
                own, there, give_send.at[g, 0, c], give_recv.at[g, 0, c], at.sibling
            )
            given[g, 0, c].start()
            keeps.append(pltpu.make_async_copy(own, there, keep_sem.at[g, c]))
            keeps[-1].start()
        point(CHUNK + c)
    run_fill(1)
    point(SPREAD)
    for g, rows_ref in enumerate(gathered):
        for c in range(pieces):
            for k in range(1, pairs):
                block = rows_ref.at[rows_of(at.far(k), c), :]
                member_copy(
                    block, block, spread_send.at[g, k - 1, c], spread_recv.at[g, k - 1, c], at.far(k)
                ).wait_recv()
                given[g, k, c] = member_copy(
                    block, block, give_send.at[g, k, c], give_recv.at[g, k, c], at.sibling
                )
                given[g, k, c].start()
    point(GIVEN)
    for g, rows_ref in enumerate(gathered):
        for c in range(pieces):
            for k in range(pairs):
                block = rows_ref.at[rows_of(at.across(k) if k else at.sibling, c), :]
                member_copy(
                    block, block, give_send.at[g, k, c], give_recv.at[g, k, c], at.sibling
                ).wait_recv()
        for c in range(pieces):
            for k in range(pairs):
                given[g, k, c].wait_send()
            for k in range(1, pairs):
                spreads[g, k, c].wait_send()
    for scatter in scatters.values():
        scatter.finish()
    arrive(END)
    point(END)
    for store in stores + keeps:
        store.wait()


def exchange(
    name, number, members, ways, rows, depth, work, inputs, outs=None, need=None, done=None, scratch=None,
    phases=None, fills=(), scatters=None, extra_work=None, gathers=None, helpers=(), pieces=4,
):
    pairs = members // 2
    others = max(pairs - 1, 1)
    outs, scratch, need, done = outs or {}, scratch or {}, need or {}, done or {}
    gathers, scatters = gathers or [], scatters or {}
    hbm, vmem = pl.BlockSpec(memory_space=pl.ANY), pl.BlockSpec(memory_space=pltpu.VMEM)
    plan = Bag(
        inputs=list(inputs), outs=list(outs), scratch=list(scratch), gathers=gathers, helpers=list(helpers),
        members=members, ways=ways, rows=rows, pieces=pieces, scatters=scatters, extra_work=extra_work,
        phases=phases, fills=list(fills), work=work,
        need=lambda n: need.get(n, 0 if phases else BEGIN), done=lambda n: done.get(n, END),
    )
    staging = [pltpu.VMEM(a.shape, a.dtype) for n, a in inputs.items() if plan.need(n) is not None]
    staging += [pltpu.VMEM(*spec) for spec in outs.values()]
    staging += list(scratch.values())
    staging += [DMA((max(len(inputs), 1),)), DMA((max(len(outs), 1),))]
    for width, chunks, _ in scatters.values():
        staging.append(pltpu.VMEM((members * rows, width), B16))
        staging += Scatter.scratch(members, rows, width, chunks)
    count = len(gathers)
    if count:
        staging += [pltpu.VMEM((rows, depth), B16)] * count
        staging += [
            DMA((count, pairs, pieces)), DMA((count, pairs, pieces)),
            DMA((count, others, pieces)), DMA((count, others, pieces)), DMA((count, pieces)),
        ]
    operands = list(inputs.values())
    shapes = [jax.ShapeDtypeStruct(*spec) for spec in outs.values()]
    shapes += [jax.ShapeDtypeStruct((members * rows, depth), B16)] * count
    spaces = [hbm] * len(shapes)
    for h in helpers:
        operands += h.inputs
        shapes += [jax.ShapeDtypeStruct(shape, dtype) for shape, dtype, _ in h.outs]
        spaces += [pl.BlockSpec(memory_space=space) for _, _, space in h.outs]
        staging += h.scratch
    results = pl.pallas_call(
        functools.partial(exchange_kernel, plan),
        out_shape=shapes,
        in_specs=[hbm] * len(operands),
        out_specs=spaces,
        scratch_shapes=staging,
        compiler_params=pltpu.CompilerParams(
            collective_id=number, has_side_effects=True, vmem_limit_bytes=VMEM_LIMIT
        ),
        cost_estimate=pl.CostEstimate(
            flops=20_000_000_000, bytes_accessed=50_000_000, transcendentals=0
        ),
        name=name,
    )(*operands)
    results = list(results)
    got = {n: results.pop(0) for n in list(outs) + list(gathers)}
    for h in helpers:
        h.results = [results.pop(0) for _ in h.outs]
    return Bag(**got)


def rms(rows, gain):
    scale = lax.rsqrt(jnp.mean(rows * rows, axis=-1, keepdims=True) + EPS)
    return rows * scale * gain


def rms_back(rows, gain, grad):
    scale = lax.rsqrt(jnp.mean(rows * rows, axis=-1, keepdims=True) + EPS)
    scaled = gain * grad
    mean = jnp.mean(scaled * rows, axis=-1, keepdims=True)
    return scale * scaled - rows * (scale * scale * scale * mean)


def gain_of(r, layer, row):
    ways = r.few.shape[1]
    return jnp.concatenate([r.few[layer, k, row : row + 1, :] for k in range(ways)], axis=1)


def layer_input(r, layer, at):
    if layer == 0:
        return r.acts_in[lax.axis_index(PIPE), at, :].astype(F32)
    return r.x[at, :].astype(F32)


def layer_cotangent(r, layer, at):
    if layer == 1:
        return r.out_grad[lax.axis_index(PIPE), at, :]
    return r.cotangent[at, :]


def work_first(r, c, at, total):
    return rms(layer_input(r, 0, at), gain_of(r, 0, 0)).astype(B16), layer_cotangent(r, 1, at)


def work_mid(layer, r, c, at, total):
    residual = layer_input(r, layer, at) + total
    r.residual[at, :] = residual
    return (rms(residual, gain_of(r, layer, 1)).astype(B16),)


def work_turn(r, c, at, total):
    out = (r.residual[at, :] + total).astype(B16)
    r.x[at, :] = out
    return (rms(out.astype(F32), gain_of(r, 1, 0)).astype(B16),)


def work_back_ffn(layer, r, c, at, total):
    depth = r.residual.shape[1]
    residual = r.residual[at, :]
    if layer == 1:
        r.last[at, :] = (residual + total[:, depth:]).astype(B16)
    grad = layer_cotangent(r, layer, at).astype(F32) + rms_back(
        residual, gain_of(r, layer, 1), total[:, :depth]
    )
    r.d_residual[at, :] = grad
    return (grad.astype(B16),)


def work_back_mix(layer, r, c, at, total):
    step = rms_back(layer_input(r, layer, at), gain_of(r, layer, 0), total)
    grad = (r.d_residual[at, :] + step).astype(B16)
    r.x_grad[at, :] = grad
    return (grad,)


def work_shared(r, scatters):
    total = scatters[SHARED].receive(0)
    _, ways, block, _ = r.shared.shape
    for j in range(2 * ways):
        r.shared[j // ways, j % ways] = total[j * block : (j + 1) * block, :]


def widen(block, axis, size):
    missing = size - block.shape[axis]
    if missing == 0:
        return block
    pads = [(0, 0)] * block.ndim
    pads[axis] = (0, missing)
    return jnp.pad(block, pads)


def on_device(
    acts_in, out_grad, mix_gain, w_mixer_in, w_query, w_shared, w_step, a_log, dt_bias, d_skip,
    w_mamba_out, w_attn_out, ffn_gain, w_gate_up, w_down,
):
    section = lax.axis_index(PIPE)
    member = lax.axis_index(TENSOR)
    members = lax.axis_size(TENSOR)
    dp = lax.axis_size(DP)
    heads = a_log.shape[1]
    real = heads * HD
    width = (heads + heads % 2) * HD
    q_real = w_query.shape[2]
    cols = Cols(width)
    units = w_gate_up.shape[3]
    rows, depth = acts_in.shape[1:]
    length = rows * members
    piece = depth // dp
    wide = cols.total - cols.b

    at_row = MixerRows(cols, members)
    q_heads = q_real // HD
    inner = jnp.concatenate(
        [widen(w_mixer_in[0, :, 0], 1, width), widen(w_mixer_in[0, :, 1], 1, width)], axis=1
    )
    share = lax.dynamic_slice_in_dim(w_shared[0], member * (piece // members), piece // members, 0)
    share = jnp.concatenate([share[:, at : at + LANES] for at in range(0, 4 * LANES, LANES)], axis=0)
    mixer_shard = jnp.concatenate(
        [fold_lanes(share)(piece), fold_lanes(widen(w_query[0], 1, LANES))(piece)]
        + [inner[:, at : at + piece] for at in range(0, 2 * width, piece)]
        + [widen(w_mamba_out[0], 0, width), widen(w_attn_out[0], 0, LANES)],
        axis=0,
    )
    steps = lax.dynamic_slice_in_dim(w_step[0], member * heads, heads, 1).T.astype(F32)
    ffn_shard = jnp.concatenate(
        [w_gate_up[0, :, j, at : at + piece] for j in range(2) for at in range(0, units, piece)]
        + [w_down[0]],
        axis=0,
    )
    few_shard = jnp.concatenate(
        [mix_gain.astype(F32), ffn_gain.astype(F32)]
        + [widen(row, 1, piece) for row in (a_log, dt_bias, d_skip)]
        + [jnp.zeros((3, piece), F32), widen(steps, 0, 8)],
        axis=0,
    )

    def run(name, number, work, inputs, outs, **more):
        return exchange(name, number, members, dp, rows, depth, work, inputs, outs, **more)

    half = piece // 2
    low_units = width + LANES
    block32, block16 = ((rows, depth), F32), ((rows, depth), B16)
    core_keeps = dict(
        proj=((length, cols.step), B16),
        step=((length, LANES), F32),
        y=((length, width), B16),
        lows=((length, low_units), B16),
        states=((length // STEP, NS, width), B16),
        lse=((length // TILE, 8, 2 * TILE), F32),
    )
    ffn_keeps = dict(gu=((length, 2 * units), B16), hidden=((length, units), B16))
    gu_spec, down_spec = ((2, dp, half, 2 * units), B16), ((2, dp, units // 2, piece), B16)
    cat_spec, out_spec = ((2, dp, half, cols.b), B16), ((2, dp, low_units // 2, piece), B16)
    shared_spec = ((2, dp, half // members, wide), F32)
    gain_row = ((8, depth), F32)
    fills_ffn = [
        lambda r: grad_columns(r.rows_ffn, r.dgu, r.g_gu),
        lambda r: grad_rows(r.hidden, r.rows_out, r.g_down),
    ]
    fill_cat = lambda r: mixer_columns(cols, members, r)
    fill_out = lambda r: grad_rows(r.lows, r.rows_back, r.g_out)

    load = Cargo(
        0, dp, mixer_shard,
        {BEGIN: 1, SENT: 2, CHUNK: 1, CHUNK + 1: 1, CHUNK + 2: 2, CHUNK + 3: 2, SPREAD: 2, GIVEN: 4},
        members, at_row.shared,
    )
    few = Few(dp, few_shard, {BEGIN: 3})
    got = run(
        "first", 0, work_first, dict(acts_in=acts_in, out_grad=out_grad), {},
        gathers=dict(rows_mix=0, rows_out=0), helpers=[few, load],
    )
    few = few.result
    first = Bag(rows_mix=got.rows_mix, mixer=load.results[0], shared_w=load.results[1], acts_in=acts_in)
    second = Bag(rows_out=got.rows_out, out_grad=out_grad)
    for layer, k in enumerate((first, second)):
        x = dict(acts_in=acts_in) if layer == 0 else dict(x=second.x)
        load = Cargo(
            layer, dp, ffn_shard,
            {
                BEGIN: 1, 0: 1, 1: 1, 2: 1, 3: 2, 4: 1, 5: 1, 6: 1, 7: 2, SENT: 1, CHUNK: 1, CHUNK + 1: 1,
                CHUNK + 2: 1, CHUNK + 3: 1, SPREAD: 2,
            },
        )
        k.add(
            run(
                f"mixer{layer}", 1 + layer, functools.partial(work_mid, layer),
                dict(x, few=few, rows_mix=k.rows_mix, mixer=k.mixer, shared_w=k.shared_w),
                dict(core_keeps, residual=block32, rest=((depth, 6 * LANES), B16)),
                need=dict({n: SENT for n in x}, rows_mix=1),
                done=dict(rest=0, proj=1, step=1, y=3, states=3, lows=7, lse=7, residual=CHUNK + 3),
                scratch=dict(state=pltpu.VMEM((NS, width), F32)),
                phases=functools.partial(core_fwd_phases, cols, members, layer, q_heads),
                scatters={PART: (depth, 4, (4, 5, 6))}, gathers=dict(rows_ffn=0), helpers=[load],
            )
        )
        k.gates = load.result
        if layer == 0:
            load = Cargo(
                1, dp, mixer_shard,
                {
                    BEGIN: 1, 1: 1, 3: 1, SENT: 2, CHUNK: 2, CHUNK + 1: 1, CHUNK + 2: 1, CHUNK + 3: 1, SPREAD: 2,
                    GIVEN: 3,
                },
                members, at_row.shared,
            )
            got = run(
                "turn", 3, work_turn,
                dict(residual=k.residual, few=few, rows_ffn=k.rows_ffn, gates=k.gates),
                dict(ffn_keeps, x=block16),
                need=dict(residual=SENT, few=SENT), done=dict(gu=3, hidden=3, x=CHUNK + 3),
                phases=lambda r, order: by_blocks(order, rows, lambda at, m: ffn_forward(r, at)),
                scatters={PART: (depth, 4, (0, 1, 2))}, gathers=dict(rows_mix=0), helpers=[load],
            )
            k.gu, k.hidden = got.gu, got.hidden
            second.rows_mix, second.x = got.rows_mix, got.x
            second.mixer, second.shared_w = load.results

    def clear_gain(r):
        r.gain_ffn[...] = jnp.zeros_like(r.gain_ffn)

    def ffn_both(r, at, m):
        ffn_forward(r, at, depth)
        ffn_backward(r, at)

    def ffn_both_phases(r, order):
        clear_gain(r)
        return by_blocks(order, rows, functools.partial(ffn_both, r))

    def ffn_back_phases(r, order):
        clear_gain(r)
        return by_blocks(order, rows, lambda at, m: ffn_backward(r, at))

    acts = Place(
        lambda r: (r.raw.x, r.last), (rows, depth), 1,
        {BEGIN: 1, CHUNK: 1, CHUNK + 1: 1, CHUNK + 2: 1, CHUNK + 3: 1},
    )
    second.add(
        run(
            "ffn1", 4, functools.partial(work_back_ffn, 1),
            dict(
                out_grad=out_grad, residual=second.residual, few=few, rows_ffn=second.rows_ffn,
                rows_out=second.rows_out, gates=second.gates, x=second.x,
            ),
            dict(gain_ffn=gain_row, g_gu=gu_spec, g_down=down_spec, d_residual=block32),
            need=dict(out_grad=SENT, residual=SENT, few=SENT, x=None),
            done=dict(gain_ffn=3, g_gu=SENT, d_residual=CHUNK + 3, g_down=SPREAD),
            scratch=dict(
                last=pltpu.VMEM(*block16),
                **{n: pltpu.VMEM(*spec) for n, spec in ffn_keeps.items()},
                dgu=pltpu.VMEM((length, 2 * units), B16),
            ),
            phases=ffn_both_phases,
            scatters={PART: (2 * depth, 4, (0, 1, 2))}, fills=fills_ffn, gathers=dict(rows_back=0), helpers=[acts],
        )
    )

    core_scratch = dict(
        dproj=pltpu.VMEM((length, cols.total), B16),
        heads=pltpu.VMEM((8, LANES), F32),
        dcore=pltpu.VMEM((length, low_units), B16),
        grad_state=pltpu.VMEM((NS, width), F32),
        skip_sum=pltpu.VMEM((STEP, width), F32),
        dk_sum=pltpu.VMEM((length, LANES), F32),
        dv_sum=pltpu.VMEM((length, LANES), F32),
        folded=pltpu.VMEM((length, wide), B16),
        gain_column=pltpu.VMEM((depth, LANES), F32),
        staged=pltpu.VMEM((depth, wide), F32),
    )

    def core_inputs(k):
        return dict(
            few=few, rows_mix=k.rows_mix, mixer=k.mixer, rows_back=k.rows_back, d_residual=k.d_residual,
            gain_ffn=k.gain_ffn, proj=k.proj, step=k.step, y=k.y, lows=k.lows, states=k.states,
            lse=k.lse, rest=k.rest,
        )

    core_need = dict(
        lows=1, proj=2, lse=2, few=3, step=3, y=3, states=3, rows_mix=4, rest=4, gain_ffn=5, g_gu=2, g_down=1,
        d_residual=SENT, x=SENT, acts_in=SENT,
    )

    def core_phases(layer, r, order):
        return core_bwd_phases(cols, layer, members, (q_heads, heads), r, order)

    def from_input(pick):
        return lambda r: (pick(r.raw), pick(r))

    def from_kernel(pick):
        return lambda r: (pick(r), pick(r))

    take_gu, take_down = (lambda r: r.g_gu), (lambda r: r.g_down)
    take_cat, take_out, take_shared = (lambda r: r.g_cat), (lambda r: r.g_out), (lambda r: r.shared)

    def back_phases(layer, r, order):
        into, attend, scan, shared, *back = core_phases(layer, r, order)
        return [into, lambda: fill_out(r), attend, scan, lambda: fill_cat(r), shared] + back

    back_scatters = {PART: (depth, 4, (6, 7, 8)), SHARED: (wide, 1, (5, 6, 5))}
    hauls = [
        Haul(
            1, dp, [from_input(take_gu), from_input(take_down)], [gu_spec, down_spec],
            {BEGIN: 1, 2: 1, 3: 1, 4: 1, SENT: 1, CHUNK + 3: 1},
        ),
        Straight(1, dp, from_kernel(take_out), out_spec, {1: 1, SENT: 1}),
        Haul(
            1, dp, [from_kernel(take_cat)], [cat_spec], {4: 1, CHUNK: 1, CHUNK + 1: 1, CHUNK + 2: 1, CHUNK + 3: 1}, line=False
        ),
    ]
    inner = dict(g_cat=pltpu.VMEM(*cat_spec), g_out=pltpu.VMEM(*out_spec))
    got = run(
        "back1", 5, functools.partial(work_back_mix, 1),
        dict(core_inputs(second), x=second.x, g_gu=second.g_gu, g_down=second.g_down),
        dict(x_grad=block16, shared=shared_spec),
        need=core_need,
        done=dict(x_grad=CHUNK + 3, shared=EXTRA),
        scratch=dict(core_scratch, **inner), phases=functools.partial(back_phases, 1),
        scatters=back_scatters, extra_work=work_shared, gathers=dict(rows_out=0), helpers=hauls,
    )
    second.add(got)
    cat_sums = hauls[2].result
    second.sums = hauls[0].results + hauls[1].results

    hauls = [
        Haul(
            1, dp, [from_input(lambda r: r.cat_sums)], [cat_spec], {BEGIN: 1, CHUNK + 3: 1}, swap=False
        ),
        Haul(
            1, dp, [from_input(take_shared)], [shared_spec], {BEGIN: 1, 3: 1, SENT: 2, CHUNK + 1: 1, GIVEN: 1}
        ),
        Haul(
            0, dp, [from_kernel(take_gu)], [gu_spec], {SENT: 1, CHUNK + 3: 1, SPREAD: 1, GIVEN: 1},
            line=False,
        ),
    ]
    got = run(
        "ffn0", 6, functools.partial(work_back_ffn, 0),
        dict(
            cotangent=second.x_grad, residual=first.residual, few=few, rows_ffn=first.rows_ffn,
            rows_out=second.rows_out, gates=first.gates, gu=first.gu, hidden=first.hidden,
            cat_sums=cat_sums, shared=second.shared,
        ),
        dict(gain_ffn=gain_row, g_down=down_spec, d_residual=block32),
        need=dict(
            cotangent=SENT, residual=SENT, few=SENT, hidden=SENT, cat_sums=SENT, shared=3
        ),
        done=dict(gain_ffn=3, d_residual=CHUNK + 3, g_down=SPREAD),
        scratch=dict(dgu=pltpu.VMEM((length, 2 * units), B16), g_gu=pltpu.VMEM(*gu_spec)),
        phases=ffn_back_phases, fills=fills_ffn, scatters={PART: (depth, 4, (0, 1, 2))}, gathers=dict(rows_back=0),
        helpers=hauls,
    )
    gu_sums = hauls[2].result
    second.sums += hauls[0].results + hauls[1].results
    first.add(got)

    hauls = [
        Haul(0, dp, [from_input(lambda r: r.gu_sums)], [gu_spec], {BEGIN: 1, 4: 1}, swap=False),
        Haul(
            0, dp, [from_input(take_down)], [down_spec], {BEGIN: 1, 1: 1, 2: 2, 3: 1, SENT: 1}
        ),
        Haul(0, dp, [from_kernel(take_out)], [out_spec], {1: 1, 3: 2, 4: 2, CHUNK + 2: 1}),
        Haul(
            0, dp, [from_kernel(take_cat)], [cat_spec],
            {4: 1, 6: 1, SENT: 1, CHUNK: 1, CHUNK + 1: 1},
        ),
        Straight(0, dp, from_kernel(take_shared), shared_spec, {EXTRA: 1}),
    ]
    x_grads = Place(
        lambda r: (r.x_grad, r.raw.x_grad1), (rows, depth), 0,
        {4: 1, CHUNK: 1, CHUNK + 1: 1, CHUNK + 2: 1, CHUNK + 3: 1},
    )
    run(
        "back0", 7, functools.partial(work_back_mix, 0),
        dict(core_inputs(first), acts_in=acts_in, x_grad1=second.x_grad, gu_sums=gu_sums, g_down=first.g_down),
        {},
        need=dict(core_need, x_grad1=None, gu_sums=3),
        scratch=dict(
            core_scratch, **inner, x_grad=pltpu.VMEM(*block16), shared=pltpu.VMEM(*shared_spec)
        ),
        phases=functools.partial(back_phases, 0), scatters=back_scatters, extra_work=work_shared, helpers=hauls + [x_grads],
    )
    first.sums = [h.result for h in hauls]
    order = [0, 1, 3, 2, 4]
    g_gates, g_down, g_cat, g_out, g_shared = [
        jnp.where(section == 0, first.sums[i], second.sums[j]).astype(F32).reshape(
            (-1,) + first.sums[i].shape[2:]
        )
        for i, j in zip(order, (0, 1, 3, 2, 4))
    ]
    g_mixer = jnp.stack([g_cat[:, :real], g_cat[:, width : width + real]], axis=1)
    table = 2 * NS + 2 * KVH * HD
    g_gains = g_shared[:, table + GAINS_AT : table + GAINS_AT + 2].T
    g_heads = g_shared[:3, table + HEADS_AT : table + HEADS_AT + heads]
    return (
        acts.result[None],
        x_grads.result[None],
        g_gains[None],
        g_mixer[None],
        g_cat[None, :, cols.q : cols.q + q_real],
        g_shared[None, :, :table],
        g_shared[None, :, table : table + HM],
        g_heads[None],
        g_out[None, :real],
        g_out[None, width : width + q_real],
        g_gates.reshape(1, piece, 2, units),
        g_down[None],
    )


def solution(mesh):
    rows = P(DP, TENSOR, None)
    by_dp, by_tensor, by_both = P(PIPE, DP), P(PIPE, TENSOR), P(PIPE, DP, TENSOR)
    wide, tall, whole = P(PIPE, DP, None, TENSOR), P(PIPE, TENSOR, DP), P(PIPE, DP, None)
    joint = P(PIPE, (DP, TENSOR), None)
    return jax.shard_map(
        on_device,
        mesh=mesh,
        in_specs=(
            rows, rows, by_dp, wide, by_both, whole, whole, by_tensor, by_tensor, by_tensor, tall, tall,
            by_dp, wide, tall,
        ),
        out_specs=(
            P(PIPE, DP, TENSOR, None), P(PIPE, DP, TENSOR, None), P(PIPE, None, (DP, TENSOR)),
            wide, by_both, joint, joint, P(PIPE, None, TENSOR), tall, tall, wide, tall,
        ),
        check_vma=False,
    )
```

```python
import functools

import jax
import jax.numpy as jnp
from jax import lax
from jax.experimental import pallas as pl
from jax.experimental.pallas import tpu as pltpu
from jax.sharding import PartitionSpec as P

HM = 24
HA = 8
KVH = 2
NS = 128
HD = 64
LANES = 128
STEP = 128
TILE = 256
EPS = 1e-05
F32 = jnp.float32
B16 = jnp.bfloat16
VMEM_LIMIT = 60 << 20
HEADS_AT = 32
GAINS_AT = 64


def nn(a, b):
    return lax.dot_general(a, b, (((1,), (0,)), ((), ())), preferred_element_type=F32)


def nt(a, b):
    return lax.dot_general(a, b, (((1,), (1,)), ((), ())), preferred_element_type=F32)


def tn(a, b):
    return lax.dot_general(a, b, (((0,), (0,)), ((), ())), preferred_element_type=F32)


def exact(a, b):
    return lax.dot_general(
        a, b, (((1,), (0,)), ((), ())), precision=lax.Precision.HIGHEST, preferred_element_type=F32
    )


def softplus(v):
    small = jnp.exp(-jnp.abs(v))
    series = small * (1.0 - small * (0.5 - small * (1.0 / 3.0 - small * 0.25)))
    return jnp.maximum(v, 0.0) + jnp.where(small < 0.02, series, jnp.log(1.0 + small))


def sigmoid(v):
    return 1.0 / (1.0 + jnp.exp(-v))


def iotas(rows, columns):
    return (
        lax.broadcasted_iota(jnp.int32, (rows, columns), 0),
        lax.broadcasted_iota(jnp.int32, (rows, columns), 1),
    )


def spread(column_block, head, rows):
    return jnp.broadcast_to(column_block[:, head : head + 1], (rows, LANES))


class Cols:
    def __init__(self, width):
        self.width = width
        self.z = 0
        self.u = width
        self.q = 2 * width
        self.b = self.q + LANES
        self.c = self.b + LANES
        self.k = self.c + LANES
        self.v = self.k + LANES
        self.step = self.v + LANES
        self.total = self.step + LANES
        self.pairs = width // LANES


class MixerRows:
    def __init__(self, cols, members):
        self.shared = 4 * LANES // members
        self.query = self.shared
        self.inner = self.query + LANES
        self.low = self.inner + 2 * cols.width
        self.total = self.low + cols.width + LANES


def fold_lanes(block):
    def folded(piece):
        count = piece // LANES
        size = block.shape[0] // count
        return jnp.concatenate([block[i * size : (i + 1) * size] for i in range(count)], axis=1)

    return folded


def unfold_lanes(block):
    return jnp.concatenate(
        [block[:, at : at + LANES] for at in range(0, block.shape[1], LANES)], axis=0
    )


def join_shared(cols, members, layer, q_heads, r):
    mixer, shared, few, rest = r.mixer, r.shared_w, r.few, r.rest
    ways, _, piece = mixer.shape
    at = MixerRows(cols, members)
    group = lax.axis_index(TENSOR) * q_heads // (HA // KVH)
    source, target = iotas(LANES, LANES)
    choose = (source == group * HD + (target & (HD - 1))).astype(B16)
    size = piece // members
    for d in range(ways):
        rows = slice(d * piece, (d + 1) * piece)
        rest[rows, :LANES] = unfold_lanes(mixer[d, at.query : at.query + LANES, :])
        for m in range(members):
            block = unfold_lanes(shared[m, d])
            to = slice(d * piece + m * size, d * piece + (m + 1) * size)
            for j in range(4):
                lanes = block[j * size : (j + 1) * size, :]
                if j >= 2:
                    lanes = nn(lanes, choose).astype(B16)
                rest[to, LANES * (j + 1) : LANES * (j + 2)] = lanes
        steps = few[layer, d, 8:16, :]
        steps = jnp.concatenate([steps, jnp.zeros((LANES - 8, piece), F32)], axis=0).T
        rest[rows, 5 * LANES :] = steps.astype(B16)


def split_heads(block, low_lanes):
    zero = jnp.zeros_like(block)
    return jnp.concatenate(
        [jnp.where(low_lanes, block, zero), jnp.where(low_lanes, zero, block)], axis=0
    )


def blocks_nn(rows_ref, rows, weights_ref, c, first=0):
    ways, _, piece = weights_ref.shape
    at = slice(first + c * piece, first + (c + 1) * piece)
    total = nn(rows_ref[rows, 0:piece], weights_ref[0, at, :])
    for d in range(1, ways):
        total += nn(rows_ref[rows, d * piece : (d + 1) * piece], weights_ref[d, at, :])
    return total


def multiply_out(lows_ref, weights_ref, first, part_ref, rows, at=0):
    ways, _, piece = weights_ref.shape
    last = first + lows_ref.shape[1]
    block = lows_ref[rows, :]
    for k in range(ways):
        part_ref[rows, at + k * piece : at + (k + 1) * piece] = nn(
            block, weights_ref[k, first:last, :]
        ).astype(B16)


def multiply_back(grad_ref, weights_ref, first, count, part_ref, rows, rows_ref, gain_sum, rest=None):
    ways, _, piece = weights_ref.shape
    for d in range(ways):
        to = slice(d * piece, (d + 1) * piece)
        total = nt(grad_ref[rows, 0:piece], weights_ref[d, first : first + piece, :])
        for c in range(1, count):
            at = slice(first + c * piece, first + (c + 1) * piece)
            total += nt(grad_ref[rows, c * piece : (c + 1) * piece], weights_ref[d, at, :])
        if rest is not None:
            total += nt(grad_ref[rows, count * piece :], rest[to, :])
        part_ref[rows, to] = total.astype(B16)
        if gain_sum is not None:
            gain_sum[0:1, to] += jnp.sum(total * rows_ref[rows, to].astype(F32), axis=0, keepdims=True)


def by_blocks(order, rows, step):
    def phase(group):
        def run():
            for member in group:
                step(pl.ds(pl.multiple_of(member * rows, rows), rows), member)

        return run

    return [phase(group) for group in order]


def skip_lanes(few_ref, layer, width):
    row, lane = iotas(width, LANES)
    own = ((row >> 6) == lane).astype(F32)
    skip = jnp.broadcast_to(few_ref[layer, 0, 4:5, :LANES], (8, LANES))
    return lax.dot_general(
        skip, own, (((1,), (1,)), ((), ())),
        precision=lax.Precision.HIGHEST, preferred_element_type=F32,
    )[0:1, :]


def core_fwd_phases(cols, members, layer, q_heads, r, order):
    rows_ref, weights_ref, few_ref = r.rows_mix, r.mixer, r.few
    proj_ref, step_ref, y_ref, lows_ref = r.proj, r.step, r.y, r.lows
    states_ref, lse_ref, part_ref, state = r.states, r.lse, r.part, r.state
    length = rows_ref.shape[0]
    width = cols.width
    piece = weights_ref.shape[2]

    at_row = MixerRows(cols, members)

    def join_all():
        join_shared(cols, members, layer, q_heads, r)

    def project_all():
        def project(i, _):
            rows = pl.ds(pl.multiple_of(i * TILE, TILE), TILE)
            for c in range(cols.q // piece):
                value = blocks_nn(rows_ref, rows, weights_ref, c, at_row.inner)
                proj_ref[rows, c * piece : (c + 1) * piece] = value.astype(B16)
            rest = nn(rows_ref[rows, :], r.rest[...])
            proj_ref[rows, cols.q : cols.b] = (rest[:, :LANES] * HD**-0.5).astype(B16)
            proj_ref[rows, cols.b : cols.step] = rest[:, LANES : 5 * LANES].astype(B16)
            step_ref[rows, :] = rest[:, 5 * LANES :]
            return 0

        lax.fori_loop(0, length // TILE, project, 0)

    def scan_part(low, high):
        ri, ci = iotas(STEP, STEP)
        lower = ri >= ci
        tril = lower.astype(F32)
        low_lanes = ci < HD
        decay = jnp.exp(few_ref[layer, 0, 2:3, :LANES])
        bias = few_ref[layer, 0, 3:4, :LANES]
        skips = skip_lanes(few_ref, layer, width)
        if low == 0:
            state[...] = jnp.zeros_like(state)

        def scan_block(b, _):
            rows = pl.ds(pl.multiple_of(b * STEP, STEP), STEP)
            dt = softplus(step_ref[rows, :] + bias)
            run = exact(tril, -dt * decay)
            run_t = run.T
            bm = proj_ref[rows, cols.b : cols.b + LANES]
            cm = proj_ref[rows, cols.c : cols.c + LANES]
            cb = jnp.where(lower, nt(cm, bm), 0.0)
            states_in = state[...]
            low_state = states_in.astype(B16)
            states_ref[b] = low_state
            carried = nn(cm, low_state)
            tails, fades = [], []
            for p in range(cols.pairs):
                lanes = slice(LANES * p, LANES * (p + 1))
                u = proj_ref[rows, cols.u + LANES * p : cols.u + LANES * (p + 1)].astype(F32)
                z = proj_ref[rows, cols.z + LANES * p : cols.z + LANES * (p + 1)].astype(F32)
                run_b = [spread(run, 2 * p + k, STEP) for k in range(2)]
                run_w = jnp.where(low_lanes, run_b[0], run_b[1])
                ud = u * jnp.where(low_lanes, spread(dt, 2 * p, STEP), spread(dt, 2 * p + 1, STEP))
                mix = jnp.concatenate(
                    [
                        (
                            jnp.exp(jnp.minimum(run_b[k] - run_t[2 * p + k : 2 * p + k + 1, :], 0.0))
                            * cb
                        ).astype(B16)
                        for k in range(2)
                    ],
                    axis=1,
                )
                inside = nn(mix, split_heads(ud, low_lanes).astype(B16))
                y = inside + carried[:, lanes] * jnp.exp(run_w) + skips[:, lanes] * u
                y_ref[rows, lanes] = y.astype(B16)
                lows_ref[rows, lanes] = (y * z * sigmoid(z)).astype(B16)
                end = run_w[STEP - 1 : STEP, :]
                tails.append((ud * jnp.exp(end - run_w)).astype(B16))
                fades.append(jnp.exp(end))
            fresh = tn(bm, jnp.concatenate(tails, axis=1))
            state[...] = states_in * jnp.concatenate(fades, axis=1) + fresh
            return 0

        lax.fori_loop(low, high, scan_block, 0)

    def attend(i):
        rk, ck = iotas(TILE, 2 * TILE)
        diagonal = rk <= jnp.where(ck < TILE, ck, ck - TILE)
        q_low = iotas(TILE, LANES)[1] < HD

        rows = pl.ds(pl.multiple_of(i * TILE, TILE), TILE)
        q2 = split_heads(proj_ref[rows, cols.q : cols.q + LANES], q_low)

        def piece(j, carry, masked):
            top, total, out = carry
            keys = pl.ds(pl.multiple_of(j * TILE, TILE), TILE)
            s = nt(proj_ref[keys, cols.k : cols.k + LANES], q2)
            if masked:
                s = jnp.where(diagonal, s, -1e30)
            new_top = jnp.maximum(top, jnp.max(s, axis=0, keepdims=True))
            p = jnp.exp(s - new_top)
            scale = jnp.exp(top - new_top)
            total = total * scale + jnp.sum(p, axis=0, keepdims=True)
            out = out * scale + tn(proj_ref[keys, cols.v : cols.v + LANES], p.astype(B16))
            return new_top, total, out

        carry = (
            jnp.full((1, 2 * TILE), -1e30, F32),
            jnp.zeros((1, 2 * TILE), F32),
            jnp.zeros((LANES, 2 * TILE), F32),
        )
        carry = lax.fori_loop(0, i, lambda j, c: piece(j, c, False), carry)
        top, total, out = piece(i, carry, True)
        out = out / total
        joined = jnp.concatenate([out[:HD, :TILE], out[HD:, TILE:]], axis=0)
        lows_ref[rows, width : width + LANES] = joined.T.astype(B16)
        lse_ref[i] = jnp.broadcast_to(top + jnp.log(total), (8, 2 * TILE))

    rows = length // members
    blocks, tiles = length // STEP, length // TILE
    together = rows == TILE

    def attend_all():
        for i in range(tiles):
            attend(i)

    def finish(at, member):
        if together:
            attend(member)
        multiply_out(lows_ref, weights_ref, at_row.low, part_ref, at)

    phases = [
        join_all,
        project_all,
        lambda: scan_part(0, blocks // 2),
        lambda: scan_part(blocks // 2, blocks),
    ]
    if not together:
        phases[3] = lambda: (scan_part(blocks // 2, blocks), attend_all())
    return phases + by_blocks(order, rows, finish)


def core_bwd_phases(cols, layer, members, q_heads, r, order):
    back_ref, weights_ref, few_ref, rows_ref = r.rows_back, r.mixer, r.few, r.rows_mix
    proj_ref, step_ref, y_ref, lows_ref = r.proj, r.step, r.y, r.lows
    states_ref, lse_ref, part_ref = r.states, r.lse, r.part
    dproj_ref, heads_ref, dcore, grad_state, skip_sum = r.dproj, r.heads, r.dcore, r.grad_state, r.skip_sum
    dk_sum, dv_sum, folded, staged = r.dk_sum, r.dv_sum, r.folded, r.staged
    length = back_ref.shape[0]
    width = cols.width
    ways, _, piece = weights_ref.shape
    blocks = length // STEP
    depth = ways * piece
    at_row = MixerRows(cols, members)
    low_rows = slice(at_row.low, at_row.low + width + LANES)

    def into_all():
        def into_core(i, _):
            rows = pl.ds(pl.multiple_of(i * TILE, TILE), TILE)
            total = nt(back_ref[rows, 0:piece], weights_ref[0, low_rows, :])
            for k in range(1, ways):
                total += nt(
                    back_ref[rows, k * piece : (k + 1) * piece], weights_ref[k, low_rows, :]
                )
            dcore[rows, :] = total.astype(B16)
            return 0

        lax.fori_loop(0, length // TILE, into_core, 0)

    def attend_all():
        rk, ck = iotas(TILE, 2 * TILE)
        diagonal = rk <= jnp.where(ck < TILE, ck, ck - TILE)
        q_low = iotas(TILE, LANES)[1] < HD
        dk_sum[...] = jnp.zeros_like(dk_sum)
        dv_sum[...] = jnp.zeros_like(dv_sum)
        half = iotas(8, LANES)
        pick_low = (half[1] < HD).astype(F32)
        pick_high = (half[1] >= HD).astype(F32)

        def attend(i, _):
            rows = pl.ds(pl.multiple_of(i * TILE, TILE), TILE)
            q2 = split_heads(proj_ref[rows, cols.q : cols.q + LANES], q_low)
            d_out = dcore[rows, width : width + LANES]
            do2 = split_heads(d_out, q_low)
            both = d_out.astype(F32) * lows_ref[rows, width : width + LANES].astype(F32)
            high = lax.Precision.HIGHEST
            deltas = [
                lax.dot_general(
                    pick, both, (((1,), (1,)), ((), ())), precision=high, preferred_element_type=F32
                )[0:1, :]
                for pick in (pick_low, pick_high)
            ]
            delta = jnp.concatenate(deltas, axis=1)
            lse = lse_ref[i][0:1, :]

            def piece_of(j, dq, masked):
                keys = pl.ds(pl.multiple_of(j * TILE, TILE), TILE)
                kk = proj_ref[keys, cols.k : cols.k + LANES]
                p = jnp.exp(nt(kk, q2) - lse)
                if masked:
                    p = jnp.where(diagonal, p, 0.0)
                ds = (p * (nt(proj_ref[keys, cols.v : cols.v + LANES], do2) - delta)).astype(B16)
                dv_sum[keys, :] += nn(p.astype(B16), do2)
                dk_sum[keys, :] += nn(ds, q2)
                return dq + tn(kk, ds)

            dq = jnp.zeros((LANES, 2 * TILE), F32)
            dq = lax.fori_loop(0, i, lambda j, c: piece_of(j, c, False), dq)
            dq = piece_of(i, dq, True)
            joined = jnp.concatenate([dq[:HD, :TILE], dq[HD:, TILE:]], axis=0) * HD**-0.5
            dproj_ref[rows, cols.q : cols.q + LANES] = joined.T.astype(B16)
            return 0

        lax.fori_loop(0, length // TILE, attend, 0)
        dproj_ref[:, cols.k : cols.k + LANES] = dk_sum[...].astype(B16)
        dproj_ref[:, cols.v : cols.v + LANES] = dv_sum[...].astype(B16)

    def scan_all():
        ri, ci = iotas(STEP, STEP)
        upper = ri <= ci
        tril = (ri >= ci).astype(F32)
        triu = upper.astype(F32)
        low_lanes = ci < HD
        decay = jnp.exp(few_ref[layer, 0, 2:3, :LANES])
        bias = few_ref[layer, 0, 3:4, :LANES]
        skips = skip_lanes(few_ref, layer, width)
        row, lane = iotas(width, LANES)
        group = ((row >> 6) == lane).astype(B16)
        grad_state[...] = jnp.zeros_like(grad_state)
        skip_sum[...] = jnp.zeros_like(skip_sum)
        heads_ref[...] = jnp.zeros_like(heads_ref)
        zero_rows = jnp.zeros((STEP - 2 * cols.pairs, LANES), F32)

        def scan_block(back, _):
            b = blocks - 1 - back
            rows = pl.ds(pl.multiple_of(b * STEP, STEP), STEP)
            raw = step_ref[rows, :] + bias
            dt = softplus(raw)
            a = -dt * decay
            run = exact(tril, a)
            run_t = run.T
            bm = proj_ref[rows, cols.b : cols.b + LANES]
            cm = proj_ref[rows, cols.c : cols.c + LANES]
            cbt = jnp.where(upper, nt(bm, cm), 0.0)
            low_state = states_ref[b]
            grads_out = grad_state[...]
            low_grad = grads_out.astype(B16)
            carried = nn(cm, low_state)
            pulled = nn(bm, low_grad)
            dcb = jnp.zeros((STEP, STEP), F32)
            dy_fades, u_tails, fades = [], [], []
            carry_terms, direct_terms, tail_terms = [], [], []
            row_sums = []
            col_sums = jnp.zeros((STEP, LANES), F32)
            for p in range(cols.pairs):
                lanes = slice(LANES * p, LANES * (p + 1))
                u16 = proj_ref[rows, cols.u + LANES * p : cols.u + LANES * (p + 1)]
                u = u16.astype(F32)
                z = proj_ref[rows, cols.z + LANES * p : cols.z + LANES * (p + 1)].astype(F32)
                y = y_ref[rows, lanes].astype(F32)
                dm = dcore[rows, lanes].astype(F32)
                sg = sigmoid(z)
                dy = dm * z * sg
                dproj_ref[rows, cols.z + LANES * p : cols.z + LANES * (p + 1)] = (
                    dm * y * sg * (1.0 + z * (1.0 - sg))
                ).astype(B16)
                dy16 = dy.astype(B16)
                skip_sum[:, lanes] += u * dy
                run_b = [spread(run, 2 * p + k, STEP) for k in range(2)]
                dt_b = [spread(dt, 2 * p + k, STEP) for k in range(2)]
                run_w = jnp.where(low_lanes, run_b[0], run_b[1])
                dt_w = jnp.where(low_lanes, dt_b[0], dt_b[1])
                end = run_w[STEP - 1 : STEP, :]
                fade = jnp.exp(run_w)
                tail = jnp.exp(end - run_w)
                dmix = nt(split_heads(u16, low_lanes), dy16)
                mixes = []
                for k in range(2):
                    gap = jnp.exp(jnp.minimum(run_t[2 * p + k : 2 * p + k + 1, :] - run_b[k], 0.0))
                    mixes.append((gap * cbt).astype(B16))
                    weighted = gap * dt_b[k] * dmix[STEP * k : STEP * (k + 1), :]
                    dcb += weighted
                    moved = weighted * cbt
                    row_sums.append(jnp.sum(moved, axis=0, keepdims=True))
                    col_sums = jnp.where(
                        ci == 2 * p + k, jnp.sum(moved, axis=1, keepdims=True), col_sums
                    )
                inside = nn(jnp.concatenate(mixes, axis=1), split_heads(dy16, low_lanes))
                pull_tail = tail * pulled[:, lanes]
                g = inside + pull_tail
                dproj_ref[rows, cols.u + LANES * p : cols.u + LANES * (p + 1)] = (
                    dt_w * g + skips[:, lanes] * dy
                ).astype(B16)
                dy_fade = dy * fade
                dy_fades.append(dy_fade.astype(B16))
                u_tails.append((u * dt_w * tail).astype(B16))
                fades.append(jnp.exp(end))
                carry_terms.append((dy_fade * carried[:, lanes]).astype(B16))
                direct_terms.append((u * g).astype(B16))
                tail_terms.append((u * pull_tail).astype(B16))
            dy_fade = jnp.concatenate(dy_fades, axis=1)
            dcb = jnp.where(upper, dcb, 0.0).astype(B16)
            dproj_ref[rows, cols.c : cols.c + LANES] = (tn(dcb, bm) + nt(dy_fade, low_state)).astype(B16)
            dproj_ref[rows, cols.b : cols.b + LANES] = (
                nn(dcb, cm) + nt(jnp.concatenate(u_tails, axis=1), low_grad)
            ).astype(B16)
            carry_term = nn(jnp.concatenate(carry_terms, axis=1), group)
            direct_term = nn(jnp.concatenate(direct_terms, axis=1), group)
            tail_term = dt * nn(jnp.concatenate(tail_terms, axis=1), group)
            overlap = jnp.sum(low_state.astype(F32) * grads_out, axis=0, keepdims=True)
            overlap = exact(jnp.broadcast_to(overlap, (8, width)), group.astype(F32))[0:1, :]
            overlap = overlap * jnp.exp(run[STEP - 1 : STEP, :])
            row_sum = jnp.concatenate(row_sums + [zero_rows], axis=0).T
            d_run = row_sum - col_sums + carry_term - tail_term
            d_a = exact(triu, d_run) + (jnp.sum(tail_term, axis=0, keepdims=True) + overlap)
            d_step = (direct_term - decay * d_a) * sigmoid(raw)
            dproj_ref[rows, cols.step : cols.step + LANES] = d_step.astype(B16)
            heads_ref[0:1, :] += jnp.sum(d_a * a, axis=0, keepdims=True)
            heads_ref[1:2, :] += jnp.sum(d_step, axis=0, keepdims=True)
            grad_state[...] = grads_out * jnp.concatenate(fades, axis=1) + tn(cm, dy_fade)
            return 0

        lax.fori_loop(0, blocks, scan_block, 0)
        skip = jnp.sum(skip_sum[...], axis=0, keepdims=True)
        heads_ref[2:3, :] = exact(jnp.broadcast_to(skip, (8, width)), group.astype(F32))[0:1, :]

    def back(at, member):
        multiply_back(
            dproj_ref, weights_ref, at_row.inner, cols.q // piece, part_ref, at, rows_ref, None, r.rest
        )

    def shared_all():
        wide = cols.total - cols.b
        member = lax.axis_index(TENSOR)
        heads = q_heads[1]
        group = member * q_heads[0] // (HA // KVH)
        source, target = iotas(wide, wide)
        kind = source >> 7
        wanted = jnp.where(
            kind < 2,
            source,
            jnp.where(
                kind < 4,
                2 * NS + (kind - 2) * KVH * HD + group * HD + (source & (HD - 1)),
                source + member * heads,
            ),
        )
        fold = ((target == wanted) & (source < 4 * LANES + heads)).astype(B16)

        def fold_rows(i, _):
            rows = pl.ds(pl.multiple_of(i * TILE, TILE), TILE)
            folded[rows, :] = nn(dproj_ref[rows, cols.b :], fold).astype(B16)
            return 0

        lax.fori_loop(0, length // TILE, fold_rows, 0)
        sub = piece // members
        half = sub // 2
        lane = iotas(piece, LANES)[1]
        head_lane = iotas(8, LANES)[1]
        shifted = jnp.where(
            (head_lane >= HEADS_AT) & (head_lane < HEADS_AT + heads),
            pltpu.roll(heads_ref[...], HEADS_AT, 1),
            0.0,
        )
        for k in range(ways):
            at = slice(k * piece, (k + 1) * piece)
            grad = tn(rows_ref[:, at], folded[...])
            raw = nn(r.rest[at, LANES:], fold)
            twice = (iotas(piece, wide)[1] >= 2 * LANES) & (iotas(piece, wide)[1] < 4 * LANES)
            own = jnp.sum(grad * jnp.where(twice, 0.5 * raw, raw), axis=1, keepdims=True)
            gains = [jnp.broadcast_to(few_ref[layer, k, i : i + 1, :], (LANES, piece)).T for i in (0, 1)]
            from_ffn = jnp.broadcast_to(r.gain_ffn[0:1, at], (LANES, piece)).T
            columns = [(own + r.gain_column[at, 0:1]) / gains[0], from_ffn / gains[1]]
            last = grad[:, wide - LANES :]
            last = jnp.where(lane == GAINS_AT, columns[0], last)
            last = jnp.where(lane == GAINS_AT + 1, columns[1], last)
            for t in range(members):
                for h in range(2):
                    to = t * (depth // members) + (h * ways + k) * half
                    rows = slice(t * sub + h * half, t * sub + (h + 1) * half)
                    staged[to : to + half, : wide - LANES] = grad[rows, : wide - LANES]
                    staged[to : to + half, wide - LANES :] = last[rows, :]
            to = pl.multiple_of(member * (depth // members) + k * half, 8)
            staged[pl.ds(to, 8), wide - LANES :] += shifted
        r.extra[...] = staged[...].astype(B16)

    return [into_all, attend_all, scan_all, shared_all] + by_blocks(order, length // members, back)


def ffn_forward(r, rows, at=0):
    rows_ref, weights_ref, gu_ref, hidden_ref = r.rows_ffn, r.gates, r.gu, r.hidden
    units = hidden_ref.shape[1]
    piece = weights_ref.shape[2]
    count = units // piece
    for c in range(count):
        to = slice(c * piece, (c + 1) * piece)
        g = blocks_nn(rows_ref, rows, weights_ref, c)
        v = blocks_nn(rows_ref, rows, weights_ref, c + count)
        gu_ref[rows, to] = g.astype(B16)
        gu_ref[rows, units + c * piece : units + (c + 1) * piece] = v.astype(B16)
        hidden_ref[rows, to] = (g * sigmoid(g) * v).astype(B16)
    multiply_out(hidden_ref, weights_ref, 2 * units, r.part, rows, at)


def ffn_backward(r, rows):
    out_ref, weights_ref, gu_ref, dgu_ref = r.rows_out, r.gates, r.gu, r.dgu
    ways, _, piece = weights_ref.shape
    units = gu_ref.shape[1] // 2
    down_rows = slice(2 * units, 3 * units)
    dh = nt(out_ref[rows, 0:piece], weights_ref[0, down_rows, :])
    for k in range(1, ways):
        dh += nt(out_ref[rows, k * piece : (k + 1) * piece], weights_ref[k, down_rows, :])
    g = gu_ref[rows, :units].astype(F32)
    v = gu_ref[rows, units:].astype(F32)
    sg = sigmoid(g)
    dgu_ref[rows, :units] = (dh * v * sg * (1.0 + g * (1.0 - sg))).astype(B16)
    dgu_ref[rows, units:] = (dh * g * sg).astype(B16)
    multiply_back(
        dgu_ref, weights_ref, 0, 2 * units // piece, r.part, rows, r.rows_ffn, r.gain_ffn
    )


def grad_columns(rows_ref, grad_ref, out_ref, step=512, weigh=None):
    _, ways, half, width = out_ref.shape
    for k in range(ways):
        block = rows_ref[:, 2 * half * k : 2 * half * (k + 1)]
        for first in range(0, width, step):
            last = min(first + step, width)
            value = tn(block, grad_ref[:, first:last])
            if weigh:
                weigh(k, first, last, value)
            value = value.astype(B16)
            out_ref[0, k, :, first:last] = value[:half, :]
            out_ref[1, k, :, first:last] = value[half:, :]


def mixer_columns(cols, members, r):
    _, _, piece = r.mixer.shape
    inner = MixerRows(cols, members).inner
    r.gain_column[...] = jnp.zeros_like(r.gain_column)

    def weigh(k, first, last, value):
        rows = slice(k * piece, (k + 1) * piece)
        if first < cols.q:
            weight = r.mixer[k, inner + first : inner + last, :]
        else:
            weight = r.rest[rows, :LANES]
        r.gain_column[rows, 0:1] += jnp.sum(value * weight.astype(F32), axis=1, keepdims=True)

    grad_columns(r.rows_mix, r.dproj, r.g_cat, piece, weigh)


def grad_rows(lows_ref, back_ref, out_ref):
    _, ways, half, piece = out_ref.shape
    for h in range(2):
        block = lows_ref[:, h * half : (h + 1) * half]
        for k in range(ways):
            out_ref[h, k] = tn(block, back_ref[:, k * piece : (k + 1) * piece]).astype(B16)


DMA = pltpu.SemaphoreType.DMA
MESH = pl.DeviceIdType.MESH
PIPE, DP, TENSOR = "pipe", "dp", "tensor"
PART, SHARED = "part", "extra"

BEGIN, SENT, EXTRA, CHUNK, SPREAD, GIVEN, END = -1, 20, 25, 30, 40, 50, 60


class Bag:
    def __init__(self, **entries):
        self.__dict__.update(entries)

    def add(self, other):
        self.__dict__.update(other.__dict__)


def remote(source, target, send, receive, device):
    return pltpu.make_async_remote_copy(
        src_ref=source, dst_ref=target, send_sem=send, recv_sem=receive,
        device_id=device, device_id_type=MESH,
    )


class Helper:
    def __init__(self, when):
        self.when = when
        self.inputs, self.outs, self.scratch = [], [], []
        self.results = None

    @property
    def result(self):
        return self.results[0]


def cross_devices(ways):
    section, place = lax.axis_index(PIPE), lax.axis_index(DP)
    return [{PIPE: 1 - section}] + [{DP: (place + k) % ways} for k in range(1, ways)]


class Few(Helper):
    def __init__(self, ways, shard, when):
        super().__init__(when)
        self.ways = ways
        self.inputs = [shard]
        self.outs = [((2, ways) + shard.shape, F32, pltpu.VMEM)]
        self.scratch = [DMA((1,)), DMA((1,)), DMA((2, ways)), DMA((2, ways)), DMA((1,))]

    def bind(self, r, inputs, outs, scratch):
        (shard,), (few,) = inputs, outs
        r.few = few
        section, place, ways = lax.axis_index(PIPE), lax.axis_index(DP), self.ways
        pair_send, pair_recv, line_send, line_recv, local = scratch
        mine = few.at[section, place]

        def over():
            return remote(shard, mine, pair_send.at[0], pair_recv.at[0], {PIPE: 1 - section})

        def line(layer, k, there):
            block = few.at[layer, there]
            return remote(
                block, block, line_send.at[layer, k], line_recv.at[layer, k], {DP: (place + k) % ways}
            )

        def start():
            over().start()
            own = pltpu.make_async_copy(shard, mine, local.at[0])
            own.start()
            own.wait()

        def spread():
            over().wait_recv()
            for layer in range(2):
                for k in range(1, ways):
                    line(layer, k, place).start()

        def finish():
            for layer in range(2):
                for k in range(1, ways):
                    line(layer, k, (place + ways - k) % ways).wait_recv()
            over().wait_send()
            for layer in range(2):
                for k in range(1, ways):
                    line(layer, k, place).wait_send()

        return [start, spread, finish]


class Cargo(Helper):
    CHUNKS = 4

    def __init__(self, layer, ways, shard, when, members=0, shared=0):
        super().__init__(when)
        self.layer, self.ways, self.rows = layer, ways, shard.shape[0]
        self.members, self.shared = members, shared
        n = self.CHUNKS
        self.first = (self.rows * 2 // 5 + 8 * n) // (16 * n) * (16 * n)
        self.inputs = [shard]
        self.outs = [((ways,) + shard.shape, shard.dtype, pl.ANY)]
        self.scratch = [DMA((n,)), DMA((n,))] + [DMA((ways, n))] * 6 + [DMA((1,))]
        if shared:
            self.outs.append(((members, ways, shared, shard.shape[1]), shard.dtype, pl.ANY))
            self.scratch += [DMA((members,))] * 4 + [DMA((1,))]

    def bind(self, r, inputs, outs, scratch):
        (shard_ref,), out_ref = inputs, outs[0]
        early_send, early_recv, up_send, up_recv, down_send, down_recv, over_send, over_recv, local = scratch[:9]
        section, place = lax.axis_index(PIPE), lax.axis_index(DP)
        partner = {PIPE: 1 - section}
        ways, chunks = self.ways, self.CHUNKS
        sizes = {True: self.first // chunks, False: (self.rows - self.first) // chunks}

        def by_role(step):
            def both():
                pl.when(section == self.layer)(lambda: step(True))
                pl.when(section != self.layer)(lambda: step(False))

            return both

        def part(owner, c):
            return pl.ds((0 if owner else self.first) + c * sizes[owner], sizes[owner])

        def early(c):
            at = part(False, c)
            return remote(
                shard_ref.at[at, :], out_ref.at[place, at, :], early_send.at[c], early_recv.at[c], partner
            )

        def line(owner, up, hop, c):
            at = part(owner, c)
            send, receive = (up_send, up_recv) if up else (down_send, down_recv)
            shard = place - hop if up else place + hop
            source = shard_ref if owner and hop == 0 else out_ref.at[shard]
            return remote(
                source.at[at, :], out_ref.at[shard, at, :], send.at[hop, c], receive.at[hop, c],
                {DP: (place + (1 if up else ways - 1)) % ways},
            )

        def sends(up, hop):
            if up:
                return (place >= hop) & (place < ways - 1)
            return (place < ways - hop) & (place > 0)

        def over(owner, shard, c, own=False):
            at = part(owner, c)
            source = shard_ref if own else out_ref.at[shard]
            return remote(
                source.at[at, :], out_ref.at[shard, at, :], over_send.at[shard, c], over_recv.at[shard, c],
                partner,
            )

        def own_copy():
            return pltpu.make_async_copy(shard_ref, out_ref.at[place], local.at[0])

        def launch(owner, c):
            for up in (True, False):
                pl.when(sends(up, 0))(lambda up=up: line(owner, up, 0, c).start())

        def start(owner):
            if owner:
                for c in range(chunks):
                    early(c).start()
                    launch(True, c)
                for c in range(chunks):
                    over(True, place, c, True).start()
                own_copy().start()

        def spread(c, owner):
            if not owner:
                early(c).wait_recv()
                launch(False, c)

        def hop(count, c, owner):
            for up in (True, False):
                shard = place - count if up else place + count

                @pl.when(shard >= 0 if up else shard < ways)
                def _(up=up, shard=shard):
                    line(owner, up, count - 1, c).wait_recv()
                    if count < ways - 1:
                        pl.when(sends(up, count))(lambda: line(owner, up, count, c).start())
                    over(owner, shard, c).start()

        def wait_over(owner, c):
            for shard in range(ways):

                def wait(shard=shard):
                    block = out_ref.at[shard, part(not owner, c), :]
                    remote(
                        block, block, over_send.at[shard, c], over_recv.at[shard, c], partner
                    ).wait_recv()

                if owner:
                    pl.when(place != shard)(wait)
                else:
                    wait()

        first_waited = 1 if self.shared else 0

        def finish(owner):
            for c in range(chunks):
                if owner or c >= first_waited:
                    wait_over(owner, c)
            for c in range(chunks):
                if owner:
                    early(c).wait_send()
                for count in range(ways - 1):
                    for up in (True, False):
                        pl.when(sends(up, count))(
                            lambda up=up, count=count: line(owner, up, count, c).wait_send()
                        )
                for shard in range(ways):

                    def wait(shard=shard):
                        over(owner, shard, c).wait_send()

                    if owner:
                        wait()
                    else:
                        pl.when(place != shard)(wait)
            if owner and not self.shared:
                own_copy().wait()

        steps = [start]
        steps += [functools.partial(spread, c) for c in range(chunks)]
        steps += [functools.partial(hop, count, c) for count in range(1, ways) for c in range(chunks)]
        steps = [by_role(step) for step in steps]
        if not self.shared:
            return steps + [by_role(finish)]

        assert self.shared <= sizes[True]
        all_ref = outs[1]
        give_send, give_recv, far_send, far_recv, keep = scratch[9:]
        me = lax.axis_index(TENSOR)
        pairs = self.members // 2
        mine, side = me // 2, me % 2
        sibling = 2 * mine + 1 - side
        share = out_ref.at[:, pl.ds(0, self.shared), :]

        def far(count):
            return 2 * ((mine + count) % pairs) + side

        def across(count):
            return 2 * ((mine + count) % pairs) + 1 - side

        def give(count):
            block = all_ref.at[far(count)]
            return remote(
                share if count == 0 else block, block, give_send.at[count], give_recv.at[count],
                {TENSOR: sibling},
            )

        def send_far(count, slot):
            return remote(
                share, all_ref.at[me], far_send.at[count], far_recv.at[slot], {TENSOR: far(count)}
            )

        def own_share():
            return pltpu.make_async_copy(share, all_ref.at[me], keep.at[0])

        def share_out():
            pl.when(section != self.layer)(lambda: wait_over(False, 0))
            pl.when(section == self.layer)(lambda: own_copy().wait())
            for count in range(1, pairs):
                send_far(count, pairs - count).start()
            give(0).start()
            own_share().start()

        def pass_on():
            for count in range(1, pairs):
                send_far(count, count).wait_recv()
                give(count).start()

        def finish_all():
            by_role(finish)()
            for count in range(pairs):
                block = all_ref.at[sibling if count == 0 else across(count)]
                remote(
                    block, block, give_send.at[count], give_recv.at[count], {TENSOR: sibling}
                ).wait_recv()
            for count in range(pairs):
                give(count).wait_send()
                if count:
                    send_far(count, pairs - count).wait_send()
            own_share().wait()

        at = len(steps) - (chunks - 1)
        return steps[:at] + [share_out] + steps[at:] + [pass_on, finish_all]


class Haul(Helper):
    def __init__(self, layer, ways, sources, specs, when, swap=True, line=True):
        super().__init__(when)
        self.layer, self.ways, self.sources, self.swap, self.line = layer, ways, sources, swap, line
        self.count = len(specs)
        self.order = sorted(range(1, ways), key=lambda k: abs(2 * k - ways)) + [0]
        for (_, blocks, rows, columns), dtype in specs:
            block = pltpu.VMEM((blocks, rows, columns), dtype)
            if swap and not line:
                self.outs.append(((blocks, rows, columns), dtype, pltpu.VMEM))
            if line:
                self.outs.append(((2, rows, columns), dtype, pltpu.VMEM))
            if swap:
                self.scratch += [block, DMA((ways,)), DMA((ways,))]
            if swap and line:
                self.scratch.append(block)
            if line:
                self.scratch += [block, pltpu.VMEM((rows, columns), dtype), DMA((ways,)), DMA((ways,))]
                self.scratch += [DMA((1,)), DMA((1,))]

    def bind(self, r, inputs, outs, scratch):
        section, place, ways = lax.axis_index(PIPE), lax.axis_index(DP), self.ways
        partner = {PIPE: 1 - section}
        scratch = list(scratch)
        arrays = []
        for source, out in zip(self.sources, outs):
            a = Bag(out=out)
            a.sent, a.read = source(r)
            a.sums = a.read
            if self.swap:
                a.swapped, a.swap_send, a.swap_recv = [scratch.pop(0) for _ in range(3)]
                a.sums = scratch.pop(0) if self.line else out
                a.sums_sent = a.sums
            else:
                a.sums_sent = a.sent
            if self.line:
                a.arrived, a.result, a.line_send, a.line_recv, a.last_send, a.last_recv = [
                    scratch.pop(0) for _ in range(6)
                ]
            arrays.append(a)

        def to(k):
            return (place + k) % ways

        def swap(a, k):
            return remote(
                a.sent.at[1 - section, to(k)], a.swapped.at[to(k)], a.swap_send.at[k], a.swap_recv.at[k],
                partner,
            )

        def line(a, k):
            return remote(
                a.sums_sent.at[to(k)], a.arrived.at[k], a.line_send.at[k], a.line_recv.at[k], {DP: to(k)}
            )

        def last(a):
            return remote(
                a.result, a.out.at[1 - self.layer], a.last_send.at[0], a.last_recv.at[0], partner
            )

        def start():
            for k in self.order:
                for a in arrays:
                    if self.swap:
                        swap(a, k).start()
                    elif k:
                        line(a, k).start()

        def fold(k):
            def step():
                for a in arrays:
                    swap(a, k).wait_recv()
                    total = a.read[section, to(k)].astype(F32) + a.swapped[to(k)].astype(F32)
                    a.sums[to(k)] = total.astype(a.sums.dtype)
                    if k and self.line:
                        line(a, k).start()

            return step

        def reduce():
            for a in arrays:
                total = a.sums[place].astype(F32)
                for k in range(1, ways):
                    line(a, k).wait_recv()
                    total += a.arrived[k].astype(F32)
                a.result[...] = total.astype(a.out.dtype)

            @pl.when(section == self.layer)
            def _():
                for a in arrays:
                    a.out[self.layer] = a.result[...]

            @pl.when(section != self.layer)
            def _():
                for a in arrays:
                    last(a).start()

        def finish():
            if self.line:

                @pl.when(section == self.layer)
                def _():
                    for a in arrays:
                        last(a).wait_recv()

                @pl.when(section != self.layer)
                def _():
                    for a in arrays:
                        last(a).wait_send()
                        a.out[...] = jnp.zeros_like(a.out)

            for k in self.order:
                for a in arrays:
                    if self.swap:
                        swap(a, k).wait_send()
                    if k and self.line:
                        line(a, k).wait_send()

        steps = [start]
        if self.swap:
            steps += [fold(k) for k in self.order]
        if self.line:
            steps.append(reduce)
        return steps + [finish]


class Straight(Helper):
    def __init__(self, layer, ways, source, spec, when):
        super().__init__(when)
        self.layer, self.ways, self.source = layer, ways, source
        (_, blocks, rows, columns), dtype = spec
        result = (2, rows, columns)
        self.outs = [(result, dtype, pltpu.VMEM)]
        self.scratch = [pltpu.VMEM((blocks,) + result, dtype), pltpu.VMEM(result, dtype)]
        self.scratch += [pltpu.VMEM(result, dtype), DMA((2, ways)), DMA((2, ways)), DMA((1,)), DMA((1,))]

    def bind(self, r, inputs, outs, scratch):
        sent, read = self.source(r)
        (out,) = outs
        arrived, result, handed, line_send, line_recv, last_send, last_recv = scratch
        section, place, ways = lax.axis_index(PIPE), lax.axis_index(DP), self.ways
        order = sorted(range(1, ways), key=lambda k: abs(2 * k - ways))

        def line(half, k):
            to = (place + k) % ways
            return remote(
                sent.at[half, to], arrived.at[k, half], line_send.at[half, k], line_recv.at[half, k], {DP: to}
            )

        def last():
            return remote(result, handed, last_send.at[0], last_recv.at[0], {PIPE: 1 - section})

        def start():
            for k in order:
                for half in range(2):
                    line(half, k).start()

        def reduce():
            for half in range(2):
                total = read[half, place].astype(F32)
                for k in range(1, ways):
                    line(half, k).wait_recv()
                    total += arrived[k, half].astype(F32)
                result[half] = total.astype(result.dtype)

            @pl.when(section != self.layer)
            def _():
                last().start()

        def finish():
            @pl.when(section == self.layer)
            def _():
                last().wait_recv()
                out[...] = (result[...].astype(F32) + handed[...].astype(F32)).astype(out.dtype)

            @pl.when(section != self.layer)
            def _():
                last().wait_send()
                out[...] = jnp.zeros_like(out)

            for k in order:
                for half in range(2):
                    line(half, k).wait_send()

        return [start, reduce, finish]


class Place(Helper):
    PIECES = 4

    def __init__(self, source, shape, late, when):
        super().__init__(when)
        self.source, self.late, self.size = source, late, shape[0] // self.PIECES
        self.outs = [((2,) + shape, B16, pl.ANY)]
        self.scratch = [DMA((self.PIECES,)), DMA((self.PIECES,)), DMA((self.PIECES,))]

    def bind(self, r, inputs, outs, scratch):
        (out,) = outs
        send, receive, local = scratch
        section = lax.axis_index(PIPE)
        rows = self.source(r)

        def over(layer, c):
            at = pl.ds(c * self.size, self.size)
            return remote(
                rows[layer].at[at, :], out.at[1 - layer, at, :], send.at[c], receive.at[c], {PIPE: 1 - section}
            )

        def own(layer, c):
            at = pl.ds(c * self.size, self.size)
            return pltpu.make_async_copy(rows[layer].at[at, :], out.at[layer, at, :], local.at[c])

        def hand(layer, c):
            pl.when(section != layer)(lambda: over(layer, c).start())
            pl.when(section == layer)(lambda: own(layer, c).start())

        def early():
            for c in range(self.PIECES):
                hand(1 - self.late, c)

        def finish():
            for c in range(self.PIECES):
                for layer in range(2):

                    @pl.when(section == layer)
                    def _(layer=layer):
                        over(1 - layer, c).wait()
                        own(layer, c).wait()

        return [early] + [functools.partial(hand, self.late, c) for c in range(self.PIECES)] + [finish]


class Members:
    def __init__(self, count):
        self.pairs = count // 2
        self.me = lax.axis_index(TENSOR)
        self.mine, self.side = self.me // 2, self.me % 2
        self.sibling = 2 * self.mine + 1 - self.side

    def far(self, k):
        return 2 * ((self.mine + k) % self.pairs) + self.side

    def across(self, k):
        return 2 * ((self.mine + k) % self.pairs) + 1 - self.side

    def order(self):
        others = range(1, self.pairs)
        return [[self.across(k) for k in others], [self.far(k) for k in others], [self.sibling], [self.me]]


def member_copy(source, target, send, receive, member):
    return remote(source, target, send, receive, {TENSOR: member})


class Scatter:
    @staticmethod
    def scratch(members, rows, width, pieces):
        pairs = members // 2
        others = max(pairs - 1, 1)
        return [
            pltpu.VMEM((pairs, rows, width), B16),
            pltpu.VMEM((others, rows, width), B16),
            pltpu.VMEM((others, rows, width), B16),
            DMA((pairs, pieces)), DMA((pairs, pieces)), DMA((others, pieces)), DMA((others, pieces)),
        ]

    def __init__(self, part_ref, members, rows, pieces, scratch):
        self.part, self.at, self.rows, self.pieces = part_ref, members, rows, pieces
        self.size = rows // pieces
        self.pair_in, self.far_out, self.far_in = scratch[:3]
        self.pair_send, self.pair_recv, self.far_send, self.far_recv = scratch[3:]

    def rows_of(self, member, c):
        return pl.ds(pl.multiple_of(member * self.rows + c * self.size, self.size), self.size)

    def chunk(self, c):
        return pl.ds(c * self.size, self.size)

    def to_pair(self, k, c):
        member = self.at.across(k) if k else self.at.sibling
        return member_copy(
            self.part.at[self.rows_of(member, c), :], self.pair_in.at[k, self.chunk(c), :],
            self.pair_send.at[k, c], self.pair_recv.at[k, c], self.at.sibling,
        )

    def to_far(self, k, c, slot):
        return member_copy(
            self.far_out.at[k - 1, self.chunk(c), :], self.far_in.at[slot - 1, self.chunk(c), :],
            self.far_send.at[k - 1, c], self.far_recv.at[slot - 1, c], self.at.far(k),
        )

    def send_across(self):
        for c in range(self.pieces):
            for k in range(1, self.at.pairs):
                self.to_pair(k, c).start()

    def send_far(self):
        for c in range(self.pieces):
            for k in range(1, self.at.pairs):
                self.to_pair(k, c).wait_recv()
                total = self.part[self.rows_of(self.at.far(k), c), :].astype(F32)
                total += self.pair_in[k, self.chunk(c), :].astype(F32)
                self.far_out[k - 1, self.chunk(c), :] = total.astype(B16)
                self.to_far(k, c, self.at.pairs - k).start()

    def send_sibling(self):
        for c in range(self.pieces):
            self.to_pair(0, c).start()

    def receive(self, c):
        self.to_pair(0, c).wait_recv()
        total = self.part[self.rows_of(self.at.me, c), :].astype(F32)
        total += self.pair_in[0, self.chunk(c), :].astype(F32)
        for k in range(1, self.at.pairs):
            self.to_far(k, c, k).wait_recv()
            total += self.far_in[k - 1, self.chunk(c), :].astype(F32)
        return total

    def finish(self):
        for c in range(self.pieces):
            for k in range(self.at.pairs):
                self.to_pair(k, c).wait_send()
                if k:
                    self.to_far(k, c, self.at.pairs - k).wait_send()


def exchange_kernel(plan, *refs):
    refs = list(refs)

    def take(count):
        return [refs.pop(0) for _ in range(count)]

    r = Bag()
    held = {name: take(1)[0] for name in plan.inputs}
    r.raw = Bag(**held)
    helper_inputs = [take(len(h.inputs)) for h in plan.helpers]
    targets = {name: take(1)[0] for name in plan.outs}
    gathered = take(len(plan.gathers))
    helper_outs = [take(len(h.outs)) for h in plan.helpers]
    loaded = [name for name in plan.inputs if plan.need(name) is not None]
    for name in loaded + plan.outs + plan.scratch:
        setattr(r, name, take(1)[0])
    load_sem, store_sem = take(2)
    at = Members(plan.members)
    pairs, pieces = at.pairs, plan.pieces
    scatters = {}
    for name, (_, count, _) in plan.scatters.items():
        setattr(r, name, take(1)[0])
        scatters[name] = Scatter(getattr(r, name), at, plan.rows, count, take(7))
    if plan.gathers:
        mine_refs = take(len(plan.gathers))
        give_send, give_recv, spread_send, spread_recv, keep_sem = take(5)
    helpers = []
    for h, inputs, outs in zip(plan.helpers, helper_inputs, helper_outs):
        helpers.append((h.bind(r, inputs, outs, take(len(h.scratch))), h.when))
    size = plan.rows // pieces

    def rows_of(member, c):
        return pl.ds(pl.multiple_of(member * plan.rows + c * size, size), size)

    def chunk(c):
        return pl.ds(c * size, size)

    loads = {}
    for i, name in enumerate(sorted(loaded, key=plan.need)):
        loads[name] = pltpu.make_async_copy(held[name], getattr(r, name), load_sem.at[i])
        loads[name].start()

    def arrive(stage):
        for name in list(loads):
            if plan.need(name) <= stage:
                loads.pop(name).wait()

    stores = []

    def flush(stage):
        for i, name in enumerate(plan.outs):
            if plan.done(name) == stage:
                store = pltpu.make_async_copy(getattr(r, name), targets[name], store_sem.at[i])
                store.start()
                stores.append(store)

    def point(stage):
        for steps, when in helpers:
            count = len(steps) - 1 if stage == END else when.get(stage, 0)
            for _ in range(min(count, len(steps))):
                steps.pop(0)()
        if stage == END:
            for steps, _ in helpers:
                while steps:
                    steps.pop(0)()
        flush(stage)

    def run_fill(i):
        if i < len(plan.fills):
            plan.fills[i](r)

    barrier = pltpu.get_barrier_semaphore()
    greeted = [{TENSOR: at.sibling}] + [{TENSOR: at.far(k)} for k in range(1, pairs)]
    if helpers:
        greeted += cross_devices(plan.ways)
    for device in greeted:
        pl.semaphore_signal(barrier, inc=1, device_id=device, device_id_type=MESH)
    pl.semaphore_wait(barrier, len(greeted))

    arrive(BEGIN)
    point(BEGIN)
    for i, phase in enumerate(plan.phases(r, at.order()) if plan.phases else []):
        arrive(i)
        phase()
        for name, (_, _, ready) in plan.scatters.items():
            for last, send in zip(
                ready, (scatters[name].send_across, scatters[name].send_far, scatters[name].send_sibling)
            ):
                if last == i:
                    send()
        point(i)
    arrive(SENT)
    if plan.phases:
        run_fill(0)
    point(SENT)
    if plan.extra_work:
        plan.extra_work(r, scatters)
        point(EXTRA)

    given, spreads, keeps = {}, {}, []
    for c in range(pieces):
        total = None
        if plan.phases:
            for name in plan.scatters:
                total = scatters[name].receive(c)
                break
        results = plan.work(r, c, chunk(c), total)
        for g, rows_ref in enumerate(gathered):
            own = mine_refs[g].at[chunk(c), :]
            there = rows_ref.at[rows_of(at.me, c), :]
            mine_refs[g][chunk(c), :] = results[g]
            for k in range(1, pairs):
                spreads[g, k, c] = member_copy(
                    own, there, spread_send.at[g, k - 1, c], spread_recv.at[g, pairs - k - 1, c], at.far(k)
                )
                spreads[g, k, c].start()
            given[g, 0, c] = member_copy(
                own, there, give_send.at[g, 0, c], give_recv.at[g, 0, c], at.sibling
            )
            given[g, 0, c].start()
            keeps.append(pltpu.make_async_copy(own, there, keep_sem.at[g, c]))
            keeps[-1].start()
        point(CHUNK + c)
    run_fill(1)
    point(SPREAD)
    for g, rows_ref in enumerate(gathered):
        for c in range(pieces):
            for k in range(1, pairs):
                block = rows_ref.at[rows_of(at.far(k), c), :]
                member_copy(
                    block, block, spread_send.at[g, k - 1, c], spread_recv.at[g, k - 1, c], at.far(k)
                ).wait_recv()
                given[g, k, c] = member_copy(
                    block, block, give_send.at[g, k, c], give_recv.at[g, k, c], at.sibling
                )
                given[g, k, c].start()
    point(GIVEN)
    for g, rows_ref in enumerate(gathered):
        for c in range(pieces):
            for k in range(pairs):
                block = rows_ref.at[rows_of(at.across(k) if k else at.sibling, c), :]
                member_copy(
                    block, block, give_send.at[g, k, c], give_recv.at[g, k, c], at.sibling
                ).wait_recv()
        for c in range(pieces):
            for k in range(pairs):
                given[g, k, c].wait_send()
            for k in range(1, pairs):
                spreads[g, k, c].wait_send()
    for scatter in scatters.values():
        scatter.finish()
    arrive(END)
    point(END)
    for store in stores + keeps:
        store.wait()


def exchange(
    name, number, members, ways, rows, depth, work, inputs, outs=None, need=None, done=None, scratch=None,
    phases=None, fills=(), scatters=None, extra_work=None, gathers=None, helpers=(), pieces=4,
):
    pairs = members // 2
    others = max(pairs - 1, 1)
    outs, scratch, need, done = outs or {}, scratch or {}, need or {}, done or {}
    gathers, scatters = gathers or [], scatters or {}
    hbm, vmem = pl.BlockSpec(memory_space=pl.ANY), pl.BlockSpec(memory_space=pltpu.VMEM)
    plan = Bag(
        inputs=list(inputs), outs=list(outs), scratch=list(scratch), gathers=gathers, helpers=list(helpers),
        members=members, ways=ways, rows=rows, pieces=pieces, scatters=scatters, extra_work=extra_work,
        phases=phases, fills=list(fills), work=work,
        need=lambda n: need.get(n, 0 if phases else BEGIN), done=lambda n: done.get(n, END),
    )
    staging = [pltpu.VMEM(a.shape, a.dtype) for n, a in inputs.items() if plan.need(n) is not None]
    staging += [pltpu.VMEM(*spec) for spec in outs.values()]
    staging += list(scratch.values())
    staging += [DMA((max(len(inputs), 1),)), DMA((max(len(outs), 1),))]
    for width, chunks, _ in scatters.values():
        staging.append(pltpu.VMEM((members * rows, width), B16))
        staging += Scatter.scratch(members, rows, width, chunks)
    count = len(gathers)
    if count:
        staging += [pltpu.VMEM((rows, depth), B16)] * count
        staging += [
            DMA((count, pairs, pieces)), DMA((count, pairs, pieces)),
            DMA((count, others, pieces)), DMA((count, others, pieces)), DMA((count, pieces)),
        ]
    operands = list(inputs.values())
    shapes = [jax.ShapeDtypeStruct(*spec) for spec in outs.values()]
    shapes += [jax.ShapeDtypeStruct((members * rows, depth), B16)] * count
    spaces = [hbm] * len(shapes)
    for h in helpers:
        operands += h.inputs
        shapes += [jax.ShapeDtypeStruct(shape, dtype) for shape, dtype, _ in h.outs]
        spaces += [pl.BlockSpec(memory_space=space) for _, _, space in h.outs]
        staging += h.scratch
    results = pl.pallas_call(
        functools.partial(exchange_kernel, plan),
        out_shape=shapes,
        in_specs=[hbm] * len(operands),
        out_specs=spaces,
        scratch_shapes=staging,
        compiler_params=pltpu.CompilerParams(
            collective_id=number, has_side_effects=True, vmem_limit_bytes=VMEM_LIMIT
        ),
        cost_estimate=pl.CostEstimate(
            flops=20_000_000_000, bytes_accessed=50_000_000, transcendentals=0
        ),
        name=name,
    )(*operands)
    results = list(results)
    got = {n: results.pop(0) for n in list(outs) + list(gathers)}
    for h in helpers:
        h.results = [results.pop(0) for _ in h.outs]
    return Bag(**got)


def rms(rows, gain):
    scale = lax.rsqrt(jnp.mean(rows * rows, axis=-1, keepdims=True) + EPS)
    return rows * scale * gain


def rms_back(rows, gain, grad):
    scale = lax.rsqrt(jnp.mean(rows * rows, axis=-1, keepdims=True) + EPS)
    scaled = gain * grad
    mean = jnp.mean(scaled * rows, axis=-1, keepdims=True)
    return scale * scaled - rows * (scale * scale * scale * mean)


def gain_of(r, layer, row):
    ways = r.few.shape[1]
    return jnp.concatenate([r.few[layer, k, row : row + 1, :] for k in range(ways)], axis=1)


def layer_input(r, layer, at):
    if layer == 0:
        return r.acts_in[lax.axis_index(PIPE), at, :].astype(F32)
    return r.x[at, :].astype(F32)


def layer_cotangent(r, layer, at):
    if layer == 1:
        return r.out_grad[lax.axis_index(PIPE), at, :]
    return r.cotangent[at, :]


def work_first(r, c, at, total):
    return rms(layer_input(r, 0, at), gain_of(r, 0, 0)).astype(B16), layer_cotangent(r, 1, at)


def work_mid(layer, r, c, at, total):
    residual = layer_input(r, layer, at) + total
    r.residual[at, :] = residual
    return (rms(residual, gain_of(r, layer, 1)).astype(B16),)


def work_turn(r, c, at, total):
    out = (r.residual[at, :] + total).astype(B16)
    r.x[at, :] = out
    return (rms(out.astype(F32), gain_of(r, 1, 0)).astype(B16),)


def work_back_ffn(layer, r, c, at, total):
    depth = r.residual.shape[1]
    residual = r.residual[at, :]
    if layer == 1:
        r.last[at, :] = (residual + total[:, depth:]).astype(B16)
    grad = layer_cotangent(r, layer, at).astype(F32) + rms_back(
        residual, gain_of(r, layer, 1), total[:, :depth]
    )
    r.d_residual[at, :] = grad
    return (grad.astype(B16),)


def work_back_mix(layer, r, c, at, total):
    step = rms_back(layer_input(r, layer, at), gain_of(r, layer, 0), total)
    grad = (r.d_residual[at, :] + step).astype(B16)
    r.x_grad[at, :] = grad
    return (grad,)


def work_shared(r, scatters):
    total = scatters[SHARED].receive(0)
    _, ways, block, _ = r.shared.shape
    for j in range(2 * ways):
        r.shared[j // ways, j % ways] = total[j * block : (j + 1) * block, :].astype(r.shared.dtype)


def widen(block, axis, size):
    missing = size - block.shape[axis]
    if missing == 0:
        return block
    pads = [(0, 0)] * block.ndim
    pads[axis] = (0, missing)
    return jnp.pad(block, pads)


def on_device(
    acts_in, out_grad, mix_gain, w_mixer_in, w_query, w_shared, w_step, a_log, dt_bias, d_skip,
    w_mamba_out, w_attn_out, ffn_gain, w_gate_up, w_down,
):
    section = lax.axis_index(PIPE)
    member = lax.axis_index(TENSOR)
    members = lax.axis_size(TENSOR)
    dp = lax.axis_size(DP)
    heads = a_log.shape[1]
    real = heads * HD
    width = (heads + heads % 2) * HD
    q_real = w_query.shape[2]
    cols = Cols(width)
    units = w_gate_up.shape[3]
    rows, depth = acts_in.shape[1:]
    length = rows * members
    piece = depth // dp
    wide = cols.total - cols.b

    at_row = MixerRows(cols, members)
    q_heads = q_real // HD
    inner = jnp.concatenate(
        [widen(w_mixer_in[0, :, 0], 1, width), widen(w_mixer_in[0, :, 1], 1, width)], axis=1
    )
    share = lax.dynamic_slice_in_dim(w_shared[0], member * (piece // members), piece // members, 0)
    share = jnp.concatenate([share[:, at : at + LANES] for at in range(0, 4 * LANES, LANES)], axis=0)
    mixer_shard = jnp.concatenate(
        [fold_lanes(share)(piece), fold_lanes(widen(w_query[0], 1, LANES))(piece)]
        + [inner[:, at : at + piece] for at in range(0, 2 * width, piece)]
        + [widen(w_mamba_out[0], 0, width), widen(w_attn_out[0], 0, LANES)],
        axis=0,
    )
    steps = lax.dynamic_slice_in_dim(w_step[0], member * heads, heads, 1).T.astype(F32)
    ffn_shard = jnp.concatenate(
        [w_gate_up[0, :, j, at : at + piece] for j in range(2) for at in range(0, units, piece)]
        + [w_down[0]],
        axis=0,
    )
    few_shard = jnp.concatenate(
        [
            mix_gain.astype(F32), ffn_gain.astype(F32),
            widen(widen(jnp.concatenate([a_log, dt_bias, d_skip]), 1, piece), 0, 6),
            widen(steps, 0, 8),
        ],
        axis=0,
    )

    def run(name, number, work, inputs, outs, **more):
        return exchange(name, number, members, dp, rows, depth, work, inputs, outs, **more)

    half = piece // 2
    low_units = width + LANES
    block32, block16 = ((rows, depth), F32), ((rows, depth), B16)
    core_keeps = dict(
        proj=((length, cols.step), B16),
        step=((length, LANES), F32),
        y=((length, width), B16),
        lows=((length, low_units), B16),
        states=((length // STEP, NS, width), B16),
        lse=((length // TILE, 8, 2 * TILE), F32),
    )
    ffn_keeps = dict(gu=((length, 2 * units), B16), hidden=((length, units), B16))
    gu_spec, down_spec = ((2, dp, half, 2 * units), B16), ((2, dp, units // 2, piece), B16)
    cat_spec, out_spec = ((2, dp, half, cols.b), B16), ((2, dp, low_units // 2, piece), B16)
    shared_spec = ((2, dp, half // members, wide), B16 if half // members % 16 == 0 else F32)
    gain_row = ((8, depth), F32)
    fills_ffn = [
        lambda r: grad_columns(r.rows_ffn, r.dgu, r.g_gu),
        lambda r: grad_rows(r.hidden, r.rows_out, r.g_down),
    ]
    fill_cat = lambda r: mixer_columns(cols, members, r)
    fill_out = lambda r: grad_rows(r.lows, r.rows_back, r.g_out)

    load = Cargo(
        0, dp, mixer_shard,
        {BEGIN: 1, SENT: 2, CHUNK: 1, CHUNK + 1: 1, CHUNK + 2: 2, CHUNK + 3: 2, SPREAD: 2, GIVEN: 4},
        members, at_row.shared,
    )
    few = Few(dp, few_shard, {BEGIN: 2, SENT: 1})
    got = run(
        "first", 0, work_first, dict(acts_in=acts_in, out_grad=out_grad), {},
        gathers=dict(rows_mix=0, rows_out=0), helpers=[few, load],
    )
    few = few.result
    first = Bag(rows_mix=got.rows_mix, mixer=load.results[0], shared_w=load.results[1], acts_in=acts_in)
    second = Bag(rows_out=got.rows_out, out_grad=out_grad)
    for layer, k in enumerate((first, second)):
        x = dict(acts_in=acts_in) if layer == 0 else dict(x=second.x)
        load = Cargo(
            layer, dp, ffn_shard,
            {
                BEGIN: 1, 0: 1, 1: 1, 2: 1, 3: 2, 4: 1, 5: 1, 6: 2, 7: 2, SENT: 1, CHUNK: 1, CHUNK + 1: 1,
                CHUNK + 2: 1, SPREAD: 2,
            },
        )
        k.add(
            run(
                f"mixer{layer}", 1 + layer, functools.partial(work_mid, layer),
                dict(x, few=few, rows_mix=k.rows_mix, mixer=k.mixer, shared_w=k.shared_w),
                dict(core_keeps, residual=block32, rest=((depth, 6 * LANES), B16)),
                need=dict({n: SENT for n in x}, rows_mix=1),
                done=dict(rest=0, proj=1, step=1, y=3, states=3, lows=7, lse=7, residual=CHUNK + 3),
                scratch=dict(state=pltpu.VMEM((NS, width), F32)),
                phases=functools.partial(core_fwd_phases, cols, members, layer, q_heads),
                scatters={PART: (depth, 4, (4, 5, 6))}, gathers=dict(rows_ffn=0), helpers=[load],
            )
        )
        k.gates = load.result
        if layer == 0:
            load = Cargo(
                1, dp, mixer_shard,
                {
                    BEGIN: 1, 1: 1, 3: 1, SENT: 2, CHUNK: 2, CHUNK + 1: 1, CHUNK + 2: 1, CHUNK + 3: 1, SPREAD: 2,
                    GIVEN: 3,
                },
                members, at_row.shared,
            )
            got = run(
                "turn", 3, work_turn,
                dict(residual=k.residual, few=few, rows_ffn=k.rows_ffn, gates=k.gates),
                dict(ffn_keeps, x=block16),
                need=dict(residual=SENT, few=SENT), done=dict(gu=3, hidden=3, x=CHUNK + 3),
                phases=lambda r, order: by_blocks(order, rows, lambda at, m: ffn_forward(r, at)),
                scatters={PART: (depth, 4, (0, 1, 2))}, gathers=dict(rows_mix=0), helpers=[load],
            )
            k.gu, k.hidden = got.gu, got.hidden
            second.rows_mix, second.x = got.rows_mix, got.x
            second.mixer, second.shared_w = load.results

    def clear_gain(r):
        r.gain_ffn[...] = jnp.zeros_like(r.gain_ffn)

    def ffn_both(r, at, m):
        ffn_forward(r, at, depth)
        ffn_backward(r, at)

    def ffn_both_phases(r, order):
        clear_gain(r)
        return by_blocks(order, rows, functools.partial(ffn_both, r))

    def ffn_back_phases(r, order):
        clear_gain(r)
        return by_blocks(order, rows, lambda at, m: ffn_backward(r, at))

    acts = Place(
        lambda r: (r.raw.x, r.last), (rows, depth), 1,
        {BEGIN: 1, CHUNK: 1, CHUNK + 1: 1, CHUNK + 2: 1, CHUNK + 3: 1},
    )
    second.add(
        run(
            "ffn1", 4, functools.partial(work_back_ffn, 1),
            dict(
                out_grad=out_grad, residual=second.residual, few=few, rows_ffn=second.rows_ffn,
                rows_out=second.rows_out, gates=second.gates, x=second.x,
            ),
            dict(gain_ffn=gain_row, g_gu=gu_spec, g_down=down_spec, d_residual=block32),
            need=dict(out_grad=SENT, residual=SENT, few=SENT, x=None),
            done=dict(gain_ffn=3, g_gu=SENT, d_residual=CHUNK + 3, g_down=SPREAD),
            scratch=dict(
                last=pltpu.VMEM(*block16),
                **{n: pltpu.VMEM(*spec) for n, spec in ffn_keeps.items()},
                dgu=pltpu.VMEM((length, 2 * units), B16),
            ),
            phases=ffn_both_phases,
            scatters={PART: (2 * depth, 4, (0, 1, 2))}, fills=fills_ffn, gathers=dict(rows_back=0), helpers=[acts],
        )
    )

    core_scratch = dict(
        dproj=pltpu.VMEM((length, cols.total), B16),
        heads=pltpu.VMEM((8, LANES), F32),
        dcore=pltpu.VMEM((length, low_units), B16),
        grad_state=pltpu.VMEM((NS, width), F32),
        skip_sum=pltpu.VMEM((STEP, width), F32),
        dk_sum=pltpu.VMEM((length, LANES), F32),
        dv_sum=pltpu.VMEM((length, LANES), F32),
        folded=pltpu.VMEM((length, wide), B16),
        gain_column=pltpu.VMEM((depth, LANES), F32),
        staged=pltpu.VMEM((depth, wide), F32),
    )

    def core_inputs(k):
        return dict(
            few=few, rows_mix=k.rows_mix, mixer=k.mixer, rows_back=k.rows_back, d_residual=k.d_residual,
            gain_ffn=k.gain_ffn, proj=k.proj, step=k.step, y=k.y, lows=k.lows, states=k.states,
            lse=k.lse, rest=k.rest,
        )

    core_need = dict(
        lows=1, proj=2, lse=2, few=3, step=3, y=3, states=3, rows_mix=4, rest=4, gain_ffn=5, g_gu=2, g_down=1,
        d_residual=SENT, x=SENT, acts_in=SENT,
    )

    def core_phases(layer, r, order):
        return core_bwd_phases(cols, layer, members, (q_heads, heads), r, order)

    def from_input(pick):
        return lambda r: (pick(r.raw), pick(r))

    def from_kernel(pick):
        return lambda r: (pick(r), pick(r))

    take_gu, take_down = (lambda r: r.g_gu), (lambda r: r.g_down)
    take_cat, take_out, take_shared = (lambda r: r.g_cat), (lambda r: r.g_out), (lambda r: r.shared)

    def back_phases(layer, r, order):
        into, attend, scan, shared, *back = core_phases(layer, r, order)
        return [into, lambda: fill_out(r), attend, scan, lambda: fill_cat(r), shared] + back

    back_scatters = {PART: (depth, 4, (6, 7, 8)), SHARED: (wide, 1, (5, 6, 5))}
    hauls = [
        Haul(
            1, dp, [from_input(take_gu), from_input(take_down)], [gu_spec, down_spec],
            {BEGIN: 1, 2: 1, 3: 1, 4: 1, SENT: 1, CHUNK + 3: 1},
        ),
        Straight(1, dp, from_kernel(take_out), out_spec, {1: 1, SENT: 1}),
        Haul(
            1, dp, [from_kernel(take_cat)], [cat_spec], {4: 1, CHUNK: 1, CHUNK + 1: 1, CHUNK + 2: 1, CHUNK + 3: 1}, line=False
        ),
    ]
    inner = dict(g_cat=pltpu.VMEM(*cat_spec), g_out=pltpu.VMEM(*out_spec))
    got = run(
        "back1", 5, functools.partial(work_back_mix, 1),
        dict(core_inputs(second), x=second.x, g_gu=second.g_gu, g_down=second.g_down),
        dict(x_grad=block16, shared=shared_spec),
        need=core_need,
        done=dict(x_grad=CHUNK + 3, shared=EXTRA),
        scratch=dict(core_scratch, **inner), phases=functools.partial(back_phases, 1),
        scatters=back_scatters, extra_work=work_shared, gathers=dict(rows_out=0), helpers=hauls,
    )
    second.add(got)
    cat_sums = hauls[2].result
    second.sums = hauls[0].results + hauls[1].results

    hauls = [
        Haul(
            1, dp, [from_input(lambda r: r.cat_sums)], [cat_spec], {BEGIN: 1, CHUNK + 3: 1}, swap=False
        ),
        Haul(
            1, dp, [from_input(take_shared)], [shared_spec], {BEGIN: 1, 3: 1, SENT: 2, CHUNK + 1: 1, GIVEN: 1}
        ),
        Haul(
            0, dp, [from_kernel(take_gu)], [gu_spec], {SENT: 1, CHUNK + 3: 1, SPREAD: 1, GIVEN: 1},
            line=False,
        ),
    ]
    got = run(
        "ffn0", 6, functools.partial(work_back_ffn, 0),
        dict(
            cotangent=second.x_grad, residual=first.residual, few=few, rows_ffn=first.rows_ffn,
            rows_out=second.rows_out, gates=first.gates, gu=first.gu, hidden=first.hidden,
            cat_sums=cat_sums, shared=second.shared,
        ),
        dict(gain_ffn=gain_row, g_down=down_spec, d_residual=block32),
        need=dict(
            cotangent=SENT, residual=SENT, few=SENT, hidden=SENT, cat_sums=SENT, shared=3
        ),
        done=dict(gain_ffn=3, d_residual=CHUNK + 3, g_down=SPREAD),
        scratch=dict(dgu=pltpu.VMEM((length, 2 * units), B16), g_gu=pltpu.VMEM(*gu_spec)),
        phases=ffn_back_phases, fills=fills_ffn, scatters={PART: (depth, 4, (0, 1, 2))}, gathers=dict(rows_back=0),
        helpers=hauls,
    )
    gu_sums = hauls[2].result
    second.sums += hauls[0].results + hauls[1].results
    first.add(got)

    hauls = [
        Haul(0, dp, [from_input(lambda r: r.gu_sums)], [gu_spec], {BEGIN: 1, 4: 1}, swap=False),
        Haul(
            0, dp, [from_input(take_down)], [down_spec], {BEGIN: 1, 1: 1, 2: 2, 3: 1, SENT: 1}
        ),
        Haul(0, dp, [from_kernel(take_out)], [out_spec], {1: 1, 3: 2, 4: 2, CHUNK + 2: 1}),
        Haul(
            0, dp, [from_kernel(take_cat)], [cat_spec],
            {4: 1, 6: 1, SENT: 1, CHUNK: 1, CHUNK + 1: 1},
        ),
        Straight(0, dp, from_kernel(take_shared), shared_spec, {EXTRA: 1}),
    ]
    x_grads = Place(
        lambda r: (r.x_grad, r.raw.x_grad1), (rows, depth), 0,
        {4: 1, CHUNK: 1, CHUNK + 1: 1, CHUNK + 2: 1, CHUNK + 3: 1},
    )
    run(
        "back0", 7, functools.partial(work_back_mix, 0),
        dict(core_inputs(first), acts_in=acts_in, x_grad1=second.x_grad, gu_sums=gu_sums, g_down=first.g_down),
        {},
        need=dict(core_need, x_grad1=None, gu_sums=3),
        scratch=dict(
            core_scratch, **inner, x_grad=pltpu.VMEM(*block16), shared=pltpu.VMEM(*shared_spec)
        ),
        phases=functools.partial(back_phases, 0), scatters=back_scatters, extra_work=work_shared, helpers=hauls + [x_grads],
    )
    first.sums = [h.result for h in hauls]
    order = [0, 1, 3, 2, 4]
    g_gates, g_down, g_cat, g_out, g_shared = [
        jnp.where(section == 0, first.sums[i], second.sums[j]).astype(F32).reshape(
            (-1,) + first.sums[i].shape[2:]
        )
        for i, j in zip(order, (0, 1, 3, 2, 4))
    ]
    g_mixer = jnp.stack([g_cat[:, :real], g_cat[:, width : width + real]], axis=1)
    table = 2 * NS + 2 * KVH * HD
    g_gains = g_shared[:, table + GAINS_AT : table + GAINS_AT + 2].T
    g_heads = g_shared[:3, table + HEADS_AT : table + HEADS_AT + heads]
    return (
        acts.result[None],
        x_grads.result[None],
        g_gains[None],
        g_mixer[None],
        g_cat[None, :, cols.q : cols.q + q_real],
        g_shared[None, :, :table],
        g_shared[None, :, table : table + HM],
        g_heads[None],
        g_out[None, :real],
        g_out[None, width : width + q_real],
        g_gates.reshape(1, piece, 2, units),
        g_down[None],
    )


def solution(mesh):
    rows = P(DP, TENSOR, None)
    by_dp, by_tensor, by_both = P(PIPE, DP), P(PIPE, TENSOR), P(PIPE, DP, TENSOR)
    wide, tall, whole = P(PIPE, DP, None, TENSOR), P(PIPE, TENSOR, DP), P(PIPE, DP, None)
    joint = P(PIPE, (DP, TENSOR), None)
    return jax.shard_map(
        on_device,
        mesh=mesh,
        in_specs=(
            rows, rows, by_dp, wide, by_both, whole, whole, by_tensor, by_tensor, by_tensor, tall, tall,
            by_dp, wide, tall,
        ),
        out_specs=(
            P(PIPE, DP, TENSOR, None), P(PIPE, DP, TENSOR, None), P(PIPE, None, (DP, TENSOR)),
            wide, by_both, joint, joint, P(PIPE, None, TENSOR), tall, tall, wide, tall,
        ),
        check_vma=False,
    )
```

```python
import functools

import jax
import jax.numpy as jnp
from jax import lax
from jax.experimental import pallas as pl
from jax.experimental.pallas import tpu as pltpu
from jax.sharding import PartitionSpec as P

HM = 24
HA = 8
KVH = 2
NS = 128
HD = 64
LANES = 128
STEP = 128
TILE = 256
EPS = 1e-05
F32 = jnp.float32
B16 = jnp.bfloat16
VMEM_LIMIT = 60 << 20
HEADS_AT = 32
GAINS_AT = 64


def nn(a, b):
    return lax.dot_general(a, b, (((1,), (0,)), ((), ())), preferred_element_type=F32)


def nt(a, b):
    return lax.dot_general(a, b, (((1,), (1,)), ((), ())), preferred_element_type=F32)


def tn(a, b):
    return lax.dot_general(a, b, (((0,), (0,)), ((), ())), preferred_element_type=F32)


def exact(a, b):
    return lax.dot_general(
        a, b, (((1,), (0,)), ((), ())), precision=lax.Precision.HIGHEST, preferred_element_type=F32
    )


def softplus(v):
    small = jnp.exp(-jnp.abs(v))
    series = small * (1.0 - small * (0.5 - small * (1.0 / 3.0 - small * 0.25)))
    return jnp.maximum(v, 0.0) + jnp.where(small < 0.02, series, jnp.log(1.0 + small))


def sigmoid(v):
    return 1.0 / (1.0 + jnp.exp(-v))


def iotas(rows, columns):
    return (
        lax.broadcasted_iota(jnp.int32, (rows, columns), 0),
        lax.broadcasted_iota(jnp.int32, (rows, columns), 1),
    )


def spread(column_block, head, rows):
    return jnp.broadcast_to(column_block[:, head : head + 1], (rows, LANES))


class Cols:
    def __init__(self, width):
        self.width = width
        self.z = 0
        self.u = width
        self.q = 2 * width
        self.b = self.q + LANES
        self.c = self.b + LANES
        self.k = self.c + LANES
        self.v = self.k + LANES
        self.step = self.v + LANES
        self.total = self.step + LANES
        self.pairs = width // LANES


class MixerRows:
    def __init__(self, cols, members):
        self.shared = 4 * LANES // members
        self.query = self.shared
        self.inner = self.query + LANES
        self.low = self.inner + 2 * cols.width
        self.total = self.low + cols.width + LANES


def fold_lanes(block):
    def folded(piece):
        count = piece // LANES
        size = block.shape[0] // count
        return jnp.concatenate([block[i * size : (i + 1) * size] for i in range(count)], axis=1)

    return folded


def unfold_lanes(block):
    return jnp.concatenate(
        [block[:, at : at + LANES] for at in range(0, block.shape[1], LANES)], axis=0
    )


def join_shared(cols, members, layer, q_heads, r):
    mixer, shared, few, rest = r.mixer, r.shared_w, r.few, r.rest
    ways, _, piece = mixer.shape
    at = MixerRows(cols, members)
    group = lax.axis_index(TENSOR) * q_heads // (HA // KVH)
    source, target = iotas(LANES, LANES)
    choose = (source == group * HD + (target & (HD - 1))).astype(B16)
    size = piece // members
    for d in range(ways):
        rows = slice(d * piece, (d + 1) * piece)
        rest[rows, :LANES] = unfold_lanes(mixer[d, at.query : at.query + LANES, :])
        for m in range(members):
            block = unfold_lanes(shared[m, d])
            to = slice(d * piece + m * size, d * piece + (m + 1) * size)
            for j in range(4):
                lanes = block[j * size : (j + 1) * size, :]
                if j >= 2:
                    lanes = nn(lanes, choose).astype(B16)
                rest[to, LANES * (j + 1) : LANES * (j + 2)] = lanes
        steps = few[layer, d, 8:16, :]
        steps = jnp.concatenate([steps, jnp.zeros((LANES - 8, piece), F32)], axis=0).T
        rest[rows, 5 * LANES :] = steps.astype(B16)


def split_heads(block, low_lanes):
    zero = jnp.zeros_like(block)
    return jnp.concatenate(
        [jnp.where(low_lanes, block, zero), jnp.where(low_lanes, zero, block)], axis=0
    )


def blocks_nn(rows_ref, rows, weights_ref, c, first=0):
    ways, _, piece = weights_ref.shape
    at = slice(first + c * piece, first + (c + 1) * piece)
    total = nn(rows_ref[rows, 0:piece], weights_ref[0, at, :])
    for d in range(1, ways):
        total += nn(rows_ref[rows, d * piece : (d + 1) * piece], weights_ref[d, at, :])
    return total


def multiply_out(lows_ref, weights_ref, first, part_ref, rows):
    ways, _, piece = weights_ref.shape
    last = first + lows_ref.shape[1]
    block = lows_ref[rows, :]
    for k in range(ways):
        part_ref[rows, k * piece : (k + 1) * piece] = nn(
            block, weights_ref[k, first:last, :]
        ).astype(B16)


def multiply_back(grad_ref, weights_ref, first, count, part_ref, rows, rows_ref, gain_sum, rest=None):
    ways, _, piece = weights_ref.shape
    for d in range(ways):
        to = slice(d * piece, (d + 1) * piece)
        total = nt(grad_ref[rows, 0:piece], weights_ref[d, first : first + piece, :])
        for c in range(1, count):
            at = slice(first + c * piece, first + (c + 1) * piece)
            total += nt(grad_ref[rows, c * piece : (c + 1) * piece], weights_ref[d, at, :])
        if rest is not None:
            total += nt(grad_ref[rows, count * piece :], rest[to, :])
        part_ref[rows, to] = total.astype(B16)
        if gain_sum is not None:
            gain_sum[0:1, to] += jnp.sum(total * rows_ref[rows, to].astype(F32), axis=0, keepdims=True)


def by_blocks(order, rows, step):
    def phase(group):
        def run():
            for member in group:
                step(pl.ds(pl.multiple_of(member * rows, rows), rows), member)

        return run

    return [phase(group) for group in order]


def skip_lanes(few_ref, layer, width):
    row, lane = iotas(width, LANES)
    own = ((row >> 6) == lane).astype(F32)
    skip = jnp.broadcast_to(few_ref[layer, 0, 4:5, :LANES], (8, LANES))
    return lax.dot_general(
        skip, own, (((1,), (1,)), ((), ())),
        precision=lax.Precision.HIGHEST, preferred_element_type=F32,
    )[0:1, :]


def core_fwd_phases(cols, members, layer, q_heads, r, order):
    rows_ref, weights_ref, few_ref = r.rows_mix, r.mixer, r.few
    proj_ref, step_ref, y_ref, lows_ref = r.proj, r.step, r.y, r.lows
    states_ref, lse_ref, part_ref, state = r.states, r.lse, r.part, r.state
    length = rows_ref.shape[0]
    width = cols.width
    piece = weights_ref.shape[2]

    at_row = MixerRows(cols, members)

    def join_all():
        join_shared(cols, members, layer, q_heads, r)

    def project_all():
        def project(i, _):
            rows = pl.ds(pl.multiple_of(i * TILE, TILE), TILE)
            for c in range(cols.q // piece):
                value = blocks_nn(rows_ref, rows, weights_ref, c, at_row.inner)
                proj_ref[rows, c * piece : (c + 1) * piece] = value.astype(B16)
            rest = nn(rows_ref[rows, :], r.rest[...])
            proj_ref[rows, cols.q : cols.b] = (rest[:, :LANES] * HD**-0.5).astype(B16)
            proj_ref[rows, cols.b : cols.step] = rest[:, LANES : 5 * LANES].astype(B16)
            step_ref[rows, :] = rest[:, 5 * LANES :]
            return 0

        lax.fori_loop(0, length // TILE, project, 0)

    def scan_part(low, high):
        ri, ci = iotas(STEP, STEP)
        lower = ri >= ci
        tril = lower.astype(F32)
        low_lanes = ci < HD
        decay = jnp.exp(few_ref[layer, 0, 2:3, :LANES])
        bias = few_ref[layer, 0, 3:4, :LANES]
        skips = skip_lanes(few_ref, layer, width)
        if low == 0:
            state[...] = jnp.zeros_like(state)

        def scan_block(b, _):
            rows = pl.ds(pl.multiple_of(b * STEP, STEP), STEP)
            dt = softplus(step_ref[rows, :] + bias)
            run = exact(tril, -dt * decay)
            run_t = run.T
            bm = proj_ref[rows, cols.b : cols.b + LANES]
            cm = proj_ref[rows, cols.c : cols.c + LANES]
            cb = jnp.where(lower, nt(cm, bm), 0.0)
            states_in = state[...]
            low_state = states_in.astype(B16)
            states_ref[b] = low_state
            carried = nn(cm, low_state)
            tails, fades = [], []
            for p in range(cols.pairs):
                lanes = slice(LANES * p, LANES * (p + 1))
                u = proj_ref[rows, cols.u + LANES * p : cols.u + LANES * (p + 1)].astype(F32)
                z = proj_ref[rows, cols.z + LANES * p : cols.z + LANES * (p + 1)].astype(F32)
                run_b = [spread(run, 2 * p + k, STEP) for k in range(2)]
                run_w = jnp.where(low_lanes, run_b[0], run_b[1])
                ud = u * jnp.where(low_lanes, spread(dt, 2 * p, STEP), spread(dt, 2 * p + 1, STEP))
                mix = jnp.concatenate(
                    [
                        (
                            jnp.exp(jnp.minimum(run_b[k] - run_t[2 * p + k : 2 * p + k + 1, :], 0.0))
                            * cb
                        ).astype(B16)
                        for k in range(2)
                    ],
                    axis=1,
                )
                inside = nn(mix, split_heads(ud, low_lanes).astype(B16))
                y = inside + carried[:, lanes] * jnp.exp(run_w) + skips[:, lanes] * u
                y_ref[rows, lanes] = y.astype(B16)
                lows_ref[rows, lanes] = (y * z * sigmoid(z)).astype(B16)
                end = run_w[STEP - 1 : STEP, :]
                tails.append((ud * jnp.exp(end - run_w)).astype(B16))
                fades.append(jnp.exp(end))
            fresh = tn(bm, jnp.concatenate(tails, axis=1))
            state[...] = states_in * jnp.concatenate(fades, axis=1) + fresh
            return 0

        lax.fori_loop(low, high, scan_block, 0)

    def attend(i):
        rk, ck = iotas(TILE, 2 * TILE)
        diagonal = rk <= jnp.where(ck < TILE, ck, ck - TILE)
        q_low = iotas(TILE, LANES)[1] < HD

        rows = pl.ds(pl.multiple_of(i * TILE, TILE), TILE)
        q2 = split_heads(proj_ref[rows, cols.q : cols.q + LANES], q_low)

        def piece(j, carry, masked):
            top, total, out = carry
            keys = pl.ds(pl.multiple_of(j * TILE, TILE), TILE)
            s = nt(proj_ref[keys, cols.k : cols.k + LANES], q2)
            if masked:
                s = jnp.where(diagonal, s, -1e30)
            new_top = jnp.maximum(top, jnp.max(s, axis=0, keepdims=True))
            p = jnp.exp(s - new_top)
            scale = jnp.exp(top - new_top)
            total = total * scale + jnp.sum(p, axis=0, keepdims=True)
            out = out * scale + tn(proj_ref[keys, cols.v : cols.v + LANES], p.astype(B16))
            return new_top, total, out

        carry = (
            jnp.full((1, 2 * TILE), -1e30, F32),
            jnp.zeros((1, 2 * TILE), F32),
            jnp.zeros((LANES, 2 * TILE), F32),
        )
        carry = lax.fori_loop(0, i, lambda j, c: piece(j, c, False), carry)
        top, total, out = piece(i, carry, True)
        out = out / total
        joined = jnp.concatenate([out[:HD, :TILE], out[HD:, TILE:]], axis=0)
        lows_ref[rows, width : width + LANES] = joined.T.astype(B16)
        lse_ref[i] = jnp.broadcast_to(top + jnp.log(total), (8, 2 * TILE))

    rows = length // members
    blocks, tiles = length // STEP, length // TILE
    together = rows == TILE

    def attend_all():
        for i in range(tiles):
            attend(i)

    def finish(at, member):
        if together:
            attend(member)
        multiply_out(lows_ref, weights_ref, at_row.low, part_ref, at)

    phases = [
        join_all,
        project_all,
        lambda: scan_part(0, blocks // 2),
        lambda: scan_part(blocks // 2, blocks),
    ]
    if not together:
        phases[3] = lambda: (scan_part(blocks // 2, blocks), attend_all())
    return phases + by_blocks(order, rows, finish)


def core_bwd_phases(cols, layer, members, q_heads, r, order):
    back_ref, weights_ref, few_ref, rows_ref = r.rows_back, r.mixer, r.few, r.rows_mix
    proj_ref, step_ref, y_ref, lows_ref = r.proj, r.step, r.y, r.lows
    states_ref, lse_ref, part_ref = r.states, r.lse, r.part
    dproj_ref, heads_ref, dcore, grad_state, skip_sum = r.dproj, r.heads, r.dcore, r.grad_state, r.skip_sum
    dk_sum, dv_sum, folded, staged = r.dk_sum, r.dv_sum, r.folded, r.staged
    length = back_ref.shape[0]
    width = cols.width
    ways, _, piece = weights_ref.shape
    blocks = length // STEP
    depth = ways * piece
    at_row = MixerRows(cols, members)
    low_rows = slice(at_row.low, at_row.low + width + LANES)

    def into_all():
        def into_core(i, _):
            rows = pl.ds(pl.multiple_of(i * TILE, TILE), TILE)
            total = nt(back_ref[rows, 0:piece], weights_ref[0, low_rows, :])
            for k in range(1, ways):
                total += nt(
                    back_ref[rows, k * piece : (k + 1) * piece], weights_ref[k, low_rows, :]
                )
            dcore[rows, :] = total.astype(B16)
            return 0

        lax.fori_loop(0, length // TILE, into_core, 0)

    def attend_all():
        rk, ck = iotas(TILE, 2 * TILE)
        diagonal = rk <= jnp.where(ck < TILE, ck, ck - TILE)
        q_low = iotas(TILE, LANES)[1] < HD
        dk_sum[...] = jnp.zeros_like(dk_sum)
        dv_sum[...] = jnp.zeros_like(dv_sum)
        half = iotas(8, LANES)
        pick_low = (half[1] < HD).astype(F32)
        pick_high = (half[1] >= HD).astype(F32)

        def attend(i, _):
            rows = pl.ds(pl.multiple_of(i * TILE, TILE), TILE)
            q2 = split_heads(proj_ref[rows, cols.q : cols.q + LANES], q_low)
            d_out = dcore[rows, width : width + LANES]
            do2 = split_heads(d_out, q_low)
            both = d_out.astype(F32) * lows_ref[rows, width : width + LANES].astype(F32)
            high = lax.Precision.HIGHEST
            deltas = [
                lax.dot_general(
                    pick, both, (((1,), (1,)), ((), ())), precision=high, preferred_element_type=F32
                )[0:1, :]
                for pick in (pick_low, pick_high)
            ]
            delta = jnp.concatenate(deltas, axis=1)
            lse = lse_ref[i][0:1, :]

            def piece_of(j, dq, masked):
                keys = pl.ds(pl.multiple_of(j * TILE, TILE), TILE)
                kk = proj_ref[keys, cols.k : cols.k + LANES]
                p = jnp.exp(nt(kk, q2) - lse)
                if masked:
                    p = jnp.where(diagonal, p, 0.0)
                ds = (p * (nt(proj_ref[keys, cols.v : cols.v + LANES], do2) - delta)).astype(B16)
                dv_sum[keys, :] += nn(p.astype(B16), do2)
                dk_sum[keys, :] += nn(ds, q2)
                return dq + tn(kk, ds)

            dq = jnp.zeros((LANES, 2 * TILE), F32)
            dq = lax.fori_loop(0, i, lambda j, c: piece_of(j, c, False), dq)
            dq = piece_of(i, dq, True)
            joined = jnp.concatenate([dq[:HD, :TILE], dq[HD:, TILE:]], axis=0) * HD**-0.5
            dproj_ref[rows, cols.q : cols.q + LANES] = joined.T.astype(B16)
            return 0

        lax.fori_loop(0, length // TILE, attend, 0)
        dproj_ref[:, cols.k : cols.k + LANES] = dk_sum[...].astype(B16)
        dproj_ref[:, cols.v : cols.v + LANES] = dv_sum[...].astype(B16)

    def scan_all():
        ri, ci = iotas(STEP, STEP)
        upper = ri <= ci
        tril = (ri >= ci).astype(F32)
        triu = upper.astype(F32)
        low_lanes = ci < HD
        decay = jnp.exp(few_ref[layer, 0, 2:3, :LANES])
        bias = few_ref[layer, 0, 3:4, :LANES]
        skips = skip_lanes(few_ref, layer, width)
        row, lane = iotas(width, LANES)
        group = ((row >> 6) == lane).astype(B16)
        grad_state[...] = jnp.zeros_like(grad_state)
        skip_sum[...] = jnp.zeros_like(skip_sum)
        heads_ref[...] = jnp.zeros_like(heads_ref)
        zero_rows = jnp.zeros((STEP - 2 * cols.pairs, LANES), F32)

        def scan_block(back, _):
            b = blocks - 1 - back
            rows = pl.ds(pl.multiple_of(b * STEP, STEP), STEP)
            raw = step_ref[rows, :] + bias
            dt = softplus(raw)
            a = -dt * decay
            run = exact(tril, a)
            run_t = run.T
            bm = proj_ref[rows, cols.b : cols.b + LANES]
            cm = proj_ref[rows, cols.c : cols.c + LANES]
            cbt = jnp.where(upper, nt(bm, cm), 0.0)
            low_state = states_ref[b]
            grads_out = grad_state[...]
            low_grad = grads_out.astype(B16)
            carried = nn(cm, low_state)
            pulled = nn(bm, low_grad)
            dcb = jnp.zeros((STEP, STEP), F32)
            dy_fades, u_tails, fades = [], [], []
            carry_terms, direct_terms, tail_terms = [], [], []
            row_sums = []
            col_sums = jnp.zeros((STEP, LANES), F32)
            for p in range(cols.pairs):
                lanes = slice(LANES * p, LANES * (p + 1))
                u16 = proj_ref[rows, cols.u + LANES * p : cols.u + LANES * (p + 1)]
                u = u16.astype(F32)
                z = proj_ref[rows, cols.z + LANES * p : cols.z + LANES * (p + 1)].astype(F32)
                y = y_ref[rows, lanes].astype(F32)
                dm = dcore[rows, lanes].astype(F32)
                sg = sigmoid(z)
                dy = dm * z * sg
                dproj_ref[rows, cols.z + LANES * p : cols.z + LANES * (p + 1)] = (
                    dm * y * sg * (1.0 + z * (1.0 - sg))
                ).astype(B16)
                dy16 = dy.astype(B16)
                skip_sum[:, lanes] += u * dy
                run_b = [spread(run, 2 * p + k, STEP) for k in range(2)]
                dt_b = [spread(dt, 2 * p + k, STEP) for k in range(2)]
                run_w = jnp.where(low_lanes, run_b[0], run_b[1])
                dt_w = jnp.where(low_lanes, dt_b[0], dt_b[1])
                end = run_w[STEP - 1 : STEP, :]
                fade = jnp.exp(run_w)
                tail = jnp.exp(end - run_w)
                dmix = nt(split_heads(u16, low_lanes), dy16)
                mixes = []
                for k in range(2):
                    gap = jnp.exp(jnp.minimum(run_t[2 * p + k : 2 * p + k + 1, :] - run_b[k], 0.0))
                    mixes.append((gap * cbt).astype(B16))
                    weighted = gap * dt_b[k] * dmix[STEP * k : STEP * (k + 1), :]
                    dcb += weighted
                    moved = weighted * cbt
                    row_sums.append(jnp.sum(moved, axis=0, keepdims=True))
                    col_sums = jnp.where(
                        ci == 2 * p + k, jnp.sum(moved, axis=1, keepdims=True), col_sums
                    )
                inside = nn(jnp.concatenate(mixes, axis=1), split_heads(dy16, low_lanes))
                pull_tail = tail * pulled[:, lanes]
                g = inside + pull_tail
                dproj_ref[rows, cols.u + LANES * p : cols.u + LANES * (p + 1)] = (
                    dt_w * g + skips[:, lanes] * dy
                ).astype(B16)
                dy_fade = dy * fade
                dy_fades.append(dy_fade.astype(B16))
                u_tails.append((u * dt_w * tail).astype(B16))
                fades.append(jnp.exp(end))
                carry_terms.append((dy_fade * carried[:, lanes]).astype(B16))
                direct_terms.append((u * g).astype(B16))
                tail_terms.append((u * pull_tail).astype(B16))
            dy_fade = jnp.concatenate(dy_fades, axis=1)
            dcb = jnp.where(upper, dcb, 0.0).astype(B16)
            dproj_ref[rows, cols.c : cols.c + LANES] = (tn(dcb, bm) + nt(dy_fade, low_state)).astype(B16)
            dproj_ref[rows, cols.b : cols.b + LANES] = (
                nn(dcb, cm) + nt(jnp.concatenate(u_tails, axis=1), low_grad)
            ).astype(B16)
            carry_term = nn(jnp.concatenate(carry_terms, axis=1), group)
            direct_term = nn(jnp.concatenate(direct_terms, axis=1), group)
            tail_term = dt * nn(jnp.concatenate(tail_terms, axis=1), group)
            overlap = jnp.sum(low_state.astype(F32) * grads_out, axis=0, keepdims=True)
            overlap = exact(jnp.broadcast_to(overlap, (8, width)), group.astype(F32))[0:1, :]
            overlap = overlap * jnp.exp(run[STEP - 1 : STEP, :])
            row_sum = jnp.concatenate(row_sums + [zero_rows], axis=0).T
            d_run = row_sum - col_sums + carry_term - tail_term
            d_a = exact(triu, d_run) + (jnp.sum(tail_term, axis=0, keepdims=True) + overlap)
            d_step = (direct_term - decay * d_a) * sigmoid(raw)
            dproj_ref[rows, cols.step : cols.step + LANES] = d_step.astype(B16)
            heads_ref[0:1, :] += jnp.sum(d_a * a, axis=0, keepdims=True)
            heads_ref[1:2, :] += jnp.sum(d_step, axis=0, keepdims=True)
            grad_state[...] = grads_out * jnp.concatenate(fades, axis=1) + tn(cm, dy_fade)
            return 0

        lax.fori_loop(0, blocks, scan_block, 0)
        skip = jnp.sum(skip_sum[...], axis=0, keepdims=True)
        heads_ref[2:3, :] = exact(jnp.broadcast_to(skip, (8, width)), group.astype(F32))[0:1, :]

    def back(at, member):
        multiply_back(
            dproj_ref, weights_ref, at_row.inner, cols.q // piece, part_ref, at, rows_ref, None, r.rest
        )

    def shared_all():
        wide = cols.total - cols.b
        member = lax.axis_index(TENSOR)
        heads = q_heads[1]
        group = member * q_heads[0] // (HA // KVH)
        source, target = iotas(wide, wide)
        kind = source >> 7
        wanted = jnp.where(
            kind < 2,
            source,
            jnp.where(
                kind < 4,
                2 * NS + (kind - 2) * KVH * HD + group * HD + (source & (HD - 1)),
                source + member * heads,
            ),
        )
        fold = ((target == wanted) & (source < 4 * LANES + heads)).astype(B16)

        def fold_rows(i, _):
            rows = pl.ds(pl.multiple_of(i * TILE, TILE), TILE)
            folded[rows, :] = nn(dproj_ref[rows, cols.b :], fold).astype(B16)
            return 0

        lax.fori_loop(0, length // TILE, fold_rows, 0)
        sub = piece // members
        half = sub // 2
        lane = iotas(piece, LANES)[1]
        head_lane = iotas(8, LANES)[1]
        shifted = jnp.where(
            (head_lane >= HEADS_AT) & (head_lane < HEADS_AT + heads),
            pltpu.roll(heads_ref[...], HEADS_AT, 1),
            0.0,
        )
        for k in range(ways):
            at = slice(k * piece, (k + 1) * piece)
            grad = tn(rows_ref[:, at], folded[...])
            raw = nn(r.rest[at, LANES:], fold)
            twice = (iotas(piece, wide)[1] >= 2 * LANES) & (iotas(piece, wide)[1] < 4 * LANES)
            own = jnp.sum(grad * jnp.where(twice, 0.5 * raw, raw), axis=1, keepdims=True)
            gains = [jnp.broadcast_to(few_ref[layer, k, i : i + 1, :], (LANES, piece)).T for i in (0, 1)]
            from_ffn = jnp.broadcast_to(r.gain_ffn[0:1, at], (LANES, piece)).T
            columns = [(own + r.gain_column[at, 0:1]) / gains[0], from_ffn / gains[1]]
            last = grad[:, wide - LANES :]
            last = jnp.where(lane == GAINS_AT, columns[0], last)
            last = jnp.where(lane == GAINS_AT + 1, columns[1], last)
            for t in range(members):
                for h in range(2):
                    to = t * (depth // members) + (h * ways + k) * half
                    rows = slice(t * sub + h * half, t * sub + (h + 1) * half)
                    staged[to : to + half, : wide - LANES] = grad[rows, : wide - LANES]
                    staged[to : to + half, wide - LANES :] = last[rows, :]
            to = pl.multiple_of(member * (depth // members) + k * half, 8)
            staged[pl.ds(to, 8), wide - LANES :] += shifted
        r.extra[...] = staged[...].astype(B16)

    return [into_all, attend_all, scan_all, shared_all] + by_blocks(order, length // members, back)


def ffn_forward(r, rows, part_ref):
    rows_ref, weights_ref, gu_ref, hidden_ref = r.rows_ffn, r.gates, r.gu, r.hidden
    units = hidden_ref.shape[1]
    piece = weights_ref.shape[2]
    count = units // piece
    for c in range(count):
        to = slice(c * piece, (c + 1) * piece)
        g = blocks_nn(rows_ref, rows, weights_ref, c)
        v = blocks_nn(rows_ref, rows, weights_ref, c + count)
        gu_ref[rows, to] = g.astype(B16)
        gu_ref[rows, units + c * piece : units + (c + 1) * piece] = v.astype(B16)
        hidden_ref[rows, to] = (g * sigmoid(g) * v).astype(B16)
    multiply_out(hidden_ref, weights_ref, 2 * units, part_ref, rows)


def ffn_backward(r, rows):
    out_ref, weights_ref, gu_ref, dgu_ref = r.rows_out, r.gates, r.gu, r.dgu
    ways, _, piece = weights_ref.shape
    units = gu_ref.shape[1] // 2
    down_rows = slice(2 * units, 3 * units)
    dh = nt(out_ref[rows, 0:piece], weights_ref[0, down_rows, :])
    for k in range(1, ways):
        dh += nt(out_ref[rows, k * piece : (k + 1) * piece], weights_ref[k, down_rows, :])
    g = gu_ref[rows, :units].astype(F32)
    v = gu_ref[rows, units:].astype(F32)
    sg = sigmoid(g)
    dgu_ref[rows, :units] = (dh * v * sg * (1.0 + g * (1.0 - sg))).astype(B16)
    dgu_ref[rows, units:] = (dh * g * sg).astype(B16)
    multiply_back(
        dgu_ref, weights_ref, 0, 2 * units // piece, r.part, rows, r.rows_ffn, r.gain_ffn
    )


def grad_columns(rows_ref, grad_ref, out_ref, step=512, weigh=None):
    _, ways, half, width = out_ref.shape
    for k in range(ways):
        block = rows_ref[:, 2 * half * k : 2 * half * (k + 1)]
        for first in range(0, width, step):
            last = min(first + step, width)
            value = tn(block, grad_ref[:, first:last])
            if weigh:
                weigh(k, first, last, value)
            value = value.astype(B16)
            out_ref[0, k, :, first:last] = value[:half, :]
            out_ref[1, k, :, first:last] = value[half:, :]


def mixer_columns(cols, members, r):
    _, _, piece = r.mixer.shape
    inner = MixerRows(cols, members).inner
    r.gain_column[...] = jnp.zeros_like(r.gain_column)

    def weigh(k, first, last, value):
        rows = slice(k * piece, (k + 1) * piece)
        if first < cols.q:
            weight = r.mixer[k, inner + first : inner + last, :]
        else:
            weight = r.rest[rows, :LANES]
        r.gain_column[rows, 0:1] += jnp.sum(value * weight.astype(F32), axis=1, keepdims=True)

    grad_columns(r.rows_mix, r.dproj, r.g_cat, piece, weigh)


def grad_rows(lows_ref, back_ref, out_ref):
    _, ways, half, piece = out_ref.shape
    for h in range(2):
        block = lows_ref[:, h * half : (h + 1) * half]
        for k in range(ways):
            out_ref[h, k] = tn(block, back_ref[:, k * piece : (k + 1) * piece]).astype(B16)


DMA = pltpu.SemaphoreType.DMA
MESH = pl.DeviceIdType.MESH
PIPE, DP, TENSOR = "pipe", "dp", "tensor"
PART, SHARED, LAST = "part", "extra", "ffn_part"

BEGIN, SENT, EXTRA, CHUNK, SPREAD, GIVEN, END = -1, 20, 25, 30, 40, 50, 60


class Bag:
    def __init__(self, **entries):
        self.__dict__.update(entries)

    def add(self, other):
        self.__dict__.update(other.__dict__)


def remote(source, target, send, receive, device):
    return pltpu.make_async_remote_copy(
        src_ref=source, dst_ref=target, send_sem=send, recv_sem=receive,
        device_id=device, device_id_type=MESH,
    )


class Helper:
    def __init__(self, when):
        self.when = when
        self.inputs, self.outs, self.scratch = [], [], []
        self.results = None

    @property
    def result(self):
        return self.results[0]


def cross_devices(ways):
    section, place = lax.axis_index(PIPE), lax.axis_index(DP)
    return [{PIPE: 1 - section}] + [{DP: (place + k) % ways} for k in range(1, ways)]


class Few(Helper):
    def __init__(self, ways, shard, when):
        super().__init__(when)
        self.ways = ways
        self.inputs = [shard]
        self.outs = [((2, ways) + shard.shape, F32, pltpu.VMEM)]
        self.scratch = [DMA((1,)), DMA((1,)), DMA((2, ways)), DMA((2, ways)), DMA((1,))]

    def bind(self, r, inputs, outs, scratch):
        (shard,), (few,) = inputs, outs
        r.few = few
        section, place, ways = lax.axis_index(PIPE), lax.axis_index(DP), self.ways
        pair_send, pair_recv, line_send, line_recv, local = scratch
        mine = few.at[section, place]

        def over():
            return remote(shard, mine, pair_send.at[0], pair_recv.at[0], {PIPE: 1 - section})

        def line(layer, k, there):
            block = few.at[layer, there]
            return remote(
                block, block, line_send.at[layer, k], line_recv.at[layer, k], {DP: (place + k) % ways}
            )

        def start():
            over().start()
            own = pltpu.make_async_copy(shard, mine, local.at[0])
            own.start()
            own.wait()

        def spread():
            over().wait_recv()
            for layer in range(2):
                for k in range(1, ways):
                    line(layer, k, place).start()

        def finish():
            for layer in range(2):
                for k in range(1, ways):
                    line(layer, k, (place + ways - k) % ways).wait_recv()
            over().wait_send()
            for layer in range(2):
                for k in range(1, ways):
                    line(layer, k, place).wait_send()

        return [start, spread, finish]


class Cargo(Helper):
    CHUNKS = 4

    def __init__(self, layer, ways, shard, when, members=0, shared=0):
        super().__init__(when)
        self.layer, self.ways, self.rows = layer, ways, shard.shape[0]
        self.members, self.shared = members, shared
        n = self.CHUNKS
        self.first = (self.rows * 2 // 5 + 8 * n) // (16 * n) * (16 * n)
        self.inputs = [shard]
        self.outs = [((ways,) + shard.shape, shard.dtype, pl.ANY)]
        self.scratch = [DMA((n,)), DMA((n,))] + [DMA((ways, n))] * 6 + [DMA((1,))]
        if shared:
            self.outs.append(((members, ways, shared, shard.shape[1]), shard.dtype, pl.ANY))
            self.scratch += [DMA((members,))] * 4 + [DMA((1,))]

    def bind(self, r, inputs, outs, scratch):
        (shard_ref,), out_ref = inputs, outs[0]
        early_send, early_recv, up_send, up_recv, down_send, down_recv, over_send, over_recv, local = scratch[:9]
        section, place = lax.axis_index(PIPE), lax.axis_index(DP)
        partner = {PIPE: 1 - section}
        ways, chunks = self.ways, self.CHUNKS
        sizes = {True: self.first // chunks, False: (self.rows - self.first) // chunks}

        def by_role(step):
            def both():
                pl.when(section == self.layer)(lambda: step(True))
                pl.when(section != self.layer)(lambda: step(False))

            return both

        def part(owner, c):
            return pl.ds((0 if owner else self.first) + c * sizes[owner], sizes[owner])

        def early(c):
            at = part(False, c)
            return remote(
                shard_ref.at[at, :], out_ref.at[place, at, :], early_send.at[c], early_recv.at[c], partner
            )

        def line(owner, up, hop, c):
            at = part(owner, c)
            send, receive = (up_send, up_recv) if up else (down_send, down_recv)
            shard = place - hop if up else place + hop
            source = shard_ref if owner and hop == 0 else out_ref.at[shard]
            return remote(
                source.at[at, :], out_ref.at[shard, at, :], send.at[hop, c], receive.at[hop, c],
                {DP: (place + (1 if up else ways - 1)) % ways},
            )

        def sends(up, hop):
            if up:
                return (place >= hop) & (place < ways - 1)
            return (place < ways - hop) & (place > 0)

        def over(owner, shard, c, own=False):
            at = part(owner, c)
            source = shard_ref if own else out_ref.at[shard]
            return remote(
                source.at[at, :], out_ref.at[shard, at, :], over_send.at[shard, c], over_recv.at[shard, c],
                partner,
            )

        def own_copy():
            return pltpu.make_async_copy(shard_ref, out_ref.at[place], local.at[0])

        def launch(owner, c):
            for up in (True, False):
                pl.when(sends(up, 0))(lambda up=up: line(owner, up, 0, c).start())

        def start(owner):
            if owner:
                for c in range(chunks):
                    early(c).start()
                    launch(True, c)
                for c in range(chunks):
                    over(True, place, c, True).start()
                own_copy().start()

        def spread(c, owner):
            if not owner:
                early(c).wait_recv()
                launch(False, c)

        def hop(count, c, owner):
            for up in (True, False):
                shard = place - count if up else place + count

                @pl.when(shard >= 0 if up else shard < ways)
                def _(up=up, shard=shard):
                    line(owner, up, count - 1, c).wait_recv()
                    if count < ways - 1:
                        pl.when(sends(up, count))(lambda: line(owner, up, count, c).start())
                    over(owner, shard, c).start()

        def wait_over(owner, c):
            for shard in range(ways):

                def wait(shard=shard):
                    block = out_ref.at[shard, part(not owner, c), :]
                    remote(
                        block, block, over_send.at[shard, c], over_recv.at[shard, c], partner
                    ).wait_recv()

                if owner:
                    pl.when(place != shard)(wait)
                else:
                    wait()

        first_waited = 1 if self.shared else 0

        def finish(owner):
            for c in range(chunks):
                if owner or c >= first_waited:
                    wait_over(owner, c)
            for c in range(chunks):
                if owner:
                    early(c).wait_send()
                for count in range(ways - 1):
                    for up in (True, False):
                        pl.when(sends(up, count))(
                            lambda up=up, count=count: line(owner, up, count, c).wait_send()
                        )
                for shard in range(ways):

                    def wait(shard=shard):
                        over(owner, shard, c).wait_send()

                    if owner:
                        wait()
                    else:
                        pl.when(place != shard)(wait)
            if owner and not self.shared:
                own_copy().wait()

        steps = [start]
        steps += [functools.partial(spread, c) for c in range(chunks)]
        steps += [functools.partial(hop, count, c) for count in range(1, ways) for c in range(chunks)]
        steps = [by_role(step) for step in steps]
        if not self.shared:
            return steps + [by_role(finish)]

        assert self.shared <= sizes[True]
        all_ref = outs[1]
        give_send, give_recv, far_send, far_recv, keep = scratch[9:]
        me = lax.axis_index(TENSOR)
        pairs = self.members // 2
        mine, side = me // 2, me % 2
        sibling = 2 * mine + 1 - side
        share = out_ref.at[:, pl.ds(0, self.shared), :]

        def far(count):
            return 2 * ((mine + count) % pairs) + side

        def across(count):
            return 2 * ((mine + count) % pairs) + 1 - side

        def give(count):
            block = all_ref.at[far(count)]
            return remote(
                share if count == 0 else block, block, give_send.at[count], give_recv.at[count],
                {TENSOR: sibling},
            )

        def send_far(count, slot):
            return remote(
                share, all_ref.at[me], far_send.at[count], far_recv.at[slot], {TENSOR: far(count)}
            )

        def own_share():
            return pltpu.make_async_copy(share, all_ref.at[me], keep.at[0])

        def share_out():
            pl.when(section != self.layer)(lambda: wait_over(False, 0))
            pl.when(section == self.layer)(lambda: own_copy().wait())
            for count in range(1, pairs):
                send_far(count, pairs - count).start()
            give(0).start()
            own_share().start()

        def pass_on():
            for count in range(1, pairs):
                send_far(count, count).wait_recv()
                give(count).start()

        def finish_all():
            by_role(finish)()
            for count in range(pairs):
                block = all_ref.at[sibling if count == 0 else across(count)]
                remote(
                    block, block, give_send.at[count], give_recv.at[count], {TENSOR: sibling}
                ).wait_recv()
            for count in range(pairs):
                give(count).wait_send()
                if count:
                    send_far(count, pairs - count).wait_send()
            own_share().wait()

        return steps + [share_out, pass_on, finish_all]


class Haul(Helper):
    def __init__(self, layer, ways, sources, specs, when, swap=True, line=True):
        super().__init__(when)
        self.layer, self.ways, self.sources, self.swap, self.line = layer, ways, sources, swap, line
        self.count = len(specs)
        self.order = sorted(range(1, ways), key=lambda k: abs(2 * k - ways)) + [0]
        for (_, blocks, rows, columns), dtype in specs:
            block = pltpu.VMEM((blocks, rows, columns), dtype)
            if swap and not line:
                self.outs.append(((blocks, rows, columns), dtype, pltpu.VMEM))
            if line:
                self.outs.append(((2, rows, columns), dtype, pltpu.VMEM))
            if swap:
                self.scratch += [block, DMA((ways,)), DMA((ways,))]
            if swap and line:
                self.scratch.append(block)
            if line:
                self.scratch += [block, pltpu.VMEM((rows, columns), dtype), DMA((ways,)), DMA((ways,))]
                self.scratch += [DMA((1,)), DMA((1,))]

    def bind(self, r, inputs, outs, scratch):
        section, place, ways = lax.axis_index(PIPE), lax.axis_index(DP), self.ways
        partner = {PIPE: 1 - section}
        scratch = list(scratch)
        arrays = []
        for source, out in zip(self.sources, outs):
            a = Bag(out=out)
            a.sent, a.read = source(r)
            a.sums = a.read
            if self.swap:
                a.swapped, a.swap_send, a.swap_recv = [scratch.pop(0) for _ in range(3)]
                a.sums = scratch.pop(0) if self.line else out
                a.sums_sent = a.sums
            else:
                a.sums_sent = a.sent
            if self.line:
                a.arrived, a.result, a.line_send, a.line_recv, a.last_send, a.last_recv = [
                    scratch.pop(0) for _ in range(6)
                ]
            arrays.append(a)

        def to(k):
            return (place + k) % ways

        def swap(a, k):
            return remote(
                a.sent.at[1 - section, to(k)], a.swapped.at[to(k)], a.swap_send.at[k], a.swap_recv.at[k],
                partner,
            )

        def line(a, k):
            return remote(
                a.sums_sent.at[to(k)], a.arrived.at[k], a.line_send.at[k], a.line_recv.at[k], {DP: to(k)}
            )

        def last(a):
            return remote(
                a.result, a.out.at[1 - self.layer], a.last_send.at[0], a.last_recv.at[0], partner
            )

        def start():
            for k in self.order:
                for a in arrays:
                    if self.swap:
                        swap(a, k).start()
                    elif k:
                        line(a, k).start()

        def fold(k):
            def step():
                for a in arrays:
                    swap(a, k).wait_recv()
                    total = a.read[section, to(k)].astype(F32) + a.swapped[to(k)].astype(F32)
                    a.sums[to(k)] = total.astype(a.sums.dtype)
                    if k and self.line:
                        line(a, k).start()

            return step

        def reduce():
            for a in arrays:
                total = a.sums[place].astype(F32)
                for k in range(1, ways):
                    line(a, k).wait_recv()
                    total += a.arrived[k].astype(F32)
                a.result[...] = total.astype(a.out.dtype)

            @pl.when(section == self.layer)
            def _():
                for a in arrays:
                    a.out[self.layer] = a.result[...]

            @pl.when(section != self.layer)
            def _():
                for a in arrays:
                    last(a).start()

        def finish():
            if self.line:

                @pl.when(section == self.layer)
                def _():
                    for a in arrays:
                        last(a).wait_recv()

                @pl.when(section != self.layer)
                def _():
                    for a in arrays:
                        last(a).wait_send()
                        a.out[...] = jnp.zeros_like(a.out)

            for k in self.order:
                for a in arrays:
                    if self.swap:
                        swap(a, k).wait_send()
                    if k and self.line:
                        line(a, k).wait_send()

        steps = [start]
        if self.swap:
            steps += [fold(k) for k in self.order]
        if self.line:
            steps.append(reduce)
        return steps + [finish]


class Straight(Helper):
    def __init__(self, layer, ways, source, spec, when):
        super().__init__(when)
        self.layer, self.ways, self.source = layer, ways, source
        (_, blocks, rows, columns), dtype = spec
        result = (2, rows, columns)
        self.outs = [(result, dtype, pltpu.VMEM)]
        self.scratch = [pltpu.VMEM((blocks,) + result, dtype), pltpu.VMEM(result, dtype)]
        self.scratch += [pltpu.VMEM(result, dtype), DMA((2, ways)), DMA((2, ways)), DMA((1,)), DMA((1,))]

    def bind(self, r, inputs, outs, scratch):
        sent, read = self.source(r)
        (out,) = outs
        arrived, result, handed, line_send, line_recv, last_send, last_recv = scratch
        section, place, ways = lax.axis_index(PIPE), lax.axis_index(DP), self.ways
        order = sorted(range(1, ways), key=lambda k: abs(2 * k - ways))

        def line(half, k):
            to = (place + k) % ways
            return remote(
                sent.at[half, to], arrived.at[k, half], line_send.at[half, k], line_recv.at[half, k], {DP: to}
            )

        def last():
            return remote(result, handed, last_send.at[0], last_recv.at[0], {PIPE: 1 - section})

        def start():
            for k in order:
                for half in range(2):
                    line(half, k).start()

        def reduce():
            for half in range(2):
                total = read[half, place].astype(F32)
                for k in range(1, ways):
                    line(half, k).wait_recv()
                    total += arrived[k, half].astype(F32)
                result[half] = total.astype(result.dtype)

            @pl.when(section != self.layer)
            def _():
                last().start()

        def finish():
            @pl.when(section == self.layer)
            def _():
                last().wait_recv()
                out[...] = (result[...].astype(F32) + handed[...].astype(F32)).astype(out.dtype)

            @pl.when(section != self.layer)
            def _():
                last().wait_send()
                out[...] = jnp.zeros_like(out)

            for k in order:
                for half in range(2):
                    line(half, k).wait_send()

        return [start, reduce, finish]


class Place(Helper):
    PIECES = 4

    def __init__(self, source, shape, late, when):
        super().__init__(when)
        self.source, self.late, self.size = source, late, shape[0] // self.PIECES
        self.outs = [((2,) + shape, B16, pl.ANY)]
        self.scratch = [DMA((self.PIECES,)), DMA((self.PIECES,)), DMA((self.PIECES,))]

    def bind(self, r, inputs, outs, scratch):
        (out,) = outs
        send, receive, local = scratch
        section = lax.axis_index(PIPE)
        rows = self.source(r)

        def over(layer, c):
            at = pl.ds(c * self.size, self.size)
            return remote(
                rows[layer].at[at, :], out.at[1 - layer, at, :], send.at[c], receive.at[c], {PIPE: 1 - section}
            )

        def own(layer, c):
            at = pl.ds(c * self.size, self.size)
            return pltpu.make_async_copy(rows[layer].at[at, :], out.at[layer, at, :], local.at[c])

        def hand(layer, c):
            pl.when(section != layer)(lambda: over(layer, c).start())
            pl.when(section == layer)(lambda: own(layer, c).start())

        def early():
            for c in range(self.PIECES):
                hand(1 - self.late, c)

        def finish():
            for c in range(self.PIECES):
                for layer in range(2):

                    @pl.when(section == layer)
                    def _(layer=layer):
                        over(1 - layer, c).wait()
                        own(layer, c).wait()

        return [early] + [functools.partial(hand, self.late, c) for c in range(self.PIECES)] + [finish]


class Settle(Helper):
    def __init__(self, layer, source, shape, when):
        super().__init__(when)
        self.layer, self.source = layer, source
        self.outs = [((2,) + shape, B16, pl.ANY)]
        self.scratch = [DMA((1,)), DMA((1,)), DMA((1,))]

    def bind(self, r, inputs, outs, scratch):
        (out,) = outs
        send, receive, local = scratch
        section = lax.axis_index(PIPE)
        rows = self.source(r)
        owner = section == self.layer

        def over():
            return remote(
                rows, out.at[1 - self.layer], send.at[0], receive.at[0], {PIPE: 1 - section}
            )

        def own():
            return pltpu.make_async_copy(rows, out.at[self.layer], local.at[0])

        def start():
            pl.when(section != self.layer)(lambda: over().start())
            pl.when(owner)(lambda: own().start())

        def finish():
            @pl.when(section != self.layer)
            def _():
                over().wait_send()

            @pl.when(owner)
            def _():
                over().wait_recv()
                own().wait()

        return [start, finish]


class Members:
    def __init__(self, count):
        self.pairs = count // 2
        self.me = lax.axis_index(TENSOR)
        self.mine, self.side = self.me // 2, self.me % 2
        self.sibling = 2 * self.mine + 1 - self.side

    def far(self, k):
        return 2 * ((self.mine + k) % self.pairs) + self.side

    def across(self, k):
        return 2 * ((self.mine + k) % self.pairs) + 1 - self.side

    def order(self):
        others = range(1, self.pairs)
        return [[self.across(k) for k in others], [self.far(k) for k in others], [self.sibling], [self.me]]


def member_copy(source, target, send, receive, member):
    return remote(source, target, send, receive, {TENSOR: member})


class Scatter:
    @staticmethod
    def scratch(members, rows, width, pieces):
        pairs = members // 2
        others = max(pairs - 1, 1)
        return [
            pltpu.VMEM((pairs, rows, width), B16),
            pltpu.VMEM((others, rows, width), B16),
            pltpu.VMEM((others, rows, width), B16),
            DMA((pairs, pieces)), DMA((pairs, pieces)), DMA((others, pieces)), DMA((others, pieces)),
        ]

    def __init__(self, part_ref, members, rows, pieces, scratch):
        self.part, self.at, self.rows, self.pieces = part_ref, members, rows, pieces
        self.size = rows // pieces
        self.pair_in, self.far_out, self.far_in = scratch[:3]
        self.pair_send, self.pair_recv, self.far_send, self.far_recv = scratch[3:]

    def rows_of(self, member, c):
        return pl.ds(pl.multiple_of(member * self.rows + c * self.size, self.size), self.size)

    def chunk(self, c):
        return pl.ds(c * self.size, self.size)

    def to_pair(self, k, c):
        member = self.at.across(k) if k else self.at.sibling
        return member_copy(
            self.part.at[self.rows_of(member, c), :], self.pair_in.at[k, self.chunk(c), :],
            self.pair_send.at[k, c], self.pair_recv.at[k, c], self.at.sibling,
        )

    def to_far(self, k, c, slot):
        return member_copy(
            self.far_out.at[k - 1, self.chunk(c), :], self.far_in.at[slot - 1, self.chunk(c), :],
            self.far_send.at[k - 1, c], self.far_recv.at[slot - 1, c], self.at.far(k),
        )

    def send_across(self):
        for c in range(self.pieces):
            for k in range(1, self.at.pairs):
                self.to_pair(k, c).start()

    def send_far(self):
        for c in range(self.pieces):
            for k in range(1, self.at.pairs):
                self.to_pair(k, c).wait_recv()
                total = self.part[self.rows_of(self.at.far(k), c), :].astype(F32)
                total += self.pair_in[k, self.chunk(c), :].astype(F32)
                self.far_out[k - 1, self.chunk(c), :] = total.astype(B16)
                self.to_far(k, c, self.at.pairs - k).start()

    def send_sibling(self):
        for c in range(self.pieces):
            self.to_pair(0, c).start()

    def receive(self, c):
        self.to_pair(0, c).wait_recv()
        total = self.part[self.rows_of(self.at.me, c), :].astype(F32)
        total += self.pair_in[0, self.chunk(c), :].astype(F32)
        for k in range(1, self.at.pairs):
            self.to_far(k, c, k).wait_recv()
            total += self.far_in[k - 1, self.chunk(c), :].astype(F32)
        return total

    def finish(self):
        for c in range(self.pieces):
            for k in range(self.at.pairs):
                self.to_pair(k, c).wait_send()
                if k:
                    self.to_far(k, c, self.at.pairs - k).wait_send()


def exchange_kernel(plan, *refs):
    refs = list(refs)

    def take(count):
        return [refs.pop(0) for _ in range(count)]

    r = Bag()
    held = {name: take(1)[0] for name in plan.inputs}
    r.raw = Bag(**held)
    helper_inputs = [take(len(h.inputs)) for h in plan.helpers]
    targets = {name: take(1)[0] for name in plan.outs}
    gathered = take(len(plan.gathers))
    helper_outs = [take(len(h.outs)) for h in plan.helpers]
    loaded = [name for name in plan.inputs if plan.need(name) is not None]
    for name in loaded + plan.outs + plan.scratch:
        setattr(r, name, take(1)[0])
    load_sem, store_sem = take(2)
    at = Members(plan.members)
    pairs, pieces = at.pairs, plan.pieces
    scatters = {}
    for name, (_, count, _) in plan.scatters.items():
        if name not in plan.inputs:
            setattr(r, name, take(1)[0])
        scatters[name] = Scatter(getattr(r, name), at, plan.rows, count, take(7))
    if plan.gathers:
        mine_refs = take(len(plan.gathers))
        give_send, give_recv, spread_send, spread_recv, keep_sem = take(5)
    helpers = []
    for h, inputs, outs in zip(plan.helpers, helper_inputs, helper_outs):
        helpers.append((h.bind(r, inputs, outs, take(len(h.scratch))), h.when))
    size = plan.rows // pieces

    def rows_of(member, c):
        return pl.ds(pl.multiple_of(member * plan.rows + c * size, size), size)

    def chunk(c):
        return pl.ds(c * size, size)

    loads = {}
    for i, name in enumerate(sorted(loaded, key=plan.need)):
        loads[name] = pltpu.make_async_copy(held[name], getattr(r, name), load_sem.at[i])
        loads[name].start()

    def arrive(stage):
        for name in list(loads):
            if plan.need(name) <= stage:
                loads.pop(name).wait()

    stores = []

    def flush(stage):
        for i, name in enumerate(plan.outs):
            if plan.done(name) == stage:
                store = pltpu.make_async_copy(getattr(r, name), targets[name], store_sem.at[i])
                store.start()
                stores.append(store)

    def point(stage):
        for steps, when in helpers:
            count = len(steps) - 1 if stage == END else when.get(stage, 0)
            for _ in range(min(count, len(steps))):
                steps.pop(0)()
        if stage == END:
            for steps, _ in helpers:
                while steps:
                    steps.pop(0)()
        flush(stage)

    def run_fill(i):
        if i < len(plan.fills):
            plan.fills[i](r)

    barrier = pltpu.get_barrier_semaphore()
    greeted = [{TENSOR: at.sibling}] + [{TENSOR: at.far(k)} for k in range(1, pairs)]
    if helpers:
        greeted += cross_devices(plan.ways)
    for device in greeted:
        pl.semaphore_signal(barrier, inc=1, device_id=device, device_id_type=MESH)
    pl.semaphore_wait(barrier, len(greeted))

    arrive(BEGIN)
    point(BEGIN)
    for i, phase in enumerate(plan.phases(r, at.order()) if plan.phases else []):
        arrive(i)
        phase()
        for name, (_, _, ready) in plan.scatters.items():
            for last, send in zip(
                ready, (scatters[name].send_across, scatters[name].send_far, scatters[name].send_sibling)
            ):
                if last == i:
                    send()
        point(i)
    arrive(SENT)
    if plan.phases:
        run_fill(0)
    point(SENT)
    if plan.extra_work:
        plan.extra_work(r, scatters)
        point(EXTRA)

    given, spreads, keeps = {}, {}, []
    for c in range(pieces):
        total = None
        if plan.phases:
            for name in plan.scatters:
                total = scatters[name].receive(c)
                break
        results = plan.work(r, c, chunk(c), total)
        for g, rows_ref in enumerate(gathered):
            own = mine_refs[g].at[chunk(c), :]
            there = rows_ref.at[rows_of(at.me, c), :]
            mine_refs[g][chunk(c), :] = results[g]
            for k in range(1, pairs):
                spreads[g, k, c] = member_copy(
                    own, there, spread_send.at[g, k - 1, c], spread_recv.at[g, pairs - k - 1, c], at.far(k)
                )
                spreads[g, k, c].start()
            given[g, 0, c] = member_copy(
                own, there, give_send.at[g, 0, c], give_recv.at[g, 0, c], at.sibling
            )
            given[g, 0, c].start()
            keeps.append(pltpu.make_async_copy(own, there, keep_sem.at[g, c]))
            keeps[-1].start()
        point(CHUNK + c)
    run_fill(1)
    point(SPREAD)
    for g, rows_ref in enumerate(gathered):
        for c in range(pieces):
            for k in range(1, pairs):
                block = rows_ref.at[rows_of(at.far(k), c), :]
                member_copy(
                    block, block, spread_send.at[g, k - 1, c], spread_recv.at[g, k - 1, c], at.far(k)
                ).wait_recv()
                given[g, k, c] = member_copy(
                    block, block, give_send.at[g, k, c], give_recv.at[g, k, c], at.sibling
                )
                given[g, k, c].start()
    point(GIVEN)
    for g, rows_ref in enumerate(gathered):
        for c in range(pieces):
            for k in range(pairs):
                block = rows_ref.at[rows_of(at.across(k) if k else at.sibling, c), :]
                member_copy(
                    block, block, give_send.at[g, k, c], give_recv.at[g, k, c], at.sibling
                ).wait_recv()
        for c in range(pieces):
            for k in range(pairs):
                given[g, k, c].wait_send()
            for k in range(1, pairs):
                spreads[g, k, c].wait_send()
    for scatter in scatters.values():
        scatter.finish()
    arrive(END)
    point(END)
    for store in stores + keeps:
        store.wait()


def exchange(
    name, number, members, ways, rows, depth, work, inputs, outs=None, need=None, done=None, scratch=None,
    phases=None, fills=(), scatters=None, extra_work=None, gathers=None, helpers=(), pieces=4,
):
    pairs = members // 2
    others = max(pairs - 1, 1)
    outs, scratch, need, done = outs or {}, scratch or {}, need or {}, done or {}
    gathers, scatters = gathers or [], scatters or {}
    hbm, vmem = pl.BlockSpec(memory_space=pl.ANY), pl.BlockSpec(memory_space=pltpu.VMEM)
    plan = Bag(
        inputs=list(inputs), outs=list(outs), scratch=list(scratch), gathers=gathers, helpers=list(helpers),
        members=members, ways=ways, rows=rows, pieces=pieces, scatters=scatters, extra_work=extra_work,
        phases=phases, fills=list(fills), work=work,
        need=lambda n: need.get(n, 0 if phases else BEGIN), done=lambda n: done.get(n, END),
    )
    staging = [pltpu.VMEM(a.shape, a.dtype) for n, a in inputs.items() if plan.need(n) is not None]
    staging += [pltpu.VMEM(*spec) for spec in outs.values()]
    staging += list(scratch.values())
    staging += [DMA((max(len(inputs), 1),)), DMA((max(len(outs), 1),))]
    for part, (width, chunks, _) in scatters.items():
        if part not in inputs:
            staging.append(pltpu.VMEM((members * rows, width), B16))
        staging += Scatter.scratch(members, rows, width, chunks)
    count = len(gathers)
    if count:
        staging += [pltpu.VMEM((rows, depth), B16)] * count
        staging += [
            DMA((count, pairs, pieces)), DMA((count, pairs, pieces)),
            DMA((count, others, pieces)), DMA((count, others, pieces)), DMA((count, pieces)),
        ]
    operands = list(inputs.values())
    shapes = [jax.ShapeDtypeStruct(*spec) for spec in outs.values()]
    shapes += [jax.ShapeDtypeStruct((members * rows, depth), B16)] * count
    spaces = [hbm] * len(shapes)
    for h in helpers:
        operands += h.inputs
        shapes += [jax.ShapeDtypeStruct(shape, dtype) for shape, dtype, _ in h.outs]
        spaces += [pl.BlockSpec(memory_space=space) for _, _, space in h.outs]
        staging += h.scratch
    results = pl.pallas_call(
        functools.partial(exchange_kernel, plan),
        out_shape=shapes,
        in_specs=[hbm] * len(operands),
        out_specs=spaces,
        scratch_shapes=staging,
        compiler_params=pltpu.CompilerParams(
            collective_id=number, has_side_effects=True, vmem_limit_bytes=VMEM_LIMIT
        ),
        cost_estimate=pl.CostEstimate(
            flops=20_000_000_000, bytes_accessed=50_000_000, transcendentals=0
        ),
        name=name,
    )(*operands)
    results = list(results)
    got = {n: results.pop(0) for n in list(outs) + list(gathers)}
    for h in helpers:
        h.results = [results.pop(0) for _ in h.outs]
    return Bag(**got)


def rms(rows, gain):
    scale = lax.rsqrt(jnp.mean(rows * rows, axis=-1, keepdims=True) + EPS)
    return rows * scale * gain


def rms_back(rows, gain, grad):
    scale = lax.rsqrt(jnp.mean(rows * rows, axis=-1, keepdims=True) + EPS)
    scaled = gain * grad
    mean = jnp.mean(scaled * rows, axis=-1, keepdims=True)
    return scale * scaled - rows * (scale * scale * scale * mean)


def gain_of(r, layer, row):
    ways = r.few.shape[1]
    return jnp.concatenate([r.few[layer, k, row : row + 1, :] for k in range(ways)], axis=1)


def layer_input(r, layer, at):
    if layer == 0:
        return r.acts_in[lax.axis_index(PIPE), at, :].astype(F32)
    return r.x[at, :].astype(F32)


def layer_cotangent(r, layer, at):
    if layer == 1:
        return r.out_grad[lax.axis_index(PIPE), at, :]
    return r.cotangent[at, :]


def work_first(r, c, at, total):
    return rms(layer_input(r, 0, at), gain_of(r, 0, 0)).astype(B16), layer_cotangent(r, 1, at)


def work_mid(layer, r, c, at, total):
    residual = layer_input(r, layer, at) + total
    r.residual[at, :] = residual
    return (rms(residual, gain_of(r, layer, 1)).astype(B16),)


def work_turn(r, c, at, total):
    out = (r.residual[at, :] + total).astype(B16)
    r.x[at, :] = out
    return (rms(out.astype(F32), gain_of(r, 1, 0)).astype(B16),)


def work_back_ffn(layer, r, c, at, total):
    residual = r.residual[at, :]
    grad = layer_cotangent(r, layer, at).astype(F32) + rms_back(
        residual, gain_of(r, layer, 1), total
    )
    r.d_residual[at, :] = grad
    return (grad.astype(B16),)


def work_back_mix(layer, r, c, at, total):
    step = rms_back(layer_input(r, layer, at), gain_of(r, layer, 0), total)
    grad = (r.d_residual[at, :] + step).astype(B16)
    r.x_grad[at, :] = grad
    return (grad,)


def work_shared(r, scatters):
    total = scatters[SHARED].receive(0)
    _, ways, block, _ = r.shared.shape
    for j in range(2 * ways):
        r.shared[j // ways, j % ways] = total[j * block : (j + 1) * block, :].astype(r.shared.dtype)


def work_last(r, scatters):
    r.last[...] = (r.residual[...] + scatters[LAST].receive(0)).astype(B16)
    work_shared(r, scatters)


def widen(block, axis, size):
    missing = size - block.shape[axis]
    if missing == 0:
        return block
    pads = [(0, 0)] * block.ndim
    pads[axis] = (0, missing)
    return jnp.pad(block, pads)


def on_device(
    acts_in, out_grad, mix_gain, w_mixer_in, w_query, w_shared, w_step, a_log, dt_bias, d_skip,
    w_mamba_out, w_attn_out, ffn_gain, w_gate_up, w_down,
):
    section = lax.axis_index(PIPE)
    member = lax.axis_index(TENSOR)
    members = lax.axis_size(TENSOR)
    dp = lax.axis_size(DP)
    heads = a_log.shape[1]
    real = heads * HD
    width = (heads + heads % 2) * HD
    q_real = w_query.shape[2]
    cols = Cols(width)
    units = w_gate_up.shape[3]
    rows, depth = acts_in.shape[1:]
    length = rows * members
    piece = depth // dp
    wide = cols.total - cols.b

    at_row = MixerRows(cols, members)
    q_heads = q_real // HD
    inner = jnp.concatenate(
        [widen(w_mixer_in[0, :, 0], 1, width), widen(w_mixer_in[0, :, 1], 1, width)], axis=1
    )
    share = lax.dynamic_slice_in_dim(w_shared[0], member * (piece // members), piece // members, 0)
    share = jnp.concatenate([share[:, at : at + LANES] for at in range(0, 4 * LANES, LANES)], axis=0)
    mixer_shard = jnp.concatenate(
        [fold_lanes(share)(piece), fold_lanes(widen(w_query[0], 1, LANES))(piece)]
        + [inner[:, at : at + piece] for at in range(0, 2 * width, piece)]
        + [widen(w_mamba_out[0], 0, width), widen(w_attn_out[0], 0, LANES)],
        axis=0,
    )
    steps = lax.dynamic_slice_in_dim(w_step[0], member * heads, heads, 1).T.astype(F32)
    ffn_shard = jnp.concatenate(
        [w_gate_up[0, :, j, at : at + piece] for j in range(2) for at in range(0, units, piece)]
        + [w_down[0]],
        axis=0,
    )
    few_shard = jnp.concatenate(
        [
            mix_gain.astype(F32), ffn_gain.astype(F32),
            widen(widen(jnp.concatenate([a_log, dt_bias, d_skip]), 1, piece), 0, 6),
            widen(steps, 0, 8),
        ],
        axis=0,
    )

    def run(name, number, work, inputs, outs, **more):
        return exchange(name, number, members, dp, rows, depth, work, inputs, outs, **more)

    half = piece // 2
    low_units = width + LANES
    block32, block16 = ((rows, depth), F32), ((rows, depth), B16)
    core_keeps = dict(
        proj=((length, cols.step), B16),
        step=((length, LANES), F32),
        y=((length, width), B16),
        lows=((length, low_units), B16),
        states=((length // STEP, NS, width), B16),
        lse=((length // TILE, 8, 2 * TILE), F32),
    )
    ffn_keeps = dict(gu=((length, 2 * units), B16), hidden=((length, units), B16))
    gu_spec, down_spec = ((2, dp, half, 2 * units), B16), ((2, dp, units // 2, piece), B16)
    cat_spec, out_spec = ((2, dp, half, cols.b), B16), ((2, dp, low_units // 2, piece), B16)
    shared_spec = ((2, dp, half // members, wide), B16 if half // members % 16 == 0 else F32)
    gain_row = ((8, depth), F32)
    fills_ffn = [
        lambda r: grad_columns(r.rows_ffn, r.dgu, r.g_gu),
        lambda r: grad_rows(r.hidden, r.rows_out, r.g_down),
    ]
    fill_cat = lambda r: mixer_columns(cols, members, r)
    fill_out = lambda r: grad_rows(r.lows, r.rows_back, r.g_out)

    load = Cargo(
        0, dp, mixer_shard,
        {BEGIN: 1, SENT: 2, CHUNK: 1, CHUNK + 1: 1, CHUNK + 2: 2, CHUNK + 3: 2, SPREAD: 2, GIVEN: 4},
        members, at_row.shared,
    )
    few = Few(dp, few_shard, {BEGIN: 2, SENT: 1})
    got = run(
        "first", 0, work_first, dict(acts_in=acts_in, out_grad=out_grad), {},
        gathers=dict(rows_mix=0, rows_out=0), helpers=[few, load],
    )
    few = few.result
    first = Bag(rows_mix=got.rows_mix, mixer=load.results[0], shared_w=load.results[1], acts_in=acts_in)
    second = Bag(rows_out=got.rows_out, out_grad=out_grad)
    for layer, k in enumerate((first, second)):
        x = dict(acts_in=acts_in) if layer == 0 else dict(x=second.x)
        load = Cargo(
            layer, dp, ffn_shard,
            {
                BEGIN: 1, 0: 1, 1: 1, 2: 1, 3: 2, 4: 1, 5: 1, 6: 2, 7: 2, SENT: 1, CHUNK: 1, CHUNK + 1: 1,
                CHUNK + 2: 1, SPREAD: 2,
            },
        )
        k.add(
            run(
                f"mixer{layer}", 1 + layer, functools.partial(work_mid, layer),
                dict(x, few=few, rows_mix=k.rows_mix, mixer=k.mixer, shared_w=k.shared_w),
                dict(core_keeps, residual=block32, rest=((depth, 6 * LANES), B16)),
                need=dict({n: SENT for n in x}, rows_mix=1),
                done=dict(rest=0, proj=1, step=1, y=3, states=3, lows=7, lse=7, residual=CHUNK + 3),
                scratch=dict(state=pltpu.VMEM((NS, width), F32)),
                phases=functools.partial(core_fwd_phases, cols, members, layer, q_heads),
                scatters={PART: (depth, 4, (4, 5, 6))}, gathers=dict(rows_ffn=0), helpers=[load],
            )
        )
        k.gates = load.result
        if layer == 0:
            load = Cargo(
                1, dp, mixer_shard,
                {
                    BEGIN: 1, 1: 1, 3: 1, SENT: 2, CHUNK: 2, CHUNK + 1: 1, CHUNK + 2: 1, CHUNK + 3: 1, SPREAD: 2,
                    GIVEN: 3,
                },
                members, at_row.shared,
            )
            got = run(
                "turn", 3, work_turn,
                dict(residual=k.residual, few=few, rows_ffn=k.rows_ffn, gates=k.gates),
                dict(ffn_keeps, x=block16),
                need=dict(residual=SENT, few=SENT), done=dict(gu=3, hidden=3, x=CHUNK + 3),
                phases=lambda r, order: by_blocks(order, rows, lambda at, m: ffn_forward(r, at, r.part)),
                scatters={PART: (depth, 4, (0, 1, 2))}, gathers=dict(rows_mix=0), helpers=[load],
            )
            k.gu, k.hidden = got.gu, got.hidden
            second.rows_mix, second.x = got.rows_mix, got.x
            second.mixer, second.shared_w = load.results

    def clear_gain(r):
        r.gain_ffn[...] = jnp.zeros_like(r.gain_ffn)

    def ffn_both(r, at, m):
        ffn_forward(r, at, r.ffn_part)
        ffn_backward(r, at)

    def ffn_both_phases(r, order):
        clear_gain(r)
        return by_blocks(order, rows, functools.partial(ffn_both, r))

    def ffn_back_phases(r, order):
        clear_gain(r)
        return by_blocks(order, rows, lambda at, m: ffn_backward(r, at))

    second.add(
        run(
            "ffn1", 4, functools.partial(work_back_ffn, 1),
            dict(
                out_grad=out_grad, residual=second.residual, few=few, rows_ffn=second.rows_ffn,
                rows_out=second.rows_out, gates=second.gates,
            ),
            dict(
                gain_ffn=gain_row, g_gu=gu_spec, g_down=down_spec, d_residual=block32,
                ffn_part=((length, depth), B16),
            ),
            need=dict(out_grad=SENT, residual=SENT, few=SENT),
            done=dict(ffn_part=3, gain_ffn=3, g_gu=SENT, d_residual=CHUNK + 3, g_down=SPREAD),
            scratch=dict(
                **{n: pltpu.VMEM(*spec) for n, spec in ffn_keeps.items()},
                dgu=pltpu.VMEM((length, 2 * units), B16),
            ),
            phases=ffn_both_phases,
            scatters={PART: (depth, 4, (0, 1, 2))}, fills=fills_ffn, gathers=dict(rows_back=0),
        )
    )

    core_scratch = dict(
        dproj=pltpu.VMEM((length, cols.total), B16),
        heads=pltpu.VMEM((8, LANES), F32),
        dcore=pltpu.VMEM((length, low_units), B16),
        grad_state=pltpu.VMEM((NS, width), F32),
        skip_sum=pltpu.VMEM((STEP, width), F32),
        dk_sum=pltpu.VMEM((length, LANES), F32),
        dv_sum=pltpu.VMEM((length, LANES), F32),
        folded=pltpu.VMEM((length, wide), B16),
        gain_column=pltpu.VMEM((depth, LANES), F32),
        staged=pltpu.VMEM((depth, wide), F32),
    )

    def core_inputs(k):
        return dict(
            few=few, rows_mix=k.rows_mix, mixer=k.mixer, rows_back=k.rows_back, d_residual=k.d_residual,
            gain_ffn=k.gain_ffn, proj=k.proj, step=k.step, y=k.y, lows=k.lows, states=k.states,
            lse=k.lse, rest=k.rest,
        )

    core_need = dict(
        lows=1, proj=2, lse=2, few=3, step=3, y=3, states=3, rows_mix=4, rest=4, gain_ffn=5, g_gu=2, g_down=1,
        d_residual=SENT, x=SENT, acts_in=SENT,
    )

    def core_phases(layer, r, order):
        return core_bwd_phases(cols, layer, members, (q_heads, heads), r, order)

    def from_input(pick):
        return lambda r: (pick(r.raw), pick(r))

    def from_kernel(pick):
        return lambda r: (pick(r), pick(r))

    take_gu, take_down = (lambda r: r.g_gu), (lambda r: r.g_down)
    take_cat, take_out, take_shared = (lambda r: r.g_cat), (lambda r: r.g_out), (lambda r: r.shared)

    first_acts = Settle(0, lambda r: r.raw.x, (rows, depth), {SENT: 1})
    def back_phases(layer, r, order):
        into, attend, scan, shared, *back = core_phases(layer, r, order)
        return [into, lambda: fill_out(r), attend, scan, lambda: fill_cat(r), shared] + back

    back_scatters = {PART: (depth, 4, (6, 7, 8)), SHARED: (wide, 1, (5, 6, 5))}
    hauls = [
        Haul(
            1, dp, [from_input(take_gu), from_input(take_down)], [gu_spec, down_spec],
            {BEGIN: 1, 2: 1, 3: 1, 4: 1, SENT: 1, CHUNK + 3: 1},
        ),
        Straight(1, dp, from_kernel(take_out), out_spec, {1: 1, SENT: 1}),
        Haul(
            1, dp, [from_kernel(take_cat)], [cat_spec], {4: 1, CHUNK: 1, CHUNK + 1: 1, CHUNK + 2: 1, CHUNK + 3: 1}, line=False
        ),
    ]
    inner = dict(g_cat=pltpu.VMEM(*cat_spec), g_out=pltpu.VMEM(*out_spec))
    got = run(
        "back1", 5, functools.partial(work_back_mix, 1),
        dict(
            core_inputs(second), x=second.x, g_gu=second.g_gu, g_down=second.g_down, ffn_part=second.ffn_part,
            residual=second.residual,
        ),
        dict(x_grad=block16, shared=shared_spec, last=block16),
        need=dict(core_need, residual=SENT),
        done=dict(x_grad=CHUNK + 3, shared=EXTRA, last=EXTRA),
        scratch=dict(core_scratch, **inner), phases=functools.partial(back_phases, 1),
        scatters=dict(back_scatters, ffn_part=(depth, 1, (0, 1, 0))), extra_work=work_last, gathers=dict(rows_out=0), helpers=hauls + [first_acts],
    )
    second.add(got)
    cat_sums = hauls[2].result
    second.sums = hauls[0].results + hauls[1].results

    hauls = [
        Haul(
            1, dp, [from_input(lambda r: r.cat_sums)], [cat_spec], {BEGIN: 1, CHUNK + 3: 1}, swap=False
        ),
        Haul(
            1, dp, [from_input(take_shared)], [shared_spec], {BEGIN: 1, 3: 1, SENT: 2, CHUNK + 1: 1, GIVEN: 1}
        ),
        Haul(
            0, dp, [from_kernel(take_gu)], [gu_spec], {SENT: 1, CHUNK + 3: 1, SPREAD: 1, GIVEN: 1},
            line=False,
        ),
    ]
    got = run(
        "ffn0", 6, functools.partial(work_back_ffn, 0),
        dict(
            cotangent=second.x_grad, residual=first.residual, few=few, rows_ffn=first.rows_ffn,
            rows_out=second.rows_out, gates=first.gates, gu=first.gu, hidden=first.hidden,
            cat_sums=cat_sums, shared=second.shared,
        ),
        dict(gain_ffn=gain_row, g_down=down_spec, d_residual=block32),
        need=dict(
            cotangent=SENT, residual=SENT, few=SENT, hidden=SENT, cat_sums=SENT, shared=3
        ),
        done=dict(gain_ffn=3, d_residual=CHUNK + 3, g_down=SPREAD),
        scratch=dict(dgu=pltpu.VMEM((length, 2 * units), B16), g_gu=pltpu.VMEM(*gu_spec)),
        phases=ffn_back_phases, fills=fills_ffn, scatters={PART: (depth, 4, (0, 1, 2))}, gathers=dict(rows_back=0),
        helpers=hauls,
    )
    gu_sums = hauls[2].result
    second.sums += hauls[0].results + hauls[1].results
    first.add(got)

    hauls = [
        Haul(0, dp, [from_input(lambda r: r.gu_sums)], [gu_spec], {BEGIN: 1, 4: 1}, swap=False),
        Haul(
            0, dp, [from_input(take_down)], [down_spec], {BEGIN: 1, 1: 1, 2: 2, 3: 1, SENT: 1}
        ),
        Haul(0, dp, [from_kernel(take_out)], [out_spec], {1: 1, 3: 2, 4: 2, CHUNK + 2: 1}),
        Haul(
            0, dp, [from_kernel(take_cat)], [cat_spec],
            {4: 1, 6: 1, SENT: 1, CHUNK: 1, CHUNK + 1: 1},
        ),
        Straight(0, dp, from_kernel(take_shared), shared_spec, {EXTRA: 1}),
    ]
    x_grads = Place(
        lambda r: (r.x_grad, r.raw.x_grad1), (rows, depth), 0,
        {4: 1, CHUNK: 1, CHUNK + 1: 1, CHUNK + 2: 1, CHUNK + 3: 1},
    )
    second_acts = Settle(1, lambda r: r.raw.last, (rows, depth), {5: 1})
    run(
        "back0", 7, functools.partial(work_back_mix, 0),
        dict(core_inputs(first), acts_in=acts_in, x_grad1=second.x_grad, gu_sums=gu_sums, g_down=first.g_down,
            last=second.last),
        {},
        need=dict(core_need, x_grad1=None, gu_sums=3, last=None),
        scratch=dict(
            core_scratch, **inner, x_grad=pltpu.VMEM(*block16), shared=pltpu.VMEM(*shared_spec)
        ),
        phases=functools.partial(back_phases, 0), scatters=back_scatters, extra_work=work_shared, helpers=hauls + [x_grads, second_acts],
    )
    first.sums = [h.result for h in hauls]
    order = [0, 1, 3, 2, 4]
    g_gates, g_down, g_cat, g_out, g_shared = [
        jnp.where(section == 0, first.sums[i], second.sums[j]).astype(F32).reshape(
            (-1,) + first.sums[i].shape[2:]
        )
        for i, j in zip(order, (0, 1, 3, 2, 4))
    ]
    g_mixer = jnp.stack([g_cat[:, :real], g_cat[:, width : width + real]], axis=1)
    table = 2 * NS + 2 * KVH * HD
    g_gains = g_shared[:, table + GAINS_AT : table + GAINS_AT + 2].T
    g_heads = g_shared[:3, table + HEADS_AT : table + HEADS_AT + heads]
    return (
        jnp.where(section == 0, first_acts.result, second_acts.result)[None],
        x_grads.result[None],
        g_gains[None],
        g_mixer[None],
        g_cat[None, :, cols.q : cols.q + q_real],
        g_shared[None, :, :table],
        g_shared[None, :, table : table + HM],
        g_heads[None],
        g_out[None, :real],
        g_out[None, width : width + q_real],
        g_gates.reshape(1, piece, 2, units),
        g_down[None],
    )


def solution(mesh):
    rows = P(DP, TENSOR, None)
    by_dp, by_tensor, by_both = P(PIPE, DP), P(PIPE, TENSOR), P(PIPE, DP, TENSOR)
    wide, tall, whole = P(PIPE, DP, None, TENSOR), P(PIPE, TENSOR, DP), P(PIPE, DP, None)
    joint = P(PIPE, (DP, TENSOR), None)
    return jax.shard_map(
        on_device,
        mesh=mesh,
        in_specs=(
            rows, rows, by_dp, wide, by_both, whole, whole, by_tensor, by_tensor, by_tensor, tall, tall,
            by_dp, wide, tall,
        ),
        out_specs=(
            P(PIPE, DP, TENSOR, None), P(PIPE, DP, TENSOR, None), P(PIPE, None, (DP, TENSOR)),
            wide, by_both, joint, joint, P(PIPE, None, TENSOR), tall, tall, wide, tall,
        ),
        check_vma=False,
    )
```

```python
import functools

import jax
import jax.numpy as jnp
from jax import lax
from jax.experimental import pallas as pl
from jax.experimental.pallas import tpu as pltpu
from jax.sharding import PartitionSpec as P

HM = 24
HA = 8
KVH = 2
NS = 128
HD = 64
LANES = 128
STEP = 128
TILE = 256
EPS = 1e-05
F32 = jnp.float32
B16 = jnp.bfloat16
VMEM_LIMIT = 60 << 20
HEADS_AT = 32
GAINS_AT = 64


def nn(a, b):
    return lax.dot_general(a, b, (((1,), (0,)), ((), ())), preferred_element_type=F32)


def nt(a, b):
    return lax.dot_general(a, b, (((1,), (1,)), ((), ())), preferred_element_type=F32)


def tn(a, b):
    return lax.dot_general(a, b, (((0,), (0,)), ((), ())), preferred_element_type=F32)


def exact(a, b):
    return lax.dot_general(
        a, b, (((1,), (0,)), ((), ())), precision=lax.Precision.HIGHEST, preferred_element_type=F32
    )


def softplus(v):
    small = jnp.exp(-jnp.abs(v))
    series = small * (1.0 - small * (0.5 - small * (1.0 / 3.0 - small * 0.25)))
    return jnp.maximum(v, 0.0) + jnp.where(small < 0.02, series, jnp.log(1.0 + small))


def sigmoid(v):
    return 1.0 / (1.0 + jnp.exp(-v))


def iotas(rows, columns):
    return (
        lax.broadcasted_iota(jnp.int32, (rows, columns), 0),
        lax.broadcasted_iota(jnp.int32, (rows, columns), 1),
    )


def spread(column_block, head, rows):
    return jnp.broadcast_to(column_block[:, head : head + 1], (rows, LANES))


class Cols:
    def __init__(self, width):
        self.width = width
        self.z = 0
        self.u = width
        self.q = 2 * width
        self.b = self.q + LANES
        self.c = self.b + LANES
        self.k = self.c + LANES
        self.v = self.k + LANES
        self.step = self.v + LANES
        self.total = self.step + LANES
        self.pairs = width // LANES


class MixerRows:
    def __init__(self, cols, members):
        self.shared = 4 * LANES // members
        self.query = self.shared
        self.inner = self.query + LANES
        self.low = self.inner + 2 * cols.width
        self.total = self.low + cols.width + LANES


def fold_lanes(block):
    def folded(piece):
        count = piece // LANES
        size = block.shape[0] // count
        return jnp.concatenate([block[i * size : (i + 1) * size] for i in range(count)], axis=1)

    return folded


def unfold_lanes(block):
    return jnp.concatenate(
        [block[:, at : at + LANES] for at in range(0, block.shape[1], LANES)], axis=0
    )


def join_shared(cols, members, layer, q_heads, r):
    mixer, shared, few, rest = r.mixer, r.shared_w, r.few, r.rest
    ways, _, piece = mixer.shape
    at = MixerRows(cols, members)
    group = lax.axis_index(TENSOR) * q_heads // (HA // KVH)
    source, target = iotas(LANES, LANES)
    choose = (source == group * HD + (target & (HD - 1))).astype(B16)
    size = piece // members
    for d in range(ways):
        rows = slice(d * piece, (d + 1) * piece)
        rest[rows, :LANES] = unfold_lanes(mixer[d, at.query : at.query + LANES, :])
        for m in range(members):
            block = unfold_lanes(shared[m, d])
            to = slice(d * piece + m * size, d * piece + (m + 1) * size)
            for j in range(4):
                lanes = block[j * size : (j + 1) * size, :]
                if j >= 2:
                    lanes = nn(lanes, choose).astype(B16)
                rest[to, LANES * (j + 1) : LANES * (j + 2)] = lanes
        steps = few[layer, d, 8:16, :]
        steps = jnp.concatenate([steps, jnp.zeros((LANES - 8, piece), F32)], axis=0).T
        rest[rows, 5 * LANES :] = steps.astype(B16)


def split_heads(block, low_lanes):
    zero = jnp.zeros_like(block)
    return jnp.concatenate(
        [jnp.where(low_lanes, block, zero), jnp.where(low_lanes, zero, block)], axis=0
    )


def blocks_nn(rows_ref, rows, weights_ref, c, first=0):
    ways, _, piece = weights_ref.shape
    at = slice(first + c * piece, first + (c + 1) * piece)
    total = nn(rows_ref[rows, 0:piece], weights_ref[0, at, :])
    for d in range(1, ways):
        total += nn(rows_ref[rows, d * piece : (d + 1) * piece], weights_ref[d, at, :])
    return total


def multiply_out(lows_ref, weights_ref, first, part_ref, rows):
    ways, _, piece = weights_ref.shape
    last = first + lows_ref.shape[1]
    block = lows_ref[rows, :]
    for k in range(ways):
        part_ref[rows, k * piece : (k + 1) * piece] = nn(
            block, weights_ref[k, first:last, :]
        ).astype(B16)


def multiply_back(grad_ref, weights_ref, first, count, part_ref, rows, rows_ref, gain_sum, rest=None):
    ways, _, piece = weights_ref.shape
    for d in range(ways):
        to = slice(d * piece, (d + 1) * piece)
        total = nt(grad_ref[rows, 0:piece], weights_ref[d, first : first + piece, :])
        for c in range(1, count):
            at = slice(first + c * piece, first + (c + 1) * piece)
            total += nt(grad_ref[rows, c * piece : (c + 1) * piece], weights_ref[d, at, :])
        if rest is not None:
            total += nt(grad_ref[rows, count * piece :], rest[to, :])
        part_ref[rows, to] = total.astype(B16)
        if gain_sum is not None:
            gain_sum[0:1, to] += jnp.sum(total * rows_ref[rows, to].astype(F32), axis=0, keepdims=True)


def by_blocks(order, rows, step):
    def phase(group):
        def run():
            for member in group:
                step(pl.ds(pl.multiple_of(member * rows, rows), rows), member)

        return run

    return [phase(group) for group in order]


def skip_lanes(few_ref, layer, width):
    row, lane = iotas(width, LANES)
    own = ((row >> 6) == lane).astype(F32)
    skip = jnp.broadcast_to(few_ref[layer, 0, 4:5, :LANES], (8, LANES))
    return lax.dot_general(
        skip, own, (((1,), (1,)), ((), ())),
        precision=lax.Precision.HIGHEST, preferred_element_type=F32,
    )[0:1, :]


def core_fwd_phases(cols, members, layer, q_heads, r, order):
    rows_ref, weights_ref, few_ref = r.rows_mix, r.mixer, r.few
    proj_ref, step_ref, y_ref, lows_ref = r.proj, r.step, r.y, r.lows
    states_ref, lse_ref, part_ref, state = r.states, r.lse, r.part, r.state
    length = rows_ref.shape[0]
    width = cols.width
    piece = weights_ref.shape[2]

    at_row = MixerRows(cols, members)

    def join_all():
        join_shared(cols, members, layer, q_heads, r)

    def project_all():
        def project(i, _):
            rows = pl.ds(pl.multiple_of(i * TILE, TILE), TILE)
            for c in range(cols.q // piece):
                value = blocks_nn(rows_ref, rows, weights_ref, c, at_row.inner)
                proj_ref[rows, c * piece : (c + 1) * piece] = value.astype(B16)
            rest = nn(rows_ref[rows, :], r.rest[...])
            proj_ref[rows, cols.q : cols.b] = (rest[:, :LANES] * HD**-0.5).astype(B16)
            proj_ref[rows, cols.b : cols.step] = rest[:, LANES : 5 * LANES].astype(B16)
            step_ref[rows, :] = rest[:, 5 * LANES :]
            return 0

        lax.fori_loop(0, length // TILE, project, 0)

    def scan_part(low, high):
        ri, ci = iotas(STEP, STEP)
        lower = ri >= ci
        tril = lower.astype(F32)
        low_lanes = ci < HD
        decay = jnp.exp(few_ref[layer, 0, 2:3, :LANES])
        bias = few_ref[layer, 0, 3:4, :LANES]
        skips = skip_lanes(few_ref, layer, width)
        if low == 0:
            state[...] = jnp.zeros_like(state)

        def scan_block(b, _):
            rows = pl.ds(pl.multiple_of(b * STEP, STEP), STEP)
            dt = softplus(step_ref[rows, :] + bias)
            run = exact(tril, -dt * decay)
            run_t = run.T
            bm = proj_ref[rows, cols.b : cols.b + LANES]
            cm = proj_ref[rows, cols.c : cols.c + LANES]
            cb = jnp.where(lower, nt(cm, bm), 0.0)
            states_in = state[...]
            low_state = states_in.astype(B16)
            states_ref[b] = low_state
            carried = nn(cm, low_state)
            tails, fades = [], []
            for p in range(cols.pairs):
                lanes = slice(LANES * p, LANES * (p + 1))
                u = proj_ref[rows, cols.u + LANES * p : cols.u + LANES * (p + 1)].astype(F32)
                z = proj_ref[rows, cols.z + LANES * p : cols.z + LANES * (p + 1)].astype(F32)
                run_b = [spread(run, 2 * p + k, STEP) for k in range(2)]
                run_w = jnp.where(low_lanes, run_b[0], run_b[1])
                ud = u * jnp.where(low_lanes, spread(dt, 2 * p, STEP), spread(dt, 2 * p + 1, STEP))
                mix = jnp.concatenate(
                    [
                        (
                            jnp.exp(jnp.minimum(run_b[k] - run_t[2 * p + k : 2 * p + k + 1, :], 0.0))
                            * cb
                        ).astype(B16)
                        for k in range(2)
                    ],
                    axis=1,
                )
                inside = nn(mix, split_heads(ud, low_lanes).astype(B16))
                y = inside + carried[:, lanes] * jnp.exp(run_w) + skips[:, lanes] * u
                y_ref[rows, lanes] = y.astype(B16)
                lows_ref[rows, lanes] = (y * z * sigmoid(z)).astype(B16)
                end = run_w[STEP - 1 : STEP, :]
                tails.append((ud * jnp.exp(end - run_w)).astype(B16))
                fades.append(jnp.exp(end))
            fresh = tn(bm, jnp.concatenate(tails, axis=1))
            state[...] = states_in * jnp.concatenate(fades, axis=1) + fresh
            return 0

        lax.fori_loop(low, high, scan_block, 0)

    def attend(i):
        rk, ck = iotas(TILE, 2 * TILE)
        diagonal = rk <= jnp.where(ck < TILE, ck, ck - TILE)
        q_low = iotas(TILE, LANES)[1] < HD

        rows = pl.ds(pl.multiple_of(i * TILE, TILE), TILE)
        q2 = split_heads(proj_ref[rows, cols.q : cols.q + LANES], q_low)

        def piece(j, carry, masked):
            top, total, out = carry
            keys = pl.ds(pl.multiple_of(j * TILE, TILE), TILE)
            s = nt(proj_ref[keys, cols.k : cols.k + LANES], q2)
            if masked:
                s = jnp.where(diagonal, s, -1e30)
            new_top = jnp.maximum(top, jnp.max(s, axis=0, keepdims=True))
            p = jnp.exp(s - new_top)
            scale = jnp.exp(top - new_top)
            total = total * scale + jnp.sum(p, axis=0, keepdims=True)
            out = out * scale + tn(proj_ref[keys, cols.v : cols.v + LANES], p.astype(B16))
            return new_top, total, out

        carry = (
            jnp.full((1, 2 * TILE), -1e30, F32),
            jnp.zeros((1, 2 * TILE), F32),
            jnp.zeros((LANES, 2 * TILE), F32),
        )
        carry = lax.fori_loop(0, i, lambda j, c: piece(j, c, False), carry)
        top, total, out = piece(i, carry, True)
        out = out / total
        joined = jnp.concatenate([out[:HD, :TILE], out[HD:, TILE:]], axis=0)
        lows_ref[rows, width : width + LANES] = joined.T.astype(B16)
        lse_ref[i] = jnp.broadcast_to(top + jnp.log(total), (8, 2 * TILE))

    rows = length // members
    blocks, tiles = length // STEP, length // TILE
    together = rows == TILE

    def attend_all():
        for i in range(tiles):
            attend(i)

    def finish(at, member):
        if together:
            attend(member)
        multiply_out(lows_ref, weights_ref, at_row.low, part_ref, at)

    phases = [
        join_all,
        project_all,
        lambda: scan_part(0, blocks // 2),
        lambda: scan_part(blocks // 2, blocks),
    ]
    if not together:
        phases[3] = lambda: (scan_part(blocks // 2, blocks), attend_all())
    return phases + by_blocks(order, rows, finish)


def core_bwd_phases(cols, layer, members, q_heads, r, order):
    back_ref, weights_ref, few_ref, rows_ref = r.rows_back, r.mixer, r.few, r.rows_mix
    proj_ref, step_ref, y_ref, lows_ref = r.proj, r.step, r.y, r.lows
    states_ref, lse_ref, part_ref = r.states, r.lse, r.part
    dproj_ref, heads_ref, dcore, grad_state, skip_sum = r.dproj, r.heads, r.dcore, r.grad_state, r.skip_sum
    dk_sum, dv_sum, folded, staged = r.dk_sum, r.dv_sum, r.folded, r.staged
    length = back_ref.shape[0]
    width = cols.width
    ways, _, piece = weights_ref.shape
    blocks = length // STEP
    depth = ways * piece
    at_row = MixerRows(cols, members)
    low_rows = slice(at_row.low, at_row.low + width + LANES)

    def into_all():
        def into_core(i, _):
            rows = pl.ds(pl.multiple_of(i * TILE, TILE), TILE)
            total = nt(back_ref[rows, 0:piece], weights_ref[0, low_rows, :])
            for k in range(1, ways):
                total += nt(
                    back_ref[rows, k * piece : (k + 1) * piece], weights_ref[k, low_rows, :]
                )
            dcore[rows, :] = total.astype(B16)
            return 0

        lax.fori_loop(0, length // TILE, into_core, 0)

    def attend_all():
        rk, ck = iotas(TILE, 2 * TILE)
        diagonal = rk <= jnp.where(ck < TILE, ck, ck - TILE)
        q_low = iotas(TILE, LANES)[1] < HD
        dk_sum[...] = jnp.zeros_like(dk_sum)
        dv_sum[...] = jnp.zeros_like(dv_sum)
        half = iotas(8, LANES)
        pick_low = (half[1] < HD).astype(F32)
        pick_high = (half[1] >= HD).astype(F32)

        def attend(i, _):
            rows = pl.ds(pl.multiple_of(i * TILE, TILE), TILE)
            q2 = split_heads(proj_ref[rows, cols.q : cols.q + LANES], q_low)
            d_out = dcore[rows, width : width + LANES]
            do2 = split_heads(d_out, q_low)
            both = d_out.astype(F32) * lows_ref[rows, width : width + LANES].astype(F32)
            high = lax.Precision.HIGHEST
            deltas = [
                lax.dot_general(
                    pick, both, (((1,), (1,)), ((), ())), precision=high, preferred_element_type=F32
                )[0:1, :]
                for pick in (pick_low, pick_high)
            ]
            delta = jnp.concatenate(deltas, axis=1)
            lse = lse_ref[i][0:1, :]

            def piece_of(j, dq, masked):
                keys = pl.ds(pl.multiple_of(j * TILE, TILE), TILE)
                kk = proj_ref[keys, cols.k : cols.k + LANES]
                p = jnp.exp(nt(kk, q2) - lse)
                if masked:
                    p = jnp.where(diagonal, p, 0.0)
                ds = (p * (nt(proj_ref[keys, cols.v : cols.v + LANES], do2) - delta)).astype(B16)
                dv_sum[keys, :] += nn(p.astype(B16), do2)
                dk_sum[keys, :] += nn(ds, q2)
                return dq + tn(kk, ds)

            dq = jnp.zeros((LANES, 2 * TILE), F32)
            dq = lax.fori_loop(0, i, lambda j, c: piece_of(j, c, False), dq)
            dq = piece_of(i, dq, True)
            joined = jnp.concatenate([dq[:HD, :TILE], dq[HD:, TILE:]], axis=0) * HD**-0.5
            dproj_ref[rows, cols.q : cols.q + LANES] = joined.T.astype(B16)
            return 0

        lax.fori_loop(0, length // TILE, attend, 0)
        dproj_ref[:, cols.k : cols.k + LANES] = dk_sum[...].astype(B16)
        dproj_ref[:, cols.v : cols.v + LANES] = dv_sum[...].astype(B16)

    def scan_all():
        ri, ci = iotas(STEP, STEP)
        upper = ri <= ci
        tril = (ri >= ci).astype(F32)
        triu = upper.astype(F32)
        low_lanes = ci < HD
        decay = jnp.exp(few_ref[layer, 0, 2:3, :LANES])
        bias = few_ref[layer, 0, 3:4, :LANES]
        skips = skip_lanes(few_ref, layer, width)
        row, lane = iotas(width, LANES)
        group = ((row >> 6) == lane).astype(B16)
        grad_state[...] = jnp.zeros_like(grad_state)
        skip_sum[...] = jnp.zeros_like(skip_sum)
        heads_ref[...] = jnp.zeros_like(heads_ref)
        zero_rows = jnp.zeros((STEP - 2 * cols.pairs, LANES), F32)

        def scan_block(back, _):
            b = blocks - 1 - back
            rows = pl.ds(pl.multiple_of(b * STEP, STEP), STEP)
            raw = step_ref[rows, :] + bias
            dt = softplus(raw)
            a = -dt * decay
            run = exact(tril, a)
            run_t = run.T
            bm = proj_ref[rows, cols.b : cols.b + LANES]
            cm = proj_ref[rows, cols.c : cols.c + LANES]
            cbt = jnp.where(upper, nt(bm, cm), 0.0)
            low_state = states_ref[b]
            grads_out = grad_state[...]
            low_grad = grads_out.astype(B16)
            carried = nn(cm, low_state)
            pulled = nn(bm, low_grad)
            dcb = jnp.zeros((STEP, STEP), F32)
            dy_fades, u_tails, fades = [], [], []
            carry_terms, direct_terms, tail_terms = [], [], []
            row_sums = []
            col_sums = jnp.zeros((STEP, LANES), F32)
            for p in range(cols.pairs):
                lanes = slice(LANES * p, LANES * (p + 1))
                u16 = proj_ref[rows, cols.u + LANES * p : cols.u + LANES * (p + 1)]
                u = u16.astype(F32)
                z = proj_ref[rows, cols.z + LANES * p : cols.z + LANES * (p + 1)].astype(F32)
                y = y_ref[rows, lanes].astype(F32)
                dm = dcore[rows, lanes].astype(F32)
                sg = sigmoid(z)
                dy = dm * z * sg
                dproj_ref[rows, cols.z + LANES * p : cols.z + LANES * (p + 1)] = (
                    dm * y * sg * (1.0 + z * (1.0 - sg))
                ).astype(B16)
                dy16 = dy.astype(B16)
                skip_sum[:, lanes] += u * dy
                run_b = [spread(run, 2 * p + k, STEP) for k in range(2)]
                dt_b = [spread(dt, 2 * p + k, STEP) for k in range(2)]
                run_w = jnp.where(low_lanes, run_b[0], run_b[1])
                dt_w = jnp.where(low_lanes, dt_b[0], dt_b[1])
                end = run_w[STEP - 1 : STEP, :]
                fade = jnp.exp(run_w)
                tail = jnp.exp(end - run_w)
                dmix = nt(split_heads(u16, low_lanes), dy16)
                mixes = []
                for k in range(2):
                    gap = jnp.exp(jnp.minimum(run_t[2 * p + k : 2 * p + k + 1, :] - run_b[k], 0.0))
                    mixes.append((gap * cbt).astype(B16))
                    weighted = gap * dt_b[k] * dmix[STEP * k : STEP * (k + 1), :]
                    dcb += weighted
                    moved = weighted * cbt
                    row_sums.append(jnp.sum(moved, axis=0, keepdims=True))
                    col_sums = jnp.where(
                        ci == 2 * p + k, jnp.sum(moved, axis=1, keepdims=True), col_sums
                    )
                inside = nn(jnp.concatenate(mixes, axis=1), split_heads(dy16, low_lanes))
                pull_tail = tail * pulled[:, lanes]
                g = inside + pull_tail
                dproj_ref[rows, cols.u + LANES * p : cols.u + LANES * (p + 1)] = (
                    dt_w * g + skips[:, lanes] * dy
                ).astype(B16)
                dy_fade = dy * fade
                dy_fades.append(dy_fade.astype(B16))
                u_tails.append((u * dt_w * tail).astype(B16))
                fades.append(jnp.exp(end))
                carry_terms.append((dy_fade * carried[:, lanes]).astype(B16))
                direct_terms.append((u * g).astype(B16))
                tail_terms.append((u * pull_tail).astype(B16))
            dy_fade = jnp.concatenate(dy_fades, axis=1)
            dcb = jnp.where(upper, dcb, 0.0).astype(B16)
            dproj_ref[rows, cols.c : cols.c + LANES] = (tn(dcb, bm) + nt(dy_fade, low_state)).astype(B16)
            dproj_ref[rows, cols.b : cols.b + LANES] = (
                nn(dcb, cm) + nt(jnp.concatenate(u_tails, axis=1), low_grad)
            ).astype(B16)
            carry_term = nn(jnp.concatenate(carry_terms, axis=1), group)
            direct_term = nn(jnp.concatenate(direct_terms, axis=1), group)
            tail_term = dt * nn(jnp.concatenate(tail_terms, axis=1), group)
            overlap = jnp.sum(low_state.astype(F32) * grads_out, axis=0, keepdims=True)
            overlap = exact(jnp.broadcast_to(overlap, (8, width)), group.astype(F32))[0:1, :]
            overlap = overlap * jnp.exp(run[STEP - 1 : STEP, :])
            row_sum = jnp.concatenate(row_sums + [zero_rows], axis=0).T
            d_run = row_sum - col_sums + carry_term - tail_term
            d_a = exact(triu, d_run) + (jnp.sum(tail_term, axis=0, keepdims=True) + overlap)
            d_step = (direct_term - decay * d_a) * sigmoid(raw)
            dproj_ref[rows, cols.step : cols.step + LANES] = d_step.astype(B16)
            heads_ref[0:1, :] += jnp.sum(d_a * a, axis=0, keepdims=True)
            heads_ref[1:2, :] += jnp.sum(d_step, axis=0, keepdims=True)
            grad_state[...] = grads_out * jnp.concatenate(fades, axis=1) + tn(cm, dy_fade)
            return 0

        lax.fori_loop(0, blocks, scan_block, 0)
        skip = jnp.sum(skip_sum[...], axis=0, keepdims=True)
        heads_ref[2:3, :] = exact(jnp.broadcast_to(skip, (8, width)), group.astype(F32))[0:1, :]

    def back(at, member):
        multiply_back(
            dproj_ref, weights_ref, at_row.inner, cols.q // piece, part_ref, at, rows_ref, None, r.rest
        )

    def shared_all():
        wide = cols.total - cols.b
        member = lax.axis_index(TENSOR)
        heads = q_heads[1]
        group = member * q_heads[0] // (HA // KVH)
        source, target = iotas(wide, wide)
        kind = source >> 7
        wanted = jnp.where(
            kind < 2,
            source,
            jnp.where(
                kind < 4,
                2 * NS + (kind - 2) * KVH * HD + group * HD + (source & (HD - 1)),
                source + member * heads,
            ),
        )
        fold = ((target == wanted) & (source < 4 * LANES + heads)).astype(B16)

        def fold_rows(i, _):
            rows = pl.ds(pl.multiple_of(i * TILE, TILE), TILE)
            folded[rows, :] = nn(dproj_ref[rows, cols.b :], fold).astype(B16)
            return 0

        lax.fori_loop(0, length // TILE, fold_rows, 0)
        sub = piece // members
        half = sub // 2
        lane = iotas(piece, LANES)[1]
        head_lane = iotas(8, LANES)[1]
        shifted = jnp.where(
            (head_lane >= HEADS_AT) & (head_lane < HEADS_AT + heads),
            pltpu.roll(heads_ref[...], HEADS_AT, 1),
            0.0,
        )
        for k in range(ways):
            at = slice(k * piece, (k + 1) * piece)
            grad = tn(rows_ref[:, at], folded[...])
            raw = nn(r.rest[at, LANES:], fold)
            twice = (iotas(piece, wide)[1] >= 2 * LANES) & (iotas(piece, wide)[1] < 4 * LANES)
            own = jnp.sum(grad * jnp.where(twice, 0.5 * raw, raw), axis=1, keepdims=True)
            gains = [jnp.broadcast_to(few_ref[layer, k, i : i + 1, :], (LANES, piece)).T for i in (0, 1)]
            from_ffn = jnp.broadcast_to(r.gain_ffn[0:1, at], (LANES, piece)).T
            columns = [(own + r.gain_column[at, 0:1]) / gains[0], from_ffn / gains[1]]
            last = grad[:, wide - LANES :]
            last = jnp.where(lane == GAINS_AT, columns[0], last)
            last = jnp.where(lane == GAINS_AT + 1, columns[1], last)
            for t in range(members):
                for h in range(2):
                    to = t * (depth // members) + (h * ways + k) * half
                    rows = slice(t * sub + h * half, t * sub + (h + 1) * half)
                    staged[to : to + half, : wide - LANES] = grad[rows, : wide - LANES]
                    staged[to : to + half, wide - LANES :] = last[rows, :]
            to = pl.multiple_of(member * (depth // members) + k * half, 8)
            staged[pl.ds(to, 8), wide - LANES :] += shifted
        r.extra[...] = staged[...].astype(B16)

    return [into_all, attend_all, scan_all, shared_all] + by_blocks(order, length // members, back)


def ffn_forward(r, rows, part_ref):
    rows_ref, weights_ref, gu_ref, hidden_ref = r.rows_ffn, r.gates, r.gu, r.hidden
    units = hidden_ref.shape[1]
    piece = weights_ref.shape[2]
    count = units // piece
    for c in range(count):
        to = slice(c * piece, (c + 1) * piece)
        g = blocks_nn(rows_ref, rows, weights_ref, c)
        v = blocks_nn(rows_ref, rows, weights_ref, c + count)
        gu_ref[rows, to] = g.astype(B16)
        gu_ref[rows, units + c * piece : units + (c + 1) * piece] = v.astype(B16)
        hidden_ref[rows, to] = (g * sigmoid(g) * v).astype(B16)
    multiply_out(hidden_ref, weights_ref, 2 * units, part_ref, rows)


def ffn_backward(r, rows):
    out_ref, weights_ref, gu_ref, dgu_ref = r.rows_out, r.gates, r.gu, r.dgu
    ways, _, piece = weights_ref.shape
    units = gu_ref.shape[1] // 2
    down_rows = slice(2 * units, 3 * units)
    dh = nt(out_ref[rows, 0:piece], weights_ref[0, down_rows, :])
    for k in range(1, ways):
        dh += nt(out_ref[rows, k * piece : (k + 1) * piece], weights_ref[k, down_rows, :])
    g = gu_ref[rows, :units].astype(F32)
    v = gu_ref[rows, units:].astype(F32)
    sg = sigmoid(g)
    dgu_ref[rows, :units] = (dh * v * sg * (1.0 + g * (1.0 - sg))).astype(B16)
    dgu_ref[rows, units:] = (dh * g * sg).astype(B16)
    multiply_back(
        dgu_ref, weights_ref, 0, 2 * units // piece, r.part, rows, r.rows_ffn, r.gain_ffn
    )


def grad_columns(rows_ref, grad_ref, out_ref, step=512, weigh=None):
    _, ways, half, width = out_ref.shape
    for k in range(ways):
        block = rows_ref[:, 2 * half * k : 2 * half * (k + 1)]
        for first in range(0, width, step):
            last = min(first + step, width)
            value = tn(block, grad_ref[:, first:last])
            if weigh:
                weigh(k, first, last, value)
            value = value.astype(B16)
            out_ref[0, k, :, first:last] = value[:half, :]
            out_ref[1, k, :, first:last] = value[half:, :]


def mixer_columns(cols, members, r):
    _, _, piece = r.mixer.shape
    inner = MixerRows(cols, members).inner
    r.gain_column[...] = jnp.zeros_like(r.gain_column)

    def weigh(k, first, last, value):
        rows = slice(k * piece, (k + 1) * piece)
        if first < cols.q:
            weight = r.mixer[k, inner + first : inner + last, :]
        else:
            weight = r.rest[rows, :LANES]
        r.gain_column[rows, 0:1] += jnp.sum(value * weight.astype(F32), axis=1, keepdims=True)

    grad_columns(r.rows_mix, r.dproj, r.g_cat, piece, weigh)


def grad_rows(lows_ref, back_ref, out_ref):
    _, ways, half, piece = out_ref.shape
    for h in range(2):
        block = lows_ref[:, h * half : (h + 1) * half]
        for k in range(ways):
            out_ref[h, k] = tn(block, back_ref[:, k * piece : (k + 1) * piece]).astype(B16)


DMA = pltpu.SemaphoreType.DMA
MESH = pl.DeviceIdType.MESH
PIPE, DP, TENSOR = "pipe", "dp", "tensor"
PART, SHARED, LAST = "part", "extra", "ffn_part"

BEGIN, SENT, EXTRA, CHUNK, SPREAD, GIVEN, END = -1, 20, 25, 30, 40, 50, 60


class Bag:
    def __init__(self, **entries):
        self.__dict__.update(entries)

    def add(self, other):
        self.__dict__.update(other.__dict__)


def remote(source, target, send, receive, device):
    return pltpu.make_async_remote_copy(
        src_ref=source, dst_ref=target, send_sem=send, recv_sem=receive,
        device_id=device, device_id_type=MESH,
    )


class Helper:
    def __init__(self, when):
        self.when = when
        self.inputs, self.outs, self.scratch = [], [], []
        self.results = None

    @property
    def result(self):
        return self.results[0]


def cross_devices(ways):
    section, place = lax.axis_index(PIPE), lax.axis_index(DP)
    return [{PIPE: 1 - section}] + [{DP: (place + k) % ways} for k in range(1, ways)]


class Few(Helper):
    def __init__(self, ways, shard, when):
        super().__init__(when)
        self.ways = ways
        self.inputs = [shard]
        self.outs = [((2, ways) + shard.shape, F32, pltpu.VMEM)]
        self.scratch = [DMA((1,)), DMA((1,)), DMA((2, ways)), DMA((2, ways)), DMA((1,))]

    def bind(self, r, inputs, outs, scratch):
        (shard,), (few,) = inputs, outs
        r.few = few
        section, place, ways = lax.axis_index(PIPE), lax.axis_index(DP), self.ways
        pair_send, pair_recv, line_send, line_recv, local = scratch
        mine = few.at[section, place]

        def over():
            return remote(shard, mine, pair_send.at[0], pair_recv.at[0], {PIPE: 1 - section})

        def line(layer, k, there):
            block = few.at[layer, there]
            return remote(
                block, block, line_send.at[layer, k], line_recv.at[layer, k], {DP: (place + k) % ways}
            )

        def start():
            over().start()
            own = pltpu.make_async_copy(shard, mine, local.at[0])
            own.start()
            own.wait()

        def spread():
            over().wait_recv()
            for layer in range(2):
                for k in range(1, ways):
                    line(layer, k, place).start()

        def finish():
            for layer in range(2):
                for k in range(1, ways):
                    line(layer, k, (place + ways - k) % ways).wait_recv()
            over().wait_send()
            for layer in range(2):
                for k in range(1, ways):
                    line(layer, k, place).wait_send()

        return [start, spread, finish]


class Cargo(Helper):
    CHUNKS = 4

    def __init__(self, layer, ways, shard, when, members=0, shared=0):
        super().__init__(when)
        self.layer, self.ways, self.rows = layer, ways, shard.shape[0]
        self.members, self.shared = members, shared
        n = self.CHUNKS
        self.first = (self.rows * 2 // 5 + 8 * n) // (16 * n) * (16 * n)
        self.inputs = [shard]
        self.outs = [((ways,) + shard.shape, shard.dtype, pl.ANY)]
        self.scratch = [DMA((n,)), DMA((n,))] + [DMA((ways, n))] * 6 + [DMA((1,))]
        if shared:
            self.outs.append(((members, ways, shared, shard.shape[1]), shard.dtype, pl.ANY))
            self.scratch += [DMA((members,))] * 4 + [DMA((1,))]

    def bind(self, r, inputs, outs, scratch):
        (shard_ref,), out_ref = inputs, outs[0]
        early_send, early_recv, up_send, up_recv, down_send, down_recv, over_send, over_recv, local = scratch[:9]
        section, place = lax.axis_index(PIPE), lax.axis_index(DP)
        partner = {PIPE: 1 - section}
        ways, chunks = self.ways, self.CHUNKS
        sizes = {True: self.first // chunks, False: (self.rows - self.first) // chunks}

        def by_role(step):
            def both():
                pl.when(section == self.layer)(lambda: step(True))
                pl.when(section != self.layer)(lambda: step(False))

            return both

        def part(owner, c):
            return pl.ds((0 if owner else self.first) + c * sizes[owner], sizes[owner])

        def early(c):
            at = part(False, c)
            return remote(
                shard_ref.at[at, :], out_ref.at[place, at, :], early_send.at[c], early_recv.at[c], partner
            )

        def line(owner, up, hop, c):
            at = part(owner, c)
            send, receive = (up_send, up_recv) if up else (down_send, down_recv)
            shard = place - hop if up else place + hop
            source = shard_ref if owner and hop == 0 else out_ref.at[shard]
            return remote(
                source.at[at, :], out_ref.at[shard, at, :], send.at[hop, c], receive.at[hop, c],
                {DP: (place + (1 if up else ways - 1)) % ways},
            )

        def sends(up, hop):
            if up:
                return (place >= hop) & (place < ways - 1)
            return (place < ways - hop) & (place > 0)

        def over(owner, shard, c, own=False):
            at = part(owner, c)
            source = shard_ref if own else out_ref.at[shard]
            return remote(
                source.at[at, :], out_ref.at[shard, at, :], over_send.at[shard, c], over_recv.at[shard, c],
                partner,
            )

        def own_copy():
            return pltpu.make_async_copy(shard_ref, out_ref.at[place], local.at[0])

        def launch(owner, c):
            for up in (True, False):
                pl.when(sends(up, 0))(lambda up=up: line(owner, up, 0, c).start())

        def start(owner):
            if owner:
                for c in range(chunks):
                    early(c).start()
                    launch(True, c)
                for c in range(chunks):
                    over(True, place, c, True).start()
                own_copy().start()

        def spread(c, owner):
            if not owner:
                early(c).wait_recv()
                launch(False, c)

        def hop(count, c, owner):
            for up in (True, False):
                shard = place - count if up else place + count

                @pl.when(shard >= 0 if up else shard < ways)
                def _(up=up, shard=shard):
                    line(owner, up, count - 1, c).wait_recv()
                    if count < ways - 1:
                        pl.when(sends(up, count))(lambda: line(owner, up, count, c).start())
                    over(owner, shard, c).start()

        def wait_over(owner, c):
            for shard in range(ways):

                def wait(shard=shard):
                    block = out_ref.at[shard, part(not owner, c), :]
                    remote(
                        block, block, over_send.at[shard, c], over_recv.at[shard, c], partner
                    ).wait_recv()

                if owner:
                    pl.when(place != shard)(wait)
                else:
                    wait()

        first_waited = 1 if self.shared else 0

        def finish(owner):
            for c in range(chunks):
                if owner or c >= first_waited:
                    wait_over(owner, c)
            for c in range(chunks):
                if owner:
                    early(c).wait_send()
                for count in range(ways - 1):
                    for up in (True, False):
                        pl.when(sends(up, count))(
                            lambda up=up, count=count: line(owner, up, count, c).wait_send()
                        )
                for shard in range(ways):

                    def wait(shard=shard):
                        over(owner, shard, c).wait_send()

                    if owner:
                        wait()
                    else:
                        pl.when(place != shard)(wait)
            if owner and not self.shared:
                own_copy().wait()

        steps = [start]
        steps += [functools.partial(spread, c) for c in range(chunks)]
        steps += [functools.partial(hop, count, c) for count in range(1, ways) for c in range(chunks)]
        steps = [by_role(step) for step in steps]
        if not self.shared:
            return steps + [by_role(finish)]

        assert self.shared <= sizes[True]
        all_ref = outs[1]
        give_send, give_recv, far_send, far_recv, keep = scratch[9:]
        me = lax.axis_index(TENSOR)
        pairs = self.members // 2
        mine, side = me // 2, me % 2
        sibling = 2 * mine + 1 - side
        share = out_ref.at[:, pl.ds(0, self.shared), :]

        def far(count):
            return 2 * ((mine + count) % pairs) + side

        def across(count):
            return 2 * ((mine + count) % pairs) + 1 - side

        def give(count):
            block = all_ref.at[far(count)]
            return remote(
                share if count == 0 else block, block, give_send.at[count], give_recv.at[count],
                {TENSOR: sibling},
            )

        def send_far(count, slot):
            return remote(
                share, all_ref.at[me], far_send.at[count], far_recv.at[slot], {TENSOR: far(count)}
            )

        def own_share():
            return pltpu.make_async_copy(share, all_ref.at[me], keep.at[0])

        def share_out():
            pl.when(section != self.layer)(lambda: wait_over(False, 0))
            pl.when(section == self.layer)(lambda: own_copy().wait())
            for count in range(1, pairs):
                send_far(count, pairs - count).start()
            give(0).start()
            own_share().start()

        def pass_on():
            for count in range(1, pairs):
                send_far(count, count).wait_recv()
                give(count).start()

        def finish_all():
            by_role(finish)()
            for count in range(pairs):
                block = all_ref.at[sibling if count == 0 else across(count)]
                remote(
                    block, block, give_send.at[count], give_recv.at[count], {TENSOR: sibling}
                ).wait_recv()
            for count in range(pairs):
                give(count).wait_send()
                if count:
                    send_far(count, pairs - count).wait_send()
            own_share().wait()

        return steps + [share_out, pass_on, finish_all]


class Haul(Helper):
    def __init__(self, layer, ways, sources, specs, when, swap=True, line=True):
        super().__init__(when)
        self.layer, self.ways, self.sources, self.swap, self.line = layer, ways, sources, swap, line
        self.count = len(specs)
        self.order = sorted(range(1, ways), key=lambda k: abs(2 * k - ways)) + [0]
        for (_, blocks, rows, columns), dtype in specs:
            block = pltpu.VMEM((blocks, rows, columns), dtype)
            if swap and not line:
                self.outs.append(((blocks, rows, columns), dtype, pltpu.VMEM))
            if line:
                self.outs.append(((2, rows, columns), dtype, pltpu.VMEM))
            if swap:
                self.scratch += [block, DMA((ways,)), DMA((ways,))]
            if swap and line:
                self.scratch.append(block)
            if line:
                self.scratch += [block, pltpu.VMEM((rows, columns), dtype), DMA((ways,)), DMA((ways,))]
                self.scratch += [DMA((1,)), DMA((1,))]

    def bind(self, r, inputs, outs, scratch):
        section, place, ways = lax.axis_index(PIPE), lax.axis_index(DP), self.ways
        partner = {PIPE: 1 - section}
        scratch = list(scratch)
        arrays = []
        for source, out in zip(self.sources, outs):
            a = Bag(out=out)
            a.sent, a.read = source(r)
            a.sums = a.read
            if self.swap:
                a.swapped, a.swap_send, a.swap_recv = [scratch.pop(0) for _ in range(3)]
                a.sums = scratch.pop(0) if self.line else out
                a.sums_sent = a.sums
            else:
                a.sums_sent = a.sent
            if self.line:
                a.arrived, a.result, a.line_send, a.line_recv, a.last_send, a.last_recv = [
                    scratch.pop(0) for _ in range(6)
                ]
            arrays.append(a)

        def to(k):
            return (place + k) % ways

        def swap(a, k):
            return remote(
                a.sent.at[1 - section, to(k)], a.swapped.at[to(k)], a.swap_send.at[k], a.swap_recv.at[k],
                partner,
            )

        def line(a, k):
            return remote(
                a.sums_sent.at[to(k)], a.arrived.at[k], a.line_send.at[k], a.line_recv.at[k], {DP: to(k)}
            )

        def last(a):
            return remote(
                a.result, a.out.at[1 - self.layer], a.last_send.at[0], a.last_recv.at[0], partner
            )

        def start():
            for k in self.order:
                for a in arrays:
                    if self.swap:
                        swap(a, k).start()
                    elif k:
                        line(a, k).start()

        def fold(k):
            def step():
                for a in arrays:
                    swap(a, k).wait_recv()
                    total = a.read[section, to(k)].astype(F32) + a.swapped[to(k)].astype(F32)
                    a.sums[to(k)] = total.astype(a.sums.dtype)
                    if k and self.line:
                        line(a, k).start()

            return step

        def reduce():
            for a in arrays:
                total = a.sums[place].astype(F32)
                for k in range(1, ways):
                    line(a, k).wait_recv()
                    total += a.arrived[k].astype(F32)
                a.result[...] = total.astype(a.out.dtype)

            @pl.when(section == self.layer)
            def _():
                for a in arrays:
                    a.out[self.layer] = a.result[...]

            @pl.when(section != self.layer)
            def _():
                for a in arrays:
                    last(a).start()

        def finish():
            if self.line:

                @pl.when(section == self.layer)
                def _():
                    for a in arrays:
                        last(a).wait_recv()

                @pl.when(section != self.layer)
                def _():
                    for a in arrays:
                        last(a).wait_send()
                        a.out[...] = jnp.zeros_like(a.out)

            for k in self.order:
                for a in arrays:
                    if self.swap:
                        swap(a, k).wait_send()
                    if k and self.line:
                        line(a, k).wait_send()

        steps = [start]
        if self.swap:
            steps += [fold(k) for k in self.order]
        if self.line:
            steps.append(reduce)
        return steps + [finish]


class Straight(Helper):
    def __init__(self, layer, ways, source, spec, when):
        super().__init__(when)
        self.layer, self.ways, self.source = layer, ways, source
        (_, blocks, rows, columns), dtype = spec
        result = (2, rows, columns)
        self.outs = [(result, dtype, pltpu.VMEM)]
        self.scratch = [pltpu.VMEM((blocks,) + result, dtype), pltpu.VMEM(result, dtype)]
        self.scratch += [pltpu.VMEM(result, dtype), DMA((2, ways)), DMA((2, ways)), DMA((1,)), DMA((1,))]

    def bind(self, r, inputs, outs, scratch):
        sent, read = self.source(r)
        (out,) = outs
        arrived, result, handed, line_send, line_recv, last_send, last_recv = scratch
        section, place, ways = lax.axis_index(PIPE), lax.axis_index(DP), self.ways
        order = sorted(range(1, ways), key=lambda k: abs(2 * k - ways))

        def line(half, k):
            to = (place + k) % ways
            return remote(
                sent.at[half, to], arrived.at[k, half], line_send.at[half, k], line_recv.at[half, k], {DP: to}
            )

        def last():
            return remote(result, handed, last_send.at[0], last_recv.at[0], {PIPE: 1 - section})

        def start():
            for k in order:
                for half in range(2):
                    line(half, k).start()

        def reduce():
            for half in range(2):
                total = read[half, place].astype(F32)
                for k in range(1, ways):
                    line(half, k).wait_recv()
                    total += arrived[k, half].astype(F32)
                result[half] = total.astype(result.dtype)

            @pl.when(section != self.layer)
            def _():
                last().start()

        def finish():
            @pl.when(section == self.layer)
            def _():
                last().wait_recv()
                out[...] = (result[...].astype(F32) + handed[...].astype(F32)).astype(out.dtype)

            @pl.when(section != self.layer)
            def _():
                last().wait_send()
                out[...] = jnp.zeros_like(out)

            for k in order:
                for half in range(2):
                    line(half, k).wait_send()

        return [start, reduce, finish]


class Place(Helper):
    PIECES = 4

    def __init__(self, source, shape, late, when):
        super().__init__(when)
        self.source, self.late, self.size = source, late, shape[0] // self.PIECES
        self.outs = [((2,) + shape, B16, pl.ANY)]
        self.scratch = [DMA((self.PIECES,)), DMA((self.PIECES,)), DMA((self.PIECES,))]

    def bind(self, r, inputs, outs, scratch):
        (out,) = outs
        send, receive, local = scratch
        section = lax.axis_index(PIPE)
        rows = self.source(r)

        def over(layer, c):
            at = pl.ds(c * self.size, self.size)
            return remote(
                rows[layer].at[at, :], out.at[1 - layer, at, :], send.at[c], receive.at[c], {PIPE: 1 - section}
            )

        def own(layer, c):
            at = pl.ds(c * self.size, self.size)
            return pltpu.make_async_copy(rows[layer].at[at, :], out.at[layer, at, :], local.at[c])

        def hand(layer, c):
            pl.when(section != layer)(lambda: over(layer, c).start())
            pl.when(section == layer)(lambda: own(layer, c).start())

        def early():
            for c in range(self.PIECES):
                hand(1 - self.late, c)

        def finish():
            for c in range(self.PIECES):
                for layer in range(2):

                    @pl.when(section == layer)
                    def _(layer=layer):
                        over(1 - layer, c).wait()
                        own(layer, c).wait()

        return [early] + [functools.partial(hand, self.late, c) for c in range(self.PIECES)] + [finish]


class Settle(Helper):
    def __init__(self, layer, source, shape, when):
        super().__init__(when)
        self.layer, self.source = layer, source
        self.outs = [((2,) + shape, B16, pl.ANY)]
        self.scratch = [DMA((1,)), DMA((1,)), DMA((1,))]

    def bind(self, r, inputs, outs, scratch):
        (out,) = outs
        send, receive, local = scratch
        section = lax.axis_index(PIPE)
        rows = self.source(r)
        owner = section == self.layer

        def over():
            return remote(
                rows, out.at[1 - self.layer], send.at[0], receive.at[0], {PIPE: 1 - section}
            )

        def own():
            return pltpu.make_async_copy(rows, out.at[self.layer], local.at[0])

        def start():
            pl.when(section != self.layer)(lambda: over().start())
            pl.when(owner)(lambda: own().start())

        def finish():
            @pl.when(section != self.layer)
            def _():
                over().wait_send()

            @pl.when(owner)
            def _():
                over().wait_recv()
                own().wait()

        return [start, finish]


class Members:
    def __init__(self, count):
        self.pairs = count // 2
        self.me = lax.axis_index(TENSOR)
        self.mine, self.side = self.me // 2, self.me % 2
        self.sibling = 2 * self.mine + 1 - self.side

    def far(self, k):
        return 2 * ((self.mine + k) % self.pairs) + self.side

    def across(self, k):
        return 2 * ((self.mine + k) % self.pairs) + 1 - self.side

    def order(self):
        others = range(1, self.pairs)
        return [[self.across(k) for k in others], [self.far(k) for k in others], [self.sibling], [self.me]]


def member_copy(source, target, send, receive, member):
    return remote(source, target, send, receive, {TENSOR: member})


class Scatter:
    @staticmethod
    def scratch(members, rows, width, pieces):
        pairs = members // 2
        others = max(pairs - 1, 1)
        return [
            pltpu.VMEM((pairs, rows, width), B16),
            pltpu.VMEM((others, rows, width), B16),
            pltpu.VMEM((others, rows, width), B16),
            DMA((pairs, pieces)), DMA((pairs, pieces)), DMA((others, pieces)), DMA((others, pieces)),
        ]

    def __init__(self, part_ref, members, rows, pieces, scratch):
        self.part, self.at, self.rows, self.pieces = part_ref, members, rows, pieces
        self.size = rows // pieces
        self.pair_in, self.far_out, self.far_in = scratch[:3]
        self.pair_send, self.pair_recv, self.far_send, self.far_recv = scratch[3:]

    def rows_of(self, member, c):
        return pl.ds(pl.multiple_of(member * self.rows + c * self.size, self.size), self.size)

    def chunk(self, c):
        return pl.ds(c * self.size, self.size)

    def to_pair(self, k, c):
        member = self.at.across(k) if k else self.at.sibling
        return member_copy(
            self.part.at[self.rows_of(member, c), :], self.pair_in.at[k, self.chunk(c), :],
            self.pair_send.at[k, c], self.pair_recv.at[k, c], self.at.sibling,
        )

    def to_far(self, k, c, slot):
        return member_copy(
            self.far_out.at[k - 1, self.chunk(c), :], self.far_in.at[slot - 1, self.chunk(c), :],
            self.far_send.at[k - 1, c], self.far_recv.at[slot - 1, c], self.at.far(k),
        )

    def send_across(self):
        for c in range(self.pieces):
            for k in range(1, self.at.pairs):
                self.to_pair(k, c).start()

    def send_far(self):
        for c in range(self.pieces):
            for k in range(1, self.at.pairs):
                self.to_pair(k, c).wait_recv()
                total = self.part[self.rows_of(self.at.far(k), c), :].astype(F32)
                total += self.pair_in[k, self.chunk(c), :].astype(F32)
                self.far_out[k - 1, self.chunk(c), :] = total.astype(B16)
                self.to_far(k, c, self.at.pairs - k).start()

    def send_sibling(self):
        for c in range(self.pieces):
            self.to_pair(0, c).start()

    def receive(self, c):
        self.to_pair(0, c).wait_recv()
        total = self.part[self.rows_of(self.at.me, c), :].astype(F32)
        total += self.pair_in[0, self.chunk(c), :].astype(F32)
        for k in range(1, self.at.pairs):
            self.to_far(k, c, k).wait_recv()
            total += self.far_in[k - 1, self.chunk(c), :].astype(F32)
        return total

    def finish(self):
        for c in range(self.pieces):
            for k in range(self.at.pairs):
                self.to_pair(k, c).wait_send()
                if k:
                    self.to_far(k, c, self.at.pairs - k).wait_send()


def exchange_kernel(plan, *refs):
    refs = list(refs)

    def take(count):
        return [refs.pop(0) for _ in range(count)]

    r = Bag()
    held = {name: take(1)[0] for name in plan.inputs}
    r.raw = Bag(**held)
    helper_inputs = [take(len(h.inputs)) for h in plan.helpers]
    targets = {name: take(1)[0] for name in plan.outs}
    gathered = take(len(plan.gathers))
    helper_outs = [take(len(h.outs)) for h in plan.helpers]
    loaded = [name for name in plan.inputs if plan.need(name) is not None]
    for name in loaded + plan.outs + plan.scratch:
        setattr(r, name, take(1)[0])
    load_sem, store_sem = take(2)
    at = Members(plan.members)
    pairs, pieces = at.pairs, plan.pieces
    scatters = {}
    for name, (_, count, _) in plan.scatters.items():
        if name not in plan.inputs:
            setattr(r, name, take(1)[0])
        scatters[name] = Scatter(getattr(r, name), at, plan.rows, count, take(7))
    if plan.gathers:
        mine_refs = take(len(plan.gathers))
        give_send, give_recv, spread_send, spread_recv, keep_sem = take(5)
    helpers = []
    for h, inputs, outs in zip(plan.helpers, helper_inputs, helper_outs):
        helpers.append((h.bind(r, inputs, outs, take(len(h.scratch))), h.when))
    size = plan.rows // pieces

    def rows_of(member, c):
        return pl.ds(pl.multiple_of(member * plan.rows + c * size, size), size)

    def chunk(c):
        return pl.ds(c * size, size)

    loads = {}
    for i, name in enumerate(sorted(loaded, key=plan.need)):
        loads[name] = pltpu.make_async_copy(held[name], getattr(r, name), load_sem.at[i])
        loads[name].start()

    def arrive(stage):
        for name in list(loads):
            if plan.need(name) <= stage:
                loads.pop(name).wait()

    stores = []

    def flush(stage):
        for i, name in enumerate(plan.outs):
            if plan.done(name) == stage:
                store = pltpu.make_async_copy(getattr(r, name), targets[name], store_sem.at[i])
                store.start()
                stores.append(store)

    def point(stage):
        for steps, when in helpers:
            count = len(steps) - 1 if stage == END else when.get(stage, 0)
            for _ in range(min(count, len(steps))):
                steps.pop(0)()
        if stage == END:
            for steps, _ in helpers:
                while steps:
                    steps.pop(0)()
        flush(stage)

    def run_fill(i):
        if i < len(plan.fills):
            plan.fills[i](r)

    barrier = pltpu.get_barrier_semaphore()
    greeted = [{TENSOR: at.sibling}] + [{TENSOR: at.far(k)} for k in range(1, pairs)]
    if helpers:
        greeted += cross_devices(plan.ways)
    for device in greeted:
        pl.semaphore_signal(barrier, inc=1, device_id=device, device_id_type=MESH)
    pl.semaphore_wait(barrier, len(greeted))

    arrive(BEGIN)
    point(BEGIN)
    for i, phase in enumerate(plan.phases(r, at.order()) if plan.phases else []):
        arrive(i)
        phase()
        for name, (_, _, ready) in plan.scatters.items():
            for last, send in zip(
                ready, (scatters[name].send_across, scatters[name].send_far, scatters[name].send_sibling)
            ):
                if last == i:
                    send()
        point(i)
    arrive(SENT)
    if plan.phases:
        run_fill(0)
    point(SENT)
    if plan.extra_work:
        plan.extra_work(r, scatters)
        point(EXTRA)

    given, spreads, keeps = {}, {}, []
    for c in range(pieces):
        total = None
        if plan.phases:
            for name in plan.scatters:
                total = scatters[name].receive(c)
                break
        results = plan.work(r, c, chunk(c), total)
        for g, rows_ref in enumerate(gathered):
            own = mine_refs[g].at[chunk(c), :]
            there = rows_ref.at[rows_of(at.me, c), :]
            mine_refs[g][chunk(c), :] = results[g]
            for k in range(1, pairs):
                spreads[g, k, c] = member_copy(
                    own, there, spread_send.at[g, k - 1, c], spread_recv.at[g, pairs - k - 1, c], at.far(k)
                )
                spreads[g, k, c].start()
            given[g, 0, c] = member_copy(
                own, there, give_send.at[g, 0, c], give_recv.at[g, 0, c], at.sibling
            )
            given[g, 0, c].start()
            keeps.append(pltpu.make_async_copy(own, there, keep_sem.at[g, c]))
            keeps[-1].start()
        point(CHUNK + c)
    run_fill(1)
    point(SPREAD)
    for g, rows_ref in enumerate(gathered):
        for c in range(pieces):
            for k in range(1, pairs):
                block = rows_ref.at[rows_of(at.far(k), c), :]
                member_copy(
                    block, block, spread_send.at[g, k - 1, c], spread_recv.at[g, k - 1, c], at.far(k)
                ).wait_recv()
                given[g, k, c] = member_copy(
                    block, block, give_send.at[g, k, c], give_recv.at[g, k, c], at.sibling
                )
                given[g, k, c].start()
    point(GIVEN)
    for g, rows_ref in enumerate(gathered):
        for c in range(pieces):
            for k in range(pairs):
                block = rows_ref.at[rows_of(at.across(k) if k else at.sibling, c), :]
                member_copy(
                    block, block, give_send.at[g, k, c], give_recv.at[g, k, c], at.sibling
                ).wait_recv()
        for c in range(pieces):
            for k in range(pairs):
                given[g, k, c].wait_send()
            for k in range(1, pairs):
                spreads[g, k, c].wait_send()
    for scatter in scatters.values():
        scatter.finish()
    arrive(END)
    point(END)
    for store in stores + keeps:
        store.wait()


def exchange(
    name, number, members, ways, rows, depth, work, inputs, outs=None, need=None, done=None, scratch=None,
    phases=None, fills=(), scatters=None, extra_work=None, gathers=None, helpers=(), pieces=4,
):
    pairs = members // 2
    others = max(pairs - 1, 1)
    outs, scratch, need, done = outs or {}, scratch or {}, need or {}, done or {}
    gathers, scatters = gathers or [], scatters or {}
    hbm, vmem = pl.BlockSpec(memory_space=pl.ANY), pl.BlockSpec(memory_space=pltpu.VMEM)
    plan = Bag(
        inputs=list(inputs), outs=list(outs), scratch=list(scratch), gathers=gathers, helpers=list(helpers),
        members=members, ways=ways, rows=rows, pieces=pieces, scatters=scatters, extra_work=extra_work,
        phases=phases, fills=list(fills), work=work,
        need=lambda n: need.get(n, 0 if phases else BEGIN), done=lambda n: done.get(n, END),
    )
    staging = [pltpu.VMEM(a.shape, a.dtype) for n, a in inputs.items() if plan.need(n) is not None]
    staging += [pltpu.VMEM(*spec) for spec in outs.values()]
    staging += list(scratch.values())
    staging += [DMA((max(len(inputs), 1),)), DMA((max(len(outs), 1),))]
    for part, (width, chunks, _) in scatters.items():
        if part not in inputs:
            staging.append(pltpu.VMEM((members * rows, width), B16))
        staging += Scatter.scratch(members, rows, width, chunks)
    count = len(gathers)
    if count:
        staging += [pltpu.VMEM((rows, depth), B16)] * count
        staging += [
            DMA((count, pairs, pieces)), DMA((count, pairs, pieces)),
            DMA((count, others, pieces)), DMA((count, others, pieces)), DMA((count, pieces)),
        ]
    operands = list(inputs.values())
    shapes = [jax.ShapeDtypeStruct(*spec) for spec in outs.values()]
    shapes += [jax.ShapeDtypeStruct((members * rows, depth), B16)] * count
    spaces = [hbm] * len(shapes)
    for h in helpers:
        operands += h.inputs
        shapes += [jax.ShapeDtypeStruct(shape, dtype) for shape, dtype, _ in h.outs]
        spaces += [pl.BlockSpec(memory_space=space) for _, _, space in h.outs]
        staging += h.scratch
    results = pl.pallas_call(
        functools.partial(exchange_kernel, plan),
        out_shape=shapes,
        in_specs=[hbm] * len(operands),
        out_specs=spaces,
        scratch_shapes=staging,
        compiler_params=pltpu.CompilerParams(
            collective_id=number, has_side_effects=True, vmem_limit_bytes=VMEM_LIMIT
        ),
        cost_estimate=pl.CostEstimate(
            flops=20_000_000_000, bytes_accessed=50_000_000, transcendentals=0
        ),
        name=name,
    )(*operands)
    results = list(results)
    got = {n: results.pop(0) for n in list(outs) + list(gathers)}
    for h in helpers:
        h.results = [results.pop(0) for _ in h.outs]
    return Bag(**got)


def rms(rows, gain):
    scale = lax.rsqrt(jnp.mean(rows * rows, axis=-1, keepdims=True) + EPS)
    return rows * scale * gain


def rms_back(rows, gain, grad):
    scale = lax.rsqrt(jnp.mean(rows * rows, axis=-1, keepdims=True) + EPS)
    scaled = gain * grad
    mean = jnp.mean(scaled * rows, axis=-1, keepdims=True)
    return scale * scaled - rows * (scale * scale * scale * mean)


def gain_of(r, layer, row):
    ways = r.few.shape[1]
    return jnp.concatenate([r.few[layer, k, row : row + 1, :] for k in range(ways)], axis=1)


def layer_input(r, layer, at):
    if layer == 0:
        return r.acts_in[lax.axis_index(PIPE), at, :].astype(F32)
    return r.x[at, :].astype(F32)


def layer_cotangent(r, layer, at):
    if layer == 1:
        return r.out_grad[lax.axis_index(PIPE), at, :]
    return r.cotangent[at, :]


def work_first(r, c, at, total):
    return rms(layer_input(r, 0, at), gain_of(r, 0, 0)).astype(B16), layer_cotangent(r, 1, at)


def work_mid(layer, r, c, at, total):
    residual = layer_input(r, layer, at) + total
    r.residual[at, :] = residual
    return (rms(residual, gain_of(r, layer, 1)).astype(B16),)


def work_turn(r, c, at, total):
    out = (r.residual[at, :] + total).astype(B16)
    r.x[at, :] = out
    return (rms(out.astype(F32), gain_of(r, 1, 0)).astype(B16),)


def work_back_ffn(layer, r, c, at, total):
    residual = r.residual[at, :]
    grad = layer_cotangent(r, layer, at).astype(F32) + rms_back(
        residual, gain_of(r, layer, 1), total
    )
    r.d_residual[at, :] = grad
    return (grad.astype(B16),)


def work_back_mix(layer, r, c, at, total):
    step = rms_back(layer_input(r, layer, at), gain_of(r, layer, 0), total)
    grad = (r.d_residual[at, :] + step).astype(B16)
    r.x_grad[at, :] = grad
    return (grad,)


def work_shared(r, scatters):
    total = scatters[SHARED].receive(0)
    _, ways, block, _ = r.shared.shape
    for j in range(2 * ways):
        r.shared[j // ways, j % ways] = total[j * block : (j + 1) * block, :].astype(r.shared.dtype)


def work_last(r, scatters):
    r.last[...] = (r.residual[...] + scatters[LAST].receive(0)).astype(B16)
    work_shared(r, scatters)


def widen(block, axis, size):
    missing = size - block.shape[axis]
    if missing == 0:
        return block
    pads = [(0, 0)] * block.ndim
    pads[axis] = (0, missing)
    return jnp.pad(block, pads)


def on_device(
    acts_in, out_grad, mix_gain, w_mixer_in, w_query, w_shared, w_step, a_log, dt_bias, d_skip,
    w_mamba_out, w_attn_out, ffn_gain, w_gate_up, w_down,
):
    section = lax.axis_index(PIPE)
    member = lax.axis_index(TENSOR)
    members = lax.axis_size(TENSOR)
    dp = lax.axis_size(DP)
    heads = a_log.shape[1]
    real = heads * HD
    width = (heads + heads % 2) * HD
    q_real = w_query.shape[2]
    cols = Cols(width)
    units = w_gate_up.shape[3]
    rows, depth = acts_in.shape[1:]
    length = rows * members
    piece = depth // dp
    wide = cols.total - cols.b

    at_row = MixerRows(cols, members)
    q_heads = q_real // HD
    inner = jnp.concatenate(
        [widen(w_mixer_in[0, :, 0], 1, width), widen(w_mixer_in[0, :, 1], 1, width)], axis=1
    )
    share = lax.dynamic_slice_in_dim(w_shared[0], member * (piece // members), piece // members, 0)
    share = jnp.concatenate([share[:, at : at + LANES] for at in range(0, 4 * LANES, LANES)], axis=0)
    mixer_shard = jnp.concatenate(
        [fold_lanes(share)(piece), fold_lanes(widen(w_query[0], 1, LANES))(piece)]
        + [inner[:, at : at + piece] for at in range(0, 2 * width, piece)]
        + [widen(w_mamba_out[0], 0, width), widen(w_attn_out[0], 0, LANES)],
        axis=0,
    )
    steps = lax.dynamic_slice_in_dim(w_step[0], member * heads, heads, 1).T.astype(F32)
    ffn_shard = jnp.concatenate(
        [w_gate_up[0, :, j, at : at + piece] for j in range(2) for at in range(0, units, piece)]
        + [w_down[0]],
        axis=0,
    )
    few_shard = jnp.concatenate(
        [
            mix_gain.astype(F32), ffn_gain.astype(F32),
            widen(widen(jnp.concatenate([a_log, dt_bias, d_skip]), 1, piece), 0, 6),
            widen(steps, 0, 8),
        ],
        axis=0,
    )

    def run(name, number, work, inputs, outs, **more):
        return exchange(name, number, members, dp, rows, depth, work, inputs, outs, **more)

    half = piece // 2
    low_units = width + LANES
    block32, block16 = ((rows, depth), F32), ((rows, depth), B16)
    core_keeps = dict(
        proj=((length, cols.step), B16),
        step=((length, LANES), F32),
        y=((length, width), B16),
        lows=((length, low_units), B16),
        states=((length // STEP, NS, width), B16),
        lse=((length // TILE, 8, 2 * TILE), F32),
    )
    ffn_keeps = dict(gu=((length, 2 * units), B16), hidden=((length, units), B16))
    gu_spec, down_spec = ((2, dp, half, 2 * units), B16), ((2, dp, units // 2, piece), B16)
    cat_spec, out_spec = ((2, dp, half, cols.b), B16), ((2, dp, low_units // 2, piece), B16)
    shared_spec = ((2, dp, half // members, wide), B16 if half // members % 16 == 0 else F32)
    gain_row = ((8, depth), F32)
    fills_ffn = [
        lambda r: grad_columns(r.rows_ffn, r.dgu, r.g_gu),
        lambda r: grad_rows(r.hidden, r.rows_out, r.g_down),
    ]
    fill_cat = lambda r: mixer_columns(cols, members, r)
    fill_out = lambda r: grad_rows(r.lows, r.rows_back, r.g_out)

    load = Cargo(
        0, dp, mixer_shard,
        {BEGIN: 1, SENT: 2, CHUNK: 1, CHUNK + 1: 1, CHUNK + 2: 2, CHUNK + 3: 2, SPREAD: 2, GIVEN: 4},
        members, at_row.shared,
    )
    few = Few(dp, few_shard, {BEGIN: 2, SENT: 1})
    got = run(
        "first", 0, work_first, dict(acts_in=acts_in, out_grad=out_grad), {},
        gathers=dict(rows_mix=0, rows_out=0), helpers=[few, load],
    )
    few = few.result
    first = Bag(rows_mix=got.rows_mix, mixer=load.results[0], shared_w=load.results[1], acts_in=acts_in)
    second = Bag(rows_out=got.rows_out, out_grad=out_grad)
    for layer, k in enumerate((first, second)):
        x = dict(acts_in=acts_in) if layer == 0 else dict(x=second.x)
        load = Cargo(
            layer, dp, ffn_shard,
            {
                BEGIN: 1, 0: 1, 1: 1, 2: 1, 3: 2, 4: 1, 5: 1, 6: 2, 7: 2, SENT: 1, CHUNK: 1, CHUNK + 1: 1,
                CHUNK + 2: 1, SPREAD: 2,
            },
        )
        k.add(
            run(
                f"mixer{layer}", 1 + layer, functools.partial(work_mid, layer),
                dict(x, few=few, rows_mix=k.rows_mix, mixer=k.mixer, shared_w=k.shared_w),
                dict(core_keeps, residual=block32, rest=((depth, 6 * LANES), B16)),
                need=dict({n: SENT for n in x}, rows_mix=1),
                done=dict(rest=0, proj=1, step=1, y=3, states=3, lows=7, lse=7, residual=CHUNK + 3),
                scratch=dict(state=pltpu.VMEM((NS, width), F32)),
                phases=functools.partial(core_fwd_phases, cols, members, layer, q_heads),
                scatters={PART: (depth, 4, (4, 5, 6))}, gathers=dict(rows_ffn=0), helpers=[load],
            )
        )
        k.gates = load.result
        if layer == 0:
            load = Cargo(
                1, dp, mixer_shard,
                {
                    BEGIN: 1, 1: 1, 3: 1, SENT: 2, CHUNK: 2, CHUNK + 1: 1, CHUNK + 2: 1, CHUNK + 3: 1, SPREAD: 2,
                    GIVEN: 3,
                },
                members, at_row.shared,
            )
            got = run(
                "turn", 3, work_turn,
                dict(residual=k.residual, few=few, rows_ffn=k.rows_ffn, gates=k.gates),
                dict(ffn_keeps, x=block16),
                need=dict(residual=SENT, few=SENT), done=dict(gu=3, hidden=3, x=CHUNK + 3),
                phases=lambda r, order: by_blocks(order, rows, lambda at, m: ffn_forward(r, at, r.part)),
                scatters={PART: (depth, 4, (0, 1, 2))}, gathers=dict(rows_mix=0), helpers=[load],
            )
            k.gu, k.hidden = got.gu, got.hidden
            second.rows_mix, second.x = got.rows_mix, got.x
            second.mixer, second.shared_w = load.results

    def clear_gain(r):
        r.gain_ffn[...] = jnp.zeros_like(r.gain_ffn)

    def ffn_both(r, at, m):
        ffn_forward(r, at, r.ffn_part)
        ffn_backward(r, at)

    def ffn_both_phases(r, order):
        clear_gain(r)
        return by_blocks(order, rows, functools.partial(ffn_both, r))

    def ffn_back_phases(r, order):
        clear_gain(r)
        return by_blocks(order, rows, lambda at, m: ffn_backward(r, at))

    second.add(
        run(
            "ffn1", 4, functools.partial(work_back_ffn, 1),
            dict(
                out_grad=out_grad, residual=second.residual, few=few, rows_ffn=second.rows_ffn,
                rows_out=second.rows_out, gates=second.gates,
            ),
            dict(
                gain_ffn=gain_row, g_gu=gu_spec, g_down=down_spec, d_residual=block32,
                ffn_part=((length, depth), B16),
            ),
            need=dict(out_grad=SENT, residual=SENT, few=SENT),
            done=dict(ffn_part=3, gain_ffn=3, g_gu=SENT, d_residual=CHUNK + 3, g_down=SPREAD),
            scratch=dict(
                **{n: pltpu.VMEM(*spec) for n, spec in ffn_keeps.items()},
                dgu=pltpu.VMEM((length, 2 * units), B16),
            ),
            phases=ffn_both_phases,
            scatters={PART: (depth, 4, (0, 1, 2))}, fills=fills_ffn, gathers=dict(rows_back=0),
        )
    )

    core_scratch = dict(
        dproj=pltpu.VMEM((length, cols.total), B16),
        heads=pltpu.VMEM((8, LANES), F32),
        dcore=pltpu.VMEM((length, low_units), B16),
        grad_state=pltpu.VMEM((NS, width), F32),
        skip_sum=pltpu.VMEM((STEP, width), F32),
        dk_sum=pltpu.VMEM((length, LANES), F32),
        dv_sum=pltpu.VMEM((length, LANES), F32),
        folded=pltpu.VMEM((length, wide), B16),
        gain_column=pltpu.VMEM((depth, LANES), F32),
        staged=pltpu.VMEM((depth, wide), F32),
    )

    def core_inputs(k):
        return dict(
            few=few, rows_mix=k.rows_mix, mixer=k.mixer, rows_back=k.rows_back, d_residual=k.d_residual,
            gain_ffn=k.gain_ffn, proj=k.proj, step=k.step, y=k.y, lows=k.lows, states=k.states,
            lse=k.lse, rest=k.rest,
        )

    core_need = dict(
        lows=1, proj=2, lse=2, few=3, step=3, y=3, states=3, rows_mix=4, rest=4, gain_ffn=5, g_gu=2, g_down=1,
        d_residual=SENT, x=SENT, acts_in=SENT,
    )

    def core_phases(layer, r, order):
        return core_bwd_phases(cols, layer, members, (q_heads, heads), r, order)

    def from_input(pick):
        return lambda r: (pick(r.raw), pick(r))

    def from_kernel(pick):
        return lambda r: (pick(r), pick(r))

    take_gu, take_down = (lambda r: r.g_gu), (lambda r: r.g_down)
    take_cat, take_out, take_shared = (lambda r: r.g_cat), (lambda r: r.g_out), (lambda r: r.shared)

    first_acts = Settle(0, lambda r: r.raw.x, (rows, depth), {SENT: 1})
    def back_phases(layer, r, order):
        into, attend, scan, shared, *back = core_phases(layer, r, order)
        return [into, lambda: fill_out(r), attend, scan, lambda: fill_cat(r), shared] + back

    back_scatters = {PART: (depth, 4, (6, 7, 8)), SHARED: (wide, 1, (5, 6, 5))}
    hauls = [
        Haul(
            1, dp, [from_input(take_gu), from_input(take_down)], [gu_spec, down_spec],
            {BEGIN: 1, 2: 1, 3: 1, 4: 1, SENT: 1, CHUNK + 3: 1},
        ),
        Straight(1, dp, from_kernel(take_out), out_spec, {1: 1, SENT: 1}),
        Haul(
            1, dp, [from_kernel(take_cat)], [cat_spec], {4: 1, CHUNK: 1, CHUNK + 1: 1, CHUNK + 2: 1, CHUNK + 3: 1}, line=False
        ),
    ]
    inner = dict(g_cat=pltpu.VMEM(*cat_spec), g_out=pltpu.VMEM(*out_spec))
    got = run(
        "back1", 5, functools.partial(work_back_mix, 1),
        dict(
            core_inputs(second), x=second.x, g_gu=second.g_gu, g_down=second.g_down, ffn_part=second.ffn_part,
            residual=second.residual,
        ),
        dict(x_grad=block16, shared=shared_spec, last=block16),
        need=dict(core_need, residual=SENT),
        done=dict(x_grad=CHUNK + 3, shared=EXTRA, last=EXTRA),
        scratch=dict(core_scratch, **inner), phases=functools.partial(back_phases, 1),
        scatters=dict(back_scatters, ffn_part=(depth, 1, (0, 1, 0))), extra_work=work_last, gathers=dict(rows_out=0), helpers=hauls + [first_acts],
    )
    second.add(got)
    cat_sums = hauls[2].result
    second.sums = hauls[0].results + hauls[1].results

    hauls = [
        Haul(
            1, dp, [from_input(lambda r: r.cat_sums)], [cat_spec], {BEGIN: 1, CHUNK + 3: 1}, swap=False
        ),
        Haul(
            1, dp, [from_input(take_shared)], [shared_spec], {BEGIN: 1, 3: 1, SENT: 2, CHUNK + 1: 1, GIVEN: 1}
        ),
        Haul(
            0, dp, [from_kernel(take_gu)], [gu_spec], {SENT: 1, CHUNK + 3: 1, SPREAD: 1, GIVEN: 1},
            line=False,
        ),
    ]
    got = run(
        "ffn0", 6, functools.partial(work_back_ffn, 0),
        dict(
            cotangent=second.x_grad, residual=first.residual, few=few, rows_ffn=first.rows_ffn,
            rows_out=second.rows_out, gates=first.gates, gu=first.gu, hidden=first.hidden,
            cat_sums=cat_sums, shared=second.shared,
        ),
        dict(gain_ffn=gain_row, g_down=down_spec, d_residual=block32),
        need=dict(
            cotangent=SENT, residual=SENT, few=SENT, hidden=SENT, cat_sums=SENT, shared=3
        ),
        done=dict(gain_ffn=3, d_residual=CHUNK + 3, g_down=SPREAD),
        scratch=dict(dgu=pltpu.VMEM((length, 2 * units), B16), g_gu=pltpu.VMEM(*gu_spec)),
        phases=ffn_back_phases, fills=fills_ffn, scatters={PART: (depth, 4, (0, 1, 2))}, gathers=dict(rows_back=0),
        helpers=hauls,
    )
    gu_sums = hauls[2].result
    second.sums += hauls[0].results + hauls[1].results
    first.add(got)

    hauls = [
        Haul(0, dp, [from_input(lambda r: r.gu_sums)], [gu_spec], {BEGIN: 1, 6: 1}, swap=False),
        Haul(
            0, dp, [from_input(take_down)], [down_spec], {BEGIN: 1, 1: 1, 2: 2, 3: 1, SENT: 1}
        ),
        Haul(0, dp, [from_kernel(take_out)], [out_spec], {1: 1, 3: 2, 4: 2, CHUNK + 2: 1}),
        Haul(
            0, dp, [from_kernel(take_cat)], [cat_spec],
            {4: 1, 6: 1, SENT: 1, CHUNK: 1, CHUNK + 1: 1},
        ),
        Haul(0, dp, [from_kernel(take_shared)], [shared_spec], {EXTRA: 1, CHUNK + 2: 2, CHUNK + 3: 2}),
    ]
    x_grads = Place(
        lambda r: (r.x_grad, r.raw.x_grad1), (rows, depth), 0,
        {4: 1, CHUNK: 1, CHUNK + 1: 1, CHUNK + 2: 1, CHUNK + 3: 1},
    )
    second_acts = Settle(1, lambda r: r.raw.last, (rows, depth), {5: 1})
    run(
        "back0", 7, functools.partial(work_back_mix, 0),
        dict(core_inputs(first), acts_in=acts_in, x_grad1=second.x_grad, gu_sums=gu_sums, g_down=first.g_down,
            last=second.last),
        {},
        need=dict(core_need, x_grad1=None, gu_sums=3, last=None),
        scratch=dict(
            core_scratch, **inner, x_grad=pltpu.VMEM(*block16), shared=pltpu.VMEM(*shared_spec)
        ),
        phases=functools.partial(back_phases, 0), scatters=back_scatters, extra_work=work_shared, helpers=hauls + [x_grads, second_acts],
    )
    first.sums = [h.result for h in hauls]
    order = [0, 1, 3, 2, 4]
    g_gates, g_down, g_cat, g_out, g_shared = [
        jnp.where(section == 0, first.sums[i], second.sums[j]).astype(F32).reshape(
            (-1,) + first.sums[i].shape[2:]
        )
        for i, j in zip(order, (0, 1, 3, 2, 4))
    ]
    g_mixer = jnp.stack([g_cat[:, :real], g_cat[:, width : width + real]], axis=1)
    table = 2 * NS + 2 * KVH * HD
    g_gains = g_shared[:, table + GAINS_AT : table + GAINS_AT + 2].T
    g_heads = g_shared[:3, table + HEADS_AT : table + HEADS_AT + heads]
    return (
        jnp.where(section == 0, first_acts.result, second_acts.result)[None],
        x_grads.result[None],
        g_gains[None],
        g_mixer[None],
        g_cat[None, :, cols.q : cols.q + q_real],
        g_shared[None, :, :table],
        g_shared[None, :, table : table + HM],
        g_heads[None],
        g_out[None, :real],
        g_out[None, width : width + q_real],
        g_gates.reshape(1, piece, 2, units),
        g_down[None],
    )


def solution(mesh):
    rows = P(DP, TENSOR, None)
    by_dp, by_tensor, by_both = P(PIPE, DP), P(PIPE, TENSOR), P(PIPE, DP, TENSOR)
    wide, tall, whole = P(PIPE, DP, None, TENSOR), P(PIPE, TENSOR, DP), P(PIPE, DP, None)
    joint = P(PIPE, (DP, TENSOR), None)
    return jax.shard_map(
        on_device,
        mesh=mesh,
        in_specs=(
            rows, rows, by_dp, wide, by_both, whole, whole, by_tensor, by_tensor, by_tensor, tall, tall,
            by_dp, wide, tall,
        ),
        out_specs=(
            P(PIPE, DP, TENSOR, None), P(PIPE, DP, TENSOR, None), P(PIPE, None, (DP, TENSOR)),
            wide, by_both, joint, joint, P(PIPE, None, TENSOR), tall, tall, wide, tall,
        ),
        check_vma=False,
    )
```
